32 devices in a mesh: rows: 4 (over x, core), cols: 8 (over z, y).
Axes of the slice: x: 2, y: 2, z: 4, core: 2. Of those that a mesh axis runs over, the one named last changes fastest.
Arguments:
- tokens: bfloat16 [1280, 8192], P(('rows', 'cols')), may hold values from -6 to 6
- norm_gain: float32 [8192], replicated, may hold values from 0.1 to 1.9
- gate_weight: bfloat16 [8192, 14336], P('rows', 'cols'), may hold values from -0.09375 to 0.09375
- up_weight: bfloat16 [8192, 14336], P('rows', 'cols'), may hold values from -0.09375 to 0.09375
- down_weight: bfloat16 [14336, 8192], P('cols'), may hold values from -0.125 to 0.125
- gate_mask: int32 [128, 224], P('rows', 'cols'), may hold values 0 or 1
- up_mask: int32 [128, 224], P('rows', 'cols'), may hold values 0 or 1
- down_mask: int32 [224, 128], P('cols'), may hold values 0 or 1
Outputs:
- branch_out: bfloat16 [1280, 8192], P(('rows', 'cols'))
The draws below stay inside these ranges and needn't reach their ends.
All inputs are finite; a program needn't handle non-finite values. No bound on the sum of `gate_mask` or of `up_mask` or of `down_mask` on one device may be relied on, other than what follows from the above.
Results may differ from the reference program's by a relative error of at most 0.025.
Values may be sent and summed in bfloat16 or wider, within the bound.
No kernel may reach another device: no remote copies, remote signals or barrier semaphores. Data moves between devices by JAX's collectives and lax.ppermute only.
A program may use at most 256 MiB of HBM per device.

```python
import jax
import jax.numpy as jnp
from jax import lax

D = 8192
FF = 14336
BLOCK = 64
TOKENS = 1280
N_ROWS = 4
N_COLS = 8


def plant(entries, own_key, low, top_value):
    shape = entries.shape
    spot = [jax.random.randint(jax.random.fold_in(own_key, axis), (), 0, shape[axis]) for axis in range(len(shape))]
    entries = entries.at[tuple(spot)].set(low)
    longest = shape.index(max(shape))
    spot[longest] = (spot[longest] + 1) % shape[longest]
    return entries.at[tuple(spot)].set(top_value)


def levels(stream_key, shape, split, smallest, high):
    level = 1.0
    for position, shards_of in split:
        draws = jax.random.uniform(jax.random.fold_in(jax.random.fold_in(stream_key, 6), position), (shards_of,), jnp.float32, smallest / len(split), high / len(split))
        level = level * jnp.repeat(jnp.exp(draws), shape[position] // shards_of).reshape((-1,) + (1,) * (len(shape) - 1 - position))
    return level


def normal_values(key, dims, deviation, limit, pieces=(), kind=jnp.bfloat16):
    gain = levels(key, dims, pieces, -0.22, 0.18) if pieces else 1.0
    drawn = jax.random.normal(key, dims, jnp.float32) * deviation * gain
    return jnp.minimum(jnp.maximum(drawn, -limit), limit).astype(kind)


def setup_inputs(seed: int = 0) -> dict:
    streams_of = jax.random.split(jax.random.key(seed), 9)
    return {
        "tokens": normal_values(streams_of[0], (TOKENS, D), 1.0, 6.0, ((0, 32),)),
        "norm_gain": jnp.clip(1.0 + 0.18 * jax.random.normal(streams_of[1], (D,), jnp.float32), 0.1, 1.9),
        "gate_weight": normal_values(streams_of[2], (D, FF), (D // 2) ** -0.5, 0.09375, ((0, 4), (1, 8))),
        "up_weight": normal_values(streams_of[3], (D, FF), (D // 2) ** -0.5, 0.09375, ((0, 4), (1, 8))),
        "down_weight": normal_values(streams_of[4], (FF, D), (FF // 8) ** -0.5, 0.125, ((0, 8),)),
        "gate_mask": plant((jax.random.randint(streams_of[5], (D // BLOCK, FF // BLOCK), 0, 2) < 1).astype(jnp.int32), jax.random.fold_in(streams_of[5], 1), 0, 1),
        "up_mask": plant((jax.random.randint(streams_of[6], (D // BLOCK, FF // BLOCK), 0, 2) < 1).astype(jnp.int32), jax.random.fold_in(streams_of[6], 1), 0, 1),
        "down_mask": plant((jax.random.randint(streams_of[7], (FF // BLOCK, D // BLOCK), 0, 2) < 1).astype(jnp.int32), jax.random.fold_in(streams_of[7], 1), 0, 1),
    }


def expand(mask):
    return jnp.repeat(jnp.repeat(mask, BLOCK, 0), BLOCK, 1).astype(jnp.bfloat16)

def grouped_sum(left, right, groups):
    inner = left.shape[1] // groups
    left_groups = jnp.transpose(left.reshape(left.shape[0], groups, inner), (1, 0, 2))
    right_groups = right.reshape(groups, inner, right.shape[1])

    def add_group(total, pair):
        part = jnp.dot(pair[0], pair[1], preferred_element_type=jnp.float32).astype(jnp.bfloat16)
        part = lax.optimization_barrier(part)
        return (total + part.astype(jnp.float32), None)
    start = jnp.zeros((left.shape[0], right.shape[1]), jnp.float32)
    total, _ = lax.scan(add_group, start, (left_groups, right_groups))
    return total

def reference(tokens, norm_gain, gate_weight, up_weight, down_weight, gate_mask, up_mask, down_mask):
    values = tokens.astype(jnp.float32)
    meansq = lax.optimization_barrier(jnp.mean(values * values, axis=-1, keepdims=True))
    normed = (values * lax.rsqrt(meansq + 1e-05) * norm_gain).astype(jnp.bfloat16)
    gate_kept = gate_weight * expand(gate_mask)
    up_kept = up_weight * expand(up_mask)
    down_kept = down_weight * expand(down_mask)
    gate = grouped_sum(normed, gate_kept, N_ROWS)
    up = grouped_sum(normed, up_kept, N_ROWS)
    hidden = (jax.nn.silu(gate) * up).astype(jnp.bfloat16)
    total = grouped_sum(hidden, down_kept, N_COLS)
    return total.astype(jnp.bfloat16)
```

```python
import functools

import jax
import jax.numpy as jnp
from jax import lax
from jax.experimental import pallas as pl
from jax.experimental.pallas import tpu as pltpu
from jax.sharding import PartitionSpec as P

BLOCK = 64
CORES = 2
PLANES = 4
VMEM = 48 * 1024 * 1024
F32 = jnp.float32
BF16 = jnp.bfloat16


def tile_of(size, most):
    tile = most
    while size % tile:
        tile //= 2
    return tile


def spread(mask):
    return jnp.repeat(mask, BLOCK, 1).astype(F32)


def rms_normed(rows_in, norm_gain):
    values = rows_in.astype(F32)
    meansq = jnp.mean(values * values, axis=-1, keepdims=True)
    return (values * lax.rsqrt(meansq + 1e-05) * norm_gain).astype(BF16)


def params(*semantics):
    return pltpu.CompilerParams(dimension_semantics=semantics, vmem_limit_bytes=VMEM)


def cost(flops, moved):
    return pl.CostEstimate(flops=flops, bytes_accessed=moved, transcendentals=0)


def mask_kernel(weight_ref, mask_ref, kept_ref):
    for block in range(weight_ref.shape[0] // BLOCK):
        rows = pl.ds(block * BLOCK, BLOCK)
        keep = jnp.broadcast_to(mask_ref[block : block + 1, :], (BLOCK, weight_ref.shape[1]))
        kept_ref[rows, :] = weight_ref[rows, :] * keep.astype(BF16)


def masked(weight, mask, rows, columns):
    depth, width = weight.shape
    return pl.pallas_call(
        mask_kernel,
        grid=(depth // rows, width // columns),
        in_specs=[
            pl.BlockSpec((rows, columns), lambda i, j: (i, j)),
            pl.BlockSpec((rows // BLOCK, columns), lambda i, j: (i, j)),
        ],
        out_specs=pl.BlockSpec((rows, columns), lambda i, j: (i, j)),
        out_shape=jax.ShapeDtypeStruct(weight.shape, weight.dtype),
        compiler_params=params("arbitrary", "arbitrary"),
        cost_estimate=cost(weight.size, 4 * weight.size),
        name="masked",
    )(weight, spread(mask))


def gate_up_kernel(*refs):
    (*parts, gate_ref, up_ref, keep_ref, send_ref, all_rows) = refs
    half = parts[0].shape[0] // 2
    kept = half * len(parts)

    @pl.when(pl.program_id(0) == 0)
    def _():
        for place, part in enumerate(parts):
            all_rows[pl.ds(place * half, half), :] = part[:half, :]
            all_rows[pl.ds(kept + place * half, half), :] = part[half:, :]

    for which, weight_ref in enumerate((gate_ref, up_ref)):
        total = jnp.dot(all_rows[...], weight_ref[...], preferred_element_type=F32).astype(BF16)
        keep_ref[which] = total[:kept]
        send_ref[which] = total[kept:]


def gate_up(parts, gate_kept, up_kept):
    rows = sum(part.shape[0] for part in parts)
    depth, width = gate_kept.shape
    tile = tile_of(width, 256)
    half = jax.ShapeDtypeStruct((2, rows // 2, width), BF16)
    whole = pl.BlockSpec(parts[0].shape, lambda i: (0, 0))
    columns = pl.BlockSpec((depth, tile), lambda i: (0, i))
    result = pl.BlockSpec((2, rows // 2, tile), lambda i: (0, 0, i))
    return pl.pallas_call(
        gate_up_kernel,
        grid=(width // tile,),
        in_specs=[whole] * len(parts) + [columns] * 2,
        out_specs=[result] * 2,
        out_shape=[half] * 2,
        scratch_shapes=[pltpu.VMEM((rows, depth), BF16)],
        compiler_params=params("arbitrary"),
        cost_estimate=cost(4 * rows * depth * width, 4 * depth * width + 4 * rows * width),
        name="gate_up",
    )(*parts, gate_kept, up_kept)


def down_kernel(hidden_ref, weight_ref, partial_ref):
    total = jnp.dot(hidden_ref[...], weight_ref[...], preferred_element_type=F32)
    partial_ref[...] = total.reshape(partial_ref.shape).astype(BF16)


def down(hidden, down_kept, groups):
    rows, depth = hidden.shape
    width = down_kept.shape[1]
    tile = tile_of(width, 1024)
    return pl.pallas_call(
        down_kernel,
        grid=(width // tile,),
        in_specs=[
            pl.BlockSpec((rows, depth), lambda i: (0, 0)),
            pl.BlockSpec((depth, tile), lambda i: (0, i)),
        ],
        out_specs=pl.BlockSpec((groups, rows // groups, tile), lambda i: (0, 0, i)),
        out_shape=jax.ShapeDtypeStruct((groups, rows // groups, width), BF16),
        compiler_params=params("arbitrary"),
        cost_estimate=cost(2 * rows * depth * width, 2 * depth * width + 2 * rows * width),
        name="down",
    )(hidden, down_kept)


def swap(values, axis, size, step):
    return lax.ppermute(values, axis, [(place, place ^ step) for place in range(size)])


def body(row_count, col_count, tokens, norm_gain, gate_weight, up_weight, down_weight, gate_mask, up_mask, down_mask):
    chips = row_count // CORES
    per_plane = col_count // PLANES
    own, _ = tokens.shape
    features, width = gate_weight.shape
    row = lax.axis_index("rows")

    normed = rms_normed(tokens, norm_gain)
    order = [chip * CORES + core for core in range(CORES) for chip in range(chips)]
    blocks = []
    for step in order:
        block = lax.dynamic_slice_in_dim(normed, (row ^ step) * features, features, 1)
        blocks.append(swap(block, "rows", row_count, step) if step else block)
    mine = jnp.concatenate(blocks, 0)

    gate_kept = masked(gate_weight, gate_mask, tile_of(features, 512), width)
    up_kept = masked(up_weight, up_mask, tile_of(features, 512), width)
    down_kept = masked(down_weight, down_mask, down_weight.shape[0], tile_of(down_weight.shape[1], 1024))

    planes = [mine]
    for plane in range(1, PLANES):
        planes.append(swap(mine, "cols", col_count, plane * per_plane))

    total = None
    for plane in range(PLANES):
        parts = [planes[plane]]
        for step in range(1, per_plane):
            parts.append(swap(planes[plane], "cols", col_count, step))
        keep, send = gate_up(parts, gate_kept, up_kept)
        came = swap(send, "rows", row_count, 1)
        sums = (keep.astype(F32) + came.astype(F32)).reshape(2, per_plane, chips, own, width)
        both = sums[:, :, 0]
        for chip in range(1, chips):
            both = both + swap(sums[:, :, chip].astype(BF16), "rows", row_count, chip * CORES).astype(F32)
        hidden = (jax.nn.silu(both[0]) * both[1]).astype(BF16)
        partial = down(hidden.reshape(per_plane * own, width), down_kept, per_plane)
        summed = partial[0].astype(F32)
        for step in range(1, per_plane):
            summed = summed + swap(partial[step], "cols", col_count, step).astype(F32)
        if plane:
            summed = swap(summed.astype(BF16), "cols", col_count, plane * per_plane).astype(F32)
        total = summed if total is None else total + summed
    return total.astype(BF16)


def solution(mesh):
    return jax.shard_map(
        functools.partial(body, mesh.shape["rows"], mesh.shape["cols"]),
        mesh=mesh,
        in_specs=(
            P(("rows", "cols"), None),
            P(),
            P("rows", "cols"),
            P("rows", "cols"),
            P("cols", None),
            P("rows", "cols"),
            P("rows", "cols"),
            P("cols", None),
        ),
        out_specs=P(("rows", "cols"), None),
        check_vma=False,
    )
```

```python
import functools

import jax
import jax.numpy as jnp
from jax import lax
from jax.experimental import pallas as pl
from jax.experimental.pallas import tpu as pltpu
from jax.sharding import PartitionSpec as P

BLOCK = 64
CORES = 2
PLANES = 4
VMEM = 14 * 1024 * 1024
F32 = jnp.float32
BF16 = jnp.bfloat16


def tile_of(size, most):
    tile = most
    while size % tile:
        tile //= 2
    return tile


def spread(mask):
    return jnp.repeat(mask, BLOCK, 1).astype(F32)[:, None, :]


def rms_normed(rows_in, norm_gain):
    values = rows_in.astype(F32)
    meansq = jnp.mean(values * values, axis=-1, keepdims=True)
    return (values * lax.rsqrt(meansq + 1e-05) * norm_gain).astype(BF16)


def params(*semantics):
    return pltpu.CompilerParams(dimension_semantics=semantics, vmem_limit_bytes=VMEM)


HURRY = 4


def cost(flops, moved):
    return pl.CostEstimate(flops=flops // HURRY, bytes_accessed=moved // HURRY, transcendentals=0)


ANYWHERE = pl.BlockSpec(memory_space=pl.ANY)
INSIDE = pl.BlockSpec(memory_space=pltpu.VMEM)


def mask_kernel(core_ref, weight_ref, mask_ref, *refs):
    del core_ref
    kept_ref = refs[-1]
    for block in range(weight_ref.shape[0] // BLOCK):
        rows = pl.ds(block * BLOCK, BLOCK)
        keep = jnp.broadcast_to(mask_ref[block], (BLOCK, weight_ref.shape[1]))
        kept_ref[rows, :] = weight_ref[rows, :] * keep.astype(BF16)


def masked(weight, mask, rows, core, shares, after):
    depth, width = weight.shape
    width = width // shares
    mask = spread(mask)
    return pl.pallas_call(
        mask_kernel,
        grid_spec=pltpu.PrefetchScalarGridSpec(
            num_scalar_prefetch=1,
            grid=(depth // rows,),
            in_specs=[
                pl.BlockSpec((rows, width), lambda i, core: (i, core[0])),
                pl.BlockSpec((rows // BLOCK, 1, width), lambda i, core: (i, 0, core[0])),
            ]
            + [ANYWHERE] * len(after),
            out_specs=pl.BlockSpec((rows, width), lambda i, core: (i, 0)),
        ),
        out_shape=jax.ShapeDtypeStruct((depth, width), weight.dtype),
        compiler_params=params("arbitrary"),
        cost_estimate=cost(0, 4 * depth * width),
        name="masked",
    )(core, pltpu.with_memory_space_constraint(weight, pltpu.HBM), mask, *after)


def resident(values):
    return pltpu.with_memory_space_constraint(values, pltpu.VMEM)


def gate_up_kernel(part_count, after_count, *refs):
    parts, (gate_ref, up_ref) = refs[:part_count], refs[part_count : part_count + 2]
    keep_ref, *send_refs, all_rows = refs[part_count + 2 + after_count :]
    half = parts[0].shape[0] // 2
    kept = half * len(parts)
    for place, part in enumerate(parts):
        all_rows[pl.ds(place * half, half), :] = part[:half, :]
        all_rows[pl.ds(kept + place * half, half), :] = part[half:, :]
    tile = tile_of(gate_ref.shape[1], 256)

    @pl.loop(0, gate_ref.shape[1] // tile)
    def _(number):
        columns = pl.ds(pl.multiple_of(number * tile, tile), tile)
        for which, weight_ref in enumerate((gate_ref, up_ref)):
            total = jnp.dot(all_rows[...], weight_ref[:, columns], preferred_element_type=F32)
            total = total.reshape(2, *keep_ref.shape[1:4], tile).astype(BF16)
            keep_ref[which, :, :, :, columns] = total[0]
            send_refs[which][:, :, :, columns] = total[1]


def gate_up(parts, gate_kept, up_kept, chips, after):
    rows = sum(part.shape[0] for part in parts)
    depth, width = gate_kept.shape
    half = jax.ShapeDtypeStruct((2, len(parts), chips, rows // (2 * len(parts) * chips), width), BF16)
    return pl.pallas_call(
        functools.partial(gate_up_kernel, len(parts), len(after)),
        in_specs=[INSIDE] * (len(parts) + 2) + [ANYWHERE] * len(after),
        out_specs=[INSIDE] * 3,
        out_shape=[half] + [jax.ShapeDtypeStruct(half.shape[1:], BF16)] * 2,
        scratch_shapes=[pltpu.VMEM((rows, depth), BF16)],
        compiler_params=pltpu.CompilerParams(vmem_limit_bytes=VMEM),
        cost_estimate=cost(4 * rows * depth * width, 0),
        name="gate_up",
    )(*parts, resident(gate_kept), resident(up_kept), *after)


def down_kernel(after_count, own_ref, other_ref, weight_ref, *refs):
    *partial_refs, both = refs[after_count:]
    groups, own, depth = own_ref.shape
    rows = groups * own
    both[:rows, :] = own_ref[...].astype(F32).reshape(rows, depth).astype(BF16)
    both[rows:, :] = other_ref[...].astype(F32).reshape(rows, depth).astype(BF16)
    tile = tile_of(weight_ref.shape[1], 512)

    @pl.loop(0, weight_ref.shape[1] // tile)
    def _(number):
        columns = pl.ds(pl.multiple_of(number * tile, tile), tile)
        total = jnp.dot(both[...], weight_ref[:, columns], preferred_element_type=F32)
        total = total.reshape(CORES, groups, own, tile)
        for place, partial_ref in enumerate(partial_refs):
            partial_ref[:, :, columns] = total[:, place].astype(BF16)


def down(own, other, down_kept, after):
    groups, rows, depth = own.shape
    width = down_kept.shape[1]
    shape = (CORES, rows, width)
    return pl.pallas_call(
        functools.partial(down_kernel, len(after)),
        in_specs=[INSIDE] * 3 + [ANYWHERE] * len(after),
        out_specs=[INSIDE] * groups,
        out_shape=[jax.ShapeDtypeStruct(shape, BF16)] * groups,
        scratch_shapes=[pltpu.VMEM((CORES * groups * rows, depth), BF16)],
        compiler_params=pltpu.CompilerParams(vmem_limit_bytes=VMEM),
        cost_estimate=cost(2 * CORES * groups * rows * depth * width, 0),
        name="down",
    )(own, other, resident(down_kept), *after)


def sums_kernel(sizes, after_count, *refs):
    to_chips, to_hidden, to_rows = sizes
    refs = list(refs)
    ins = [[refs.pop(0) for _ in range(size)] for size in sizes]
    del refs[:after_count]

    if to_chips:
        keep_ref, *came_refs = ins[0]
        for chip in range(1, keep_ref.shape[2]):
            sent_ref = refs.pop(0)
            for which in range(2):
                for group in range(keep_ref.shape[1]):
                    came = came_refs[which][group, chip].astype(F32)
                    sent_ref[which, group] = (keep_ref[which, group, chip].astype(F32) + came).astype(BF16)
    if to_hidden:
        keep_ref, *came_refs = ins[1][:3]
        chip_refs = ins[1][3:]
        hidden_ref = refs.pop(0)
        for group in range(keep_ref.shape[1]):
            both = []
            for which in range(2):
                total = keep_ref[which, group, 0].astype(F32) + came_refs[which][group, 0].astype(F32)
                for chip_ref in chip_refs:
                    total = total + chip_ref[which, group].astype(F32)
                both.append(total)
            hidden_ref[group] = (jax.nn.silu(both[0]) * both[1]).astype(BF16)
    if to_rows:
        summed_ref = refs.pop(0)
        for core in range(CORES):
            total = ins[2][0][core].astype(F32)
            for ref in ins[2][1:]:
                total = total + ref[core].astype(F32)
            summed_ref[core] = total.astype(BF16)


def sums(to_chips, to_hidden, to_rows, after):
    shapes = []
    if to_chips:
        two, groups, chips, own, width = to_chips[0].shape
        shapes += [(two, groups, own, width)] * (chips - 1)
    if to_hidden:
        shapes.append((to_hidden[0].shape[1], *to_hidden[0].shape[3:]))
    if to_rows:
        shapes.append(to_rows[0].shape)
    given = [*to_chips, *to_hidden, *to_rows]
    results = list(pl.pallas_call(
        functools.partial(sums_kernel, (len(to_chips), len(to_hidden), len(to_rows)), len(after)),
        in_specs=[INSIDE] * len(given) + [ANYWHERE] * len(after),
        out_specs=[INSIDE] * len(shapes),
        out_shape=[jax.ShapeDtypeStruct(shape, BF16) for shape in shapes],
        compiler_params=pltpu.CompilerParams(vmem_limit_bytes=VMEM),
        cost_estimate=cost(0, 4000000),
        name="sums",
    )(*given, *after))
    sent = [results.pop(0) for _ in range(chips - 1)] if to_chips else []
    hidden = results.pop(0) if to_hidden else None
    summed = results.pop(0) if to_rows else None
    return sent, hidden, summed


def swap(values, axis, size, step):
    return lax.ppermute(values, axis, [(place, place ^ step) for place in range(size)])


def body(row_count, col_count, tokens, norm_gain, gate_weight, up_weight, down_weight, gate_mask, up_mask, down_mask):
    chips = row_count // CORES
    per_plane = col_count // PLANES
    features, width = gate_weight.shape
    row = lax.axis_index("rows")
    core = row % CORES
    place = jnp.reshape(core, (1,)).astype(jnp.int32)
    nowhere = jnp.zeros((1,), jnp.int32)

    normed = rms_normed(tokens, norm_gain)
    blocks = []
    for step in [chip * CORES + other for other in range(CORES) for chip in range(chips)]:
        block = lax.dynamic_slice_in_dim(normed, (row ^ step) * features, features, 1)
        blocks.append(swap(block, "rows", row_count, step) if step else block)
    mine = jnp.concatenate(blocks, 0)

    order = [0, *range(1, PLANES, 2), *range(2, PLANES, 2)]
    planes = {0: mine}
    for plane in order[1:]:
        planes[plane] = swap(mine, "cols", col_count, plane * per_plane)
    parts = {}
    for plane in order:
        parts[plane] = [planes[plane]]
        for step in range(1, per_plane):
            parts[plane].append(swap(planes[plane], "cols", col_count, step))

    gate_kept = masked(gate_weight, gate_mask, tile_of(features, 256), nowhere, 1, [])
    up_kept = masked(up_weight, up_mask, tile_of(features, 256), nowhere, 1, [gate_kept])

    halves, came, chip_sums, hiddens, others, partials, rows_in = {}, {}, {}, {}, {}, {}, {}
    last = [up_kept]
    down_kept = None
    arrived = []
    steps = len(order)
    for number in range(steps + 3):
        now, before, earlier, first = (
            order[at] if 0 <= at < steps else None for at in range(number, number - 4, -1)
        )
        if now is not None:
            halves[now] = gate_up(parts[now], gate_kept, up_kept, chips, last)
            came[now] = [swap(part, "rows", row_count, 1) for part in halves[now][1:]]
            last = [halves[now][0]]
        if number == 0:
            down_kept = masked(down_weight, down_mask, 2 * BLOCK, place, CORES, last + [planes[1], planes[order[2]]])
            last = [down_kept]
        if earlier is not None:
            partials[earlier] = down(hiddens[earlier], others[earlier], down_kept, last)
            last = [partials[earlier][0]]
            rows_in[earlier] = [partials[earlier][0]]
            for step in range(1, per_plane):
                rows_in[earlier].append(swap(partials[earlier][step], "cols", col_count, step))
        to_chips = [halves[now][0], *came[now]] if now is not None else []
        to_hidden = [halves[before][0], *came[before], *chip_sums[before]] if before is not None else []
        to_rows = rows_in[first] if first is not None else []
        sent, hidden, summed = sums(to_chips, to_hidden, to_rows, last)
        last = (sent + [hidden, summed])[:1]
        if sent:
            chip_sums[now] = [
                swap(part, "rows", row_count, (chip + 1) * CORES) for chip, part in enumerate(sent)
            ]
        if hidden is not None:
            hiddens[before] = hidden
            others[before] = swap(hidden, "rows", row_count, 1)
            last = [hidden]
        if summed is not None:
            last = [summed]
            arrived.append(swap(summed, "cols", col_count, first * per_plane) if first else summed)

    total = arrived[0].astype(F32)
    for part in arrived[1:]:
        total = total + part.astype(F32)
    mine_now = total[0].astype(BF16)
    other = swap(total[1].astype(BF16), "rows", row_count, 1)
    left = jnp.where(core == 0, mine_now, other)
    right = jnp.where(core == 0, other, mine_now)
    return jnp.concatenate([left, right], 1)


def solution(mesh):
    return jax.shard_map(
        functools.partial(body, mesh.shape["rows"], mesh.shape["cols"]),
        mesh=mesh,
        in_specs=(
            P(("rows", "cols"), None),
            P(),
            P("rows", "cols"),
            P("rows", "cols"),
            P("cols", None),
            P("rows", "cols"),
            P("rows", "cols"),
            P("cols", None),
        ),
        out_specs=P(("rows", "cols"), None),
        check_vma=False,
    )
```

```python
import functools

import jax
import jax.numpy as jnp
from jax import lax
from jax.experimental import pallas as pl
from jax.experimental.pallas import tpu as pltpu
from jax.sharding import PartitionSpec as P

BLOCK = 64
CORES = 2
PLANES = 4
VMEM = 12 * 1024 * 1024
F32 = jnp.float32
BF16 = jnp.bfloat16


def tile_of(size, most):
    tile = most
    while size % tile:
        tile //= 2
    return tile


def rms_normed(rows_in, norm_gain):
    values = rows_in.astype(F32)
    meansq = jnp.mean(values * values, axis=-1, keepdims=True)
    return (values * lax.rsqrt(meansq + 1e-05) * norm_gain).astype(BF16)


def params(*semantics):
    return pltpu.CompilerParams(dimension_semantics=semantics, vmem_limit_bytes=VMEM)


HURRY = 1000


def cost(flops, moved):
    return pl.CostEstimate(flops=flops // HURRY, bytes_accessed=moved // HURRY, transcendentals=0)


ANYWHERE = pl.BlockSpec(memory_space=pl.ANY)
INSIDE = pl.BlockSpec(memory_space=pltpu.VMEM)


def mask_kernel(after_count, core_ref, weight_ref, mask_ref, *refs):
    kept_ref, spread = refs[after_count:]
    depth, width = weight_ref.shape
    blocks = depth // BLOCK
    step = pl.program_id(0)

    @pl.when(step == 0)
    def _():
        marks = mask_ref.shape[1]
        first = core_ref[0] * (width // BLOCK)
        owner = lax.broadcasted_iota(jnp.int32, (marks, width), 1) // BLOCK + first
        chosen = (owner == lax.broadcasted_iota(jnp.int32, (marks, width), 0)).astype(F32)
        spread[...] = jnp.dot(mask_ref[...].astype(F32), chosen, preferred_element_type=F32)

    for block in range(blocks):
        rows = pl.ds(block * BLOCK, BLOCK)
        keep = jnp.broadcast_to(spread[pl.ds(step * blocks + block, 1), :], (BLOCK, width))
        kept_ref[rows, :] = weight_ref[rows, :] * keep.astype(BF16)


def masked(weight, mask, rows, core, shares, after):
    depth, width = weight.shape
    width = width // shares
    return pl.pallas_call(
        functools.partial(mask_kernel, len(after)),
        grid_spec=pltpu.PrefetchScalarGridSpec(
            num_scalar_prefetch=1,
            grid=(depth // rows,),
            in_specs=[
                pl.BlockSpec((rows, width), lambda i, core: (i, core[0])),
                pl.BlockSpec(mask.shape, lambda i, core: (0, 0)),
            ]
            + [ANYWHERE] * len(after),
            out_specs=pl.BlockSpec((rows, width), lambda i, core: (i, 0)),
            scratch_shapes=[pltpu.VMEM((mask.shape[0], width), F32)],
        ),
        out_shape=jax.ShapeDtypeStruct((depth, width), weight.dtype),
        compiler_params=params("arbitrary"),
        cost_estimate=cost(0, 4 * depth * width),
        name="masked",
    )(core, pltpu.with_memory_space_constraint(weight, pltpu.HBM), mask, *after)


def assemble_kernel(after_count, *refs):
    block_refs, mine_ref = refs[: -1 - after_count], refs[-1]
    rows = jnp.concatenate([block_ref[...].astype(F32) for block_ref in block_refs], 0)
    mine_ref[...] = rows.astype(BF16)


def assemble(blocks, after):
    shape = (sum(block.shape[0] for block in blocks), blocks[0].shape[1])
    return pl.pallas_call(
        functools.partial(assemble_kernel, len(after)),
        in_specs=[INSIDE] * len(blocks) + [ANYWHERE] * len(after),
        out_specs=INSIDE,
        out_shape=jax.ShapeDtypeStruct(shape, BF16),
        compiler_params=pltpu.CompilerParams(vmem_limit_bytes=VMEM // 2),
        cost_estimate=cost(0, 1000000),
        name="assemble",
    )(*blocks, *after)


def resident(values):
    return pltpu.with_memory_space_constraint(values, pltpu.VMEM)


def gate_up_kernel(part_count, after_count, *refs):
    parts, (gate_ref, up_ref) = refs[:part_count], refs[part_count : part_count + 2]
    keep_ref, near_ref, *far_refs, all_rows = refs[part_count + 2 + after_count :]
    half = parts[0].shape[0] // 2
    kept = half * len(parts)
    for place, part in enumerate(parts):
        all_rows[pl.ds(place * half, half), :] = part[:half, :]
        all_rows[pl.ds(kept + place * half, half), :] = part[half:, :]
    tile = tile_of(gate_ref.shape[1], 256)

    @pl.loop(0, gate_ref.shape[1] // tile)
    def _(number):
        columns = pl.ds(pl.multiple_of(number * tile, tile), tile)
        for which, weight_ref in enumerate((gate_ref, up_ref)):
            total = jnp.dot(all_rows[...], weight_ref[:, columns], preferred_element_type=F32)
            total = total.reshape(2, *keep_ref.shape[1:4], tile).astype(BF16)
            keep_ref[which, :, :, :, columns] = total[0]
            near_ref[which, :, :, columns] = total[1, :, 0]
            far_refs[which][:, :, :, columns] = total[1, :, 1:]


def gate_up(parts, gate_kept, up_kept, chips, after):
    rows = sum(part.shape[0] for part in parts)
    depth, width = gate_kept.shape
    groups, own = len(parts), rows // (2 * len(parts) * chips)
    shapes = [(2, groups, chips, own, width), (2, groups, own, width)] + [(groups, chips - 1, own, width)] * 2
    return pl.pallas_call(
        functools.partial(gate_up_kernel, len(parts), len(after)),
        in_specs=[INSIDE] * (len(parts) + 2) + [ANYWHERE] * len(after),
        out_specs=[INSIDE] * len(shapes),
        out_shape=[jax.ShapeDtypeStruct(shape, BF16) for shape in shapes],
        scratch_shapes=[pltpu.VMEM((rows, depth), BF16)],
        compiler_params=pltpu.CompilerParams(vmem_limit_bytes=VMEM // 2),
        cost_estimate=cost(4 * rows * depth * width, 0),
        name="gate_up",
    )(*parts, resident(gate_kept), resident(up_kept), *after)


def down_kernel(after_count, own_ref, other_ref, weight_ref, *refs):
    *partial_refs, both = refs[after_count:]
    groups, own, depth = own_ref.shape
    rows = groups * own
    both[:rows, :] = own_ref[...].astype(F32).reshape(rows, depth).astype(BF16)
    both[rows:, :] = other_ref[...].astype(F32).reshape(rows, depth).astype(BF16)
    tile = tile_of(weight_ref.shape[1], 512)

    @pl.loop(0, weight_ref.shape[1] // tile)
    def _(number):
        columns = pl.ds(pl.multiple_of(number * tile, tile), tile)
        total = jnp.dot(both[...], weight_ref[:, columns], preferred_element_type=F32)
        total = total.reshape(CORES, groups, own, tile)
        for place, partial_ref in enumerate(partial_refs):
            partial_ref[:, :, columns] = total[:, place].astype(BF16)


def down(own, other, down_kept, after):
    groups, rows, depth = own.shape
    width = down_kept.shape[1]
    shape = (CORES, rows, width)
    return pl.pallas_call(
        functools.partial(down_kernel, len(after)),
        in_specs=[INSIDE] * 3 + [ANYWHERE] * len(after),
        out_specs=[INSIDE] * groups,
        out_shape=[jax.ShapeDtypeStruct(shape, BF16)] * groups,
        scratch_shapes=[pltpu.VMEM((CORES * groups * rows, depth), BF16)],
        compiler_params=pltpu.CompilerParams(vmem_limit_bytes=VMEM // 2),
        cost_estimate=cost(2 * CORES * groups * rows * depth * width, 0),
        name="down",
    )(own, other, resident(down_kept), *after)


def sums_kernel(sizes, after_count, *refs):
    to_chips, to_hidden, to_rows = sizes
    refs = list(refs)
    ins = [[refs.pop(0) for _ in range(size)] for size in sizes]
    del refs[:after_count]

    if to_chips:
        keep_ref, *came_refs = ins[0]
        for chip in range(1, keep_ref.shape[2]):
            sent_ref = refs.pop(0)
            for which in range(2):
                for group in range(keep_ref.shape[1]):
                    came = came_refs[which][group, chip - 1].astype(F32)
                    sent_ref[which, group] = (keep_ref[which, group, chip].astype(F32) + came).astype(BF16)
    if to_hidden:
        keep_ref, came_ref, *chip_refs = ins[1]
        hidden_ref = refs.pop(0)
        for group in range(keep_ref.shape[1]):
            both = []
            for which in range(2):
                total = keep_ref[which, group, 0].astype(F32) + came_ref[which, group].astype(F32)
                for chip_ref in chip_refs:
                    total = total + chip_ref[which, group].astype(F32)
                both.append(total)
            hidden_ref[group] = (jax.nn.silu(both[0]) * both[1]).astype(BF16)
    if to_rows:
        summed_ref = refs.pop(0)
        for core in range(CORES):
            total = ins[2][0][core].astype(F32)
            for ref in ins[2][1:]:
                total = total + ref[core].astype(F32)
            summed_ref[core] = total.astype(BF16)


def sums(to_chips, to_hidden, to_rows, after):
    shapes = []
    if to_chips:
        two, groups, chips, own, width = to_chips[0].shape
        shapes += [(two, groups, own, width)] * (chips - 1)
    if to_hidden:
        shapes.append((to_hidden[0].shape[1], *to_hidden[0].shape[3:]))
    if to_rows:
        shapes.append(to_rows[0].shape)
    given = [*to_chips, *to_hidden, *to_rows]
    results = list(pl.pallas_call(
        functools.partial(sums_kernel, (len(to_chips), len(to_hidden), len(to_rows)), len(after)),
        in_specs=[INSIDE] * len(given) + [ANYWHERE] * len(after),
        out_specs=[INSIDE] * len(shapes),
        out_shape=[jax.ShapeDtypeStruct(shape, BF16) for shape in shapes],
        compiler_params=pltpu.CompilerParams(vmem_limit_bytes=VMEM // 2),
        cost_estimate=cost(0, 4000000),
        name="sums",
    )(*given, *after))
    sent = [results.pop(0) for _ in range(chips - 1)] if to_chips else []
    hidden = results.pop(0) if to_hidden else None
    summed = results.pop(0) if to_rows else None
    return sent, hidden, summed


def swap(values, axis, size, step):
    return lax.ppermute(values, axis, [(place, place ^ step) for place in range(size)])


def body(row_count, col_count, tokens, norm_gain, gate_weight, up_weight, down_weight, gate_mask, up_mask, down_mask):
    chips = row_count // CORES
    per_plane = col_count // PLANES
    features, width = gate_weight.shape
    row = lax.axis_index("rows")
    core = row % CORES
    place = jnp.reshape(core, (1,)).astype(jnp.int32)
    nowhere = jnp.zeros((1,), jnp.int32)

    normed = rms_normed(tokens, norm_gain)
    blocks = []
    for step in [chip * CORES + other for other in range(CORES) for chip in range(chips)]:
        block = lax.dynamic_slice_in_dim(normed, (row ^ step) * features, features, 1)
        blocks.append(swap(block, "rows", row_count, step) if step else block)
    gate_kept = masked(gate_weight, gate_mask, tile_of(features, 256), nowhere, 1, [normed])
    mine = assemble(blocks, [gate_kept])

    def behind(values, after):
        return lax.optimization_barrier((values, *after))[0] if after else values

    def by_plane(values, plane, after=()):
        return swap(behind(values, after), "cols", col_count, plane * per_plane)

    def by_row_of_plane(values, step, after=()):
        return swap(behind(values, after), "cols", col_count, step)

    def by_chip(values, chip, after=()):
        return swap(behind(values, after), "rows", row_count, chip * CORES)

    def by_core(values):
        return swap(values, "rows", row_count, 1)

    up_kept = masked(up_weight, up_mask, tile_of(features, 256), nowhere, 1, [mine])
    down_kept = masked(down_weight, down_mask, 2 * BLOCK, place, CORES, [up_kept])

    parts, halves, came, chip_sums, hiddens, others, rows_in, arrived, partials, near = ({} for _ in range(10))
    last = [down_kept]

    def forward(plane, after=()):
        parts[plane] = [planes[plane]]
        for step in range(1, per_plane):
            parts[plane].append(by_row_of_plane(planes[plane], step, after))

    def multiply_in(plane, after=()):
        halves[plane] = gate_up(parts[plane], gate_kept, up_kept, chips, last + list(after))
        came[plane] = [by_core(part) for part in halves[plane][2:]]
        last[:] = [halves[plane][0]]

    def multiply_out(plane, after=()):
        partials[plane] = down(hiddens[plane], others[plane], down_kept, last + list(after))
        last[:] = [partials[plane][0]]

    def send_rows(plane, after=()):
        rows_in[plane] = [partials[plane][0]]
        for step in range(1, per_plane):
            rows_in[plane].append(by_row_of_plane(partials[plane][step], step, after))

    def add(chip=None, hide=None, rows=None, after=(), chip_after=()):
        to_chips = [halves[chip][0], *came[chip]] if chip is not None else []
        to_hidden = [halves[hide][0], near[hide], *chip_sums[hide]] if hide is not None else []
        to_rows = rows_in[rows] if rows is not None else []
        sent, hidden, summed = sums(to_chips, to_hidden, to_rows, last + list(after))
        if chip is not None:
            chip_sums[chip] = [by_chip(part, number + 1, chip_after) for number, part in enumerate(sent)]
            near[chip] = by_core(behind(halves[chip][1], sent[:1]))
            last[:] = sent[:1]
        if hide is not None:
            hiddens[hide], others[hide] = hidden, by_core(hidden)
            last[:] = [hidden]
        if rows is not None:
            arrived[rows] = by_plane(summed, rows) if rows else summed
            last[:] = [summed]

    planes = {0: mine, 3: by_plane(mine, 3), 1: by_plane(mine, 1)}
    forward(0)
    multiply_in(0)
    planes[2] = by_plane(mine, 2, [planes[3], planes[1]])
    forward(3, last)
    add(chip=0, after=[planes[3], planes[1]])
    add(hide=0)
    forward(1, parts[3][1:])
    multiply_in(3)
    add(chip=3)
    forward(2, parts[1][1:] + last)
    multiply_in(1, [planes[2]])
    add(hide=3)
    add(chip=1)
    multiply_out(3)
    send_rows(3, parts[2][1:])
    multiply_in(2)
    add(hide=1)
    add(chip=2)
    multiply_out(0)
    send_rows(0, rows_in[3][1:])
    add(rows=3)
    multiply_out(1)
    add(hide=2)
    multiply_out(2)
    send_rows(2, rows_in[0][1:])
    add(rows=0, after=[arrived[3]])
    add(rows=2)
    send_rows(1, rows_in[2][1:] + last)
    add(rows=1)

    arrived = [arrived[plane] for plane in (0, 3, 1, 2)]
    total = arrived[0].astype(F32)
    for part in arrived[1:]:
        total = total + part.astype(F32)
    mine_now = total[0].astype(BF16)
    other = by_core(total[1].astype(BF16))
    left = jnp.where(core == 0, mine_now, other)
    right = jnp.where(core == 0, other, mine_now)
    return jnp.concatenate([left, right], 1)


def solution(mesh):
    return jax.shard_map(
        functools.partial(body, mesh.shape["rows"], mesh.shape["cols"]),
        mesh=mesh,
        in_specs=(
            P(("rows", "cols"), None),
            P(),
            P("rows", "cols"),
            P("rows", "cols"),
            P("cols", None),
            P("rows", "cols"),
            P("rows", "cols"),
            P("cols", None),
        ),
        out_specs=P(("rows", "cols"), None),
        check_vma=False,
    )
```

```python
import functools

import jax
import jax.numpy as jnp
from jax import lax
from jax.experimental import pallas as pl
from jax.experimental.pallas import tpu as pltpu
from jax.sharding import PartitionSpec as P

BLOCK = 64
CORES = 2
PLANES = 4
NEXT = ((0, 1), (1, 0), (2, 3), (3, 2))
ACROSS = ((1, 2), (2, 1))
BEYOND = ((1, 3), (2, 0))
OUTWARD = ((1, 0), (2, 3))
INWARD = ((0, 1), (3, 2))
VMEM = 12 * 1024 * 1024
F32 = jnp.float32
BF16 = jnp.bfloat16


def tile_of(size, most):
    tile = most
    while size % tile:
        tile //= 2
    return tile


def rms_normed(rows_in, norm_gain):
    values = rows_in.astype(F32)
    meansq = jnp.mean(values * values, axis=-1, keepdims=True)
    return (values * lax.rsqrt(meansq + 1e-05) * norm_gain).astype(BF16)


def params(*semantics):
    return pltpu.CompilerParams(dimension_semantics=semantics, vmem_limit_bytes=VMEM)


HURRY = 1000


def cost(flops, moved):
    return pl.CostEstimate(flops=flops // HURRY, bytes_accessed=moved // HURRY, transcendentals=0)


ANYWHERE = pl.BlockSpec(memory_space=pl.ANY)
TOKEN = jax.ShapeDtypeStruct((8, 128), F32)
INSIDE = pl.BlockSpec(memory_space=pltpu.VMEM)


def mask_kernel(after_count, core_ref, weight_ref, mask_ref, *refs):
    kept_ref, token_ref, spread = refs[after_count:]
    token_ref[...] = jnp.zeros_like(token_ref)
    depth, width = weight_ref.shape
    blocks = depth // BLOCK
    step = pl.program_id(0)

    @pl.when(step == 0)
    def _():
        marks = mask_ref.shape[1]
        first = core_ref[0] * (width // BLOCK)
        owner = lax.broadcasted_iota(jnp.int32, (marks, width), 1) // BLOCK + first
        chosen = (owner == lax.broadcasted_iota(jnp.int32, (marks, width), 0)).astype(F32)
        spread[...] = jnp.dot(mask_ref[...].astype(F32), chosen, preferred_element_type=F32)

    for block in range(blocks):
        rows = pl.ds(block * BLOCK, BLOCK)
        keep = jnp.broadcast_to(spread[pl.ds(step * blocks + block, 1), :], (BLOCK, width))
        kept_ref[rows, :] = weight_ref[rows, :] * keep.astype(BF16)


def masked(weight, mask, rows, core, shares, after):
    depth, width = weight.shape
    width = width // shares
    return pl.pallas_call(
        functools.partial(mask_kernel, len(after)),
        grid_spec=pltpu.PrefetchScalarGridSpec(
            num_scalar_prefetch=1,
            grid=(depth // rows,),
            in_specs=[
                pl.BlockSpec((rows, width), lambda i, core: (i, core[0])),
                pl.BlockSpec(mask.shape, lambda i, core: (0, 0)),
            ]
            + [ANYWHERE] * len(after),
            out_specs=[
                pl.BlockSpec((rows, width), lambda i, core: (i, 0)),
                pl.BlockSpec(TOKEN.shape, lambda i, core: (0, 0)),
            ],
            scratch_shapes=[pltpu.VMEM((mask.shape[0], width), F32)],
        ),
        out_shape=[jax.ShapeDtypeStruct((depth, width), weight.dtype), TOKEN],
        compiler_params=params("arbitrary"),
        cost_estimate=cost(0, 4 * depth * width),
        name="masked",
    )(core, pltpu.with_memory_space_constraint(weight, pltpu.HBM), mask, *after)


def assemble_kernel(after_count, *refs):
    block_refs, (mine_ref, token_ref) = refs[: -2 - after_count], refs[-2:]
    token_ref[...] = jnp.zeros_like(token_ref)
    rows = jnp.concatenate([block_ref[...].astype(F32) for block_ref in block_refs], 0)
    mine_ref[...] = rows.astype(BF16)


def assemble(blocks, after):
    shape = (sum(block.shape[0] for block in blocks), blocks[0].shape[1])
    return pl.pallas_call(
        functools.partial(assemble_kernel, len(after)),
        in_specs=[INSIDE] * len(blocks) + [ANYWHERE] * len(after),
        out_specs=[INSIDE] * 2,
        out_shape=[jax.ShapeDtypeStruct(shape, BF16), TOKEN],
        compiler_params=pltpu.CompilerParams(vmem_limit_bytes=VMEM // 2),
        cost_estimate=cost(0, 1000000),
        name="assemble",
    )(*blocks, *after)


def resident(values):
    return pltpu.with_memory_space_constraint(values, pltpu.VMEM)


def gate_up_kernel(part_count, after_count, *refs):
    parts, (gate_ref, up_ref) = refs[:part_count], refs[part_count : part_count + 2]
    keep_ref, near_ref, *far_refs, token_ref, all_rows = refs[part_count + 2 + after_count :]
    token_ref[...] = jnp.zeros_like(token_ref)
    half = parts[0].shape[0] // 2
    kept = half * len(parts)
    for place, part in enumerate(parts):
        all_rows[pl.ds(place * half, half), :] = part[:half, :]
        all_rows[pl.ds(kept + place * half, half), :] = part[half:, :]
    tile = tile_of(gate_ref.shape[1], 256)

    @pl.loop(0, gate_ref.shape[1] // tile)
    def _(number):
        columns = pl.ds(pl.multiple_of(number * tile, tile), tile)
        for which, weight_ref in enumerate((gate_ref, up_ref)):
            total = jnp.dot(all_rows[...], weight_ref[:, columns], preferred_element_type=F32)
            total = total.reshape(2, *keep_ref.shape[1:4], tile).astype(BF16)
            keep_ref[which, :, :, :, columns] = total[0]
            near_ref[which, :, :, columns] = total[1, :, 0]
            far_refs[which][:, :, :, columns] = total[1, :, 1:]


def gate_up(parts, gate_kept, up_kept, chips, after):
    rows = sum(part.shape[0] for part in parts)
    depth, width = gate_kept.shape
    groups, own = len(parts), rows // (2 * len(parts) * chips)
    shapes = [(2, groups, chips, own, width), (2, groups, own, width)] + [(groups, chips - 1, own, width)] * 2
    return pl.pallas_call(
        functools.partial(gate_up_kernel, len(parts), len(after)),
        in_specs=[INSIDE] * (len(parts) + 2) + [ANYWHERE] * len(after),
        out_specs=[INSIDE] * (len(shapes) + 1),
        out_shape=[jax.ShapeDtypeStruct(shape, BF16) for shape in shapes] + [TOKEN],
        scratch_shapes=[pltpu.VMEM((rows, depth), BF16)],
        compiler_params=pltpu.CompilerParams(vmem_limit_bytes=VMEM // 2),
        cost_estimate=cost(4 * rows * depth * width, 0),
        name="gate_up",
    )(*parts, resident(gate_kept), resident(up_kept), *after)


def down_kernel(after_count, own_ref, other_ref, weight_ref, *refs):
    *partial_refs, token_ref, both = refs[after_count:]
    token_ref[...] = jnp.zeros_like(token_ref)
    groups, own, depth = own_ref.shape
    rows = groups * own
    both[:rows, :] = own_ref[...].astype(F32).reshape(rows, depth).astype(BF16)
    both[rows:, :] = other_ref[...].astype(F32).reshape(rows, depth).astype(BF16)
    tile = tile_of(weight_ref.shape[1], 512)

    @pl.loop(0, weight_ref.shape[1] // tile)
    def _(number):
        columns = pl.ds(pl.multiple_of(number * tile, tile), tile)
        total = jnp.dot(both[...], weight_ref[:, columns], preferred_element_type=F32)
        total = total.reshape(CORES, groups, own, tile)
        for place, partial_ref in enumerate(partial_refs):
            partial_ref[:, :, columns] = total[:, place].astype(BF16)


def down(own, other, down_kept, after):
    groups, rows, depth = own.shape
    width = down_kept.shape[1]
    shape = (CORES, rows, width)
    return pl.pallas_call(
        functools.partial(down_kernel, len(after)),
        in_specs=[INSIDE] * 3 + [ANYWHERE] * len(after),
        out_specs=[INSIDE] * (groups + 1),
        out_shape=[jax.ShapeDtypeStruct(shape, BF16)] * groups + [TOKEN],
        scratch_shapes=[pltpu.VMEM((CORES * groups * rows, depth), BF16)],
        compiler_params=pltpu.CompilerParams(vmem_limit_bytes=VMEM // 2),
        cost_estimate=cost(2 * CORES * groups * rows * depth * width, 0),
        name="down",
    )(own, other, resident(down_kept), *after)


def sums_kernel(sizes, after_count, *refs):
    to_chips, to_hidden, *to_rows = sizes
    refs = list(refs)
    refs.pop()[...] = jnp.zeros(TOKEN.shape, F32)
    ins = [[refs.pop(0) for _ in range(size)] for size in sizes]
    del refs[:after_count]

    if to_chips:
        keep_ref, *came_refs = ins[0]
        for chip in range(1, keep_ref.shape[2]):
            sent_ref = refs.pop(0)
            for which in range(2):
                for group in range(keep_ref.shape[1]):
                    came = came_refs[which][group, chip - 1].astype(F32)
                    sent_ref[which, group] = (keep_ref[which, group, chip].astype(F32) + came).astype(BF16)
    if to_hidden:
        keep_ref, came_ref, *chip_refs = ins[1]
        hidden_ref = refs.pop(0)
        for group in range(keep_ref.shape[1]):
            both = []
            for which in range(2):
                total = keep_ref[which, group, 0].astype(F32) + came_ref[which, group].astype(F32)
                for chip_ref in chip_refs:
                    total = total + chip_ref[which, group].astype(F32)
                both.append(total)
            hidden_ref[group] = (jax.nn.silu(both[0]) * both[1]).astype(BF16)
    for part_refs in ins[2:]:
        summed_ref = refs.pop(0)
        for core in range(CORES):
            total = part_refs[0][core].astype(F32)
            for part_ref in part_refs[1:]:
                total = total + part_ref[core].astype(F32)
            summed_ref[core] = total.astype(BF16)


def sums(to_chips, to_hidden, to_rows, after):
    shapes = []
    if to_chips:
        two, groups, chips, own, width = to_chips[0].shape
        shapes += [(two, groups, own, width)] * (chips - 1)
    if to_hidden:
        shapes.append((to_hidden[0].shape[1], *to_hidden[0].shape[3:]))
    shapes += [parts[0].shape for parts in to_rows]
    given = [to_chips, to_hidden, *to_rows]
    sizes = tuple(len(parts) for parts in given)
    given = [part for parts in given for part in parts]
    results = list(pl.pallas_call(
        functools.partial(sums_kernel, sizes, len(after)),
        in_specs=[INSIDE] * len(given) + [ANYWHERE] * len(after),
        out_specs=[INSIDE] * (len(shapes) + 1),
        out_shape=[jax.ShapeDtypeStruct(shape, BF16) for shape in shapes] + [TOKEN],
        compiler_params=pltpu.CompilerParams(vmem_limit_bytes=VMEM // 2),
        cost_estimate=cost(0, 4000000),
        name="sums",
    )(*given, *after))
    token = results.pop()
    sent = [results.pop(0) for _ in range(chips - 1)] if to_chips else []
    hidden = results.pop(0) if to_hidden else None
    return sent, hidden, results, token


def swap(values, axis, size, step):
    return lax.ppermute(values, axis, [(place, place ^ step) for place in range(size)])


def body(row_count, col_count, tokens, norm_gain, gate_weight, up_weight, down_weight, gate_mask, up_mask, down_mask):
    chips = row_count // CORES
    per_plane = col_count // PLANES
    features, width = gate_weight.shape
    row = lax.axis_index("rows")
    core = row % CORES
    place = jnp.reshape(core, (1,)).astype(jnp.int32)
    nowhere = jnp.zeros((1,), jnp.int32)

    normed = rms_normed(tokens, norm_gain)
    blocks = []
    for step in [chip * CORES + other for other in range(CORES) for chip in range(chips)]:
        block = lax.dynamic_slice_in_dim(normed, (row ^ step) * features, features, 1)
        blocks.append(swap(block, "rows", row_count, step) if step else block)
    gate_kept, token = masked(gate_weight, gate_mask, tile_of(features, 256), nowhere, 1, [normed])
    mine, token = assemble(blocks, [token])

    def behind(values, after):
        return lax.optimization_barrier((values, *after))[0] if after else values

    def by_plane(values, planes, after=()):
        pairs = [(a * per_plane + b, c * per_plane + b) for a, c in planes for b in range(per_plane)]
        return lax.ppermute(behind(values, after), "cols", pairs)

    def by_row_of_plane(values, step, after=()):
        return swap(behind(values, after), "cols", col_count, step)

    def by_chip(values, chip, after=()):
        return swap(behind(values, after), "rows", row_count, chip * CORES)

    def by_core(values, after=()):
        return swap(behind(values, after), "rows", row_count, 1)

    inner = (lax.axis_index("cols") // per_plane) % 3 != 0
    parts, halves, near, came, chip_sums, hiddens, others, rows_in, partials = ({} for _ in range(9))
    last = [token]

    def forward(plane, values, after=()):
        parts[plane] = [values]
        for step in range(1, per_plane):
            parts[plane].append(by_row_of_plane(values, step, after))

    def multiply_in(plane, after=(), send_after=()):
        *halves[plane], last[0] = gate_up(parts[plane], gate_kept, up_kept, chips, last + list(after))
        came[plane] = [by_core(part, send_after) for part in halves[plane][2:]]

    def multiply_out(plane, after=(), send_after=()):
        *partials[plane], last[0] = down(hiddens[plane], others[plane], down_kept, last + list(after))
        rows_in[plane] = [partials[plane][0]]
        for step in range(1, per_plane):
            rows_in[plane].append(by_row_of_plane(partials[plane][step], step, send_after))

    def to_chips(plane, send_after=()):
        sent, _, _, last[0] = sums([halves[plane][0], *came[plane]], [], [], last)
        chip_sums[plane] = [by_chip(part, number + 1, send_after) for number, part in enumerate(sent)]
        near[plane] = by_core(halves[plane][1], last)

    def to_hidden(plane):
        _, hiddens[plane], _, last[0] = sums([], [halves[plane][0], near[plane], *chip_sums[plane]], [], last)
        others[plane] = by_core(hiddens[plane])

    def to_rows(*lists, after=()):
        _, _, summed, last[0] = sums([], [], lists, last + list(after))
        return summed

    next_mine = by_plane(mine, NEXT)
    across_mine = by_plane(mine, ACROSS)
    forward(0, mine)
    up_kept, last[0] = masked(up_weight, up_mask, tile_of(features, 256), nowhere, 1, last)
    across_next = by_plane(next_mine, ACROSS, last)
    outward_mine = by_plane(across_mine, OUTWARD, last)
    forward(1, next_mine, [*parts[0][1:], *last])
    down_kept, last[0] = masked(
        down_weight, down_mask, 2 * BLOCK, place, CORES, last + [next_mine, across_mine, *parts[0][1:]]
    )
    two_away = jnp.where(inner, across_next, outward_mine)
    outward_next = by_plane(across_next, OUTWARD, last)
    forward(2, two_away, parts[1][1:])
    multiply_in(1, [across_next, outward_mine])
    to_chips(1)
    three_away = jnp.where(inner, across_mine, outward_next)
    forward(3, three_away, [*parts[2][1:], *last])
    multiply_in(2, [near[1]])
    to_hidden(1)
    to_chips(2)
    multiply_out(1, send_after=parts[3][1:])
    multiply_in(3, [near[2]])
    to_hidden(2)
    to_chips(3)
    multiply_out(2, send_after=rows_in[1][1:])
    (one,) = to_rows(rows_in[1])
    next_one = by_plane(one, NEXT)
    multiply_in(0, [near[3]], chip_sums[3])
    to_hidden(3)
    multiply_out(3, send_after=rows_in[2][1:])
    (two,) = to_rows(rows_in[2], after=[next_one])
    inward_two = by_plane(two, INWARD)
    to_chips(0)
    three, three_and_two = to_rows(rows_in[3], [*rows_in[3], inward_two])
    inward_three = by_plane(three, INWARD)
    across_three = by_plane(three_and_two, ACROSS)
    to_hidden(0)
    multiply_out(0, send_after=rows_in[3][1:])
    (two_and_three,) = to_rows([two, inward_three])
    beyond_two = by_plane(two_and_three, BEYOND)
    arrived = [*rows_in[0], next_one, across_three, beyond_two]

    total = arrived[0].astype(F32)
    for part in arrived[1:]:
        total = total + part.astype(F32)
    mine_now = total[0].astype(BF16)
    other = by_core(total[1].astype(BF16))
    left = jnp.where(core == 0, mine_now, other)
    right = jnp.where(core == 0, other, mine_now)
    return jnp.concatenate([left, right], 1)


def solution(mesh):
    return jax.shard_map(
        functools.partial(body, mesh.shape["rows"], mesh.shape["cols"]),
        mesh=mesh,
        in_specs=(
            P(("rows", "cols"), None),
            P(),
            P("rows", "cols"),
            P("rows", "cols"),
            P("cols", None),
            P("rows", "cols"),
            P("rows", "cols"),
            P("cols", None),
        ),
        out_specs=P(("rows", "cols"), None),
        check_vma=False,
    )
```

```python
import functools

import jax
import jax.numpy as jnp
from jax import lax
from jax.experimental import pallas as pl
from jax.experimental.pallas import tpu as pltpu
from jax.sharding import PartitionSpec as P

BLOCK = 64
CORES = 2
PLANES = 4
VMEM = 12 * 1024 * 1024
F32 = jnp.float32
BF16 = jnp.bfloat16


def tile_of(size, most):
    tile = most
    while size % tile:
        tile //= 2
    return tile


def rms_normed(rows_in, norm_gain):
    values = rows_in.astype(F32)
    meansq = jnp.mean(values * values, axis=-1, keepdims=True)
    return (values * lax.rsqrt(meansq + 1e-05) * norm_gain).astype(BF16)


def params(*semantics):
    return pltpu.CompilerParams(dimension_semantics=semantics, vmem_limit_bytes=VMEM)


HURRY = 1000


def cost(flops, moved):
    return pl.CostEstimate(flops=flops // HURRY, bytes_accessed=moved // HURRY, transcendentals=0)


ANYWHERE = pl.BlockSpec(memory_space=pl.ANY)
TOKEN = jax.ShapeDtypeStruct((8, 128), F32)
INSIDE = pl.BlockSpec(memory_space=pltpu.VMEM)


def mask_kernel(after_count, core_ref, weight_ref, mask_ref, *refs):
    kept_ref, token_ref, spread = refs[after_count:]
    token_ref[...] = jnp.zeros_like(token_ref)
    depth, width = weight_ref.shape
    blocks = depth // BLOCK
    step = pl.program_id(0)

    @pl.when(step == 0)
    def _():
        marks = mask_ref.shape[1]
        first = core_ref[0] * (width // BLOCK)
        owner = lax.broadcasted_iota(jnp.int32, (marks, width), 1) // BLOCK + first
        chosen = (owner == lax.broadcasted_iota(jnp.int32, (marks, width), 0)).astype(F32)
        spread[...] = jnp.dot(mask_ref[...].astype(F32), chosen, preferred_element_type=F32)

    for block in range(blocks):
        rows = pl.ds(block * BLOCK, BLOCK)
        keep = jnp.broadcast_to(spread[pl.ds(step * blocks + block, 1), :], (BLOCK, width))
        kept_ref[rows, :] = weight_ref[rows, :] * keep.astype(BF16)


def masked(weight, mask, rows, core, shares, after):
    depth, width = weight.shape
    width = width // shares
    return pl.pallas_call(
        functools.partial(mask_kernel, len(after)),
        grid_spec=pltpu.PrefetchScalarGridSpec(
            num_scalar_prefetch=1,
            grid=(depth // rows,),
            in_specs=[
                pl.BlockSpec((rows, width), lambda i, core: (i, core[0])),
                pl.BlockSpec(mask.shape, lambda i, core: (0, 0)),
            ]
            + [ANYWHERE] * len(after),
            out_specs=[
                pl.BlockSpec((rows, width), lambda i, core: (i, 0)),
                pl.BlockSpec(TOKEN.shape, lambda i, core: (0, 0)),
            ],
            scratch_shapes=[pltpu.VMEM((mask.shape[0], width), F32)],
        ),
        out_shape=[jax.ShapeDtypeStruct((depth, width), weight.dtype), TOKEN],
        compiler_params=params("arbitrary"),
        cost_estimate=cost(0, 4 * depth * width),
        name="masked",
    )(core, pltpu.with_memory_space_constraint(weight, pltpu.HBM), mask, *after)


def assemble_kernel(after_count, *refs):
    block_refs, (mine_ref, token_ref) = refs[: -2 - after_count], refs[-2:]
    token_ref[...] = jnp.zeros_like(token_ref)
    rows = jnp.concatenate([block_ref[...].astype(F32) for block_ref in block_refs], 0)
    mine_ref[...] = rows.astype(BF16)


def assemble(blocks, after):
    shape = (sum(block.shape[0] for block in blocks), blocks[0].shape[1])
    return pl.pallas_call(
        functools.partial(assemble_kernel, len(after)),
        in_specs=[INSIDE] * len(blocks) + [ANYWHERE] * len(after),
        out_specs=[INSIDE] * 2,
        out_shape=[jax.ShapeDtypeStruct(shape, BF16), TOKEN],
        compiler_params=pltpu.CompilerParams(vmem_limit_bytes=VMEM // 2),
        cost_estimate=cost(0, 1000000),
        name="assemble",
    )(*blocks, *after)


def resident(values):
    return pltpu.with_memory_space_constraint(values, pltpu.VMEM)


def gate_up_kernel(part_count, after_count, *refs):
    parts, (gate_ref, up_ref) = refs[:part_count], refs[part_count : part_count + 2]
    keep_ref, near_ref, far_ref, token_ref, all_rows = refs[part_count + 2 + after_count :]
    token_ref[...] = jnp.zeros_like(token_ref)
    half = parts[0].shape[0] // 2
    kept = half * len(parts)
    for place, part in enumerate(parts):
        all_rows[pl.ds(place * half, half), :] = part[:half, :]
        all_rows[pl.ds(kept + place * half, half), :] = part[half:, :]
    tile = tile_of(gate_ref.shape[1], 256)

    @pl.loop(0, gate_ref.shape[1] // tile)
    def _(number):
        columns = pl.ds(pl.multiple_of(number * tile, tile), tile)
        for which, weight_ref in enumerate((gate_ref, up_ref)):
            total = jnp.dot(all_rows[...], weight_ref[:, columns], preferred_element_type=F32)
            total = total.reshape(2, *keep_ref.shape[1:4], tile).astype(BF16)
            keep_ref[which, :, :, :, columns] = total[0]
            near_ref[which, :, :, columns] = total[1, :, 0]
            far_ref[which, :, :, :, columns] = total[1, :, 1:]


def gate_up(parts, gate_kept, up_kept, chips, after):
    rows = sum(part.shape[0] for part in parts)
    depth, width = gate_kept.shape
    groups, own = len(parts), rows // (2 * len(parts) * chips)
    shapes = [(2, groups, chips, own, width), (2, groups, own, width), (2, groups, chips - 1, own, width)]
    return pl.pallas_call(
        functools.partial(gate_up_kernel, len(parts), len(after)),
        in_specs=[INSIDE] * (len(parts) + 2) + [ANYWHERE] * len(after),
        out_specs=[INSIDE] * (len(shapes) + 1),
        out_shape=[jax.ShapeDtypeStruct(shape, BF16) for shape in shapes] + [TOKEN],
        scratch_shapes=[pltpu.VMEM((rows, depth), BF16)],
        compiler_params=pltpu.CompilerParams(vmem_limit_bytes=VMEM // 2),
        cost_estimate=cost(4 * rows * depth * width, 0),
        name="gate_up",
    )(*parts, resident(gate_kept), resident(up_kept), *after)


def down_kernel(after_count, own_ref, other_ref, weight_ref, *refs):
    *partial_refs, token_ref, both = refs[after_count:]
    token_ref[...] = jnp.zeros_like(token_ref)
    groups, own, depth = own_ref.shape
    rows = groups * own
    both[:rows, :] = own_ref[...].astype(F32).reshape(rows, depth).astype(BF16)
    both[rows:, :] = other_ref[...].astype(F32).reshape(rows, depth).astype(BF16)
    tile = tile_of(weight_ref.shape[1], 512)

    @pl.loop(0, weight_ref.shape[1] // tile)
    def _(number):
        columns = pl.ds(pl.multiple_of(number * tile, tile), tile)
        total = jnp.dot(both[...], weight_ref[:, columns], preferred_element_type=F32)
        total = total.reshape(CORES, groups, own, tile)
        for place, partial_ref in enumerate(partial_refs):
            partial_ref[:, :, columns] = total[:, place].astype(BF16)


def down(own, other, down_kept, after):
    groups, rows, depth = own.shape
    width = down_kept.shape[1]
    shape = (CORES, rows, width)
    return pl.pallas_call(
        functools.partial(down_kernel, len(after)),
        in_specs=[INSIDE] * 3 + [ANYWHERE] * len(after),
        out_specs=[INSIDE] * (groups + 1),
        out_shape=[jax.ShapeDtypeStruct(shape, BF16)] * groups + [TOKEN],
        scratch_shapes=[pltpu.VMEM((CORES * groups * rows, depth), BF16)],
        compiler_params=pltpu.CompilerParams(vmem_limit_bytes=VMEM // 2),
        cost_estimate=cost(2 * CORES * groups * rows * depth * width, 0),
        name="down",
    )(own, other, resident(down_kept), *after)


def sums_kernel(sizes, after_count, *refs):
    to_chips, to_hidden, *to_rows = sizes
    refs = list(refs)
    refs.pop()[...] = jnp.zeros(TOKEN.shape, F32)
    ins = [[refs.pop(0) for _ in range(size)] for size in sizes]
    del refs[:after_count]

    if to_chips:
        keep_ref, came_ref = ins[0]
        for chip in range(1, keep_ref.shape[2]):
            sent_ref = refs.pop(0)
            for which in range(2):
                for group in range(keep_ref.shape[1]):
                    came = came_ref[which, group, chip - 1].astype(F32)
                    sent_ref[which, group] = (keep_ref[which, group, chip].astype(F32) + came).astype(BF16)
    if to_hidden:
        keep_ref, came_ref, *chip_refs = ins[1]
        hidden_ref = refs.pop(0)
        for group in range(keep_ref.shape[1]):
            both = []
            for which in range(2):
                total = keep_ref[which, group, 0].astype(F32) + came_ref[which, group].astype(F32)
                for chip_ref in chip_refs:
                    total = total + chip_ref[which, group].astype(F32)
                both.append(total)
            hidden_ref[group] = (jax.nn.silu(both[0]) * both[1]).astype(BF16)
    for part_refs in ins[2:]:
        summed_ref = refs.pop(0)
        for core in range(CORES):
            total = part_refs[0][core].astype(F32)
            for part_ref in part_refs[1:]:
                total = total + part_ref[core].astype(F32)
            summed_ref[core] = total.astype(BF16)


def sums(to_chips, to_hidden, to_rows, after):
    shapes = []
    if to_chips:
        two, groups, chips, own, width = to_chips[0].shape
        shapes += [(two, groups, own, width)] * (chips - 1)
    if to_hidden:
        shapes.append((to_hidden[0].shape[1], *to_hidden[0].shape[3:]))
    shapes += [parts[0].shape for parts in to_rows]
    given = [to_chips, to_hidden, *to_rows]
    sizes = tuple(len(parts) for parts in given)
    given = [part for parts in given for part in parts]
    results = list(pl.pallas_call(
        functools.partial(sums_kernel, sizes, len(after)),
        in_specs=[INSIDE] * len(given) + [ANYWHERE] * len(after),
        out_specs=[INSIDE] * (len(shapes) + 1),
        out_shape=[jax.ShapeDtypeStruct(shape, BF16) for shape in shapes] + [TOKEN],
        compiler_params=pltpu.CompilerParams(vmem_limit_bytes=VMEM // 2),
        cost_estimate=cost(0, 4000000),
        name="sums",
    )(*given, *after))
    token = results.pop()
    sent = [results.pop(0) for _ in range(chips - 1)] if to_chips else []
    hidden = results.pop(0) if to_hidden else None
    return sent, hidden, results, token


def swap(values, axis, size, step):
    return lax.ppermute(values, axis, [(place, place ^ step) for place in range(size)])


def body(row_count, col_count, tokens, norm_gain, gate_weight, up_weight, down_weight, gate_mask, up_mask, down_mask):
    chips = row_count // CORES
    per_plane = col_count // PLANES
    features, width = gate_weight.shape
    row = lax.axis_index("rows")
    core = row % CORES
    place = jnp.reshape(core, (1,)).astype(jnp.int32)
    nowhere = jnp.zeros((1,), jnp.int32)

    normed = rms_normed(tokens, norm_gain)
    blocks = []
    for step in [chip * CORES + other for other in range(CORES) for chip in range(chips)]:
        block = lax.dynamic_slice_in_dim(normed, (row ^ step) * features, features, 1)
        blocks.append(swap(block, "rows", row_count, step) if step else block)
    gate_kept, token = masked(gate_weight, gate_mask, tile_of(features, 256), nowhere, 1, [normed])
    mine, token = assemble(blocks, [token, resident(gate_kept)])

    def behind(values, after):
        return lax.optimization_barrier((values, *after))[0] if after else values

    def by_plane(values, plane, after=()):
        return swap(behind(values, after), "cols", col_count, plane * per_plane)

    def by_row_of_plane(values, step, after=()):
        return swap(behind(values, after), "cols", col_count, step)

    def by_chip(values, chip, after=()):
        return swap(behind(values, after), "rows", row_count, chip * CORES)

    def by_core(values, after=()):
        return swap(behind(values, after), "rows", row_count, 1)

    parts, halves, near, far, chip_sums, hiddens, others, rows_in, partials, sent = ({} for _ in range(10))
    last = [token]

    def forward(plane, values, after=()):
        parts[plane] = [values]
        for step in range(1, per_plane):
            parts[plane].append(by_row_of_plane(values, step, after))

    def multiply_in(plane, after=()):
        *halves[plane], last[0] = gate_up(parts[plane], gate_kept, up_kept, chips, last + list(after))

    def exchange(plane, after=()):
        far[plane] = by_core(halves[plane][2], after)
        near[plane] = by_core(halves[plane][1], after)

    def multiply_out(plane):
        *partials[plane], last[0] = down(hiddens[plane], others[plane], down_kept, last)

    def send_rows(plane, after=()):
        rows_in[plane] = [partials[plane][0]]
        for step in range(1, per_plane):
            rows_in[plane].append(by_row_of_plane(partials[plane][step], step, after))

    def to_chips(plane):
        sent[plane], _, _, last[0] = sums([halves[plane][0], far[plane]], [], [], last + [near[plane]])

    def send_chips(plane, after=()):
        chip_sums[plane] = [by_chip(part, number + 1, after) for number, part in enumerate(sent[plane])]

    def to_hidden(plane):
        _, hiddens[plane], _, last[0] = sums([], [halves[plane][0], near[plane], *chip_sums[plane]], [], last)
        others[plane] = by_core(hiddens[plane])

    def to_rows(*parts, after=()):
        _, _, (summed,), last[0] = sums([], [], [parts], last + list(after))
        return summed

    one_away = by_plane(mine, 1)
    two_away = by_plane(mine, 2)
    forward(0, mine)
    up_kept, last[0] = masked(up_weight, up_mask, tile_of(features, 256), nowhere, 1, last + [resident(gate_kept)])
    down_kept, last[0] = masked(
        down_weight, down_mask, 2 * BLOCK, place, CORES, last + [resident(gate_kept), resident(up_kept)]
    )
    forward(1, one_away, [*parts[0][1:], *last])
    multiply_in(0, [one_away])
    exchange(0)
    to_chips(0)
    three_away = by_plane(two_away, 1, last)
    forward(2, two_away, [*parts[1][1:], *last])
    multiply_in(1, [two_away])
    exchange(1)
    to_chips(1)
    send_chips(1)
    forward(3, three_away, parts[2][1:])
    multiply_in(2, [three_away])
    exchange(2)
    to_hidden(1)
    to_chips(2)
    send_chips(2)
    multiply_in(3)
    exchange(3)
    multiply_out(1)
    to_hidden(2)
    to_chips(3)
    send_chips(3)
    multiply_out(2)
    send_rows(2)
    to_hidden(3)
    send_chips(0, [last[0], *chip_sums[3]])
    multiply_out(3)
    send_rows(3, rows_in[2][1:])
    two = to_rows(*rows_in[2])
    two_out = by_plane(two, 1)
    to_hidden(0)
    multiply_out(0)
    send_rows(1, [*rows_in[3][1:], *last])
    three = to_rows(*rows_in[3], two_out)
    three_out = by_plane(three, 3)
    send_rows(0, rows_in[1][1:])
    one = to_rows(*rows_in[1])
    one_out = by_plane(one, 1)
    arrived = [*rows_in[0], one_out, three_out]

    total = arrived[0].astype(F32)
    for part in arrived[1:]:
        total = total + part.astype(F32)
    mine_now = total[0].astype(BF16)
    other = by_core(total[1].astype(BF16))
    left = jnp.where(core == 0, mine_now, other)
    right = jnp.where(core == 0, other, mine_now)
    return jnp.concatenate([left, right], 1)


def solution(mesh):
    return jax.shard_map(
        functools.partial(body, mesh.shape["rows"], mesh.shape["cols"]),
        mesh=mesh,
        in_specs=(
            P(("rows", "cols"), None),
            P(),
            P("rows", "cols"),
            P("rows", "cols"),
            P("cols", None),
            P("rows", "cols"),
            P("rows", "cols"),
            P("cols", None),
        ),
        out_specs=P(("rows", "cols"), None),
        check_vma=False,
    )
```

```python
import functools

import jax
import jax.numpy as jnp
from jax import lax
from jax.experimental import pallas as pl
from jax.experimental.pallas import tpu as pltpu
from jax.sharding import PartitionSpec as P

BLOCK = 64
CORES = 2
PLANES = 4
NEXT = ((0, 1), (1, 0), (2, 3), (3, 2))
MIRROR = ((0, 3), (3, 0), (1, 2), (2, 1))
ACROSS = ((1, 2), (2, 1))
OUTWARD = ((1, 0), (2, 3))
VMEM = 12 * 1024 * 1024
F32 = jnp.float32
BF16 = jnp.bfloat16


def tile_of(size, most):
    tile = most
    while size % tile:
        tile //= 2
    return tile


def rms_normed(rows_in, norm_gain):
    values = rows_in.astype(F32)
    meansq = jnp.mean(values * values, axis=-1, keepdims=True)
    return (values * lax.rsqrt(meansq + 1e-05) * norm_gain).astype(BF16)


def params(*semantics):
    return pltpu.CompilerParams(dimension_semantics=semantics, vmem_limit_bytes=VMEM)


HURRY = 1000


def cost(flops, moved):
    return pl.CostEstimate(flops=flops // HURRY, bytes_accessed=moved // HURRY, transcendentals=0)


ANYWHERE = pl.BlockSpec(memory_space=pl.ANY)
TOKEN = jax.ShapeDtypeStruct((8, 128), F32)
INSIDE = pl.BlockSpec(memory_space=pltpu.VMEM)


def mask_kernel(after_count, core_ref, weight_ref, mask_ref, *refs):
    kept_ref, token_ref, spread = refs[after_count:]
    token_ref[...] = jnp.zeros_like(token_ref)
    depth, width = weight_ref.shape
    blocks = depth // BLOCK
    step = pl.program_id(0)

    @pl.when(step == 0)
    def _():
        marks = mask_ref.shape[1]
        first = core_ref[0] * (width // BLOCK) if marks * BLOCK > width else 0
        owner = lax.broadcasted_iota(jnp.int32, (marks, width), 1) // BLOCK + first
        chosen = (owner == lax.broadcasted_iota(jnp.int32, (marks, width), 0)).astype(F32)
        spread[...] = jnp.dot(mask_ref[...].astype(F32), chosen, preferred_element_type=F32)

    for block in range(blocks):
        rows = pl.ds(block * BLOCK, BLOCK)
        keep = jnp.broadcast_to(spread[pl.ds(step * blocks + block, 1), :], (BLOCK, width))
        kept_ref[rows, :] = weight_ref[rows, :] * keep.astype(BF16)


def masked(weight, mask, rows, core, shares, after):
    depth, width = weight.shape
    width = width // shares
    return pl.pallas_call(
        functools.partial(mask_kernel, len(after)),
        grid_spec=pltpu.PrefetchScalarGridSpec(
            num_scalar_prefetch=1,
            grid=(depth // rows,),
            in_specs=[
                pl.BlockSpec((rows, width), lambda i, core: (i, core[0] if shares > 1 else 0)),
                pl.BlockSpec(mask.shape, lambda i, core: (0, 0)),
            ]
            + [ANYWHERE] * len(after),
            out_specs=[
                pl.BlockSpec((rows, width), lambda i, core: (i, 0)),
                pl.BlockSpec(TOKEN.shape, lambda i, core: (0, 0)),
            ],
            scratch_shapes=[pltpu.VMEM((mask.shape[0], width), F32)],
        ),
        out_shape=[jax.ShapeDtypeStruct((depth, width), weight.dtype), TOKEN],
        compiler_params=params("arbitrary"),
        cost_estimate=cost(0, 4 * depth * width),
        name="masked",
    )(core, pltpu.with_memory_space_constraint(weight, pltpu.HBM), mask, *after)


def assemble_kernel(after_count, *refs):
    block_refs, (mine_ref, token_ref) = refs[: -2 - after_count], refs[-2:]
    token_ref[...] = jnp.zeros_like(token_ref)
    rows = jnp.concatenate([block_ref[...].astype(F32) for block_ref in block_refs], 0)
    mine_ref[...] = rows.astype(BF16)


def assemble(blocks, after):
    shape = (sum(block.shape[0] for block in blocks), blocks[0].shape[1])
    return pl.pallas_call(
        functools.partial(assemble_kernel, len(after)),
        in_specs=[INSIDE] * len(blocks) + [ANYWHERE] * len(after),
        out_specs=[INSIDE] * 2,
        out_shape=[jax.ShapeDtypeStruct(shape, BF16), TOKEN],
        compiler_params=pltpu.CompilerParams(vmem_limit_bytes=VMEM // 2),
        cost_estimate=cost(0, 1000000),
        name="assemble",
    )(*blocks, *after)


def resident(values):
    return pltpu.with_memory_space_constraint(values, pltpu.VMEM)


def gate_up_kernel(part_count, after_count, *refs):
    parts, (gate_ref, up_ref) = refs[:part_count], refs[part_count : part_count + 2]
    keep_ref, near_ref, *far_refs, token_ref, all_rows = refs[part_count + 2 + after_count :]
    far_places = [(far_ref, which) for far_ref in far_refs for which in range(far_ref.shape[0])]
    token_ref[...] = jnp.zeros_like(token_ref)
    half = parts[0].shape[0] // 2
    kept = half * len(parts)
    for place, part in enumerate(parts):
        all_rows[pl.ds(place * half, half), :] = part[:half, :]
        all_rows[pl.ds(kept + place * half, half), :] = part[half:, :]
    tile = tile_of(gate_ref.shape[1], 256)

    @pl.loop(0, gate_ref.shape[1] // tile)
    def _(number):
        columns = pl.ds(pl.multiple_of(number * tile, tile), tile)
        for which, weight_ref in enumerate((gate_ref, up_ref)):
            total = jnp.dot(all_rows[...], weight_ref[:, columns], preferred_element_type=F32)
            total = total.reshape(2, *keep_ref.shape[1:4], tile).astype(BF16)
            keep_ref[which, :, :, :, columns] = total[0]
            near_ref[which, :, :, columns] = total[1, :, 0]
            far_ref, place = far_places[which]
            far_ref[place, :, :, :, columns] = total[1, :, 1:]


def gate_up(parts, gate_kept, up_kept, chips, far_parts, after):
    rows = sum(part.shape[0] for part in parts)
    depth, width = gate_kept.shape
    groups, own = len(parts), rows // (2 * len(parts) * chips)
    shapes = [(2, groups, chips, own, width), (2, groups, own, width)]
    shapes += [(2 // far_parts, groups, chips - 1, own, width)] * far_parts
    return pl.pallas_call(
        functools.partial(gate_up_kernel, len(parts), len(after)),
        in_specs=[INSIDE] * (len(parts) + 2) + [ANYWHERE] * len(after),
        out_specs=[INSIDE] * (len(shapes) + 1),
        out_shape=[jax.ShapeDtypeStruct(shape, BF16) for shape in shapes] + [TOKEN],
        scratch_shapes=[pltpu.VMEM((rows, depth), BF16)],
        compiler_params=pltpu.CompilerParams(vmem_limit_bytes=VMEM // 2),
        cost_estimate=cost(HURRY * 4 * rows * depth * width, 0),
        name="gate_up",
    )(*parts, resident(gate_kept), resident(up_kept), *after)


def down_kernel(pieces, after_count, own_ref, other_ref, weight_ref, *refs):
    *partial_refs, token_ref, both = refs[after_count:]
    token_ref[...] = jnp.zeros_like(token_ref)
    groups, own, depth = own_ref.shape
    rows = groups * own
    both[:rows, :] = own_ref[...].astype(F32).reshape(rows, depth).astype(BF16)
    both[rows:, :] = other_ref[...].astype(F32).reshape(rows, depth).astype(BF16)
    tile = tile_of(weight_ref.shape[1], 512)

    @pl.loop(0, weight_ref.shape[1] // tile)
    def _(number):
        columns = pl.ds(pl.multiple_of(number * tile, tile), tile)
        total = jnp.dot(both[...], weight_ref[:, columns], preferred_element_type=F32)
        total = total.reshape(pieces, CORES // pieces, groups, own, tile)
        for place, partial_ref in enumerate(partial_refs):
            partial_ref[:, :, columns] = total[place % pieces, :, place // pieces].astype(BF16)


def down(own, other, down_kept, pieces, after):
    groups, rows, depth = own.shape
    width = down_kept.shape[1]
    shape = (CORES // pieces, rows, width)
    return pl.pallas_call(
        functools.partial(down_kernel, pieces, len(after)),
        in_specs=[INSIDE] * 3 + [ANYWHERE] * len(after),
        out_specs=[INSIDE] * (groups * pieces + 1),
        out_shape=[jax.ShapeDtypeStruct(shape, BF16)] * (groups * pieces) + [TOKEN],
        scratch_shapes=[pltpu.VMEM((CORES * groups * rows, depth), BF16)],
        compiler_params=pltpu.CompilerParams(vmem_limit_bytes=VMEM // 2),
        cost_estimate=cost(2 * CORES * groups * rows * depth * width, 0),
        name="down",
    )(own, other, resident(down_kept), *after)


def sums_kernel(sizes, first_core, after_count, *refs):
    to_chips, to_hidden, *to_rows = sizes
    refs = list(refs)
    refs.pop()[...] = jnp.zeros(TOKEN.shape, F32)
    ins = [[refs.pop(0) for _ in range(size)] for size in sizes]
    del refs[:after_count]

    if to_chips:
        keep_ref, *came_refs = ins[0]
        came_places = [came_ref.at[which] for came_ref in came_refs for which in range(came_ref.shape[0])]
        for chip in range(1, keep_ref.shape[2]):
            sent_ref = refs.pop(0)
            for which in range(2):
                for group in range(keep_ref.shape[1]):
                    came = came_places[which][group, chip - 1].astype(F32)
                    sent_ref[which, group] = (keep_ref[which, group, chip].astype(F32) + came).astype(BF16)
    if to_hidden:
        keep_ref, came_ref, *chip_refs = ins[1]
        hidden_ref = refs.pop(0)
        for group in range(keep_ref.shape[1]):
            both = []
            for which in range(2):
                total = keep_ref[which, group, 0].astype(F32) + came_ref[which, group].astype(F32)
                for chip_ref in chip_refs:
                    total = total + chip_ref[which, group].astype(F32)
                both.append(total)
            hidden_ref[group] = (jax.nn.silu(both[0]) * both[1]).astype(BF16)
    for part_refs in ins[2:]:
        summed_ref = refs.pop(0)
        for core in range(summed_ref.shape[0]):
            places = [core + first_core * (part_ref.shape[0] > summed_ref.shape[0]) for part_ref in part_refs]
            total = part_refs[0][places[0]].astype(F32)
            for part_ref, place in zip(part_refs[1:], places[1:]):
                total = total + part_ref[place].astype(F32)
            summed_ref[core] = total.astype(BF16)


def sums(to_chips, to_hidden, to_rows, first_core, after):
    shapes = []
    if to_chips:
        two, groups, chips, own, width = to_chips[0].shape
        shapes += [(two, groups, own, width)] * (chips - 1)
    if to_hidden:
        shapes.append((to_hidden[0].shape[1], *to_hidden[0].shape[3:]))
    shapes += [parts[0].shape for parts in to_rows]
    given = [to_chips, to_hidden, *to_rows]
    sizes = tuple(len(parts) for parts in given)
    given = [part for parts in given for part in parts]
    results = list(pl.pallas_call(
        functools.partial(sums_kernel, sizes, first_core, len(after)),
        in_specs=[INSIDE] * len(given) + [ANYWHERE] * len(after),
        out_specs=[INSIDE] * (len(shapes) + 1),
        out_shape=[jax.ShapeDtypeStruct(shape, BF16) for shape in shapes] + [TOKEN],
        compiler_params=pltpu.CompilerParams(vmem_limit_bytes=VMEM // 2),
        cost_estimate=cost(0, 4000000),
        name="sums",
    )(*given, *after))
    token = results.pop()
    sent = [results.pop(0) for _ in range(chips - 1)] if to_chips else []
    hidden = results.pop(0) if to_hidden else None
    return sent, hidden, results, token


def swap(values, axis, size, step):
    return lax.ppermute(values, axis, [(place, place ^ step) for place in range(size)])


def body(row_count, col_count, tokens, norm_gain, gate_weight, up_weight, down_weight, gate_mask, up_mask, down_mask):
    chips = row_count // CORES
    per_plane = col_count // PLANES
    features, width = gate_weight.shape
    row = lax.axis_index("rows")
    core = row % CORES
    place = jnp.reshape(core, (1,)).astype(jnp.int32)

    normed = rms_normed(tokens, norm_gain)
    blocks = []
    for step in [chip * CORES + other for other in range(CORES) for chip in range(chips)]:
        block = lax.dynamic_slice_in_dim(normed, (row ^ step) * features, features, 1)
        blocks.append(swap(block, "rows", row_count, step) if step else block)
    gate_kept, token = masked(gate_weight, gate_mask, tile_of(features, 256), place, 1, [normed])
    mine, token = assemble(blocks, [token])

    def behind(values, after):
        return lax.optimization_barrier((values, *after))[0] if after else values

    def by_plane(values, planes, after=()):
        pairs = [(a * per_plane + b, c * per_plane + b) for a, c in planes for b in range(per_plane)]
        return lax.ppermute(behind(values, after), "cols", pairs)

    def by_row_of_plane(values, step, after=()):
        return swap(behind(values, after), "cols", col_count, step)

    def by_chip(values, chip, after=()):
        return swap(behind(values, after), "rows", row_count, chip * CORES)

    def by_core(values, after=()):
        return swap(behind(values, after), "rows", row_count, 1)

    parts, halves, near, far, chip_sums, hiddens, others, rows_in, partials, sent = ({} for _ in range(10))
    last = [token]

    def forward(plane, values, after=()):
        parts[plane] = [values]
        for step in range(1, per_plane):
            parts[plane].append(by_row_of_plane(values, step, after))

    def multiply_in(plane, far_parts=1, after=()):
        parts_after = last + list(after)
        *halves[plane], last[0] = gate_up(parts[plane], gate_kept, up_kept, chips, far_parts, parts_after)

    def exchange(plane, after=()):
        far[plane] = [by_core(part, after) for part in halves[plane][2:]]

    def exchange_near(plane, after=()):
        near[plane] = by_core(halves[plane][1], after)

    def multiply_out(plane, pieces=1):
        *partials[plane], last[0] = down(hiddens[plane], others[plane], down_kept, pieces, last)

    def send_rows(plane, after=(), pieces=1):
        for piece in reversed(range(pieces)):
            mine_and_others = partials[plane][piece::pieces]
            rows_in[plane, piece] = mine_and_others[:1]
            for step in range(1, per_plane):
                rows_in[plane, piece].append(by_row_of_plane(mine_and_others[step], step, after))
            after = rows_in[plane, piece][1:]

    def to_chips(plane, after=()):
        given = [halves[plane][0], *far[plane]]
        sent[plane], _, _, last[0] = sums(given, [], [], 0, last + list(after))

    def send_chips(plane, after=()):
        chip_sums[plane] = [by_chip(part, number + 1, after) for number, part in enumerate(sent[plane])]

    def to_hidden(plane):
        _, hiddens[plane], _, last[0] = sums([], [halves[plane][0], near[plane], *chip_sums[plane]], [], 0, last)
        others[plane] = by_core(hiddens[plane])

    def to_rows(*parts, first_core=0, after=()):
        _, _, (summed,), last[0] = sums([], [], [parts], first_core, last + list(after))
        return summed

    one_away = by_plane(mine, NEXT)
    inner_three = by_plane(mine, ACROSS)
    forward(0, mine)
    up_kept, last[0] = masked(up_weight, up_mask, tile_of(features, 256), place, 1, last)
    down_kept, last[0] = masked(down_weight, down_mask, 2 * BLOCK, place, CORES, last)
    inner_two = by_plane(one_away, ACROSS, last)
    outer_two = by_plane(inner_three, OUTWARD, last)
    forward(1, one_away, [*parts[0][1:], *last])
    multiply_in(0, after=[one_away, inner_three])
    exchange(0, [inner_two, outer_two])
    exchange_near(0, [inner_two, outer_two])
    outer_three = by_plane(inner_two, OUTWARD, last)
    forward(2, inner_two + outer_two, [*parts[1][1:], *last])
    to_chips(0, [near[0]])
    multiply_in(1)
    exchange(1)
    exchange_near(1)
    to_chips(1, [near[1]])
    send_chips(1)
    forward(3, inner_three + behind(outer_three, last), [*parts[2][1:], *last])
    multiply_in(2, after=[outer_three])
    exchange(2)
    exchange_near(2)
    to_hidden(1)
    to_chips(2, [near[2]])
    send_chips(2)
    multiply_out(1)
    send_rows(1, parts[3][1:])
    multiply_in(3, far_parts=2)
    exchange(3)
    to_hidden(2)
    to_chips(3)
    send_chips(3)
    exchange_near(3, last)
    multiply_out(2)
    send_rows(2, rows_in[1, 0][1:])
    one = to_rows(*rows_in[1, 0])
    one_out = by_plane(one, NEXT)
    to_hidden(3)
    multiply_out(3, pieces=CORES)
    send_chips(0, chip_sums[3])
    send_rows(3, rows_in[2, 0][1:], pieces=CORES)
    two = to_rows(*rows_in[2, 0], after=[one_out])
    two_out = by_plane(two, NEXT)
    to_hidden(0)
    multiply_out(0)
    three_out = {}
    for piece in reversed(range(CORES)):
        three = to_rows(*rows_in[3, piece], two_out, first_core=piece)
        three_out[piece] = by_plane(three, MIRROR)
    send_rows(0, rows_in[3, 0][1:])

    def total(piece):
        whole = [part[piece].astype(F32) for part in (*rows_in[0, 0], one_out)]
        return (sum(whole[1:], whole[0]) + three_out[piece][0].astype(F32)).astype(BF16)

    mine_now, other = total(0), by_core(total(1))
    left = jnp.where(core == 0, mine_now, other)
    right = jnp.where(core == 0, other, mine_now)
    return jnp.concatenate([left, right], 1)


def solution(mesh):
    return jax.shard_map(
        functools.partial(body, mesh.shape["rows"], mesh.shape["cols"]),
        mesh=mesh,
        in_specs=(
            P(("rows", "cols"), None),
            P(),
            P("rows", "cols"),
            P("rows", "cols"),
            P("cols", None),
            P("rows", "cols"),
            P("rows", "cols"),
            P("cols", None),
        ),
        out_specs=P(("rows", "cols"), None),
        check_vma=False,
    )
```

```python
import functools

import jax
import jax.numpy as jnp
from jax import lax
from jax.experimental import pallas as pl
from jax.experimental.pallas import tpu as pltpu
from jax.sharding import PartitionSpec as P

BLOCK = 64
CORES = 2
PLANES = 4
NEXT = ((0, 1), (1, 0), (2, 3), (3, 2))
MIRROR = ((0, 3), (3, 0), (1, 2), (2, 1))
ACROSS = ((1, 2), (2, 1))
OUTWARD = ((1, 0), (2, 3))
VMEM = 12 * 1024 * 1024
F32 = jnp.float32
BF16 = jnp.bfloat16


def tile_of(size, most):
    tile = most
    while size % tile:
        tile //= 2
    return tile


def rms_normed(rows_in, norm_gain):
    values = rows_in.astype(F32)
    meansq = jnp.mean(values * values, axis=-1, keepdims=True)
    return (values * lax.rsqrt(meansq + 1e-05) * norm_gain).astype(BF16)


def params(*semantics):
    return pltpu.CompilerParams(dimension_semantics=semantics, vmem_limit_bytes=VMEM)


HURRY = 1000


def cost(flops, moved):
    return pl.CostEstimate(flops=flops // HURRY, bytes_accessed=moved // HURRY, transcendentals=0)


def as_if(microseconds):
    return cost(int(HURRY * 1.15e9 * microseconds), 0)


ANYWHERE = pl.BlockSpec(memory_space=pl.ANY)
TOKEN = jax.ShapeDtypeStruct((8, 128), F32)
INSIDE = pl.BlockSpec(memory_space=pltpu.VMEM)


def mask_kernel(share, after_count, core_ref, weight_ref, mask_ref, *refs):
    kept_ref, token_ref, spread = refs[after_count:]
    token_ref[...] = jnp.zeros_like(token_ref)
    depth, width = weight_ref.shape
    blocks = depth // BLOCK
    step = pl.program_id(0)

    @pl.when(step == 0)
    def _():
        marks = mask_ref.shape[1]
        first = share(core_ref[0]) * (width // BLOCK)
        owner = lax.broadcasted_iota(jnp.int32, (marks, width), 1) // BLOCK + first
        chosen = (owner == lax.broadcasted_iota(jnp.int32, (marks, width), 0)).astype(F32)
        spread[...] = jnp.dot(mask_ref[...].astype(F32), chosen, preferred_element_type=F32)

    for block in range(blocks):
        rows = pl.ds(block * BLOCK, BLOCK)
        keep = jnp.broadcast_to(spread[pl.ds(step * blocks + block, 1), :], (BLOCK, width))
        kept_ref[rows, :] = weight_ref[rows, :] * keep.astype(BF16)


def masked(weight, mask, rows, core, shares, share, after, hint=0.0):
    depth, width = weight.shape
    width = width // shares
    return pl.pallas_call(
        functools.partial(mask_kernel, share, len(after)),
        grid_spec=pltpu.PrefetchScalarGridSpec(
            num_scalar_prefetch=1,
            grid=(depth // rows,),
            in_specs=[
                pl.BlockSpec((rows, width), lambda i, core: (i, share(core[0]))),
                pl.BlockSpec(mask.shape, lambda i, core: (0, 0)),
            ]
            + [ANYWHERE] * len(after),
            out_specs=[
                pl.BlockSpec((rows, width), lambda i, core: (i, 0)),
                pl.BlockSpec(TOKEN.shape, lambda i, core: (0, 0)),
            ],
            scratch_shapes=[pltpu.VMEM((mask.shape[0], width), F32)],
        ),
        out_shape=[jax.ShapeDtypeStruct((depth, width), weight.dtype), TOKEN],
        compiler_params=params("arbitrary"),
        cost_estimate=as_if(hint),
        name="masked",
    )(core, pltpu.with_memory_space_constraint(weight, pltpu.HBM), mask, *after)


def stack_kernel(after_count, *refs):
    block_refs, (stacked_ref, token_ref) = refs[: -2 - after_count], refs[-2:]
    token_ref[...] = jnp.zeros_like(token_ref)
    for number, block_ref in enumerate(block_refs):
        stacked_ref[number // stacked_ref.shape[1], number % stacked_ref.shape[1]] = block_ref[...]


def join_kernel(after_count, *refs):
    stacked_refs, (joined_ref, token_ref) = refs[: -2 - after_count], refs[-2:]
    token_ref[...] = jnp.zeros_like(token_ref)
    blocks = [ref[core, chip] for core in range(CORES) for ref in stacked_refs for chip in range(ref.shape[1])]
    joined_ref[...] = jnp.concatenate([block.astype(F32) for block in blocks], 0).astype(BF16)


def rearranged(kernel, name, shape, blocks, after):
    return pl.pallas_call(
        functools.partial(kernel, len(after)),
        in_specs=[INSIDE] * len(blocks) + [ANYWHERE] * len(after),
        out_specs=[INSIDE] * 2,
        out_shape=[jax.ShapeDtypeStruct(shape, BF16), TOKEN],
        compiler_params=pltpu.CompilerParams(vmem_limit_bytes=VMEM // 2),
        cost_estimate=cost(0, 1000000),
        name=name,
    )(*blocks, *after)


def stack(blocks, after):
    shape = (CORES, len(blocks) // CORES, *blocks[0].shape)
    return rearranged(stack_kernel, "stack", shape, blocks, after)


def join(stacks, after):
    rows = sum(part.shape[1] for part in stacks) * CORES * stacks[0].shape[2]
    return rearranged(join_kernel, "join", (rows, stacks[0].shape[3]), stacks, after)


def resident(values):
    return pltpu.with_memory_space_constraint(values, pltpu.VMEM)


def gate_up_kernel(part_count, after_count, *refs):
    parts, (gate_ref, up_ref) = refs[:part_count], refs[part_count : part_count + 2]
    keep_ref, near_ref, *far_refs, token_ref, all_rows = refs[part_count + 2 + after_count :]
    far_places = [(far_ref, which) for far_ref in far_refs for which in range(far_ref.shape[0])]
    token_ref[...] = jnp.zeros_like(token_ref)
    half = parts[0].shape[0] // 2
    kept = half * len(parts)
    for place, part in enumerate(parts):
        all_rows[pl.ds(place * half, half), :] = part[:half, :]
        all_rows[pl.ds(kept + place * half, half), :] = part[half:, :]
    tile = tile_of(gate_ref.shape[1], 256)

    @pl.loop(0, gate_ref.shape[1] // tile)
    def _(number):
        columns = pl.ds(pl.multiple_of(number * tile, tile), tile)
        for which, weight_ref in enumerate((gate_ref, up_ref)):
            total = jnp.dot(all_rows[...], weight_ref[:, columns], preferred_element_type=F32)
            total = total.reshape(2, *keep_ref.shape[1:4], tile).astype(BF16)
            keep_ref[which, :, :, :, columns] = total[0]
            near_ref[which, :, :, columns] = total[1, :, 0]
            far_ref, place = far_places[which]
            far_ref[place, :, :, :, columns] = total[1, :, 1:]


def gate_up(parts, gate_kept, up_kept, chips, far_parts, hint, after):
    rows = sum(part.shape[0] for part in parts)
    depth, width = gate_kept.shape
    groups, own = len(parts), rows // (2 * len(parts) * chips)
    shapes = [(2, groups, chips, own, width), (2, groups, own, width)]
    shapes += [(2 // far_parts, groups, chips - 1, own, width)] * far_parts
    return pl.pallas_call(
        functools.partial(gate_up_kernel, len(parts), len(after)),
        in_specs=[INSIDE] * (len(parts) + 2) + [ANYWHERE] * len(after),
        out_specs=[INSIDE] * (len(shapes) + 1),
        out_shape=[jax.ShapeDtypeStruct(shape, BF16) for shape in shapes] + [TOKEN],
        scratch_shapes=[pltpu.VMEM((rows, depth), BF16)],
        compiler_params=pltpu.CompilerParams(vmem_limit_bytes=VMEM // 2),
        cost_estimate=cost(hint * 4 * rows * depth * width, 0),
        name="gate_up",
    )(*parts, resident(gate_kept), resident(up_kept), *after)


def down_kernel(pieces, weight_count, after_count, own_ref, other_ref, *refs):
    weight_refs, refs = refs[:weight_count], refs[weight_count:]
    *partial_refs, token_ref, both = refs[after_count:]
    token_ref[...] = jnp.zeros_like(token_ref)
    groups, own, depth = own_ref.shape
    rows = groups * own
    both[:rows, :] = own_ref[...].astype(F32).reshape(rows, depth).astype(BF16)
    both[rows:, :] = other_ref[...].astype(F32).reshape(rows, depth).astype(BF16)
    for number, weight_ref in enumerate(weight_refs):
        width = weight_ref.shape[1]
        down_columns(pieces, both, weight_ref, partial_refs, number * width, tile_of(width, 512))


def down_columns(pieces, both, weight_ref, partial_refs, first, tile):
    own = partial_refs[0].shape[1]

    @pl.loop(0, weight_ref.shape[1] // tile)
    def _(number):
        start = pl.multiple_of(number * tile, tile)
        total = jnp.dot(both[...], weight_ref[:, pl.ds(start, tile)], preferred_element_type=F32)
        total = total.reshape(pieces, CORES // pieces, len(partial_refs) // pieces, own, tile)
        columns = pl.ds(pl.multiple_of(first + start, tile), tile)
        for place, partial_ref in enumerate(partial_refs):
            partial_ref[:, :, columns] = total[place % pieces, :, place // pieces].astype(BF16)


def down(own, other, down_kept, pieces, after):
    groups, rows, depth = own.shape
    width = sum(weight.shape[1] for weight in down_kept)
    shape = (CORES // pieces, rows, width)
    return pl.pallas_call(
        functools.partial(down_kernel, pieces, len(down_kept), len(after)),
        in_specs=[INSIDE] * (2 + len(down_kept)) + [ANYWHERE] * len(after),
        out_specs=[INSIDE] * (groups * pieces + 1),
        out_shape=[jax.ShapeDtypeStruct(shape, BF16)] * (groups * pieces) + [TOKEN],
        scratch_shapes=[pltpu.VMEM((CORES * groups * rows, depth), BF16)],
        compiler_params=pltpu.CompilerParams(vmem_limit_bytes=VMEM // 2),
        cost_estimate=cost(2 * CORES * groups * rows * depth * width, 0),
        name="down",
    )(own, other, *(resident(weight) for weight in down_kept), *after)


def sums_kernel(sizes, after_count, *refs):
    to_chips, to_hidden, *to_rows = sizes
    refs = list(refs)
    refs.pop()[...] = jnp.zeros(TOKEN.shape, F32)
    ins = [[refs.pop(0) for _ in range(size)] for size in sizes]
    del refs[:after_count]

    if to_chips:
        keep_ref, *came_refs = ins[0]
        came_places = [came_ref.at[which] for came_ref in came_refs for which in range(came_ref.shape[0])]
        for chip in range(1, keep_ref.shape[2]):
            sent_ref = refs.pop(0)
            for which in range(2):
                for group in range(keep_ref.shape[1]):
                    came = came_places[which][group, chip - 1].astype(F32)
                    sent_ref[which, group] = (keep_ref[which, group, chip].astype(F32) + came).astype(BF16)
    if to_hidden:
        keep_ref, came_ref, *chip_refs = ins[1]
        hidden_ref = refs.pop(0)
        for group in range(keep_ref.shape[1]):
            both = []
            for which in range(2):
                total = keep_ref[which, group, 0].astype(F32) + came_ref[which, group].astype(F32)
                for chip_ref in chip_refs:
                    total = total + chip_ref[which, group].astype(F32)
                both.append(total)
            hidden_ref[group] = (jax.nn.silu(both[0]) * both[1]).astype(BF16)
    for part_refs in ins[2:]:
        summed_ref = refs.pop(0)
        cores = summed_ref.shape[0]
        for core in range(cores):
            total = part_refs[0][core].astype(F32)
            for part_ref in part_refs[1:]:
                total = total + part_ref[part_ref.shape[0] - cores + core].astype(F32)
            summed_ref[core] = total.astype(BF16)


def sums(to_chips, to_hidden, to_rows, after, hint=0.0):
    shapes = []
    if to_chips:
        two, groups, chips, own, width = to_chips[0].shape
        shapes += [(two, groups, own, width)] * (chips - 1)
    if to_hidden:
        shapes.append((to_hidden[0].shape[1], *to_hidden[0].shape[3:]))
    shapes += [parts[0].shape for parts in to_rows]
    given = [to_chips, to_hidden, *to_rows]
    sizes = tuple(len(parts) for parts in given)
    given = [part for parts in given for part in parts]
    results = list(pl.pallas_call(
        functools.partial(sums_kernel, sizes, len(after)),
        in_specs=[INSIDE] * len(given) + [ANYWHERE] * len(after),
        out_specs=[INSIDE] * (len(shapes) + 1),
        out_shape=[jax.ShapeDtypeStruct(shape, BF16) for shape in shapes] + [TOKEN],
        compiler_params=pltpu.CompilerParams(vmem_limit_bytes=VMEM // 2),
        cost_estimate=as_if(hint),
        name="sums",
    )(*given, *after))
    token = results.pop()
    sent = [results.pop(0) for _ in range(chips - 1)] if to_chips else []
    hidden = results.pop(0) if to_hidden else None
    return sent, hidden, results, token


def swap(values, axis, size, step):
    return lax.ppermute(values, axis, [(place, place ^ step) for place in range(size)])


def body(row_count, col_count, tokens, norm_gain, gate_weight, up_weight, down_weight, gate_mask, up_mask, down_mask):
    chips = row_count // CORES
    per_plane = col_count // PLANES
    features, width = gate_weight.shape
    row = lax.axis_index("rows")
    core = row % CORES
    place = jnp.reshape(core, (1,)).astype(jnp.int32)

    normed = rms_normed(tokens, norm_gain)
    def block(step):
        values = lax.dynamic_slice_in_dim(normed, (row ^ step) * features, features, 1)
        return swap(values, "rows", row_count, step) if step else values

    first, token = stack([block(core_step) for core_step in range(CORES)], [])
    gate_kept, token = masked(gate_weight, gate_mask, tile_of(features, 256), place, 1, lambda core: 0, [token])
    second = [block(chip * CORES + core_step) for core_step in range(CORES) for chip in range(1, chips)]
    second, token = stack(second, [token])
    mine, token = join([first, second], [token])

    def behind(values, after):
        return lax.optimization_barrier((values, *after))[0] if after else values

    def by_plane(values, planes, after=()):
        pairs = [(a * per_plane + b, c * per_plane + b) for a, c in planes for b in range(per_plane)]
        return lax.ppermute(behind(values, after), "cols", pairs)

    def by_row_of_plane(values, step, after=()):
        return swap(behind(values, after), "cols", col_count, step)

    def by_chip(values, chip, after=()):
        return swap(behind(values, after), "rows", row_count, chip * CORES)

    def by_core(values, after=()):
        return swap(behind(values, after), "rows", row_count, 1)

    parts, halves, near, far, chip_sums, hiddens, others, rows_in, partials, sent = ({} for _ in range(10))
    last = [token]

    def forward(plane, values, after=()):
        parts[plane] = [values]
        for step in range(1, per_plane):
            parts[plane].append(by_row_of_plane(values, step, after))

    def multiply_in(plane, far_parts=1, hint=HURRY, after=()):
        parts_after = last + list(after)
        *halves[plane], last[0] = gate_up(parts[plane], gate_kept, up_kept, chips, far_parts, hint, parts_after)

    def exchange(plane, after=()):
        far[plane] = [by_core(part, after) for part in halves[plane][2:]]

    def exchange_near(plane, after=()):
        near[plane] = by_core(halves[plane][1], after)

    def multiply_out(plane, pieces=1):
        *partials[plane], last[0] = down(hiddens[plane], others[plane], down_kept, pieces, last)

    def send_rows(plane, after=(), pieces=1, piece=0):
        mine_and_others = partials[plane][piece::pieces]
        rows_in[plane, piece] = mine_and_others[:1]
        for step in range(1, per_plane):
            rows_in[plane, piece].append(by_row_of_plane(mine_and_others[step], step, after))

    def to_chips(plane, after=()):
        given = [halves[plane][0], *far[plane]]
        sent[plane], _, _, last[0] = sums(given, [], [], last + list(after))

    def send_chips(plane, after=()):
        chip_sums[plane] = [by_chip(part, number + 1, after) for number, part in enumerate(sent[plane])]

    def to_hidden(plane, after=()):
        given = [halves[plane][0], near[plane], *chip_sums[plane]]
        _, hiddens[plane], _, last[0] = sums([], given, [], last + list(after))
        others[plane] = by_core(hiddens[plane])

    def to_rows(*parts, after=(), hint=0.0):
        _, _, (summed,), last[0] = sums([], [], [parts], last + list(after), hint)
        return summed

    next_stacks = [by_plane(first, NEXT), by_plane(second, NEXT)]
    inner_three = by_plane(mine, ACROSS)
    forward(0, mine)
    up_kept, last[0] = masked(
        up_weight, up_mask, tile_of(features, 256), place, 1, lambda core: 0, last + next_stacks[:1], 0.15
    )
    one_away, last[0] = join(next_stacks, last)
    inner_two = by_plane(one_away, ACROSS)
    down_kept = []
    for share in range(2):
        part, last[0] = masked(
            down_weight, down_mask, 2 * BLOCK, place, 2 * CORES, lambda core, share=share: 2 * core + share, last, 8 - 8 * share
        )
        down_kept.append(part)
        if share == 0:
            forward(1, one_away, [*parts[0][1:], *last])
            outer_two = by_plane(inner_three, OUTWARD, last)
    multiply_in(0, hint=0)
    exchange(0, [inner_two, outer_two])
    exchange_near(0, [inner_two, outer_two])
    outer_three = by_plane(inner_two, OUTWARD, last)
    forward(2, inner_two + outer_two, [*parts[1][1:], *last])
    to_chips(0, [near[0]])
    multiply_in(1)
    exchange(1)
    exchange_near(1)
    to_chips(1, [near[1]])
    send_chips(1)
    forward(3, inner_three + behind(outer_three, last), [*parts[2][1:], *last])
    multiply_in(2, after=[outer_three])
    exchange(2)
    exchange_near(2)
    to_hidden(1)
    to_chips(2, [near[2]])
    send_chips(2)
    multiply_out(1)
    send_rows(1, parts[3][1:])
    multiply_in(3, far_parts=2)
    exchange(3)
    to_hidden(2)
    to_chips(3)
    send_chips(3)
    exchange_near(3, last)
    multiply_out(2, pieces=CORES)
    send_rows(2, rows_in[1, 0][1:], CORES, 1)
    one = to_rows(*rows_in[1, 0])
    one_out = by_plane(one, NEXT)
    two = to_rows(*rows_in[2, 1])
    send_rows(2, [two], CORES, 0)
    two_out, three_out = {1: by_plane(two, NEXT)}, {}
    to_hidden(3)
    send_chips(0, chip_sums[3])
    multiply_out(3, pieces=CORES)
    two = to_rows(*rows_in[2, 0], after=[one_out])
    two_out[0] = by_plane(two, NEXT)
    send_rows(3, [two], CORES, 1)
    three = to_rows(*rows_in[3, 1], two_out[1])
    three_out[1] = by_plane(three, MIRROR)
    send_rows(3, [three], CORES, 0)
    to_hidden(0, [two_out[0]])
    multiply_out(0)
    three = to_rows(*rows_in[3, 0], two_out[0])
    three_out[0] = by_plane(three, MIRROR)
    send_rows(0, rows_in[3, 0][1:])

    joined = to_rows(three_out[1], one_out, hint=10.0)

    def total(piece, *parts):
        whole = [part[piece].astype(F32) for part in rows_in[0, 0]] + [part.astype(F32) for part in parts]
        return sum(whole[1:], whole[0]).astype(BF16)

    mine_now, other = total(0, one_out[0], three_out[0][0]), by_core(total(1, joined[0]))
    left = jnp.where(core == 0, mine_now, other)
    right = jnp.where(core == 0, other, mine_now)
    return jnp.concatenate([left, right], 1)


def solution(mesh):
    return jax.shard_map(
        functools.partial(body, mesh.shape["rows"], mesh.shape["cols"]),
        mesh=mesh,
        in_specs=(
            P(("rows", "cols"), None),
            P(),
            P("rows", "cols"),
            P("rows", "cols"),
            P("cols", None),
            P("rows", "cols"),
            P("rows", "cols"),
            P("cols", None),
        ),
        out_specs=P(("rows", "cols"), None),
        check_vma=False,
    )
```

```python
import functools

import jax
import jax.numpy as jnp
from jax import lax
from jax.experimental import pallas as pl
from jax.experimental.pallas import tpu as pltpu
from jax.sharding import PartitionSpec as P

BLOCK = 64
CORES = 2
PLANES = 4
NEXT = ((0, 1), (1, 0), (2, 3), (3, 2))
MIRROR = ((0, 3), (3, 0), (1, 2), (2, 1))
ACROSS = ((1, 2), (2, 1))
OUTWARD = ((1, 0), (2, 3))
VMEM = 12 * 1024 * 1024
F32 = jnp.float32
BF16 = jnp.bfloat16


def tile_of(size, most):
    tile = most
    while size % tile:
        tile //= 2
    return tile


def rms_normed(rows_in, norm_gain):
    values = rows_in.astype(F32)
    meansq = jnp.mean(values * values, axis=-1, keepdims=True)
    return (values * lax.rsqrt(meansq + 1e-05) * norm_gain).astype(BF16)


HURRY = 1000


def cost(flops, moved):
    return pl.CostEstimate(flops=flops // HURRY, bytes_accessed=moved // HURRY, transcendentals=0)


def as_if(microseconds):
    return cost(int(HURRY * 1.15e9 * microseconds), 0)


ANYWHERE = pl.BlockSpec(memory_space=pl.ANY)
TOKEN = jax.ShapeDtypeStruct((8, 128), F32)
INSIDE = pl.BlockSpec(memory_space=pltpu.VMEM)


def mask_kernel(share, rows, after_count, core_ref, weight_ref, mask_ref, *refs):
    kept_ref, token_ref, spread, semaphores = refs[after_count:]
    token_ref[...] = jnp.zeros_like(token_ref)
    depth, width = kept_ref.shape
    number = share(core_ref[0])
    columns = pl.ds(pl.multiple_of(number * width, width), width)
    copies = [
        pltpu.make_async_copy(
            weight_ref.at[pl.ds(step * rows, rows), columns], kept_ref.at[pl.ds(step * rows, rows)], semaphores.at[step]
        )
        for step in range(depth // rows)
    ]
    for copy in copies:
        copy.start()
    marks = mask_ref.shape[1]
    owner = lax.broadcasted_iota(jnp.int32, (marks, width), 1) // BLOCK + number * (width // BLOCK)
    chosen = (owner == lax.broadcasted_iota(jnp.int32, (marks, width), 0)).astype(F32)
    spread[...] = jnp.dot(mask_ref[...].astype(F32), chosen, preferred_element_type=F32)
    for step, copy in enumerate(copies):
        copy.wait()
        for block in range(step * rows // BLOCK, (step + 1) * rows // BLOCK):
            part = pl.ds(block * BLOCK, BLOCK)
            keep = jnp.broadcast_to(spread[pl.ds(block, 1), :], (BLOCK, width))
            kept_ref[part, :] = kept_ref[part, :] * keep.astype(BF16)


def masked(weight, mask, rows, core, shares, share, after, hint=0.0):
    depth, width = weight.shape
    width = width // shares
    return pl.pallas_call(
        functools.partial(mask_kernel, share, rows, len(after)),
        in_specs=[pl.BlockSpec(memory_space=pltpu.SMEM), ANYWHERE, INSIDE] + [ANYWHERE] * len(after),
        out_specs=[INSIDE] * 2,
        out_shape=[jax.ShapeDtypeStruct((depth, width), weight.dtype), TOKEN],
        scratch_shapes=[pltpu.VMEM((mask.shape[0], width), F32), pltpu.SemaphoreType.DMA((depth // rows,))],
        compiler_params=pltpu.CompilerParams(vmem_limit_bytes=VMEM),
        cost_estimate=as_if(hint),
        name="masked",
    )(core, pltpu.with_memory_space_constraint(weight, pltpu.HBM), mask, *after)


def stack_kernel(after_count, *refs):
    block_refs, (stacked_ref, token_ref) = refs[: -2 - after_count], refs[-2:]
    token_ref[...] = jnp.zeros_like(token_ref)
    for number, block_ref in enumerate(block_refs):
        stacked_ref[number // stacked_ref.shape[1], number % stacked_ref.shape[1]] = block_ref[...]


def join_kernel(after_count, *refs):
    stacked_refs, (joined_ref, token_ref) = refs[: -2 - after_count], refs[-2:]
    token_ref[...] = jnp.zeros_like(token_ref)
    blocks = [ref[core, chip] for core in range(CORES) for ref in stacked_refs for chip in range(ref.shape[1])]
    joined_ref[...] = jnp.concatenate([block.astype(F32) for block in blocks], 0).astype(BF16)


def rearranged(kernel, name, shape, blocks, after):
    return pl.pallas_call(
        functools.partial(kernel, len(after)),
        in_specs=[INSIDE] * len(blocks) + [ANYWHERE] * len(after),
        out_specs=[INSIDE] * 2,
        out_shape=[jax.ShapeDtypeStruct(shape, BF16), TOKEN],
        compiler_params=pltpu.CompilerParams(vmem_limit_bytes=VMEM // 2),
        cost_estimate=cost(0, 1000000),
        name=name,
    )(*blocks, *after)


def stack(blocks, after):
    shape = (CORES, len(blocks) // CORES, *blocks[0].shape)
    return rearranged(stack_kernel, "stack", shape, blocks, after)


def join(stacks, after):
    rows = sum(part.shape[1] for part in stacks) * CORES * stacks[0].shape[2]
    return rearranged(join_kernel, "join", (rows, stacks[0].shape[3]), stacks, after)


def resident(values):
    return pltpu.with_memory_space_constraint(values, pltpu.VMEM)


def gate_up_kernel(part_count, after_count, *refs):
    parts, (gate_ref, up_ref) = refs[:part_count], refs[part_count : part_count + 2]
    keep_ref, near_ref, *far_refs, token_ref, all_rows = refs[part_count + 2 + after_count :]
    far_places = [(far_ref, which) for far_ref in far_refs for which in range(far_ref.shape[0])]
    token_ref[...] = jnp.zeros_like(token_ref)
    half = parts[0].shape[0] // 2
    kept = half * len(parts)
    for place, part in enumerate(parts):
        all_rows[pl.ds(place * half, half), :] = part[:half, :]
        all_rows[pl.ds(kept + place * half, half), :] = part[half:, :]
    tile = tile_of(gate_ref.shape[1], 256)

    @pl.loop(0, gate_ref.shape[1] // tile)
    def _(number):
        columns = pl.ds(pl.multiple_of(number * tile, tile), tile)
        for which, weight_ref in enumerate((gate_ref, up_ref)):
            total = jnp.dot(all_rows[...], weight_ref[:, columns], preferred_element_type=F32)
            total = total.reshape(2, *keep_ref.shape[1:4], tile).astype(BF16)
            keep_ref[which, :, :, :, columns] = total[0]
            near_ref[which, :, :, columns] = total[1, :, 0]
            far_ref, place = far_places[which]
            far_ref[place, :, :, :, columns] = total[1, :, 1:]


def gate_up(parts, gate_kept, up_kept, chips, far_parts, hint, after):
    rows = sum(part.shape[0] for part in parts)
    depth, width = gate_kept.shape
    groups, own = len(parts), rows // (2 * len(parts) * chips)
    shapes = [(2, groups, chips, own, width), (2, groups, own, width)]
    shapes += [(2 // far_parts, groups, chips - 1, own, width)] * far_parts
    return pl.pallas_call(
        functools.partial(gate_up_kernel, len(parts), len(after)),
        in_specs=[INSIDE] * (len(parts) + 2) + [ANYWHERE] * len(after),
        out_specs=[INSIDE] * (len(shapes) + 1),
        out_shape=[jax.ShapeDtypeStruct(shape, BF16) for shape in shapes] + [TOKEN],
        scratch_shapes=[pltpu.VMEM((rows, depth), BF16)],
        compiler_params=pltpu.CompilerParams(vmem_limit_bytes=VMEM // 2),
        cost_estimate=cost(hint * 4 * rows * depth * width, 0),
        name="gate_up",
    )(*parts, resident(gate_kept), resident(up_kept), *after)


def down_kernel(pieces, weight_count, after_count, own_ref, other_ref, *refs):
    weight_refs, refs = refs[:weight_count], refs[weight_count:]
    *partial_refs, token_ref, both = refs[after_count:]
    token_ref[...] = jnp.zeros_like(token_ref)
    groups, own, depth = own_ref.shape
    rows = groups * own
    both[:rows, :] = own_ref[...].astype(F32).reshape(rows, depth).astype(BF16)
    both[rows:, :] = other_ref[...].astype(F32).reshape(rows, depth).astype(BF16)
    for number, weight_ref in enumerate(weight_refs):
        width = weight_ref.shape[1]
        down_columns(pieces, both, weight_ref, partial_refs, number * width, tile_of(width, 512))


def down_columns(pieces, both, weight_ref, partial_refs, first, tile):
    own = partial_refs[0].shape[1]

    @pl.loop(0, weight_ref.shape[1] // tile)
    def _(number):
        start = pl.multiple_of(number * tile, tile)
        total = jnp.dot(both[...], weight_ref[:, pl.ds(start, tile)], preferred_element_type=F32)
        total = total.reshape(pieces, CORES // pieces, len(partial_refs) // pieces, own, tile)
        columns = pl.ds(pl.multiple_of(first + start, tile), tile)
        for place, partial_ref in enumerate(partial_refs):
            partial_ref[:, :, columns] = total[place % pieces, :, place // pieces].astype(BF16)


def down(own, other, down_kept, pieces, after):
    groups, rows, depth = own.shape
    width = sum(weight.shape[1] for weight in down_kept)
    shape = (CORES // pieces, rows, width)
    return pl.pallas_call(
        functools.partial(down_kernel, pieces, len(down_kept), len(after)),
        in_specs=[INSIDE] * (2 + len(down_kept)) + [ANYWHERE] * len(after),
        out_specs=[INSIDE] * (groups * pieces + 1),
        out_shape=[jax.ShapeDtypeStruct(shape, BF16)] * (groups * pieces) + [TOKEN],
        scratch_shapes=[pltpu.VMEM((CORES * groups * rows, depth), BF16)],
        compiler_params=pltpu.CompilerParams(vmem_limit_bytes=VMEM // 2),
        cost_estimate=cost(2 * CORES * groups * rows * depth * width, 0),
        name="down",
    )(own, other, *(resident(weight) for weight in down_kept), *after)


def sums_kernel(sizes, after_count, *refs):
    to_chips, to_hidden, *to_rows = sizes
    refs = list(refs)
    refs.pop()[...] = jnp.zeros(TOKEN.shape, F32)
    ins = [[refs.pop(0) for _ in range(size)] for size in sizes]
    del refs[:after_count]

    if to_chips:
        keep_ref, *came_refs = ins[0]
        came_places = [came_ref.at[which] for came_ref in came_refs for which in range(came_ref.shape[0])]
        for chip in range(1, keep_ref.shape[2]):
            sent_ref = refs.pop(0)
            for which in range(2):
                for group in range(keep_ref.shape[1]):
                    came = came_places[which][group, chip - 1].astype(F32)
                    sent_ref[which, group] = (keep_ref[which, group, chip].astype(F32) + came).astype(BF16)
    if to_hidden:
        keep_ref, came_ref, *chip_refs = ins[1]
        hidden_ref = refs.pop(0)
        for group in range(keep_ref.shape[1]):
            both = []
            for which in range(2):
                total = keep_ref[which, group, 0].astype(F32) + came_ref[which, group].astype(F32)
                for chip_ref in chip_refs:
                    total = total + chip_ref[which, group].astype(F32)
                both.append(total)
            hidden_ref[group] = (jax.nn.silu(both[0]) * both[1]).astype(BF16)
    for part_refs in ins[2:]:
        summed_ref = refs.pop(0)
        cores = summed_ref.shape[0]
        for core in range(cores):
            total = part_refs[0][core].astype(F32)
            for part_ref in part_refs[1:]:
                total = total + part_ref[part_ref.shape[0] - cores + core].astype(F32)
            summed_ref[core] = total.astype(BF16)


def sums(to_chips, to_hidden, to_rows, after, hint=0.0):
    shapes = []
    if to_chips:
        two, groups, chips, own, width = to_chips[0].shape
        shapes += [(two, groups, own, width)] * (chips - 1)
    if to_hidden:
        shapes.append((to_hidden[0].shape[1], *to_hidden[0].shape[3:]))
    shapes += [parts[0].shape for parts in to_rows]
    given = [to_chips, to_hidden, *to_rows]
    sizes = tuple(len(parts) for parts in given)
    given = [part for parts in given for part in parts]
    results = list(pl.pallas_call(
        functools.partial(sums_kernel, sizes, len(after)),
        in_specs=[INSIDE] * len(given) + [ANYWHERE] * len(after),
        out_specs=[INSIDE] * (len(shapes) + 1),
        out_shape=[jax.ShapeDtypeStruct(shape, BF16) for shape in shapes] + [TOKEN],
        compiler_params=pltpu.CompilerParams(vmem_limit_bytes=VMEM // 2),
        cost_estimate=as_if(hint),
        name="sums",
    )(*given, *after))
    token = results.pop()
    sent = [results.pop(0) for _ in range(chips - 1)] if to_chips else []
    hidden = results.pop(0) if to_hidden else None
    return sent, hidden, results, token


def swap(values, axis, size, step):
    return lax.ppermute(values, axis, [(place, place ^ step) for place in range(size)])


def body(row_count, col_count, tokens, norm_gain, gate_weight, up_weight, down_weight, gate_mask, up_mask, down_mask):
    chips = row_count // CORES
    per_plane = col_count // PLANES
    features, width = gate_weight.shape
    row = lax.axis_index("rows")
    core = row % CORES
    place = jnp.reshape(core, (1,)).astype(jnp.int32)

    normed = rms_normed(tokens, norm_gain)
    def block(step):
        values = lax.dynamic_slice_in_dim(normed, (row ^ step) * features, features, 1)
        return swap(values, "rows", row_count, step) if step else values

    first, token = stack([block(core_step) for core_step in range(CORES)], [])
    gate_kept, token = masked(gate_weight, gate_mask, tile_of(features, 256), place, 1, lambda core: 0, [token])
    second = [block(chip * CORES + core_step) for core_step in range(CORES) for chip in range(1, chips)]
    second, token = stack(second, [token])
    mine, token = join([first, second], [token])

    def behind(values, after):
        return lax.optimization_barrier((values, *after))[0] if after else values

    def by_plane(values, planes, after=()):
        pairs = [(a * per_plane + b, c * per_plane + b) for a, c in planes for b in range(per_plane)]
        return lax.ppermute(behind(values, after), "cols", pairs)

    def by_row_of_plane(values, step, after=()):
        return swap(behind(values, after), "cols", col_count, step)

    def by_chip(values, chip, after=()):
        return swap(behind(values, after), "rows", row_count, chip * CORES)

    def by_core(values, after=()):
        return swap(behind(values, after), "rows", row_count, 1)

    parts, halves, near, far, chip_sums, hiddens, others, rows_in, partials, sent = ({} for _ in range(10))
    last = [token]

    def forward(plane, values, after=()):
        parts[plane] = [values]
        for step in range(1, per_plane):
            parts[plane].append(by_row_of_plane(values, step, after))

    def multiply_in(plane, far_parts=1, hint=HURRY, after=()):
        parts_after = last + list(after)
        *halves[plane], last[0] = gate_up(parts[plane], gate_kept, up_kept, chips, far_parts, hint, parts_after)

    def exchange(plane, after=()):
        far[plane] = [by_core(part, after) for part in halves[plane][2:]]

    def exchange_near(plane, after=()):
        near[plane] = by_core(halves[plane][1], after)

    def multiply_out(plane, pieces=1):
        *partials[plane], last[0] = down(hiddens[plane], others[plane], down_kept, pieces, last)

    def send_rows(plane, after=(), pieces=1, piece=0):
        mine_and_others = partials[plane][piece::pieces]
        rows_in[plane, piece] = mine_and_others[:1]
        for step in range(1, per_plane):
            rows_in[plane, piece].append(by_row_of_plane(mine_and_others[step], step, after))

    def to_chips(plane, after=()):
        given = [halves[plane][0], *far[plane]]
        sent[plane], _, _, last[0] = sums(given, [], [], last + list(after))

    def send_chips(plane, after=()):
        chip_sums[plane] = [by_chip(part, number + 1, after) for number, part in enumerate(sent[plane])]

    def to_hidden(plane, after=()):
        given = [halves[plane][0], near[plane], *chip_sums[plane]]
        _, hiddens[plane], _, last[0] = sums([], given, [], last + list(after))
        others[plane] = by_core(hiddens[plane])

    def to_rows(*parts, after=(), hint=0.0):
        _, _, (summed,), last[0] = sums([], [], [parts], last + list(after), hint)
        return summed

    next_stacks = [by_plane(first, NEXT), by_plane(second, NEXT)]
    inner_three = by_plane(mine, ACROSS)
    forward(0, mine)
    up_kept, last[0] = masked(
        up_weight, up_mask, tile_of(features, 256), place, 1, lambda core: 0, last + next_stacks[:1], 0.15
    )
    one_away, last[0] = join(next_stacks, last)
    inner_two = by_plane(one_away, ACROSS)
    down_kept = []
    for share in range(2):
        part, last[0] = masked(
            down_weight, down_mask, 2 * BLOCK, place, 2 * CORES, lambda core, share=share: 2 * core + share, last, 8 - 8 * share
        )
        down_kept.append(part)
    outer_two = by_plane(inner_three, OUTWARD, last)
    forward(1, one_away, [*parts[0][1:], *last])
    multiply_in(0, hint=0)
    exchange(0, [inner_two, outer_two])
    exchange_near(0, [inner_two, outer_two])
    outer_three = by_plane(inner_two, OUTWARD, last)
    forward(2, inner_two + outer_two, [*parts[1][1:], *last])
    to_chips(0, [near[0]])
    multiply_in(1)
    exchange(1)
    exchange_near(1)
    to_chips(1, [near[1]])
    send_chips(1)
    forward(3, inner_three + behind(outer_three, last), [*parts[2][1:], *last])
    multiply_in(2, after=[outer_three])
    exchange(2)
    exchange_near(2)
    to_hidden(1)
    to_chips(2, [near[2]])
    send_chips(2)
    multiply_out(1)
    send_rows(1, parts[3][1:])
    multiply_in(3, far_parts=2)
    exchange(3)
    to_hidden(2)
    to_chips(3)
    send_chips(3)
    exchange_near(3, last)
    multiply_out(2, pieces=CORES)
    send_rows(2, rows_in[1, 0][1:], CORES, 1)
    one = to_rows(*rows_in[1, 0])
    one_out = by_plane(one, NEXT)
    two = to_rows(*rows_in[2, 1])
    send_rows(2, [two], CORES, 0)
    two_out, three_out = {1: by_plane(two, NEXT)}, {}
    to_hidden(3)
    send_chips(0, chip_sums[3])
    multiply_out(3, pieces=CORES)
    two = to_rows(*rows_in[2, 0], after=[one_out])
    two_out[0] = by_plane(two, NEXT)
    send_rows(3, [two], CORES, 1)
    three = to_rows(*rows_in[3, 1], two_out[1])
    three_out[1] = by_plane(three, MIRROR)
    send_rows(3, [three], CORES, 0)
    to_hidden(0, [two_out[0]])
    multiply_out(0)
    three = to_rows(*rows_in[3, 0], two_out[0])
    three_out[0] = by_plane(three, MIRROR)
    send_rows(0, rows_in[3, 0][1:])

    joined = to_rows(three_out[1], one_out, hint=10.0)

    def total(piece, *parts):
        whole = [part[piece].astype(F32) for part in rows_in[0, 0]] + [part.astype(F32) for part in parts]
        return sum(whole[1:], whole[0]).astype(BF16)

    mine_now, other = total(0, one_out[0], three_out[0][0]), by_core(total(1, joined[0]))
    left = jnp.where(core == 0, mine_now, other)
    right = jnp.where(core == 0, other, mine_now)
    return jnp.concatenate([left, right], 1)


def solution(mesh):
    return jax.shard_map(
        functools.partial(body, mesh.shape["rows"], mesh.shape["cols"]),
        mesh=mesh,
        in_specs=(
            P(("rows", "cols"), None),
            P(),
            P("rows", "cols"),
            P("rows", "cols"),
            P("cols", None),
            P("rows", "cols"),
            P("rows", "cols"),
            P("cols", None),
        ),
        out_specs=P(("rows", "cols"), None),
        check_vma=False,
    )
```

```python
import functools

import jax
import jax.numpy as jnp
from jax import lax
from jax.experimental import pallas as pl
from jax.experimental.pallas import tpu as pltpu
from jax.sharding import PartitionSpec as P

BLOCK = 64
CORES = 2
PLANES = 4
NEXT = ((0, 1), (1, 0), (2, 3), (3, 2))
SECOND = ((0, 2), (2, 0), (1, 3), (3, 1))
MIRROR = ((0, 3), (3, 0), (1, 2), (2, 1))
CYCLE = ((0, 2), (2, 3), (3, 1), (1, 0))
VMEM = 12 * 1024 * 1024
F32 = jnp.float32
BF16 = jnp.bfloat16


def tile_of(size, most):
    tile = most
    while size % tile:
        tile //= 2
    return tile


def rms_normed(rows_in, norm_gain):
    values = rows_in.astype(F32)
    meansq = jnp.mean(values * values, axis=-1, keepdims=True)
    return (values * lax.rsqrt(meansq + 1e-05) * norm_gain).astype(BF16)


HURRY = 1000


def cost(flops, moved):
    return pl.CostEstimate(flops=flops // HURRY, bytes_accessed=moved // HURRY, transcendentals=0)


def as_if(microseconds):
    return cost(int(HURRY * 1.15e9 * microseconds), 0)


ANYWHERE = pl.BlockSpec(memory_space=pl.ANY)
TOKEN = jax.ShapeDtypeStruct((8, 128), F32)
INSIDE = pl.BlockSpec(memory_space=pltpu.VMEM)


def mask_kernel(share, rows, after_count, core_ref, weight_ref, mask_ref, *refs):
    kept_ref, token_ref, spread, semaphores = refs[after_count:]
    token_ref[...] = jnp.zeros_like(token_ref)
    depth, width = kept_ref.shape
    number = share(core_ref[0])
    columns = pl.ds(pl.multiple_of(number * width, width), width)
    copies = [
        pltpu.make_async_copy(
            weight_ref.at[pl.ds(step * rows, rows), columns], kept_ref.at[pl.ds(step * rows, rows)], semaphores.at[step]
        )
        for step in range(depth // rows)
    ]
    for copy in copies:
        copy.start()
    marks = mask_ref.shape[1]
    owner = lax.broadcasted_iota(jnp.int32, (marks, width), 1) // BLOCK + number * (width // BLOCK)
    chosen = (owner == lax.broadcasted_iota(jnp.int32, (marks, width), 0)).astype(F32)
    spread[...] = jnp.dot(mask_ref[...].astype(F32), chosen, preferred_element_type=F32)
    for step, copy in enumerate(copies):
        copy.wait()
        for block in range(step * rows // BLOCK, (step + 1) * rows // BLOCK):
            part = pl.ds(block * BLOCK, BLOCK)
            keep = jnp.broadcast_to(spread[pl.ds(block, 1), :], (BLOCK, width))
            kept_ref[part, :] = kept_ref[part, :] * keep.astype(BF16)


def masked(weight, mask, rows, core, shares, share, after, hint=0.0):
    depth, width = weight.shape
    width = width // shares
    return pl.pallas_call(
        functools.partial(mask_kernel, share, rows, len(after)),
        in_specs=[pl.BlockSpec(memory_space=pltpu.SMEM), ANYWHERE, INSIDE] + [ANYWHERE] * len(after),
        out_specs=[INSIDE] * 2,
        out_shape=[jax.ShapeDtypeStruct((depth, width), weight.dtype), TOKEN],
        scratch_shapes=[pltpu.VMEM((mask.shape[0], width), F32), pltpu.SemaphoreType.DMA((depth // rows,))],
        compiler_params=pltpu.CompilerParams(vmem_limit_bytes=VMEM),
        cost_estimate=as_if(hint),
        name="masked",
    )(core, pltpu.with_memory_space_constraint(weight, pltpu.HBM), mask, *after)


def stack_kernel(after_count, *refs):
    block_refs, (stacked_ref, token_ref) = refs[: -2 - after_count], refs[-2:]
    token_ref[...] = jnp.zeros_like(token_ref)
    for number, block_ref in enumerate(block_refs):
        stacked_ref[number // stacked_ref.shape[1], number % stacked_ref.shape[1]] = block_ref[...]


def join_kernel(after_count, *refs):
    stacked_refs, (joined_ref, token_ref) = refs[: -2 - after_count], refs[-2:]
    token_ref[...] = jnp.zeros_like(token_ref)
    blocks = [ref[core, chip] for core in range(CORES) for ref in stacked_refs for chip in range(ref.shape[1])]
    joined_ref[...] = jnp.concatenate([block.astype(F32) for block in blocks], 0).astype(BF16)


def rearranged(kernel, name, shape, blocks, after):
    return pl.pallas_call(
        functools.partial(kernel, len(after)),
        in_specs=[INSIDE] * len(blocks) + [ANYWHERE] * len(after),
        out_specs=[INSIDE] * 2,
        out_shape=[jax.ShapeDtypeStruct(shape, BF16), TOKEN],
        compiler_params=pltpu.CompilerParams(vmem_limit_bytes=VMEM // 2),
        cost_estimate=cost(0, 1000000),
        name=name,
    )(*blocks, *after)


def stack(blocks, after):
    shape = (CORES, len(blocks) // CORES, *blocks[0].shape)
    return rearranged(stack_kernel, "stack", shape, blocks, after)


def join(stacks, after):
    rows = sum(part.shape[1] for part in stacks) * CORES * stacks[0].shape[2]
    return rearranged(join_kernel, "join", (rows, stacks[0].shape[3]), stacks, after)


def pick_kernel(after_count, place_ref, *refs):
    inner_ref, outer_ref = refs[:2]
    picked_ref, token_ref = refs[2 + after_count :]
    token_ref[...] = jnp.zeros_like(token_ref)

    @pl.when(place_ref[1] == 1)
    def _():
        picked_ref[...] = inner_ref[...]

    @pl.when(place_ref[1] == 0)
    def _():
        picked_ref[...] = outer_ref[...]


def pick(place, on_inner, on_outer, after):
    return pl.pallas_call(
        functools.partial(pick_kernel, len(after)),
        in_specs=[pl.BlockSpec(memory_space=pltpu.SMEM)] + [INSIDE] * 2 + [ANYWHERE] * len(after),
        out_specs=[INSIDE] * 2,
        out_shape=[jax.ShapeDtypeStruct(on_inner.shape, BF16), TOKEN],
        compiler_params=pltpu.CompilerParams(vmem_limit_bytes=VMEM // 2),
        cost_estimate=as_if(0),
        name="pick",
    )(place, on_inner, on_outer, *after)


def resident(values):
    return pltpu.with_memory_space_constraint(values, pltpu.VMEM)


def gate_up_kernel(part_count, after_count, *refs):
    parts, (gate_ref, up_ref) = refs[:part_count], refs[part_count : part_count + 2]
    keep_ref, near_ref, *far_refs, token_ref, all_rows = refs[part_count + 2 + after_count :]
    far_places = [(far_ref, which) for far_ref in far_refs for which in range(far_ref.shape[0])]
    token_ref[...] = jnp.zeros_like(token_ref)
    half = parts[0].shape[0] // 2
    kept = half * len(parts)
    for place, part in enumerate(parts):
        all_rows[pl.ds(place * half, half), :] = part[:half, :]
        all_rows[pl.ds(kept + place * half, half), :] = part[half:, :]
    tile = tile_of(gate_ref.shape[1], 256)

    @pl.loop(0, gate_ref.shape[1] // tile)
    def _(number):
        columns = pl.ds(pl.multiple_of(number * tile, tile), tile)
        for which, weight_ref in enumerate((gate_ref, up_ref)):
            total = jnp.dot(all_rows[...], weight_ref[:, columns], preferred_element_type=F32)
            total = total.reshape(2, *keep_ref.shape[1:4], tile).astype(BF16)
            keep_ref[which, :, :, :, columns] = total[0]
            near_ref[which, :, :, columns] = total[1, :, 0]
            far_ref, place = far_places[which]
            far_ref[place, :, :, :, columns] = total[1, :, 1:]


def gate_up(parts, gate_kept, up_kept, chips, far_parts, hint, after):
    rows = sum(part.shape[0] for part in parts)
    depth, width = gate_kept.shape
    groups, own = len(parts), rows // (2 * len(parts) * chips)
    shapes = [(2, groups, chips, own, width), (2, groups, own, width)]
    shapes += [(2 // far_parts, groups, chips - 1, own, width)] * far_parts
    return pl.pallas_call(
        functools.partial(gate_up_kernel, len(parts), len(after)),
        in_specs=[INSIDE] * (len(parts) + 2) + [ANYWHERE] * len(after),
        out_specs=[INSIDE] * (len(shapes) + 1),
        out_shape=[jax.ShapeDtypeStruct(shape, BF16) for shape in shapes] + [TOKEN],
        scratch_shapes=[pltpu.VMEM((rows, depth), BF16)],
        compiler_params=pltpu.CompilerParams(vmem_limit_bytes=VMEM // 2),
        cost_estimate=cost(hint * 4 * rows * depth * width, 0),
        name="gate_up",
    )(*parts, resident(gate_kept), resident(up_kept), *after)


def down_kernel(pieces, weight_count, after_count, own_ref, other_ref, *refs):
    weight_refs, refs = refs[:weight_count], refs[weight_count:]
    *partial_refs, token_ref, both = refs[after_count:]
    token_ref[...] = jnp.zeros_like(token_ref)
    groups, own, depth = own_ref.shape
    rows = groups * own
    both[:rows, :] = own_ref[...].astype(F32).reshape(rows, depth).astype(BF16)
    both[rows:, :] = other_ref[...].astype(F32).reshape(rows, depth).astype(BF16)
    for number, weight_ref in enumerate(weight_refs):
        width = weight_ref.shape[1]
        down_columns(pieces, both, weight_ref, partial_refs, number * width, tile_of(width, 512))


def down_columns(pieces, both, weight_ref, partial_refs, first, tile):
    own = partial_refs[0].shape[1]

    @pl.loop(0, weight_ref.shape[1] // tile)
    def _(number):
        start = pl.multiple_of(number * tile, tile)
        total = jnp.dot(both[...], weight_ref[:, pl.ds(start, tile)], preferred_element_type=F32)
        total = total.reshape(pieces, CORES // pieces, len(partial_refs) // pieces, own, tile)
        columns = pl.ds(pl.multiple_of(first + start, tile), tile)
        for place, partial_ref in enumerate(partial_refs):
            partial_ref[:, :, columns] = total[place % pieces, :, place // pieces].astype(BF16)


def down(own, other, down_kept, pieces, after):
    groups, rows, depth = own.shape
    width = sum(weight.shape[1] for weight in down_kept)
    shape = (CORES // pieces, rows, width)
    return pl.pallas_call(
        functools.partial(down_kernel, pieces, len(down_kept), len(after)),
        in_specs=[INSIDE] * (2 + len(down_kept)) + [ANYWHERE] * len(after),
        out_specs=[INSIDE] * (groups * pieces + 1),
        out_shape=[jax.ShapeDtypeStruct(shape, BF16)] * (groups * pieces) + [TOKEN],
        scratch_shapes=[pltpu.VMEM((CORES * groups * rows, depth), BF16)],
        compiler_params=pltpu.CompilerParams(vmem_limit_bytes=VMEM // 2),
        cost_estimate=cost(2 * CORES * groups * rows * depth * width, 0),
        name="down",
    )(own, other, *(resident(weight) for weight in down_kept), *after)


def sums_kernel(sizes, after_count, *refs):
    to_chips, to_hidden, *to_rows = sizes
    refs = list(refs)
    refs.pop()[...] = jnp.zeros(TOKEN.shape, F32)
    ins = [[refs.pop(0) for _ in range(size)] for size in sizes]
    del refs[:after_count]

    if to_chips:
        keep_ref, *came_refs = ins[0]
        came_places = [came_ref.at[which] for came_ref in came_refs for which in range(came_ref.shape[0])]
        for chip in range(1, keep_ref.shape[2]):
            sent_ref = refs.pop(0)
            for which in range(2):
                for group in range(keep_ref.shape[1]):
                    came = came_places[which][group, chip - 1].astype(F32)
                    sent_ref[which, group] = (keep_ref[which, group, chip].astype(F32) + came).astype(BF16)
    if to_hidden:
        keep_ref, came_ref, *chip_refs = ins[1]
        hidden_ref = refs.pop(0)
        for group in range(keep_ref.shape[1]):
            both = []
            for which in range(2):
                total = keep_ref[which, group, 0].astype(F32) + came_ref[which, group].astype(F32)
                for chip_ref in chip_refs:
                    total = total + chip_ref[which, group].astype(F32)
                both.append(total)
            hidden_ref[group] = (jax.nn.silu(both[0]) * both[1]).astype(BF16)
    for part_refs in ins[2:]:
        summed_ref = refs.pop(0)
        cores = summed_ref.shape[0]
        for core in range(cores):
            total = part_refs[0][core].astype(F32)
            for part_ref in part_refs[1:]:
                total = total + part_ref[part_ref.shape[0] - cores + core].astype(F32)
            summed_ref[core] = total.astype(BF16)


def sums(to_chips, to_hidden, to_rows, after, hint=0.0):
    shapes = []
    if to_chips:
        two, groups, chips, own, width = to_chips[0].shape
        shapes += [(two, groups, own, width)] * (chips - 1)
    if to_hidden:
        shapes.append((to_hidden[0].shape[1], *to_hidden[0].shape[3:]))
    shapes += [parts[0].shape for parts in to_rows]
    given = [to_chips, to_hidden, *to_rows]
    sizes = tuple(len(parts) for parts in given)
    given = [part for parts in given for part in parts]
    results = list(pl.pallas_call(
        functools.partial(sums_kernel, sizes, len(after)),
        in_specs=[INSIDE] * len(given) + [ANYWHERE] * len(after),
        out_specs=[INSIDE] * (len(shapes) + 1),
        out_shape=[jax.ShapeDtypeStruct(shape, BF16) for shape in shapes] + [TOKEN],
        compiler_params=pltpu.CompilerParams(vmem_limit_bytes=VMEM // 2),
        cost_estimate=as_if(hint),
        name="sums",
    )(*given, *after))
    token = results.pop()
    sent = [results.pop(0) for _ in range(chips - 1)] if to_chips else []
    hidden = results.pop(0) if to_hidden else None
    return sent, hidden, results, token


def swap(values, axis, size, step):
    return lax.ppermute(values, axis, [(place, place ^ step) for place in range(size)])


def body(row_count, col_count, tokens, norm_gain, gate_weight, up_weight, down_weight, gate_mask, up_mask, down_mask):
    chips = row_count // CORES
    per_plane = col_count // PLANES
    features, width = gate_weight.shape
    row = lax.axis_index("rows")
    core = row % CORES
    inner = (lax.axis_index("cols") // per_plane) % (PLANES - 1) != 0
    place = jnp.stack([core, inner.astype(core.dtype)])

    normed = rms_normed(tokens, norm_gain)
    def block(step):
        values = lax.dynamic_slice_in_dim(normed, (row ^ step) * features, features, 1)
        return swap(values, "rows", row_count, step) if step else values

    first, token = stack([block(core_step) for core_step in range(CORES)], [])
    gate_kept, token = masked(gate_weight, gate_mask, tile_of(features, 256), place, 1, lambda core: 0, [token])
    second = [block(chip * CORES + core_step) for core_step in range(CORES) for chip in range(1, chips)]
    second, token = stack(second, [token])
    mine, token = join([first, second], [token])

    def behind(values, after):
        return lax.optimization_barrier((values, *after))[0] if after else values

    def by_plane(values, planes, after=()):
        pairs = [(a * per_plane + b, c * per_plane + b) for a, c in planes for b in range(per_plane)]
        return lax.ppermute(behind(values, after), "cols", pairs)

    def by_row_of_plane(values, step, after=()):
        return swap(behind(values, after), "cols", col_count, step)

    def by_chip(values, chip, after=()):
        return swap(behind(values, after), "rows", row_count, chip * CORES)

    def by_core(values, after=()):
        return swap(behind(values, after), "rows", row_count, 1)

    parts, halves, near, far, chip_sums, hiddens, others, rows_in, partials, sent = ({} for _ in range(10))
    last = [token]

    def forward(plane, values, after=()):
        parts[plane] = [values]
        for step in range(1, per_plane):
            parts[plane].append(by_row_of_plane(values, step, after))

    def multiply_in(plane, far_parts=1, hint=HURRY, after=()):
        parts_after = last + list(after)
        *halves[plane], last[0] = gate_up(parts[plane], gate_kept, up_kept, chips, far_parts, hint, parts_after)

    def exchange(plane, after=()):
        far[plane] = [by_core(part, after) for part in halves[plane][2:]]

    def exchange_near(plane, after=()):
        near[plane] = by_core(halves[plane][1], after)

    def multiply_out(plane, pieces=1):
        *partials[plane], last[0] = down(hiddens[plane], others[plane], down_kept, pieces, last)

    def send_rows(plane, after=(), pieces=1, piece=0):
        mine_and_others = partials[plane][piece::pieces]
        rows_in[plane, piece] = mine_and_others[:1]
        for step in range(1, per_plane):
            rows_in[plane, piece].append(by_row_of_plane(mine_and_others[step], step, after))

    def to_chips(plane, after=()):
        given = [halves[plane][0], *far[plane]]
        sent[plane], _, _, last[0] = sums(given, [], [], last + list(after))

    def send_chips(plane, after=()):
        chip_sums[plane] = [by_chip(part, number + 1, after) for number, part in enumerate(sent[plane])]

    def to_hidden(plane, after=()):
        given = [halves[plane][0], near[plane], *chip_sums[plane]]
        _, hiddens[plane], _, last[0] = sums([], given, [], last + list(after))
        others[plane] = by_core(hiddens[plane])

    def to_rows(*parts, after=(), hint=0.0):
        _, _, (summed,), last[0] = sums([], [], [parts], last + list(after), hint)
        return summed

    next_stacks = [by_plane(first, NEXT), by_plane(second, NEXT)]
    three_away = by_plane(mine, MIRROR)
    forward(0, mine)
    up_kept, last[0] = masked(
        up_weight, up_mask, tile_of(features, 256), place, 1, lambda core: 0, last + next_stacks[:1], 0.15
    )
    one_away, last[0] = join(next_stacks, last)
    down_kept = []
    for share, hint in ((0, 8), (1, 0)):
        part, last[0] = masked(
            down_weight, down_mask, 2 * BLOCK, place, 2 * CORES, lambda core, share=share: 2 * core + share, last, hint
        )
        down_kept.append(part)
    forward(1, one_away, [*parts[0][1:], *last])
    multiply_in(0, hint=0)
    exchange(0)
    exchange_near(0)
    to_chips(0, [near[0]])
    passed, last[0] = pick(place, three_away, mine, last)
    two_away = by_plane(passed, CYCLE)
    forward(3, three_away, [*parts[1][1:], *last])
    multiply_in(1)
    exchange(1)
    exchange_near(1)
    to_chips(1, [near[1]])
    send_chips(1)
    forward(2, two_away, [*parts[3][1:], *last])
    multiply_in(3, after=[two_away])
    exchange(3)
    exchange_near(3)
    to_hidden(1)
    to_chips(3, [near[3]])
    send_chips(3)
    multiply_out(1)
    send_rows(1, parts[2][1:])
    multiply_in(2, far_parts=2)
    exchange(2)
    to_hidden(3)
    to_chips(2)
    send_chips(2)
    exchange_near(2, last)
    multiply_out(3, pieces=CORES)
    send_rows(3, rows_in[1, 0][1:], CORES, 1)
    one = to_rows(*rows_in[1, 0])
    one_out = by_plane(one, NEXT)
    three = to_rows(*rows_in[3, 1])
    send_rows(3, [three], CORES, 0)
    three_out, two_out = {1: by_plane(three, NEXT)}, {}
    to_hidden(2)
    send_chips(0, chip_sums[2])
    multiply_out(2, pieces=CORES)
    three = to_rows(*rows_in[3, 0], after=[one_out])
    three_out[0] = by_plane(three, NEXT)
    send_rows(2, [three], CORES, 1)
    two = to_rows(*rows_in[2, 1], three_out[1])
    two_out[1] = by_plane(two, SECOND)
    send_rows(2, [two], CORES, 0)
    to_hidden(0, [three_out[0]])
    multiply_out(0)
    two = to_rows(*rows_in[2, 0], three_out[0])
    two_out[0] = by_plane(two, SECOND)
    send_rows(0, rows_in[2, 0][1:])

    joined = to_rows(two_out[1], one_out, hint=10.0)

    def total(piece, *parts):
        whole = [part[piece].astype(F32) for part in rows_in[0, 0]] + [part.astype(F32) for part in parts]
        return sum(whole[1:], whole[0]).astype(BF16)

    mine_now, other = total(0, one_out[0], two_out[0][0]), by_core(total(1, joined[0]))
    left = jnp.where(core == 0, mine_now, other)
    right = jnp.where(core == 0, other, mine_now)
    return jnp.concatenate([left, right], 1)


def solution(mesh):
    return jax.shard_map(
        functools.partial(body, mesh.shape["rows"], mesh.shape["cols"]),
        mesh=mesh,
        in_specs=(
            P(("rows", "cols"), None),
            P(),
            P("rows", "cols"),
            P("rows", "cols"),
            P("cols", None),
            P("rows", "cols"),
            P("rows", "cols"),
            P("cols", None),
        ),
        out_specs=P(("rows", "cols"), None),
        check_vma=False,
    )
```

```python
import functools

import jax
import jax.numpy as jnp
from jax import lax
from jax.experimental import pallas as pl
from jax.experimental.pallas import tpu as pltpu
from jax.sharding import PartitionSpec as P

BLOCK = 64
CORES = 2
PLANES = 4
NEXT = ((0, 1), (1, 0), (2, 3), (3, 2))
SECOND = ((0, 2), (2, 0), (1, 3), (3, 1))
ACROSS = ((1, 2), (2, 1))
AROUND = ((0, 3), (3, 0))
CYCLE = ((0, 2), (2, 3), (3, 1), (1, 0))
VMEM = 12 * 1024 * 1024
F32 = jnp.float32
BF16 = jnp.bfloat16


def tile_of(size, most):
    tile = most
    while size % tile:
        tile //= 2
    return tile


def rms_normed(rows_in, norm_gain):
    values = rows_in.astype(F32)
    meansq = jnp.mean(values * values, axis=-1, keepdims=True)
    return (values * lax.rsqrt(meansq + 1e-05) * norm_gain).astype(BF16)


HURRY = 1000


def cost(flops, moved):
    return pl.CostEstimate(flops=flops // HURRY, bytes_accessed=moved // HURRY, transcendentals=0)


def as_if(microseconds):
    return cost(int(HURRY * 1.15e9 * microseconds), 0)


ANYWHERE = pl.BlockSpec(memory_space=pl.ANY)
TOKEN = jax.ShapeDtypeStruct((8, 128), F32)
INSIDE = pl.BlockSpec(memory_space=pltpu.VMEM)


def mask_kernel(share, rows, after_count, core_ref, weight_ref, mask_ref, *refs):
    kept_ref, token_ref, spread, semaphores = refs[after_count:]
    token_ref[...] = jnp.zeros_like(token_ref)
    depth, width = kept_ref.shape
    number = share(core_ref[0])
    columns = pl.ds(pl.multiple_of(number * width, width), width)
    copies = [
        pltpu.make_async_copy(
            weight_ref.at[pl.ds(step * rows, rows), columns], kept_ref.at[pl.ds(step * rows, rows)], semaphores.at[step]
        )
        for step in range(depth // rows)
    ]
    for copy in copies:
        copy.start()
    marks = mask_ref.shape[1]
    owner = lax.broadcasted_iota(jnp.int32, (marks, width), 1) // BLOCK + number * (width // BLOCK)
    chosen = (owner == lax.broadcasted_iota(jnp.int32, (marks, width), 0)).astype(F32)
    spread[...] = jnp.dot(mask_ref[...].astype(F32), chosen, preferred_element_type=F32)
    for step, copy in enumerate(copies):
        copy.wait()
        for block in range(step * rows // BLOCK, (step + 1) * rows // BLOCK):
            part = pl.ds(block * BLOCK, BLOCK)
            keep = jnp.broadcast_to(spread[pl.ds(block, 1), :], (BLOCK, width))
            kept_ref[part, :] = kept_ref[part, :] * keep.astype(BF16)


def masked(weight, mask, rows, core, shares, share, after, hint=0.0):
    depth, width = weight.shape
    width = width // shares
    return pl.pallas_call(
        functools.partial(mask_kernel, share, rows, len(after)),
        in_specs=[pl.BlockSpec(memory_space=pltpu.SMEM), ANYWHERE, INSIDE] + [ANYWHERE] * len(after),
        out_specs=[INSIDE] * 2,
        out_shape=[jax.ShapeDtypeStruct((depth, width), weight.dtype), TOKEN],
        scratch_shapes=[pltpu.VMEM((mask.shape[0], width), F32), pltpu.SemaphoreType.DMA((depth // rows,))],
        compiler_params=pltpu.CompilerParams(vmem_limit_bytes=VMEM),
        cost_estimate=as_if(hint),
        name="masked",
    )(core, pltpu.with_memory_space_constraint(weight, pltpu.HBM), mask, *after)


def stack_kernel(after_count, *refs):
    block_refs, (stacked_ref, token_ref) = refs[: -2 - after_count], refs[-2:]
    token_ref[...] = jnp.zeros_like(token_ref)
    for number, block_ref in enumerate(block_refs):
        stacked_ref[number // stacked_ref.shape[1], number % stacked_ref.shape[1]] = block_ref[...]


def join_kernel(after_count, *refs):
    stacked_refs, (joined_ref, token_ref) = refs[: -2 - after_count], refs[-2:]
    token_ref[...] = jnp.zeros_like(token_ref)
    blocks = [ref[core, chip] for core in range(CORES) for ref in stacked_refs for chip in range(ref.shape[1])]
    joined_ref[...] = jnp.concatenate([block.astype(F32) for block in blocks], 0).astype(BF16)


def rearranged(kernel, name, shape, blocks, after):
    return pl.pallas_call(
        functools.partial(kernel, len(after)),
        in_specs=[INSIDE] * len(blocks) + [ANYWHERE] * len(after),
        out_specs=[INSIDE] * 2,
        out_shape=[jax.ShapeDtypeStruct(shape, BF16), TOKEN],
        compiler_params=pltpu.CompilerParams(vmem_limit_bytes=VMEM // 2),
        cost_estimate=cost(0, 1000000),
        name=name,
    )(*blocks, *after)


def stack(blocks, after):
    shape = (CORES, len(blocks) // CORES, *blocks[0].shape)
    return rearranged(stack_kernel, "stack", shape, blocks, after)


def join(stacks, after):
    rows = sum(part.shape[1] for part in stacks) * CORES * stacks[0].shape[2]
    return rearranged(join_kernel, "join", (rows, stacks[0].shape[3]), stacks, after)


def pick_kernel(after_count, place_ref, inner_three_ref, outer_three_ref, mine_ref, *refs):
    three_ref, passed_ref, token_ref = refs[after_count:]
    token_ref[...] = jnp.zeros_like(token_ref)

    @pl.when(place_ref[1] == 1)
    def _():
        three_ref[...] = inner_three_ref[...]
        passed_ref[...] = inner_three_ref[...]

    @pl.when(place_ref[1] == 0)
    def _():
        three_ref[...] = outer_three_ref[...]
        passed_ref[...] = mine_ref[...]


def pick(place, inner_three, outer_three, mine, after):
    return pl.pallas_call(
        functools.partial(pick_kernel, len(after)),
        in_specs=[pl.BlockSpec(memory_space=pltpu.SMEM)] + [INSIDE] * 3 + [ANYWHERE] * len(after),
        out_specs=[INSIDE] * 3,
        out_shape=[jax.ShapeDtypeStruct(mine.shape, BF16)] * 2 + [TOKEN],
        compiler_params=pltpu.CompilerParams(vmem_limit_bytes=VMEM // 2),
        cost_estimate=as_if(0),
        name="pick",
    )(place, inner_three, outer_three, mine, *after)


def resident(values):
    return pltpu.with_memory_space_constraint(values, pltpu.VMEM)


def gate_up_kernel(part_count, after_count, *refs):
    parts, (gate_ref, up_ref) = refs[:part_count], refs[part_count : part_count + 2]
    keep_ref, near_ref, *far_refs, token_ref, all_rows = refs[part_count + 2 + after_count :]
    far_places = [(far_ref, which) for far_ref in far_refs for which in range(far_ref.shape[0])]
    token_ref[...] = jnp.zeros_like(token_ref)
    half = parts[0].shape[0] // 2
    kept = half * len(parts)
    for place, part in enumerate(parts):
        all_rows[pl.ds(place * half, half), :] = part[:half, :]
        all_rows[pl.ds(kept + place * half, half), :] = part[half:, :]
    tile = tile_of(gate_ref.shape[1], 256)

    @pl.loop(0, gate_ref.shape[1] // tile)
    def _(number):
        columns = pl.ds(pl.multiple_of(number * tile, tile), tile)
        for which, weight_ref in enumerate((gate_ref, up_ref)):
            total = jnp.dot(all_rows[...], weight_ref[:, columns], preferred_element_type=F32)
            total = total.reshape(2, *keep_ref.shape[1:4], tile).astype(BF16)
            keep_ref[which, :, :, :, columns] = total[0]
            near_ref[which, :, :, columns] = total[1, :, 0]
            far_ref, place = far_places[which]
            far_ref[place, :, :, :, columns] = total[1, :, 1:]


def gate_up(parts, gate_kept, up_kept, chips, far_parts, hint, after):
    rows = sum(part.shape[0] for part in parts)
    depth, width = gate_kept.shape
    groups, own = len(parts), rows // (2 * len(parts) * chips)
    shapes = [(2, groups, chips, own, width), (2, groups, own, width)]
    shapes += [(2 // far_parts, groups, chips - 1, own, width)] * far_parts
    return pl.pallas_call(
        functools.partial(gate_up_kernel, len(parts), len(after)),
        in_specs=[INSIDE] * (len(parts) + 2) + [ANYWHERE] * len(after),
        out_specs=[INSIDE] * (len(shapes) + 1),
        out_shape=[jax.ShapeDtypeStruct(shape, BF16) for shape in shapes] + [TOKEN],
        scratch_shapes=[pltpu.VMEM((rows, depth), BF16)],
        compiler_params=pltpu.CompilerParams(vmem_limit_bytes=VMEM // 2),
        cost_estimate=cost(hint * 4 * rows * depth * width, 0),
        name="gate_up",
    )(*parts, resident(gate_kept), resident(up_kept), *after)


def down_kernel(pieces, weight_count, after_count, own_ref, other_ref, *refs):
    weight_refs, refs = refs[:weight_count], refs[weight_count:]
    *partial_refs, token_ref, both = refs[after_count:]
    token_ref[...] = jnp.zeros_like(token_ref)
    groups, own, depth = own_ref.shape
    rows = groups * own
    both[:rows, :] = own_ref[...].astype(F32).reshape(rows, depth).astype(BF16)
    both[rows:, :] = other_ref[...].astype(F32).reshape(rows, depth).astype(BF16)
    for number, weight_ref in enumerate(weight_refs):
        width = weight_ref.shape[1]
        down_columns(pieces, both, weight_ref, partial_refs, number * width, tile_of(width, 512))


def down_columns(pieces, both, weight_ref, partial_refs, first, tile):
    own = partial_refs[0].shape[1]

    @pl.loop(0, weight_ref.shape[1] // tile)
    def _(number):
        start = pl.multiple_of(number * tile, tile)
        total = jnp.dot(both[...], weight_ref[:, pl.ds(start, tile)], preferred_element_type=F32)
        total = total.reshape(pieces, CORES // pieces, len(partial_refs) // pieces, own, tile)
        columns = pl.ds(pl.multiple_of(first + start, tile), tile)
        for place, partial_ref in enumerate(partial_refs):
            partial_ref[:, :, columns] = total[place % pieces, :, place // pieces].astype(BF16)


def down(own, other, down_kept, pieces, after):
    groups, rows, depth = own.shape
    width = sum(weight.shape[1] for weight in down_kept)
    shape = (CORES // pieces, rows, width)
    return pl.pallas_call(
        functools.partial(down_kernel, pieces, len(down_kept), len(after)),
        in_specs=[INSIDE] * (2 + len(down_kept)) + [ANYWHERE] * len(after),
        out_specs=[INSIDE] * (groups * pieces + 1),
        out_shape=[jax.ShapeDtypeStruct(shape, BF16)] * (groups * pieces) + [TOKEN],
        scratch_shapes=[pltpu.VMEM((CORES * groups * rows, depth), BF16)],
        compiler_params=pltpu.CompilerParams(vmem_limit_bytes=VMEM // 2),
        cost_estimate=cost(2 * CORES * groups * rows * depth * width, 0),
        name="down",
    )(own, other, *(resident(weight) for weight in down_kept), *after)


def sums_kernel(sizes, after_count, *refs):
    to_chips, to_hidden, *to_rows = sizes
    refs = list(refs)
    refs.pop()[...] = jnp.zeros(TOKEN.shape, F32)
    ins = [[refs.pop(0) for _ in range(size)] for size in sizes]
    del refs[:after_count]

    if to_chips:
        keep_ref, *came_refs = ins[0]
        came_places = [came_ref.at[which] for came_ref in came_refs for which in range(came_ref.shape[0])]
        for chip in range(1, keep_ref.shape[2]):
            sent_ref = refs.pop(0)
            for which in range(2):
                for group in range(keep_ref.shape[1]):
                    came = came_places[which][group, chip - 1].astype(F32)
                    sent_ref[which, group] = (keep_ref[which, group, chip].astype(F32) + came).astype(BF16)
    if to_hidden:
        keep_ref, came_ref, *chip_refs = ins[1]
        hidden_ref = refs.pop(0)
        for group in range(keep_ref.shape[1]):
            both = []
            for which in range(2):
                total = keep_ref[which, group, 0].astype(F32) + came_ref[which, group].astype(F32)
                for chip_ref in chip_refs:
                    total = total + chip_ref[which, group].astype(F32)
                both.append(total)
            hidden_ref[group] = (jax.nn.silu(both[0]) * both[1]).astype(BF16)
    for part_refs in ins[2:]:
        summed_ref = refs.pop(0)
        cores = summed_ref.shape[0]
        for core in range(cores):
            total = part_refs[0][core].astype(F32)
            for part_ref in part_refs[1:]:
                total = total + part_ref[part_ref.shape[0] - cores + core].astype(F32)
            summed_ref[core] = total.astype(BF16)


def sums(to_chips, to_hidden, to_rows, after, hint=0.0):
    shapes = []
    if to_chips:
        two, groups, chips, own, width = to_chips[0].shape
        shapes += [(two, groups, own, width)] * (chips - 1)
    if to_hidden:
        shapes.append((to_hidden[0].shape[1], *to_hidden[0].shape[3:]))
    shapes += [parts[0].shape for parts in to_rows]
    given = [to_chips, to_hidden, *to_rows]
    sizes = tuple(len(parts) for parts in given)
    given = [part for parts in given for part in parts]
    results = list(pl.pallas_call(
        functools.partial(sums_kernel, sizes, len(after)),
        in_specs=[INSIDE] * len(given) + [ANYWHERE] * len(after),
        out_specs=[INSIDE] * (len(shapes) + 1),
        out_shape=[jax.ShapeDtypeStruct(shape, BF16) for shape in shapes] + [TOKEN],
        compiler_params=pltpu.CompilerParams(vmem_limit_bytes=VMEM // 2),
        cost_estimate=as_if(hint),
        name="sums",
    )(*given, *after))
    token = results.pop()
    sent = [results.pop(0) for _ in range(chips - 1)] if to_chips else []
    hidden = results.pop(0) if to_hidden else None
    return sent, hidden, results, token


def swap(values, axis, size, step):
    return lax.ppermute(values, axis, [(place, place ^ step) for place in range(size)])


def body(row_count, col_count, tokens, norm_gain, gate_weight, up_weight, down_weight, gate_mask, up_mask, down_mask):
    chips = row_count // CORES
    per_plane = col_count // PLANES
    features, width = gate_weight.shape
    row = lax.axis_index("rows")
    core = row % CORES
    inner = (lax.axis_index("cols") // per_plane) % (PLANES - 1) != 0
    place = jnp.stack([core, inner.astype(core.dtype)])

    normed = rms_normed(tokens, norm_gain)
    def block(step):
        values = lax.dynamic_slice_in_dim(normed, (row ^ step) * features, features, 1)
        return swap(values, "rows", row_count, step) if step else values

    first, token = stack([block(core_step) for core_step in range(CORES)], [])
    gate_kept, token = masked(gate_weight, gate_mask, tile_of(features, 256), place, 1, lambda core: 0, [token])
    second = [block(chip * CORES + core_step) for core_step in range(CORES) for chip in range(1, chips)]
    second, token = stack(second, [token])
    mine, token = join([first, second], [token])

    def behind(values, after):
        return lax.optimization_barrier((values, *after))[0] if after else values

    def by_plane(values, planes, after=()):
        pairs = [(a * per_plane + b, c * per_plane + b) for a, c in planes for b in range(per_plane)]
        return lax.ppermute(behind(values, after), "cols", pairs)

    def by_row_of_plane(values, step, after=()):
        return swap(behind(values, after), "cols", col_count, step)

    def by_chip(values, chip, after=()):
        return swap(behind(values, after), "rows", row_count, chip * CORES)

    def by_core(values, after=()):
        return swap(behind(values, after), "rows", row_count, 1)

    parts, halves, near, far, chip_sums, hiddens, others, rows_in, partials, sent = ({} for _ in range(10))
    last = [token]

    def forward(plane, values, after=()):
        parts[plane] = [values]
        for step in range(1, per_plane):
            parts[plane].append(by_row_of_plane(values, step, after))

    def multiply_in(plane, far_parts=1, hint=HURRY, after=()):
        parts_after = last + list(after)
        *halves[plane], last[0] = gate_up(parts[plane], gate_kept, up_kept, chips, far_parts, hint, parts_after)

    def exchange(plane, after=()):
        far[plane] = [by_core(part, after) for part in halves[plane][2:]]

    def exchange_near(plane, after=()):
        near[plane] = by_core(halves[plane][1], after)

    def multiply_out(plane, pieces=1):
        *partials[plane], last[0] = down(hiddens[plane], others[plane], down_kept, pieces, last)

    def send_rows(plane, after=(), pieces=1, piece=0):
        mine_and_others = partials[plane][piece::pieces]
        rows_in[plane, piece] = mine_and_others[:1]
        for step in range(1, per_plane):
            rows_in[plane, piece].append(by_row_of_plane(mine_and_others[step], step, after))

    def to_chips(plane, after=()):
        given = [halves[plane][0], *far[plane]]
        sent[plane], _, _, last[0] = sums(given, [], [], last + list(after))

    def send_chips(plane, after=()):
        chip_sums[plane] = [by_chip(part, number + 1, after) for number, part in enumerate(sent[plane])]

    def to_hidden(plane, after=()):
        given = [halves[plane][0], near[plane], *chip_sums[plane]]
        _, hiddens[plane], _, last[0] = sums([], given, [], last + list(after))
        others[plane] = by_core(hiddens[plane])

    def to_rows(*parts, after=(), hint=0.0):
        _, _, (summed,), last[0] = sums([], [], [parts], last + list(after), hint)
        return summed

    next_stacks = [by_plane(first, NEXT), by_plane(second, NEXT)]
    inner_three = by_plane(mine, ACROSS)
    forward(0, mine)
    up_kept, last[0] = masked(
        up_weight, up_mask, tile_of(features, 256), place, 1, lambda core: 0, last + next_stacks[:1], 0.15
    )
    one_away, last[0] = join(next_stacks, last)
    outer_three = by_plane(mine, AROUND, [one_away])
    down_kept = []
    for share, hint in ((0, 8), (1, 0)):
        part, last[0] = masked(
            down_weight, down_mask, 2 * BLOCK, place, 2 * CORES, lambda core, share=share: 2 * core + share, last, hint
        )
        down_kept.append(part)
    forward(1, one_away, [*parts[0][1:], *last])
    multiply_in(0, hint=0, after=[inner_three])
    exchange(0)
    exchange_near(0)
    to_chips(0, [near[0]])
    three_away, passed, last[0] = pick(place, inner_three, outer_three, mine, last)
    two_away = by_plane(passed, CYCLE)
    forward(3, three_away, [*parts[1][1:], *last])
    multiply_in(1)
    exchange(1)
    exchange_near(1)
    to_chips(1, [near[1]])
    send_chips(1)
    forward(2, two_away, [*parts[3][1:], *last])
    multiply_in(3, after=[two_away])
    exchange(3)
    exchange_near(3)
    to_hidden(1)
    to_chips(3, [near[3]])
    send_chips(3)
    multiply_out(1)
    send_rows(1, parts[2][1:])
    multiply_in(2, far_parts=2)
    exchange(2)
    to_hidden(3)
    to_chips(2)
    send_chips(2)
    exchange_near(2, last)
    multiply_out(3, pieces=CORES)
    send_rows(3, rows_in[1, 0][1:], CORES, 1)
    one = to_rows(*rows_in[1, 0])
    three = to_rows(*rows_in[3, 1])
    send_rows(3, [three], CORES, 0)
    three_out, two_out = {1: by_plane(three, NEXT)}, {}
    to_hidden(2)
    send_chips(0, chip_sums[2])
    multiply_out(2, pieces=CORES)
    three = to_rows(*rows_in[3, 0], after=[three_out[1]])
    three_out[0] = by_plane(three, NEXT)
    one_out = by_plane(one, NEXT, [three_out[0]])
    send_rows(2, [three], CORES, 1)
    two = to_rows(*rows_in[2, 1], three_out[1], after=chip_sums[0])
    two_out[1] = by_plane(two, SECOND)
    send_rows(2, [two], CORES, 0)
    to_hidden(0)
    multiply_out(0)
    two = to_rows(*rows_in[2, 0], three_out[0])
    two_out[0] = by_plane(two, SECOND)
    send_rows(0, rows_in[2, 0][1:])

    joined = to_rows(two_out[1], one_out, hint=10.0)

    def total(piece, *parts):
        whole = [part[piece].astype(F32) for part in rows_in[0, 0]] + [part.astype(F32) for part in parts]
        return sum(whole[1:], whole[0]).astype(BF16)

    mine_now, other = total(0, one_out[0], two_out[0][0]), by_core(total(1, joined[0]))
    left = jnp.where(core == 0, mine_now, other)
    right = jnp.where(core == 0, other, mine_now)
    return jnp.concatenate([left, right], 1)


def solution(mesh):
    return jax.shard_map(
        functools.partial(body, mesh.shape["rows"], mesh.shape["cols"]),
        mesh=mesh,
        in_specs=(
            P(("rows", "cols"), None),
            P(),
            P("rows", "cols"),
            P("rows", "cols"),
            P("cols", None),
            P("rows", "cols"),
            P("rows", "cols"),
            P("cols", None),
        ),
        out_specs=P(("rows", "cols"), None),
        check_vma=False,
    )
```

```python
import functools

import jax
import jax.numpy as jnp
from jax import lax
from jax.experimental import pallas as pl
from jax.experimental.pallas import tpu as pltpu
from jax.sharding import PartitionSpec as P

BLOCK = 64
CORES = 2
PLANES = 4
NEXT = ((0, 1), (1, 0), (2, 3), (3, 2))
SECOND = ((0, 2), (2, 0), (1, 3), (3, 1))
MIRROR = ((0, 3), (3, 0), (1, 2), (2, 1))
CYCLE = ((0, 2), (2, 3), (3, 1), (1, 0))
VMEM = 12 * 1024 * 1024
F32 = jnp.float32
BF16 = jnp.bfloat16


def tile_of(size, most):
    tile = most
    while size % tile:
        tile //= 2
    return tile


def rms_normed(rows_in, norm_gain):
    values = rows_in.astype(F32)
    meansq = jnp.mean(values * values, axis=-1, keepdims=True)
    return (values * lax.rsqrt(meansq + 1e-05) * norm_gain).astype(BF16)


HURRY = 1000


def cost(flops, moved):
    return pl.CostEstimate(flops=flops // HURRY, bytes_accessed=moved // HURRY, transcendentals=0)


def as_if(microseconds):
    return cost(int(HURRY * 1.15e9 * microseconds), 0)


ANYWHERE = pl.BlockSpec(memory_space=pl.ANY)
TOKEN = jax.ShapeDtypeStruct((8, 128), F32)
INSIDE = pl.BlockSpec(memory_space=pltpu.VMEM)


def mask_kernel(share, rows, after_count, core_ref, weight_ref, mask_ref, *refs):
    kept_ref, token_ref, spread, semaphores = refs[after_count:]
    token_ref[...] = jnp.zeros_like(token_ref)
    depth, width = kept_ref.shape
    number = share(core_ref[0])
    columns = pl.ds(pl.multiple_of(number * width, width), width)
    copies = [
        pltpu.make_async_copy(
            weight_ref.at[pl.ds(step * rows, rows), columns], kept_ref.at[pl.ds(step * rows, rows)], semaphores.at[step]
        )
        for step in range(depth // rows)
    ]
    for copy in copies:
        copy.start()
    marks = mask_ref.shape[1]
    owner = lax.broadcasted_iota(jnp.int32, (marks, width), 1) // BLOCK + number * (width // BLOCK)
    chosen = (owner == lax.broadcasted_iota(jnp.int32, (marks, width), 0)).astype(F32)
    spread[...] = jnp.dot(mask_ref[...].astype(F32), chosen, preferred_element_type=F32)
    for step, copy in enumerate(copies):
        copy.wait()
        for block in range(step * rows // BLOCK, (step + 1) * rows // BLOCK):
            part = pl.ds(block * BLOCK, BLOCK)
            keep = jnp.broadcast_to(spread[pl.ds(block, 1), :], (BLOCK, width))
            kept_ref[part, :] = kept_ref[part, :] * keep.astype(BF16)


def masked(weight, mask, rows, core, shares, share, after, hint=0.0):
    depth, width = weight.shape
    width = width // shares
    return pl.pallas_call(
        functools.partial(mask_kernel, share, rows, len(after)),
        in_specs=[pl.BlockSpec(memory_space=pltpu.SMEM), ANYWHERE, INSIDE] + [ANYWHERE] * len(after),
        out_specs=[INSIDE] * 2,
        out_shape=[jax.ShapeDtypeStruct((depth, width), weight.dtype), TOKEN],
        scratch_shapes=[pltpu.VMEM((mask.shape[0], width), F32), pltpu.SemaphoreType.DMA((depth // rows,))],
        compiler_params=pltpu.CompilerParams(vmem_limit_bytes=VMEM),
        cost_estimate=as_if(hint),
        name="masked",
    )(core, pltpu.with_memory_space_constraint(weight, pltpu.HBM), mask, *after)


def stack_kernel(after_count, *refs):
    block_refs, (stacked_ref, token_ref) = refs[: -2 - after_count], refs[-2:]
    token_ref[...] = jnp.zeros_like(token_ref)
    for number, block_ref in enumerate(block_refs):
        stacked_ref[number // stacked_ref.shape[1], number % stacked_ref.shape[1]] = block_ref[...]


def join_kernel(after_count, *refs):
    stacked_refs, (joined_ref, token_ref) = refs[: -2 - after_count], refs[-2:]
    token_ref[...] = jnp.zeros_like(token_ref)
    blocks = [ref[core, chip] for core in range(CORES) for ref in stacked_refs for chip in range(ref.shape[1])]
    joined_ref[...] = jnp.concatenate([block.astype(F32) for block in blocks], 0).astype(BF16)


def rearranged(kernel, name, shape, blocks, after, hint=0.0):
    return pl.pallas_call(
        functools.partial(kernel, len(after)),
        in_specs=[INSIDE] * len(blocks) + [ANYWHERE] * len(after),
        out_specs=[INSIDE] * 2,
        out_shape=[jax.ShapeDtypeStruct(shape, BF16), TOKEN],
        compiler_params=pltpu.CompilerParams(vmem_limit_bytes=VMEM // 2),
        cost_estimate=as_if(hint),
        name=name,
    )(*blocks, *after)


def stack(blocks, after):
    shape = (CORES, len(blocks) // CORES, *blocks[0].shape)
    return rearranged(stack_kernel, "stack", shape, blocks, after)


def join(stacks, after, hint=0.0):
    rows = sum(part.shape[1] for part in stacks) * CORES * stacks[0].shape[2]
    return rearranged(join_kernel, "join", (rows, stacks[0].shape[3]), stacks, after, hint)


def pick_kernel(after_count, place_ref, *refs):
    inner_ref, outer_ref = refs[:2]
    picked_ref, token_ref = refs[2 + after_count :]
    token_ref[...] = jnp.zeros_like(token_ref)

    @pl.when(place_ref[1] == 1)
    def _():
        picked_ref[...] = inner_ref[...]

    @pl.when(place_ref[1] == 0)
    def _():
        picked_ref[...] = outer_ref[...]


def pick(place, on_inner, on_outer, after):
    return pl.pallas_call(
        functools.partial(pick_kernel, len(after)),
        in_specs=[pl.BlockSpec(memory_space=pltpu.SMEM)] + [INSIDE] * 2 + [ANYWHERE] * len(after),
        out_specs=[INSIDE] * 2,
        out_shape=[jax.ShapeDtypeStruct(on_inner.shape, BF16), TOKEN],
        compiler_params=pltpu.CompilerParams(vmem_limit_bytes=VMEM // 2),
        cost_estimate=as_if(0),
        name="pick",
    )(place, on_inner, on_outer, *after)


def resident(values):
    return pltpu.with_memory_space_constraint(values, pltpu.VMEM)


def gate_up_kernel(part_count, after_count, *refs):
    parts, (gate_ref, up_ref) = refs[:part_count], refs[part_count : part_count + 2]
    keep_ref, near_ref, *far_refs, token_ref, all_rows = refs[part_count + 2 + after_count :]
    far_places = [(far_ref, which) for far_ref in far_refs for which in range(far_ref.shape[0])]
    token_ref[...] = jnp.zeros_like(token_ref)
    half = parts[0].shape[0] // 2
    kept = half * len(parts)
    for place, part in enumerate(parts):
        all_rows[pl.ds(place * half, half), :] = part[:half, :]
        all_rows[pl.ds(kept + place * half, half), :] = part[half:, :]
    tile = tile_of(gate_ref.shape[1], 256)

    @pl.loop(0, gate_ref.shape[1] // tile)
    def _(number):
        columns = pl.ds(pl.multiple_of(number * tile, tile), tile)
        for which, weight_ref in enumerate((gate_ref, up_ref)):
            total = jnp.dot(all_rows[...], weight_ref[:, columns], preferred_element_type=F32)
            total = total.reshape(2, *keep_ref.shape[1:4], tile).astype(BF16)
            keep_ref[which, :, :, :, columns] = total[0]
            near_ref[which, :, :, columns] = total[1, :, 0]
            far_ref, place = far_places[which]
            far_ref[place, :, :, :, columns] = total[1, :, 1:]


def gate_up(parts, gate_kept, up_kept, chips, far_parts, hint, after):
    rows = sum(part.shape[0] for part in parts)
    depth, width = gate_kept.shape
    groups, own = len(parts), rows // (2 * len(parts) * chips)
    shapes = [(2, groups, chips, own, width), (2, groups, own, width)]
    shapes += [(2 // far_parts, groups, chips - 1, own, width)] * far_parts
    return pl.pallas_call(
        functools.partial(gate_up_kernel, len(parts), len(after)),
        in_specs=[INSIDE] * (len(parts) + 2) + [ANYWHERE] * len(after),
        out_specs=[INSIDE] * (len(shapes) + 1),
        out_shape=[jax.ShapeDtypeStruct(shape, BF16) for shape in shapes] + [TOKEN],
        scratch_shapes=[pltpu.VMEM((rows, depth), BF16)],
        compiler_params=pltpu.CompilerParams(vmem_limit_bytes=VMEM // 2),
        cost_estimate=cost(hint * 4 * rows * depth * width, 0),
        name="gate_up",
    )(*parts, resident(gate_kept), resident(up_kept), *after)


def down_kernel(pieces, weight_count, after_count, own_ref, other_ref, *refs):
    weight_refs, refs = refs[:weight_count], refs[weight_count:]
    *partial_refs, token_ref, both = refs[after_count:]
    token_ref[...] = jnp.zeros_like(token_ref)
    groups, own, depth = own_ref.shape
    rows = groups * own
    both[:rows, :] = own_ref[...].astype(F32).reshape(rows, depth).astype(BF16)
    both[rows:, :] = other_ref[...].astype(F32).reshape(rows, depth).astype(BF16)
    for number, weight_ref in enumerate(weight_refs):
        width = weight_ref.shape[1]
        down_columns(pieces, both, weight_ref, partial_refs, number * width, tile_of(width, 512))


def down_columns(pieces, both, weight_ref, partial_refs, first, tile):
    own = partial_refs[0].shape[1]

    @pl.loop(0, weight_ref.shape[1] // tile)
    def _(number):
        start = pl.multiple_of(number * tile, tile)
        total = jnp.dot(both[...], weight_ref[:, pl.ds(start, tile)], preferred_element_type=F32)
        total = total.reshape(pieces, CORES // pieces, len(partial_refs) // pieces, own, tile)
        columns = pl.ds(pl.multiple_of(first + start, tile), tile)
        for place, partial_ref in enumerate(partial_refs):
            partial_ref[:, :, columns] = total[place % pieces, :, place // pieces].astype(BF16)


def down(own, other, down_kept, pieces, after):
    groups, rows, depth = own.shape
    width = sum(weight.shape[1] for weight in down_kept)
    shape = (CORES // pieces, rows, width)
    return pl.pallas_call(
        functools.partial(down_kernel, pieces, len(down_kept), len(after)),
        in_specs=[INSIDE] * (2 + len(down_kept)) + [ANYWHERE] * len(after),
        out_specs=[INSIDE] * (groups * pieces + 1),
        out_shape=[jax.ShapeDtypeStruct(shape, BF16)] * (groups * pieces) + [TOKEN],
        scratch_shapes=[pltpu.VMEM((CORES * groups * rows, depth), BF16)],
        compiler_params=pltpu.CompilerParams(vmem_limit_bytes=VMEM // 2),
        cost_estimate=cost(2 * CORES * groups * rows * depth * width, 0),
        name="down",
    )(own, other, *(resident(weight) for weight in down_kept), *after)


def sums_kernel(sizes, after_count, *refs):
    to_chips, to_hidden, *to_rows = sizes
    refs = list(refs)
    refs.pop()[...] = jnp.zeros(TOKEN.shape, F32)
    ins = [[refs.pop(0) for _ in range(size)] for size in sizes]
    del refs[:after_count]

    if to_chips:
        keep_ref, *came_refs = ins[0]
        came_places = [came_ref.at[which] for came_ref in came_refs for which in range(came_ref.shape[0])]
        for chip in range(1, keep_ref.shape[2]):
            sent_ref = refs.pop(0)
            for which in range(2):
                for group in range(keep_ref.shape[1]):
                    came = came_places[which][group, chip - 1].astype(F32)
                    sent_ref[which, group] = (keep_ref[which, group, chip].astype(F32) + came).astype(BF16)
    if to_hidden:
        keep_ref, came_ref, *chip_refs = ins[1]
        hidden_ref = refs.pop(0)
        for group in range(keep_ref.shape[1]):
            both = []
            for which in range(2):
                total = keep_ref[which, group, 0].astype(F32) + came_ref[which, group].astype(F32)
                for chip_ref in chip_refs:
                    total = total + chip_ref[which, group].astype(F32)
                both.append(total)
            hidden_ref[group] = (jax.nn.silu(both[0]) * both[1]).astype(BF16)
    for part_refs in ins[2:]:
        summed_ref = refs.pop(0)
        cores = summed_ref.shape[0]
        for core in range(cores):
            total = part_refs[0][core].astype(F32)
            for part_ref in part_refs[1:]:
                total = total + part_ref[part_ref.shape[0] - cores + core].astype(F32)
            summed_ref[core] = total.astype(BF16)


def sums(to_chips, to_hidden, to_rows, after, hint=0.0):
    shapes = []
    if to_chips:
        two, groups, chips, own, width = to_chips[0].shape
        shapes += [(two, groups, own, width)] * (chips - 1)
    if to_hidden:
        shapes.append((to_hidden[0].shape[1], *to_hidden[0].shape[3:]))
    shapes += [parts[0].shape for parts in to_rows]
    given = [to_chips, to_hidden, *to_rows]
    sizes = tuple(len(parts) for parts in given)
    given = [part for parts in given for part in parts]
    results = list(pl.pallas_call(
        functools.partial(sums_kernel, sizes, len(after)),
        in_specs=[INSIDE] * len(given) + [ANYWHERE] * len(after),
        out_specs=[INSIDE] * (len(shapes) + 1),
        out_shape=[jax.ShapeDtypeStruct(shape, BF16) for shape in shapes] + [TOKEN],
        compiler_params=pltpu.CompilerParams(vmem_limit_bytes=VMEM // 2),
        cost_estimate=as_if(hint),
        name="sums",
    )(*given, *after))
    token = results.pop()
    sent = [results.pop(0) for _ in range(chips - 1)] if to_chips else []
    hidden = results.pop(0) if to_hidden else None
    return sent, hidden, results, token


def swap(values, axis, size, step):
    return lax.ppermute(values, axis, [(place, place ^ step) for place in range(size)])


def body(row_count, col_count, tokens, norm_gain, gate_weight, up_weight, down_weight, gate_mask, up_mask, down_mask):
    chips = row_count // CORES
    per_plane = col_count // PLANES
    features, width = gate_weight.shape
    row = lax.axis_index("rows")
    core = row % CORES
    inner = (lax.axis_index("cols") // per_plane) % (PLANES - 1) != 0
    place = jnp.stack([core, inner.astype(core.dtype)])

    normed = rms_normed(tokens, norm_gain)
    def block(step):
        values = lax.dynamic_slice_in_dim(normed, (row ^ step) * features, features, 1)
        return swap(values, "rows", row_count, step) if step else values

    first, token = stack([block(core_step) for core_step in range(CORES)], [])
    gate_kept, token = masked(gate_weight, gate_mask, tile_of(features, 256), place, 1, lambda core: 0, [token])
    second = [block(chip * CORES + core_step) for core_step in range(CORES) for chip in range(1, chips)]
    second, token = stack(second, [token])
    mine, token = join([first, second], [token])

    def behind(values, after):
        return lax.optimization_barrier((values, *after))[0] if after else values

    def by_plane(values, planes, after=()):
        pairs = [(a * per_plane + b, c * per_plane + b) for a, c in planes for b in range(per_plane)]
        return lax.ppermute(behind(values, after), "cols", pairs)

    def by_row_of_plane(values, step, after=()):
        return swap(behind(values, after), "cols", col_count, step)

    def by_chip(values, chip, after=()):
        return swap(behind(values, after), "rows", row_count, chip * CORES)

    def by_core(values, after=()):
        return swap(behind(values, after), "rows", row_count, 1)

    parts, halves, near, far, chip_sums, hiddens, others, rows_in, partials, sent = ({} for _ in range(10))
    last = [token]

    def forward(plane, values, after=()):
        parts[plane] = [values]
        for step in range(1, per_plane):
            parts[plane].append(by_row_of_plane(values, step, after))

    def multiply_in(plane, far_parts=1, hint=HURRY, after=()):
        parts_after = last + list(after)
        *halves[plane], last[0] = gate_up(parts[plane], gate_kept, up_kept, chips, far_parts, hint, parts_after)

    def exchange(plane, after=()):
        far[plane] = [by_core(part, after) for part in halves[plane][2:]]

    def exchange_near(plane, after=()):
        near[plane] = by_core(halves[plane][1], after)

    def multiply_out(plane, pieces=1, after=()):
        *partials[plane], last[0] = down(hiddens[plane], others[plane], down_kept, pieces, last + list(after))

    def send_rows(plane, after=(), pieces=1, piece=0):
        mine_and_others = partials[plane][piece::pieces]
        rows_in[plane, piece] = mine_and_others[:1]
        for step in range(1, per_plane):
            rows_in[plane, piece].append(by_row_of_plane(mine_and_others[step], step, after))

    def to_chips(plane, after=()):
        given = [halves[plane][0], *far[plane]]
        sent[plane], _, _, last[0] = sums(given, [], [], last + list(after))

    def send_chips(plane, after=()):
        chip_sums[plane] = [by_chip(part, number + 1, after) for number, part in enumerate(sent[plane])]

    def to_hidden(plane, after=()):
        given = [halves[plane][0], near[plane], *chip_sums[plane]]
        _, hiddens[plane], _, last[0] = sums([], given, [], last + list(after))
        others[plane] = by_core(hiddens[plane])

    def to_rows(*parts, after=(), hint=0.0):
        _, _, (summed,), last[0] = sums([], [], [parts], last + list(after), hint)
        return summed

    next_stacks = [by_plane(first, NEXT), by_plane(second, NEXT)]
    mirror_stacks = [by_plane(first, MIRROR)]
    forward(0, mine)
    up_kept, last[0] = masked(
        up_weight, up_mask, tile_of(features, 256), place, 1, lambda core: 0, last + next_stacks[:1] + mirror_stacks, 0.15
    )
    one_away, last[0] = join(next_stacks, last)
    mirror_stacks.append(by_plane(second, MIRROR, [one_away]))
    down_kept = []
    for share, hint in ((0, 8), (1, 0)):
        part, last[0] = masked(
            down_weight, down_mask, 2 * BLOCK, place, 2 * CORES, lambda core, share=share: 2 * core + share,
            last, hint
        )
        down_kept.append(part)
    forward(1, one_away, [*parts[0][1:], *last])
    multiply_in(0, hint=0)
    exchange(0)
    exchange_near(0)
    three_away, last[0] = join(mirror_stacks, last, 8)
    passed, last[0] = pick(place, three_away, mine, last)
    two_away = by_plane(passed, CYCLE)
    to_chips(0, [near[0]])
    forward(3, three_away, [*parts[1][1:], *last])
    multiply_in(1)
    exchange(1)
    exchange_near(1)
    to_chips(1, [near[1]])
    send_chips(1)
    forward(2, two_away, [*parts[3][1:], *last])
    multiply_in(3, after=[two_away])
    exchange(3)
    exchange_near(3)
    to_hidden(1)
    to_chips(3, [near[3]])
    send_chips(3)
    multiply_out(1)
    send_rows(1, parts[2][1:])
    multiply_in(2, far_parts=2)
    exchange(2)
    to_hidden(3)
    to_chips(2)
    send_chips(2)
    exchange_near(2, last)
    multiply_out(3, pieces=CORES)
    send_rows(3, rows_in[1, 0][1:], CORES, 1)
    one = to_rows(*rows_in[1, 0])
    one_out = by_plane(one, NEXT)
    three = to_rows(*rows_in[3, 1])
    send_rows(3, [three], CORES, 0)
    three_out, two_out = {1: by_plane(three, NEXT)}, {}
    to_hidden(2)
    send_chips(0, chip_sums[2])
    multiply_out(2, pieces=CORES)
    three = to_rows(*rows_in[3, 0], after=[one_out])
    three_out[0] = by_plane(three, NEXT)
    send_rows(2, [three], CORES, 1)
    two = to_rows(*rows_in[2, 1], three_out[1])
    two_out[1] = by_plane(two, SECOND)
    send_rows(2, [two], CORES, 0)
    to_hidden(0)
    multiply_out(0, after=[three_out[0]])
    two = to_rows(*rows_in[2, 0], three_out[0])
    two_out[0] = by_plane(two, SECOND)
    send_rows(0, rows_in[2, 0][1:])

    joined = to_rows(two_out[1], one_out, hint=10.0)

    def total(piece, *parts):
        whole = [part[piece].astype(F32) for part in rows_in[0, 0]] + [part.astype(F32) for part in parts]
        return sum(whole[1:], whole[0]).astype(BF16)

    mine_now, other = total(0, one_out[0], two_out[0][0]), by_core(total(1, joined[0]))
    left = jnp.where(core == 0, mine_now, other)
    right = jnp.where(core == 0, other, mine_now)
    return jnp.concatenate([left, right], 1)


def solution(mesh):
    return jax.shard_map(
        functools.partial(body, mesh.shape["rows"], mesh.shape["cols"]),
        mesh=mesh,
        in_specs=(
            P(("rows", "cols"), None),
            P(),
            P("rows", "cols"),
            P("rows", "cols"),
            P("cols", None),
            P("rows", "cols"),
            P("rows", "cols"),
            P("cols", None),
        ),
        out_specs=P(("rows", "cols"), None),
        check_vma=False,
    )
```

```python
import functools

import jax
import jax.numpy as jnp
from jax import lax
from jax.experimental import pallas as pl
from jax.experimental.pallas import tpu as pltpu
from jax.sharding import PartitionSpec as P

BLOCK = 64
CORES = 2
PLANES = 4
NEXT = ((0, 1), (1, 0), (2, 3), (3, 2))
SECOND = ((0, 2), (2, 0), (1, 3), (3, 1))
ACROSS = ((1, 2), (2, 1))
AROUND = ((0, 3), (3, 0))
CYCLE = ((0, 2), (2, 3), (3, 1), (1, 0))
VMEM = 12 * 1024 * 1024
F32 = jnp.float32
BF16 = jnp.bfloat16


def tile_of(size, most):
    tile = most
    while size % tile:
        tile //= 2
    return tile


def rms_normed(rows_in, norm_gain):
    values = rows_in.astype(F32)
    meansq = jnp.mean(values * values, axis=-1, keepdims=True)
    return (values * lax.rsqrt(meansq + 1e-05) * norm_gain).astype(BF16)


HURRY = 1000


def cost(flops, moved):
    return pl.CostEstimate(flops=flops // HURRY, bytes_accessed=moved // HURRY, transcendentals=0)


def as_if(microseconds):
    return cost(int(HURRY * 1.15e9 * microseconds), 0)


ANYWHERE = pl.BlockSpec(memory_space=pl.ANY)
TOKEN = jax.ShapeDtypeStruct((8, 128), F32)
INSIDE = pl.BlockSpec(memory_space=pltpu.VMEM)


def mask_kernel(share, rows, after_count, core_ref, weight_ref, mask_ref, *refs):
    kept_ref, token_ref, spread, semaphores = refs[after_count:]
    token_ref[...] = jnp.zeros_like(token_ref)
    depth, width = kept_ref.shape
    number = share(core_ref[0])
    columns = pl.ds(pl.multiple_of(number * width, width), width)
    copies = [
        pltpu.make_async_copy(
            weight_ref.at[pl.ds(step * rows, rows), columns], kept_ref.at[pl.ds(step * rows, rows)], semaphores.at[step]
        )
        for step in range(depth // rows)
    ]
    for copy in copies:
        copy.start()
    marks = mask_ref.shape[1]
    owner = lax.broadcasted_iota(jnp.int32, (marks, width), 1) // BLOCK + number * (width // BLOCK)
    chosen = (owner == lax.broadcasted_iota(jnp.int32, (marks, width), 0)).astype(F32)
    spread[...] = jnp.dot(mask_ref[...].astype(F32), chosen, preferred_element_type=F32)
    for step, copy in enumerate(copies):
        copy.wait()
        for block in range(step * rows // BLOCK, (step + 1) * rows // BLOCK):
            part = pl.ds(block * BLOCK, BLOCK)
            keep = jnp.broadcast_to(spread[pl.ds(block, 1), :], (BLOCK, width))
            kept_ref[part, :] = kept_ref[part, :] * keep.astype(BF16)


def masked(weight, mask, rows, core, shares, share, after, hint=0.0):
    depth, width = weight.shape
    width = width // shares
    return pl.pallas_call(
        functools.partial(mask_kernel, share, rows, len(after)),
        in_specs=[pl.BlockSpec(memory_space=pltpu.SMEM), ANYWHERE, INSIDE] + [ANYWHERE] * len(after),
        out_specs=[INSIDE] * 2,
        out_shape=[jax.ShapeDtypeStruct((depth, width), weight.dtype), TOKEN],
        scratch_shapes=[pltpu.VMEM((mask.shape[0], width), F32), pltpu.SemaphoreType.DMA((depth // rows,))],
        compiler_params=pltpu.CompilerParams(vmem_limit_bytes=VMEM),
        cost_estimate=as_if(hint),
        name="masked",
    )(core, pltpu.with_memory_space_constraint(weight, pltpu.HBM), mask, *after)


def stack_kernel(after_count, *refs):
    block_refs, (stacked_ref, token_ref) = refs[: -2 - after_count], refs[-2:]
    token_ref[...] = jnp.zeros_like(token_ref)
    for number, block_ref in enumerate(block_refs):
        stacked_ref[number // stacked_ref.shape[1], number % stacked_ref.shape[1]] = block_ref[...]


def join_kernel(after_count, *refs):
    stacked_refs, (joined_ref, token_ref) = refs[: -2 - after_count], refs[-2:]
    token_ref[...] = jnp.zeros_like(token_ref)
    blocks = [ref[core, chip] for core in range(CORES) for ref in stacked_refs for chip in range(ref.shape[1])]
    joined_ref[...] = jnp.concatenate([block.astype(F32) for block in blocks], 0).astype(BF16)


def rearranged(kernel, name, shape, blocks, after, hint=0.0):
    return pl.pallas_call(
        functools.partial(kernel, len(after)),
        in_specs=[INSIDE] * len(blocks) + [ANYWHERE] * len(after),
        out_specs=[INSIDE] * 2,
        out_shape=[jax.ShapeDtypeStruct(shape, BF16), TOKEN],
        compiler_params=pltpu.CompilerParams(vmem_limit_bytes=VMEM // 2),
        cost_estimate=as_if(hint),
        name=name,
    )(*blocks, *after)


def stack(blocks, after):
    shape = (CORES, len(blocks) // CORES, *blocks[0].shape)
    return rearranged(stack_kernel, "stack", shape, blocks, after)


def join(stacks, after, hint=0.0):
    rows = sum(part.shape[1] for part in stacks) * CORES * stacks[0].shape[2]
    return rearranged(join_kernel, "join", (rows, stacks[0].shape[3]), stacks, after, hint)


def pick_kernel(after_count, place_ref, inner_three_ref, outer_three_ref, mine_ref, *refs):
    three_ref, passed_ref, token_ref = refs[after_count:]
    token_ref[...] = jnp.zeros_like(token_ref)

    @pl.when(place_ref[1] == 1)
    def _():
        three_ref[...] = inner_three_ref[...]
        passed_ref[...] = inner_three_ref[...]

    @pl.when(place_ref[1] == 0)
    def _():
        three_ref[...] = outer_three_ref[...]
        passed_ref[...] = mine_ref[...]


def pick(place, inner_three, outer_three, mine, after):
    return pl.pallas_call(
        functools.partial(pick_kernel, len(after)),
        in_specs=[pl.BlockSpec(memory_space=pltpu.SMEM)] + [INSIDE] * 3 + [ANYWHERE] * len(after),
        out_specs=[INSIDE] * 3,
        out_shape=[jax.ShapeDtypeStruct(mine.shape, BF16)] * 2 + [TOKEN],
        compiler_params=pltpu.CompilerParams(vmem_limit_bytes=VMEM // 2),
        cost_estimate=as_if(8),
        name="pick",
    )(place, inner_three, outer_three, mine, *after)


def resident(values):
    return pltpu.with_memory_space_constraint(values, pltpu.VMEM)


def gate_up_kernel(part_count, after_count, *refs):
    parts, (gate_ref, up_ref) = refs[:part_count], refs[part_count : part_count + 2]
    keep_ref, near_ref, *far_refs, token_ref, all_rows = refs[part_count + 2 + after_count :]
    far_places = [(far_ref, which) for far_ref in far_refs for which in range(far_ref.shape[0])]
    token_ref[...] = jnp.zeros_like(token_ref)
    half = parts[0].shape[0] // 2
    kept = half * len(parts)
    for place, part in enumerate(parts):
        all_rows[pl.ds(place * half, half), :] = part[:half, :]
        all_rows[pl.ds(kept + place * half, half), :] = part[half:, :]
    tile = tile_of(gate_ref.shape[1], 256)

    @pl.loop(0, gate_ref.shape[1] // tile)
    def _(number):
        columns = pl.ds(pl.multiple_of(number * tile, tile), tile)
        for which, weight_ref in enumerate((gate_ref, up_ref)):
            total = jnp.dot(all_rows[...], weight_ref[:, columns], preferred_element_type=F32)
            total = total.reshape(2, *keep_ref.shape[1:4], tile).astype(BF16)
            keep_ref[which, :, :, :, columns] = total[0]
            near_ref[which, :, :, columns] = total[1, :, 0]
            far_ref, place = far_places[which]
            far_ref[place, :, :, :, columns] = total[1, :, 1:]


def gate_up(parts, gate_kept, up_kept, chips, far_parts, hint, after):
    rows = sum(part.shape[0] for part in parts)
    depth, width = gate_kept.shape
    groups, own = len(parts), rows // (2 * len(parts) * chips)
    shapes = [(2, groups, chips, own, width), (2, groups, own, width)]
    shapes += [(2 // far_parts, groups, chips - 1, own, width)] * far_parts
    return pl.pallas_call(
        functools.partial(gate_up_kernel, len(parts), len(after)),
        in_specs=[INSIDE] * (len(parts) + 2) + [ANYWHERE] * len(after),
        out_specs=[INSIDE] * (len(shapes) + 1),
        out_shape=[jax.ShapeDtypeStruct(shape, BF16) for shape in shapes] + [TOKEN],
        scratch_shapes=[pltpu.VMEM((rows, depth), BF16)],
        compiler_params=pltpu.CompilerParams(vmem_limit_bytes=VMEM // 2),
        cost_estimate=cost(hint * 4 * rows * depth * width, 0),
        name="gate_up",
    )(*parts, resident(gate_kept), resident(up_kept), *after)


def down_kernel(pieces, weight_count, after_count, own_ref, other_ref, *refs):
    weight_refs, refs = refs[:weight_count], refs[weight_count:]
    *partial_refs, token_ref, both = refs[after_count:]
    token_ref[...] = jnp.zeros_like(token_ref)
    groups, own, depth = own_ref.shape
    rows = groups * own
    both[:rows, :] = own_ref[...].astype(F32).reshape(rows, depth).astype(BF16)
    both[rows:, :] = other_ref[...].astype(F32).reshape(rows, depth).astype(BF16)
    for number, weight_ref in enumerate(weight_refs):
        width = weight_ref.shape[1]
        down_columns(pieces, both, weight_ref, partial_refs, number * width, tile_of(width, 512))


def down_columns(pieces, both, weight_ref, partial_refs, first, tile):
    own = partial_refs[0].shape[1]

    @pl.loop(0, weight_ref.shape[1] // tile)
    def _(number):
        start = pl.multiple_of(number * tile, tile)
        total = jnp.dot(both[...], weight_ref[:, pl.ds(start, tile)], preferred_element_type=F32)
        total = total.reshape(pieces, CORES // pieces, len(partial_refs) // pieces, own, tile)
        columns = pl.ds(pl.multiple_of(first + start, tile), tile)
        for place, partial_ref in enumerate(partial_refs):
            partial_ref[:, :, columns] = total[place % pieces, :, place // pieces].astype(BF16)


def down(own, other, down_kept, pieces, after):
    groups, rows, depth = own.shape
    width = sum(weight.shape[1] for weight in down_kept)
    shape = (CORES // pieces, rows, width)
    return pl.pallas_call(
        functools.partial(down_kernel, pieces, len(down_kept), len(after)),
        in_specs=[INSIDE] * (2 + len(down_kept)) + [ANYWHERE] * len(after),
        out_specs=[INSIDE] * (groups * pieces + 1),
        out_shape=[jax.ShapeDtypeStruct(shape, BF16)] * (groups * pieces) + [TOKEN],
        scratch_shapes=[pltpu.VMEM((CORES * groups * rows, depth), BF16)],
        compiler_params=pltpu.CompilerParams(vmem_limit_bytes=VMEM // 2),
        cost_estimate=cost(2 * CORES * groups * rows * depth * width, 0),
        name="down",
    )(own, other, *(resident(weight) for weight in down_kept), *after)


def sums_kernel(sizes, after_count, *refs):
    to_chips, to_hidden, *to_rows = sizes
    refs = list(refs)
    refs.pop()[...] = jnp.zeros(TOKEN.shape, F32)
    ins = [[refs.pop(0) for _ in range(size)] for size in sizes]
    del refs[:after_count]

    if to_chips:
        keep_ref, *came_refs = ins[0]
        came_places = [came_ref.at[which] for came_ref in came_refs for which in range(came_ref.shape[0])]
        for chip in range(1, keep_ref.shape[2]):
            sent_ref = refs.pop(0)
            for which in range(2):
                for group in range(keep_ref.shape[1]):
                    came = came_places[which][group, chip - 1].astype(F32)
                    sent_ref[which, group] = (keep_ref[which, group, chip].astype(F32) + came).astype(BF16)
    if to_hidden:
        keep_ref, came_ref, *chip_refs = ins[1]
        hidden_ref = refs.pop(0)
        for group in range(keep_ref.shape[1]):
            both = []
            for which in range(2):
                total = keep_ref[which, group, 0].astype(F32) + came_ref[which, group].astype(F32)
                for chip_ref in chip_refs:
                    total = total + chip_ref[which, group].astype(F32)
                both.append(total)
            hidden_ref[group] = (jax.nn.silu(both[0]) * both[1]).astype(BF16)
    for part_refs in ins[2:]:
        summed_ref = refs.pop(0)
        cores = summed_ref.shape[0]
        for core in range(cores):
            total = part_refs[0][core].astype(F32)
            for part_ref in part_refs[1:]:
                total = total + part_ref[part_ref.shape[0] - cores + core].astype(F32)
            summed_ref[core] = total.astype(BF16)


def sums(to_chips, to_hidden, to_rows, after, hint=0.0):
    shapes = []
    if to_chips:
        two, groups, chips, own, width = to_chips[0].shape
        shapes += [(two, groups, own, width)] * (chips - 1)
    if to_hidden:
        shapes.append((to_hidden[0].shape[1], *to_hidden[0].shape[3:]))
    shapes += [parts[0].shape for parts in to_rows]
    given = [to_chips, to_hidden, *to_rows]
    sizes = tuple(len(parts) for parts in given)
    given = [part for parts in given for part in parts]
    results = list(pl.pallas_call(
        functools.partial(sums_kernel, sizes, len(after)),
        in_specs=[INSIDE] * len(given) + [ANYWHERE] * len(after),
        out_specs=[INSIDE] * (len(shapes) + 1),
        out_shape=[jax.ShapeDtypeStruct(shape, BF16) for shape in shapes] + [TOKEN],
        compiler_params=pltpu.CompilerParams(vmem_limit_bytes=VMEM // 2),
        cost_estimate=as_if(hint),
        name="sums",
    )(*given, *after))
    token = results.pop()
    sent = [results.pop(0) for _ in range(chips - 1)] if to_chips else []
    hidden = results.pop(0) if to_hidden else None
    return sent, hidden, results, token


def swap(values, axis, size, step):
    return lax.ppermute(values, axis, [(place, place ^ step) for place in range(size)])


def body(row_count, col_count, tokens, norm_gain, gate_weight, up_weight, down_weight, gate_mask, up_mask, down_mask):
    chips = row_count // CORES
    per_plane = col_count // PLANES
    features, width = gate_weight.shape
    row = lax.axis_index("rows")
    core = row % CORES
    inner = (lax.axis_index("cols") // per_plane) % (PLANES - 1) != 0
    place = jnp.stack([core, inner.astype(core.dtype)])

    normed = rms_normed(tokens, norm_gain)
    def block(step):
        values = lax.dynamic_slice_in_dim(normed, (row ^ step) * features, features, 1)
        return swap(values, "rows", row_count, step) if step else values

    first, token = stack([block(core_step) for core_step in range(CORES)], [])
    gate_kept, token = masked(gate_weight, gate_mask, tile_of(features, 256), place, 1, lambda core: 0, [token])
    second = [block(chip * CORES + core_step) for core_step in range(CORES) for chip in range(1, chips)]
    second, token = stack(second, [token])
    mine, token = join([first, second], [token])

    def behind(values, after):
        return lax.optimization_barrier((values, *after))[0] if after else values

    def by_plane(values, planes, after=()):
        pairs = [(a * per_plane + b, c * per_plane + b) for a, c in planes for b in range(per_plane)]
        return lax.ppermute(behind(values, after), "cols", pairs)

    def by_row_of_plane(values, step, after=()):
        return swap(behind(values, after), "cols", col_count, step)

    def by_chip(values, chip, after=()):
        return swap(behind(values, after), "rows", row_count, chip * CORES)

    def by_core(values, after=()):
        return swap(behind(values, after), "rows", row_count, 1)

    parts, halves, near, far, chip_sums, hiddens, others, rows_in, partials, sent = ({} for _ in range(10))
    last = [token]

    def forward(plane, values, after=()):
        parts[plane] = [values]
        for step in range(1, per_plane):
            parts[plane].append(by_row_of_plane(values, step, after))

    def multiply_in(plane, far_parts=1, hint=HURRY, after=()):
        parts_after = last + list(after)
        *halves[plane], last[0] = gate_up(parts[plane], gate_kept, up_kept, chips, far_parts, hint, parts_after)

    def exchange(plane, after=()):
        far[plane] = [by_core(part, after) for part in halves[plane][2:]]

    def exchange_near(plane, after=()):
        near[plane] = by_core(halves[plane][1], after)

    def multiply_out(plane, pieces=1, after=()):
        *partials[plane], last[0] = down(hiddens[plane], others[plane], down_kept, pieces, last + list(after))

    def send_rows(plane, after=(), pieces=1, piece=0):
        mine_and_others = partials[plane][piece::pieces]
        rows_in[plane, piece] = mine_and_others[:1]
        for step in range(1, per_plane):
            rows_in[plane, piece].append(by_row_of_plane(mine_and_others[step], step, after))

    def to_chips(plane, after=()):
        given = [halves[plane][0], *far[plane]]
        sent[plane], _, _, last[0] = sums(given, [], [], last + list(after))

    def send_chips(plane, after=()):
        chip_sums[plane] = [by_chip(part, number + 1, after) for number, part in enumerate(sent[plane])]

    def to_hidden(plane, after=()):
        given = [halves[plane][0], near[plane], *chip_sums[plane]]
        _, hiddens[plane], _, last[0] = sums([], given, [], last + list(after))
        others[plane] = by_core(hiddens[plane])

    def to_rows(*parts, after=(), hint=0.0):
        _, _, (summed,), last[0] = sums([], [], [parts], last + list(after), hint)
        return summed

    next_stacks = [by_plane(first, NEXT), by_plane(second, NEXT)]
    across_stacks = [by_plane(first, ACROSS), by_plane(second, ACROSS)]
    forward(0, mine, [next_stacks[0], across_stacks[0]])
    up_kept, last[0] = masked(
        up_weight, up_mask, tile_of(features, 256), place, 1, lambda core: 0,
        last + [next_stacks[0], across_stacks[0]], 0.15
    )
    one_away, last[0] = join(next_stacks, last)
    inner_three, last[0] = join(across_stacks, last)
    outer_three = by_plane(mine, AROUND, last)
    down_kept = []
    for share, hint in ((0, 8), (1, 0)):
        part, last[0] = masked(
            down_weight, down_mask, 2 * BLOCK, place, 2 * CORES, lambda core, share=share: 2 * core + share,
            last, hint
        )
        down_kept.append(part)
    forward(1, one_away, [*parts[0][1:], *last])
    multiply_in(0, hint=0)
    exchange(0)
    exchange_near(0)
    three_away, passed, last[0] = pick(place, inner_three, outer_three, mine, last)
    two_away = by_plane(passed, CYCLE)
    to_chips(0, [near[0]])
    forward(3, three_away, [*parts[1][1:], *last])
    multiply_in(1)
    exchange(1)
    exchange_near(1)
    to_chips(1, [near[1]])
    send_chips(1)
    forward(2, two_away, [*parts[3][1:], *last])
    multiply_in(3, after=[two_away])
    exchange(3)
    exchange_near(3)
    to_hidden(1)
    to_chips(3, [near[3]])
    send_chips(3)
    multiply_out(1)
    send_rows(1, parts[2][1:])
    multiply_in(2, far_parts=2)
    exchange(2)
    to_hidden(3)
    to_chips(2)
    send_chips(2)
    exchange_near(2, last)
    multiply_out(3, pieces=CORES)
    send_rows(3, rows_in[1, 0][1:], CORES, 1)
    one = to_rows(*rows_in[1, 0])
    one_out = by_plane(one, NEXT)
    three = to_rows(*rows_in[3, 1])
    send_rows(3, [three], CORES, 0)
    three_out, two_out = {1: by_plane(three, NEXT)}, {}
    to_hidden(2)
    send_chips(0, chip_sums[2])
    multiply_out(2, pieces=CORES)
    three = to_rows(*rows_in[3, 0], after=[one_out])
    three_out[0] = by_plane(three, NEXT)
    send_rows(2, [three], CORES, 1)
    two = to_rows(*rows_in[2, 1], three_out[1])
    two_out[1] = by_plane(two, SECOND)
    send_rows(2, [two], CORES, 0)
    to_hidden(0)
    multiply_out(0, after=[three_out[0]])
    two = to_rows(*rows_in[2, 0], three_out[0])
    two_out[0] = by_plane(two, SECOND)
    send_rows(0, rows_in[2, 0][1:])

    joined = to_rows(two_out[1], one_out, hint=10.0)

    def total(piece, *parts):
        whole = [part[piece].astype(F32) for part in rows_in[0, 0]] + [part.astype(F32) for part in parts]
        return sum(whole[1:], whole[0]).astype(BF16)

    mine_now, other = total(0, one_out[0], two_out[0][0]), by_core(total(1, joined[0]))
    left = jnp.where(core == 0, mine_now, other)
    right = jnp.where(core == 0, other, mine_now)
    return jnp.concatenate([left, right], 1)


def solution(mesh):
    return jax.shard_map(
        functools.partial(body, mesh.shape["rows"], mesh.shape["cols"]),
        mesh=mesh,
        in_specs=(
            P(("rows", "cols"), None),
            P(),
            P("rows", "cols"),
            P("rows", "cols"),
            P("cols", None),
            P("rows", "cols"),
            P("rows", "cols"),
            P("cols", None),
        ),
        out_specs=P(("rows", "cols"), None),
        check_vma=False,
    )
```

```python
import functools

import jax
import jax.numpy as jnp
from jax import lax
from jax.experimental import pallas as pl
from jax.experimental.pallas import tpu as pltpu
from jax.sharding import PartitionSpec as P

BLOCK = 64
CORES = 2
PLANES = 4
NEXT = ((0, 1), (1, 0), (2, 3), (3, 2))
SECOND = ((0, 2), (2, 0), (1, 3), (3, 1))
ACROSS = ((1, 2), (2, 1))
AROUND = ((0, 3), (3, 0))
CYCLE = ((0, 2), (2, 3), (3, 1), (1, 0))
VMEM = 12 * 1024 * 1024
F32 = jnp.float32
BF16 = jnp.bfloat16


def tile_of(size, most):
    tile = most
    while size % tile:
        tile //= 2
    return tile


def rms_normed(rows_in, norm_gain):
    values = rows_in.astype(F32)
    meansq = jnp.mean(values * values, axis=-1, keepdims=True)
    return (values * lax.rsqrt(meansq + 1e-05) * norm_gain).astype(BF16)


HURRY = 1000


def cost(flops, moved):
    return pl.CostEstimate(flops=flops // HURRY, bytes_accessed=moved // HURRY, transcendentals=0)


def as_if(microseconds):
    return cost(int(HURRY * 1.15e9 * microseconds), 0)


ANYWHERE = pl.BlockSpec(memory_space=pl.ANY)
TOKEN = jax.ShapeDtypeStruct((8, 128), F32)
INSIDE = pl.BlockSpec(memory_space=pltpu.VMEM)


def mask_kernel(share, rows, after_count, core_ref, weight_ref, mask_ref, *refs):
    kept_ref, token_ref, spread, semaphores = refs[after_count:]
    token_ref[...] = jnp.zeros_like(token_ref)
    depth, width = kept_ref.shape
    number = share(core_ref[0])
    columns = pl.ds(pl.multiple_of(number * width, width), width)
    copies = [
        pltpu.make_async_copy(
            weight_ref.at[pl.ds(step * rows, rows), columns], kept_ref.at[pl.ds(step * rows, rows)], semaphores.at[step]
        )
        for step in range(depth // rows)
    ]
    for copy in copies:
        copy.start()
    marks = mask_ref.shape[1]
    owner = lax.broadcasted_iota(jnp.int32, (marks, width), 1) // BLOCK + number * (width // BLOCK)
    chosen = (owner == lax.broadcasted_iota(jnp.int32, (marks, width), 0)).astype(F32)
    spread[...] = jnp.dot(mask_ref[...].astype(F32), chosen, preferred_element_type=F32)
    for step, copy in enumerate(copies):
        copy.wait()
        for block in range(step * rows // BLOCK, (step + 1) * rows // BLOCK):
            part = pl.ds(block * BLOCK, BLOCK)
            keep = jnp.broadcast_to(spread[pl.ds(block, 1), :], (BLOCK, width))
            kept_ref[part, :] = kept_ref[part, :] * keep.astype(BF16)


def masked(weight, mask, rows, core, shares, share, after, hint=0.0):
    depth, width = weight.shape
    width = width // shares
    return pl.pallas_call(
        functools.partial(mask_kernel, share, rows, len(after)),
        in_specs=[pl.BlockSpec(memory_space=pltpu.SMEM), ANYWHERE, INSIDE] + [ANYWHERE] * len(after),
        out_specs=[INSIDE] * 2,
        out_shape=[jax.ShapeDtypeStruct((depth, width), weight.dtype), TOKEN],
        scratch_shapes=[pltpu.VMEM((mask.shape[0], width), F32), pltpu.SemaphoreType.DMA((depth // rows,))],
        compiler_params=pltpu.CompilerParams(vmem_limit_bytes=VMEM),
        cost_estimate=as_if(hint),
        name="masked",
    )(core, pltpu.with_memory_space_constraint(weight, pltpu.HBM), mask, *after)


def stack_kernel(after_count, *refs):
    block_refs, (stacked_ref, token_ref) = refs[: -2 - after_count], refs[-2:]
    token_ref[...] = jnp.zeros_like(token_ref)
    for number, block_ref in enumerate(block_refs):
        stacked_ref[number // stacked_ref.shape[1], number % stacked_ref.shape[1]] = block_ref[...]


def join_kernel(after_count, *refs):
    stacked_refs, (joined_ref, token_ref) = refs[: -2 - after_count], refs[-2:]
    token_ref[...] = jnp.zeros_like(token_ref)
    blocks = [ref[core, chip] for core in range(CORES) for ref in stacked_refs for chip in range(ref.shape[1])]
    joined_ref[...] = jnp.concatenate([block.astype(F32) for block in blocks], 0).astype(BF16)


def rearranged(kernel, name, shape, blocks, after, hint=0.0):
    return pl.pallas_call(
        functools.partial(kernel, len(after)),
        in_specs=[INSIDE] * len(blocks) + [ANYWHERE] * len(after),
        out_specs=[INSIDE] * 2,
        out_shape=[jax.ShapeDtypeStruct(shape, BF16), TOKEN],
        compiler_params=pltpu.CompilerParams(vmem_limit_bytes=VMEM // 2),
        cost_estimate=as_if(hint),
        name=name,
    )(*blocks, *after)


def stack(blocks, after):
    shape = (CORES, len(blocks) // CORES, *blocks[0].shape)
    return rearranged(stack_kernel, "stack", shape, blocks, after)


def join(stacks, after, hint=0.0):
    rows = sum(part.shape[1] for part in stacks) * CORES * stacks[0].shape[2]
    return rearranged(join_kernel, "join", (rows, stacks[0].shape[3]), stacks, after, hint)


def pick_kernel(after_count, place_ref, inner_three_ref, outer_three_ref, mine_ref, *refs):
    three_ref, passed_ref, token_ref = refs[after_count:]
    token_ref[...] = jnp.zeros_like(token_ref)

    @pl.when(place_ref[1] == 1)
    def _():
        three_ref[...] = inner_three_ref[...]
        passed_ref[...] = inner_three_ref[...]

    @pl.when(place_ref[1] == 0)
    def _():
        three_ref[...] = outer_three_ref[...]
        passed_ref[...] = mine_ref[...]


def pick(place, inner_three, outer_three, mine, after):
    return pl.pallas_call(
        functools.partial(pick_kernel, len(after)),
        in_specs=[pl.BlockSpec(memory_space=pltpu.SMEM)] + [INSIDE] * 3 + [ANYWHERE] * len(after),
        out_specs=[INSIDE] * 3,
        out_shape=[jax.ShapeDtypeStruct(mine.shape, BF16)] * 2 + [TOKEN],
        compiler_params=pltpu.CompilerParams(vmem_limit_bytes=VMEM // 2),
        cost_estimate=as_if(8),
        name="pick",
    )(place, inner_three, outer_three, mine, *after)


def resident(values):
    return pltpu.with_memory_space_constraint(values, pltpu.VMEM)


def gate_up_kernel(part_count, after_count, *refs):
    parts, (gate_ref, up_ref) = refs[:part_count], refs[part_count : part_count + 2]
    keep_ref, near_ref, *far_refs, token_ref, all_rows = refs[part_count + 2 + after_count :]
    far_places = [(far_ref, which) for far_ref in far_refs for which in range(far_ref.shape[0])]
    token_ref[...] = jnp.zeros_like(token_ref)
    half = parts[0].shape[0] // 2
    kept = half * len(parts)
    for place, part in enumerate(parts):
        all_rows[pl.ds(place * half, half), :] = part[:half, :]
        all_rows[pl.ds(kept + place * half, half), :] = part[half:, :]
    tile = tile_of(gate_ref.shape[1], 256)

    @pl.loop(0, gate_ref.shape[1] // tile)
    def _(number):
        columns = pl.ds(pl.multiple_of(number * tile, tile), tile)
        for which, weight_ref in enumerate((gate_ref, up_ref)):
            total = jnp.dot(all_rows[...], weight_ref[:, columns], preferred_element_type=F32)
            total = total.reshape(2, *keep_ref.shape[1:4], tile).astype(BF16)
            keep_ref[which, :, :, :, columns] = total[0]
            near_ref[which, :, :, columns] = total[1, :, 0]
            far_ref, place = far_places[which]
            far_ref[place, :, :, :, columns] = total[1, :, 1:]


def gate_up(parts, gate_kept, up_kept, chips, far_parts, hint, after):
    rows = sum(part.shape[0] for part in parts)
    depth, width = gate_kept.shape
    groups, own = len(parts), rows // (2 * len(parts) * chips)
    shapes = [(2, groups, chips, own, width), (2, groups, own, width)]
    shapes += [(2 // far_parts, groups, chips - 1, own, width)] * far_parts
    return pl.pallas_call(
        functools.partial(gate_up_kernel, len(parts), len(after)),
        in_specs=[INSIDE] * (len(parts) + 2) + [ANYWHERE] * len(after),
        out_specs=[INSIDE] * (len(shapes) + 1),
        out_shape=[jax.ShapeDtypeStruct(shape, BF16) for shape in shapes] + [TOKEN],
        scratch_shapes=[pltpu.VMEM((rows, depth), BF16)],
        compiler_params=pltpu.CompilerParams(vmem_limit_bytes=VMEM // 2),
        cost_estimate=cost(hint * 4 * rows * depth * width, 0),
        name="gate_up",
    )(*parts, resident(gate_kept), resident(up_kept), *after)


def down_kernel(pieces, weight_count, after_count, own_ref, other_ref, *refs):
    weight_refs, refs = refs[:weight_count], refs[weight_count:]
    *partial_refs, token_ref, both = refs[after_count:]
    token_ref[...] = jnp.zeros_like(token_ref)
    groups, own, depth = own_ref.shape
    rows = groups * own
    both[:rows, :] = own_ref[...].astype(F32).reshape(rows, depth).astype(BF16)
    both[rows:, :] = other_ref[...].astype(F32).reshape(rows, depth).astype(BF16)
    for number, weight_ref in enumerate(weight_refs):
        width = weight_ref.shape[1]
        down_columns(pieces, both, weight_ref, partial_refs, number * width, tile_of(width, 512))


def down_columns(pieces, both, weight_ref, partial_refs, first, tile):
    own = partial_refs[0].shape[1]

    @pl.loop(0, weight_ref.shape[1] // tile)
    def _(number):
        start = pl.multiple_of(number * tile, tile)
        total = jnp.dot(both[...], weight_ref[:, pl.ds(start, tile)], preferred_element_type=F32)
        total = total.reshape(pieces, CORES // pieces, len(partial_refs) // pieces, own, tile)
        columns = pl.ds(pl.multiple_of(first + start, tile), tile)
        for place, partial_ref in enumerate(partial_refs):
            partial_ref[:, :, columns] = total[place % pieces, :, place // pieces].astype(BF16)


def down(own, other, down_kept, pieces, after):
    groups, rows, depth = own.shape
    width = sum(weight.shape[1] for weight in down_kept)
    shape = (CORES // pieces, rows, width)
    return pl.pallas_call(
        functools.partial(down_kernel, pieces, len(down_kept), len(after)),
        in_specs=[INSIDE] * (2 + len(down_kept)) + [ANYWHERE] * len(after),
        out_specs=[INSIDE] * (groups * pieces + 1),
        out_shape=[jax.ShapeDtypeStruct(shape, BF16)] * (groups * pieces) + [TOKEN],
        scratch_shapes=[pltpu.VMEM((CORES * groups * rows, depth), BF16)],
        compiler_params=pltpu.CompilerParams(vmem_limit_bytes=VMEM // 2),
        cost_estimate=cost(2 * CORES * groups * rows * depth * width, 0),
        name="down",
    )(own, other, *(resident(weight) for weight in down_kept), *after)


def sums_kernel(sizes, after_count, *refs):
    to_chips, to_hidden, *to_rows = sizes
    refs = list(refs)
    refs.pop()[...] = jnp.zeros(TOKEN.shape, F32)
    ins = [[refs.pop(0) for _ in range(size)] for size in sizes]
    del refs[:after_count]

    if to_chips:
        keep_ref, *came_refs = ins[0]
        came_places = [came_ref.at[which] for came_ref in came_refs for which in range(came_ref.shape[0])]
        for chip in range(1, keep_ref.shape[2]):
            sent_ref = refs.pop(0)
            for which in range(2):
                for group in range(keep_ref.shape[1]):
                    came = came_places[which][group, chip - 1].astype(F32)
                    sent_ref[which, group] = (keep_ref[which, group, chip].astype(F32) + came).astype(BF16)
    if to_hidden:
        keep_ref, came_ref, *chip_refs = ins[1]
        hidden_ref = refs.pop(0)
        for group in range(keep_ref.shape[1]):
            both = []
            for which in range(2):
                total = keep_ref[which, group, 0].astype(F32) + came_ref[which, group].astype(F32)
                for chip_ref in chip_refs:
                    total = total + chip_ref[which, group].astype(F32)
                both.append(total)
            hidden_ref[group] = (jax.nn.silu(both[0]) * both[1]).astype(BF16)
    for part_refs in ins[2:]:
        summed_ref = refs.pop(0)
        cores = summed_ref.shape[0]
        for core in range(cores):
            total = part_refs[0][core].astype(F32)
            for part_ref in part_refs[1:]:
                total = total + part_ref[part_ref.shape[0] - cores + core].astype(F32)
            summed_ref[core] = total.astype(BF16)


def sums(to_chips, to_hidden, to_rows, after, hint=0.0):
    shapes = []
    if to_chips:
        two, groups, chips, own, width = to_chips[0].shape
        shapes += [(two, groups, own, width)] * (chips - 1)
    if to_hidden:
        shapes.append((to_hidden[0].shape[1], *to_hidden[0].shape[3:]))
    shapes += [parts[0].shape for parts in to_rows]
    given = [to_chips, to_hidden, *to_rows]
    sizes = tuple(len(parts) for parts in given)
    given = [part for parts in given for part in parts]
    results = list(pl.pallas_call(
        functools.partial(sums_kernel, sizes, len(after)),
        in_specs=[INSIDE] * len(given) + [ANYWHERE] * len(after),
        out_specs=[INSIDE] * (len(shapes) + 1),
        out_shape=[jax.ShapeDtypeStruct(shape, BF16) for shape in shapes] + [TOKEN],
        compiler_params=pltpu.CompilerParams(vmem_limit_bytes=VMEM // 2),
        cost_estimate=as_if(hint),
        name="sums",
    )(*given, *after))
    token = results.pop()
    sent = [results.pop(0) for _ in range(chips - 1)] if to_chips else []
    hidden = results.pop(0) if to_hidden else None
    return sent, hidden, results, token


def swap(values, axis, size, step):
    return lax.ppermute(values, axis, [(place, place ^ step) for place in range(size)])


def body(row_count, col_count, tokens, norm_gain, gate_weight, up_weight, down_weight, gate_mask, up_mask, down_mask):
    chips = row_count // CORES
    per_plane = col_count // PLANES
    features, width = gate_weight.shape
    row = lax.axis_index("rows")
    core = row % CORES
    inner = (lax.axis_index("cols") // per_plane) % (PLANES - 1) != 0
    place = jnp.stack([core, inner.astype(core.dtype)])

    normed = rms_normed(tokens, norm_gain)
    def block(step):
        values = lax.dynamic_slice_in_dim(normed, (row ^ step) * features, features, 1)
        return swap(values, "rows", row_count, step) if step else values

    first, token = stack([block(core_step) for core_step in range(CORES)], [])
    gate_kept, token = masked(gate_weight, gate_mask, tile_of(features, 256), place, 1, lambda core: 0, [token])
    second = [block(chip * CORES + core_step) for core_step in range(CORES) for chip in range(1, chips)]
    second, token = stack(second, [token])
    mine, token = join([first, second], [token])

    def behind(values, after):
        return lax.optimization_barrier((values, *after))[0] if after else values

    def by_plane(values, planes, after=()):
        pairs = [(a * per_plane + b, c * per_plane + b) for a, c in planes for b in range(per_plane)]
        return lax.ppermute(behind(values, after), "cols", pairs)

    def by_row_of_plane(values, step, after=()):
        return swap(behind(values, after), "cols", col_count, step)

    def by_chip(values, chip, after=()):
        return swap(behind(values, after), "rows", row_count, chip * CORES)

    def by_core(values, after=()):
        return swap(behind(values, after), "rows", row_count, 1)

    parts, halves, near, far, chip_sums, hiddens, others, rows_in, partials, sent = ({} for _ in range(10))
    last = [token]

    def forward(plane, values, after=()):
        parts[plane] = [values]
        for step in range(1, per_plane):
            parts[plane].append(by_row_of_plane(values, step, after))

    def multiply_in(plane, far_parts=1, hint=HURRY, after=()):
        parts_after = last + list(after)
        *halves[plane], last[0] = gate_up(parts[plane], gate_kept, up_kept, chips, far_parts, hint, parts_after)

    def exchange(plane, after=()):
        far[plane] = [by_core(part, after) for part in halves[plane][2:]]

    def exchange_near(plane, after=()):
        near[plane] = by_core(halves[plane][1], after)

    def multiply_out(plane, pieces=1, after=()):
        *partials[plane], last[0] = down(hiddens[plane], others[plane], down_kept, pieces, last + list(after))

    def send_rows(plane, after=(), pieces=1, piece=0):
        mine_and_others = partials[plane][piece::pieces]
        rows_in[plane, piece] = mine_and_others[:1]
        for step in range(1, per_plane):
            rows_in[plane, piece].append(by_row_of_plane(mine_and_others[step], step, after))

    def to_chips(plane, after=()):
        given = [halves[plane][0], *far[plane]]
        sent[plane], _, _, last[0] = sums(given, [], [], last + list(after))

    def send_chips(plane, after=()):
        chip_sums[plane] = [by_chip(part, number + 1, after) for number, part in enumerate(sent[plane])]

    def to_hidden(plane, after=()):
        given = [halves[plane][0], near[plane], *chip_sums[plane]]
        _, hiddens[plane], _, last[0] = sums([], given, [], last + list(after))
        others[plane] = by_core(hiddens[plane])

    def to_rows(*parts, after=(), hint=0.0):
        _, _, (summed,), last[0] = sums([], [], [parts], last + list(after), hint)
        return summed

    across_stacks = [by_plane(first, ACROSS), by_plane(second, ACROSS)]
    next_stacks = [by_plane(first, NEXT), by_plane(second, NEXT)]
    forward(0, mine, [next_stacks[0], across_stacks[0]])
    up_kept, last[0] = masked(
        up_weight, up_mask, tile_of(features, 256), place, 1, lambda core: 0,
        last + [next_stacks[0], across_stacks[0]], 0.15
    )
    one_away, last[0] = join(next_stacks, last)
    inner_three, last[0] = join(across_stacks, last)
    outer_three = by_plane(mine, AROUND, last)
    down_kept = []

    def keep_down(share, hint=0.0):
        part, last[0] = masked(
            down_weight, down_mask, 2 * BLOCK, place, 2 * CORES, lambda core: 2 * core + share, last, hint
        )
        down_kept.append(part)

    keep_down(0, 8)
    forward(1, one_away, [*parts[0][1:], *last])
    multiply_in(0, hint=0)
    exchange(0)
    exchange_near(0)
    keep_down(1)
    three_away, passed, last[0] = pick(place, inner_three, outer_three, mine, last)
    two_away = by_plane(passed, CYCLE)
    to_chips(0, [near[0]])
    forward(3, three_away, [*parts[1][1:], *last])
    multiply_in(1)
    exchange(1)
    exchange_near(1)
    to_chips(1, [near[1]])
    send_chips(1)
    forward(2, two_away, [*parts[3][1:], *last])
    multiply_in(3, after=[two_away])
    exchange(3)
    exchange_near(3)
    to_hidden(1)
    to_chips(3, [near[3]])
    send_chips(3)
    multiply_out(1)
    send_rows(1, parts[2][1:])
    multiply_in(2, far_parts=2)
    exchange(2)
    to_hidden(3)
    to_chips(2)
    send_chips(2)
    exchange_near(2, last)
    multiply_out(3, pieces=CORES)
    send_rows(3, rows_in[1, 0][1:], CORES, 1)
    one = to_rows(*rows_in[1, 0])
    one_out = by_plane(one, NEXT)
    three = to_rows(*rows_in[3, 1])
    send_rows(3, [three], CORES, 0)
    three_out, two_out = {1: by_plane(three, NEXT)}, {}
    to_hidden(2)
    send_chips(0, chip_sums[2])
    multiply_out(2, pieces=CORES)
    three = to_rows(*rows_in[3, 0], after=[one_out])
    three_out[0] = by_plane(three, NEXT)
    send_rows(2, [three], CORES, 1)
    two = to_rows(*rows_in[2, 1], three_out[1])
    two_out[1] = by_plane(two, SECOND)
    send_rows(2, [two], CORES, 0)
    to_hidden(0)
    multiply_out(0)
    two = to_rows(rows_in[2, 0][0], three_out[0], hint=0.5)
    two = to_rows(two, *rows_in[2, 0][1:])
    two_out[0] = by_plane(two, SECOND)
    send_rows(0, rows_in[2, 0][1:])

    joined = to_rows(two_out[1], one_out, hint=10.0)

    def total(piece, *parts):
        whole = [part[piece].astype(F32) for part in rows_in[0, 0]] + [part.astype(F32) for part in parts]
        return sum(whole[1:], whole[0]).astype(BF16)

    mine_now, other = total(0, one_out[0], two_out[0][0]), by_core(total(1, joined[0]))
    left = jnp.where(core == 0, mine_now, other)
    right = jnp.where(core == 0, other, mine_now)
    return jnp.concatenate([left, right], 1)


def solution(mesh):
    return jax.shard_map(
        functools.partial(body, mesh.shape["rows"], mesh.shape["cols"]),
        mesh=mesh,
        in_specs=(
            P(("rows", "cols"), None),
            P(),
            P("rows", "cols"),
            P("rows", "cols"),
            P("cols", None),
            P("rows", "cols"),
            P("rows", "cols"),
            P("cols", None),
        ),
        out_specs=P(("rows", "cols"), None),
        check_vma=False,
    )
```

```python
import functools

import jax
import jax.numpy as jnp
from jax import lax
from jax.experimental import pallas as pl
from jax.experimental.pallas import tpu as pltpu
from jax.sharding import PartitionSpec as P

BLOCK = 64
CORES = 2
PLANES = 4
NEXT = ((0, 1), (1, 0), (2, 3), (3, 2))
SECOND = ((0, 2), (2, 0), (1, 3), (3, 1))
ACROSS = ((1, 2), (2, 1))
AROUND = ((0, 3), (3, 0))
CYCLE = ((0, 2), (2, 3), (3, 1), (1, 0))
VMEM = 12 * 1024 * 1024
F32 = jnp.float32
BF16 = jnp.bfloat16


def tile_of(size, most):
    tile = most
    while size % tile:
        tile //= 2
    return tile


def rms_normed(rows_in, norm_gain):
    values = rows_in.astype(F32)
    meansq = jnp.mean(values * values, axis=-1, keepdims=True)
    return (values * lax.rsqrt(meansq + 1e-05) * norm_gain).astype(BF16)


HURRY = 1000


def cost(flops, moved):
    return pl.CostEstimate(flops=flops // HURRY, bytes_accessed=moved // HURRY, transcendentals=0)


def as_if(microseconds):
    return cost(int(HURRY * 1.15e9 * microseconds), 0)


ANYWHERE = pl.BlockSpec(memory_space=pl.ANY)
TOKEN = jax.ShapeDtypeStruct((8, 128), F32)
INSIDE = pl.BlockSpec(memory_space=pltpu.VMEM)


def mask_kernel(share, rows, after_count, core_ref, weight_ref, mask_ref, *refs):
    kept_ref, token_ref, spread, semaphores = refs[after_count:]
    token_ref[...] = jnp.zeros_like(token_ref)
    depth, width = kept_ref.shape
    number = share(core_ref[0])
    columns = pl.ds(pl.multiple_of(number * width, width), width)
    copies = [
        pltpu.make_async_copy(
            weight_ref.at[pl.ds(step * rows, rows), columns], kept_ref.at[pl.ds(step * rows, rows)], semaphores.at[step]
        )
        for step in range(depth // rows)
    ]
    for copy in copies:
        copy.start()
    marks = mask_ref.shape[1]
    owner = lax.broadcasted_iota(jnp.int32, (marks, width), 1) // BLOCK + number * (width // BLOCK)
    chosen = (owner == lax.broadcasted_iota(jnp.int32, (marks, width), 0)).astype(F32)
    spread[...] = jnp.dot(mask_ref[...].astype(F32), chosen, preferred_element_type=F32)
    for step, copy in enumerate(copies):
        copy.wait()
        for block in range(step * rows // BLOCK, (step + 1) * rows // BLOCK):
            part = pl.ds(block * BLOCK, BLOCK)
            keep = jnp.broadcast_to(spread[pl.ds(block, 1), :], (BLOCK, width))
            kept_ref[part, :] = kept_ref[part, :] * keep.astype(BF16)


def masked(weight, mask, rows, core, shares, share, after, hint=0.0):
    depth, width = weight.shape
    width = width // shares
    return pl.pallas_call(
        functools.partial(mask_kernel, share, rows, len(after)),
        in_specs=[pl.BlockSpec(memory_space=pltpu.SMEM), ANYWHERE, INSIDE] + [ANYWHERE] * len(after),
        out_specs=[INSIDE] * 2,
        out_shape=[jax.ShapeDtypeStruct((depth, width), weight.dtype), TOKEN],
        scratch_shapes=[pltpu.VMEM((mask.shape[0], width), F32), pltpu.SemaphoreType.DMA((depth // rows,))],
        compiler_params=pltpu.CompilerParams(vmem_limit_bytes=VMEM),
        cost_estimate=as_if(hint),
        name="masked",
    )(core, pltpu.with_memory_space_constraint(weight, pltpu.HBM), mask, *after)


def stack_kernel(after_count, *refs):
    block_refs, (stacked_ref, token_ref) = refs[: -2 - after_count], refs[-2:]
    token_ref[...] = jnp.zeros_like(token_ref)
    for number, block_ref in enumerate(block_refs):
        stacked_ref[number // stacked_ref.shape[1], number % stacked_ref.shape[1]] = block_ref[...]


def join_kernel(after_count, *refs):
    stacked_refs, (joined_ref, token_ref) = refs[: -2 - after_count], refs[-2:]
    token_ref[...] = jnp.zeros_like(token_ref)
    blocks = [ref[core, chip] for core in range(CORES) for ref in stacked_refs for chip in range(ref.shape[1])]
    joined_ref[...] = jnp.concatenate([block.astype(F32) for block in blocks], 0).astype(BF16)


def rearranged(kernel, name, shape, blocks, after, hint=0.0):
    return pl.pallas_call(
        functools.partial(kernel, len(after)),
        in_specs=[INSIDE] * len(blocks) + [ANYWHERE] * len(after),
        out_specs=[INSIDE] * 2,
        out_shape=[jax.ShapeDtypeStruct(shape, BF16), TOKEN],
        compiler_params=pltpu.CompilerParams(vmem_limit_bytes=VMEM // 2),
        cost_estimate=as_if(hint),
        name=name,
    )(*blocks, *after)


def wait_kernel(*refs):
    refs[-1][...] = jnp.zeros_like(refs[-1])


def waited(after, hint):
    return pl.pallas_call(
        wait_kernel,
        in_specs=[ANYWHERE] * len(after),
        out_specs=INSIDE,
        out_shape=TOKEN,
        compiler_params=pltpu.CompilerParams(vmem_limit_bytes=VMEM // 2),
        cost_estimate=as_if(hint),
        name="waited",
    )(*after)


def stack(blocks, after):
    shape = (CORES, len(blocks) // CORES, *blocks[0].shape)
    return rearranged(stack_kernel, "stack", shape, blocks, after)


def join(stacks, after, hint=0.0):
    rows = sum(part.shape[1] for part in stacks) * CORES * stacks[0].shape[2]
    return rearranged(join_kernel, "join", (rows, stacks[0].shape[3]), stacks, after, hint)


def pick_kernel(after_count, place_ref, inner_three_ref, outer_three_ref, mine_ref, *refs):
    three_ref, passed_ref, token_ref = refs[after_count:]
    token_ref[...] = jnp.zeros_like(token_ref)

    @pl.when(place_ref[1] == 1)
    def _():
        three_ref[...] = inner_three_ref[...]
        passed_ref[...] = inner_three_ref[...]

    @pl.when(place_ref[1] == 0)
    def _():
        three_ref[...] = outer_three_ref[...]
        passed_ref[...] = mine_ref[...]


def pick(place, inner_three, outer_three, mine, after):
    return pl.pallas_call(
        functools.partial(pick_kernel, len(after)),
        in_specs=[pl.BlockSpec(memory_space=pltpu.SMEM)] + [INSIDE] * 3 + [ANYWHERE] * len(after),
        out_specs=[INSIDE] * 3,
        out_shape=[jax.ShapeDtypeStruct(mine.shape, BF16)] * 2 + [TOKEN],
        compiler_params=pltpu.CompilerParams(vmem_limit_bytes=VMEM // 2),
        cost_estimate=as_if(8),
        name="pick",
    )(place, inner_three, outer_three, mine, *after)


def resident(values):
    return pltpu.with_memory_space_constraint(values, pltpu.VMEM)


def gate_up_kernel(part_count, after_count, *refs):
    parts, (gate_ref, up_ref) = refs[:part_count], refs[part_count : part_count + 2]
    keep_ref, near_ref, *far_refs, token_ref, all_rows = refs[part_count + 2 + after_count :]
    far_places = [(far_ref, which) for far_ref in far_refs for which in range(far_ref.shape[0])]
    token_ref[...] = jnp.zeros_like(token_ref)
    half = parts[0].shape[0] // 2
    kept = half * len(parts)
    for place, part in enumerate(parts):
        all_rows[pl.ds(place * half, half), :] = part[:half, :]
        all_rows[pl.ds(kept + place * half, half), :] = part[half:, :]
    tile = tile_of(gate_ref.shape[1], 256)

    @pl.loop(0, gate_ref.shape[1] // tile)
    def _(number):
        columns = pl.ds(pl.multiple_of(number * tile, tile), tile)
        for which, weight_ref in enumerate((gate_ref, up_ref)):
            total = jnp.dot(all_rows[...], weight_ref[:, columns], preferred_element_type=F32)
            total = total.reshape(2, *keep_ref.shape[1:4], tile).astype(BF16)
            keep_ref[which, :, :, :, columns] = total[0]
            near_ref[which, :, :, columns] = total[1, :, 0]
            far_ref, place = far_places[which]
            far_ref[place, :, :, :, columns] = total[1, :, 1:]


def gate_up(parts, gate_kept, up_kept, chips, far_parts, hint, after):
    rows = sum(part.shape[0] for part in parts)
    depth, width = gate_kept.shape
    groups, own = len(parts), rows // (2 * len(parts) * chips)
    shapes = [(2, groups, chips, own, width), (2, groups, own, width)]
    shapes += [(2 // far_parts, groups, chips - 1, own, width)] * far_parts
    return pl.pallas_call(
        functools.partial(gate_up_kernel, len(parts), len(after)),
        in_specs=[INSIDE] * (len(parts) + 2) + [ANYWHERE] * len(after),
        out_specs=[INSIDE] * (len(shapes) + 1),
        out_shape=[jax.ShapeDtypeStruct(shape, BF16) for shape in shapes] + [TOKEN],
        scratch_shapes=[pltpu.VMEM((rows, depth), BF16)],
        compiler_params=pltpu.CompilerParams(vmem_limit_bytes=VMEM // 2),
        cost_estimate=cost(hint * 4 * rows * depth * width, 0),
        name="gate_up",
    )(*parts, resident(gate_kept), resident(up_kept), *after)


def down_kernel(pieces, weight_count, after_count, own_ref, other_ref, *refs):
    weight_refs, refs = refs[:weight_count], refs[weight_count:]
    *partial_refs, token_ref, both = refs[after_count:]
    token_ref[...] = jnp.zeros_like(token_ref)
    groups, own, depth = own_ref.shape
    rows = groups * own
    both[:rows, :] = own_ref[...].astype(F32).reshape(rows, depth).astype(BF16)
    both[rows:, :] = other_ref[...].astype(F32).reshape(rows, depth).astype(BF16)
    for number, weight_ref in enumerate(weight_refs):
        width = weight_ref.shape[1]
        down_columns(pieces, both, weight_ref, partial_refs, number * width, tile_of(width, 512))


def down_columns(pieces, both, weight_ref, partial_refs, first, tile):
    own = partial_refs[0].shape[1]

    @pl.loop(0, weight_ref.shape[1] // tile)
    def _(number):
        start = pl.multiple_of(number * tile, tile)
        total = jnp.dot(both[...], weight_ref[:, pl.ds(start, tile)], preferred_element_type=F32)
        total = total.reshape(pieces, CORES // pieces, len(partial_refs) // pieces, own, tile)
        columns = pl.ds(pl.multiple_of(first + start, tile), tile)
        for place, partial_ref in enumerate(partial_refs):
            partial_ref[:, :, columns] = total[place % pieces, :, place // pieces].astype(BF16)


def down(own, other, down_kept, pieces, after):
    groups, rows, depth = own.shape
    width = sum(weight.shape[1] for weight in down_kept)
    shape = (CORES // pieces, rows, width)
    return pl.pallas_call(
        functools.partial(down_kernel, pieces, len(down_kept), len(after)),
        in_specs=[INSIDE] * (2 + len(down_kept)) + [ANYWHERE] * len(after),
        out_specs=[INSIDE] * (groups * pieces + 1),
        out_shape=[jax.ShapeDtypeStruct(shape, BF16)] * (groups * pieces) + [TOKEN],
        scratch_shapes=[pltpu.VMEM((CORES * groups * rows, depth), BF16)],
        compiler_params=pltpu.CompilerParams(vmem_limit_bytes=VMEM // 2),
        cost_estimate=cost(2 * CORES * groups * rows * depth * width, 0),
        name="down",
    )(own, other, *(resident(weight) for weight in down_kept), *after)


def sums_kernel(sizes, after_count, *refs):
    to_chips, to_hidden, *to_rows = sizes
    refs = list(refs)
    refs.pop()[...] = jnp.zeros(TOKEN.shape, F32)
    ins = [[refs.pop(0) for _ in range(size)] for size in sizes]
    del refs[:after_count]

    if to_chips:
        keep_ref, *came_refs = ins[0]
        came_places = [came_ref.at[which] for came_ref in came_refs for which in range(came_ref.shape[0])]
        for chip in range(1, keep_ref.shape[2]):
            sent_ref = refs.pop(0)
            for which in range(2):
                for group in range(keep_ref.shape[1]):
                    came = came_places[which][group, chip - 1].astype(F32)
                    sent_ref[which, group] = (keep_ref[which, group, chip].astype(F32) + came).astype(BF16)
    if to_hidden:
        keep_ref, came_ref, *chip_refs = ins[1]
        hidden_ref = refs.pop(0)
        for group in range(keep_ref.shape[1]):
            both = []
            for which in range(2):
                total = keep_ref[which, group, 0].astype(F32) + came_ref[which, group].astype(F32)
                for chip_ref in chip_refs:
                    total = total + chip_ref[which, group].astype(F32)
                both.append(total)
            hidden_ref[group] = (jax.nn.silu(both[0]) * both[1]).astype(BF16)
    for part_refs in ins[2:]:
        summed_ref = refs.pop(0)
        cores = summed_ref.shape[0]
        for core in range(cores):
            total = part_refs[0][core].astype(F32)
            for part_ref in part_refs[1:]:
                total = total + part_ref[part_ref.shape[0] - cores + core].astype(F32)
            summed_ref[core] = total.astype(BF16)


def sums(to_chips, to_hidden, to_rows, after, hint=0.0):
    shapes = []
    if to_chips:
        two, groups, chips, own, width = to_chips[0].shape
        shapes += [(two, groups, own, width)] * (chips - 1)
    if to_hidden:
        shapes.append((to_hidden[0].shape[1], *to_hidden[0].shape[3:]))
    shapes += [parts[0].shape for parts in to_rows]
    given = [to_chips, to_hidden, *to_rows]
    sizes = tuple(len(parts) for parts in given)
    given = [part for parts in given for part in parts]
    results = list(pl.pallas_call(
        functools.partial(sums_kernel, sizes, len(after)),
        in_specs=[INSIDE] * len(given) + [ANYWHERE] * len(after),
        out_specs=[INSIDE] * (len(shapes) + 1),
        out_shape=[jax.ShapeDtypeStruct(shape, BF16) for shape in shapes] + [TOKEN],
        compiler_params=pltpu.CompilerParams(vmem_limit_bytes=VMEM // 2),
        cost_estimate=as_if(hint),
        name="sums",
    )(*given, *after))
    token = results.pop()
    sent = [results.pop(0) for _ in range(chips - 1)] if to_chips else []
    hidden = results.pop(0) if to_hidden else None
    return sent, hidden, results, token


def swap(values, axis, size, step):
    return lax.ppermute(values, axis, [(place, place ^ step) for place in range(size)])


def body(row_count, col_count, tokens, norm_gain, gate_weight, up_weight, down_weight, gate_mask, up_mask, down_mask):
    chips = row_count // CORES
    per_plane = col_count // PLANES
    features, width = gate_weight.shape
    row = lax.axis_index("rows")
    core = row % CORES
    inner = (lax.axis_index("cols") // per_plane) % (PLANES - 1) != 0
    place = jnp.stack([core, inner.astype(core.dtype)])

    normed = rms_normed(tokens, norm_gain)
    def block(step):
        return lax.dynamic_slice_in_dim(normed, (row ^ step) * features, features, 1)

    from_core = swap(jnp.stack([block(chip * CORES + 1) for chip in range(chips)]), "rows", row_count, 1)
    to_chips_rows = [stack([block(chip * CORES), from_core[chip]], [])[0] for chip in range(1, chips)]
    first, token = stack([block(0), from_core[0]], to_chips_rows[:1])
    gate_kept, token = masked(gate_weight, gate_mask, tile_of(features, 256), place, 1, lambda core: 0, [token])
    second = [swap(part, "rows", row_count, (chip + 1) * CORES) for chip, part in enumerate(to_chips_rows)]
    second = jnp.concatenate(second, 1) if len(second) > 1 else second[0]
    second = lax.optimization_barrier((second, token))[0]
    mine, token = join([first, second], [token])

    def behind(values, after):
        return lax.optimization_barrier((values, *after))[0] if after else values

    def by_plane(values, planes, after=()):
        pairs = [(a * per_plane + b, c * per_plane + b) for a, c in planes for b in range(per_plane)]
        return lax.ppermute(behind(values, after), "cols", pairs)

    def by_row_of_plane(values, step, after=()):
        return swap(behind(values, after), "cols", col_count, step)

    def by_chip(values, chip, after=()):
        return swap(behind(values, after), "rows", row_count, chip * CORES)

    def by_core(values, after=()):
        return swap(behind(values, after), "rows", row_count, 1)

    parts, halves, near, far, chip_sums, hiddens, others, rows_in, partials, sent = ({} for _ in range(10))
    last = [token]

    def forward(plane, values, after=()):
        parts[plane] = [values]
        for step in range(1, per_plane):
            parts[plane].append(by_row_of_plane(values, step, after))

    def multiply_in(plane, far_parts=1, hint=HURRY, after=()):
        parts_after = last + list(after)
        *halves[plane], last[0] = gate_up(parts[plane], gate_kept, up_kept, chips, far_parts, hint, parts_after)

    def exchange(plane, after=()):
        far[plane] = [by_core(part, after) for part in halves[plane][2:]]

    def exchange_near(plane, after=()):
        near[plane] = by_core(halves[plane][1], after)

    def multiply_out(plane, pieces=1, after=()):
        *partials[plane], last[0] = down(hiddens[plane], others[plane], down_kept, pieces, last + list(after))

    def send_rows(plane, after=(), pieces=1, piece=0):
        mine_and_others = partials[plane][piece::pieces]
        rows_in[plane, piece] = mine_and_others[:1]
        for step in range(1, per_plane):
            rows_in[plane, piece].append(by_row_of_plane(mine_and_others[step], step, after))

    def to_chips(plane, after=()):
        given = [halves[plane][0], *far[plane]]
        sent[plane], _, _, last[0] = sums(given, [], [], last + list(after))

    def send_chips(plane, after=()):
        chip_sums[plane] = [by_chip(part, number + 1, after) for number, part in enumerate(sent[plane])]

    def to_hidden(plane, after=()):
        given = [halves[plane][0], near[plane], *chip_sums[plane]]
        _, hiddens[plane], _, last[0] = sums([], given, [], last + list(after))
        others[plane] = by_core(hiddens[plane])

    def to_rows(*parts, after=(), hint=0.0):
        _, _, (summed,), last[0] = sums([], [], [parts], last + list(after), hint)
        return summed

    next_stacks = [by_plane(first, NEXT), by_plane(second, NEXT)]
    across_stacks = [by_plane(first, ACROSS), by_plane(second, ACROSS)]
    row_stacks = {
        step: [by_row_of_plane(first, step), by_row_of_plane(second, step)] for step in range(1, per_plane)
    }
    up_kept, last[0] = masked(
        up_weight, up_mask, tile_of(features, 256), place, 1, lambda core: 0, last + next_stacks[:1], 0.15
    )
    last[0] = waited([*last, across_stacks[0], *(stacks[0] for stacks in row_stacks.values())], 0.07)
    one_away, last[0] = join(next_stacks, last)
    inner_three, last[0] = join(across_stacks, last)
    outer_three = by_plane(mine, AROUND, last)
    down_kept = []

    def keep_down(share, hint=0.0):
        part, last[0] = masked(
            down_weight, down_mask, 2 * BLOCK, place, 2 * CORES, lambda core: 2 * core + share, last, hint
        )
        down_kept.append(part)

    keep_down(0, 8)
    parts[0] = [mine]
    for stacks in row_stacks.values():
        part, last[0] = join(stacks, last)
        parts[0].append(part)
    forward(1, one_away, last)
    multiply_in(0, hint=0)
    exchange(0)
    exchange_near(0)
    keep_down(1)
    three_away, passed, last[0] = pick(place, inner_three, outer_three, mine, last)
    two_away = by_plane(passed, CYCLE)
    to_chips(0, [near[0]])
    forward(3, three_away, [*parts[1][1:], *last])
    multiply_in(1)
    exchange(1)
    exchange_near(1)
    to_chips(1, [near[1]])
    send_chips(1)
    forward(2, two_away, [*parts[3][1:], *last])
    multiply_in(3, after=[two_away])
    exchange(3)
    exchange_near(3)
    to_hidden(1)
    to_chips(3, [near[3]])
    send_chips(3)
    multiply_out(1)
    send_rows(1, parts[2][1:])
    multiply_in(2, far_parts=2)
    exchange(2)
    to_hidden(3)
    to_chips(2)
    send_chips(2)
    exchange_near(2, last)
    multiply_out(3, pieces=CORES)
    send_rows(3, rows_in[1, 0][1:], CORES, 1)
    one = to_rows(*rows_in[1, 0])
    one_out = by_plane(one, NEXT)
    three = to_rows(*rows_in[3, 1])
    send_rows(3, [three], CORES, 0)
    three_out, two_out = {1: by_plane(three, NEXT)}, {}
    to_hidden(2)
    send_chips(0, chip_sums[2])
    multiply_out(2, pieces=CORES)
    three = to_rows(*rows_in[3, 0], after=[one_out])
    three_out[0] = by_plane(three, NEXT)
    send_rows(2, [three], CORES, 1)
    two = to_rows(*rows_in[2, 1], three_out[1])
    two_out[1] = by_plane(two, SECOND)
    send_rows(2, [two], CORES, 0)
    to_hidden(0)
    multiply_out(0)
    two = to_rows(rows_in[2, 0][0], three_out[0], hint=0.5)
    two = to_rows(two, *rows_in[2, 0][1:])
    two_out[0] = by_plane(two, SECOND)
    send_rows(0, rows_in[2, 0][1:])

    joined = to_rows(two_out[1], one_out, hint=10.0)

    def total(piece, *parts):
        whole = [part[piece].astype(F32) for part in rows_in[0, 0]] + [part.astype(F32) for part in parts]
        return sum(whole[1:], whole[0]).astype(BF16)

    mine_now, other = total(0, one_out[0], two_out[0][0]), by_core(total(1, joined[0]))
    left = jnp.where(core == 0, mine_now, other)
    right = jnp.where(core == 0, other, mine_now)
    return jnp.concatenate([left, right], 1)


def solution(mesh):
    return jax.shard_map(
        functools.partial(body, mesh.shape["rows"], mesh.shape["cols"]),
        mesh=mesh,
        in_specs=(
            P(("rows", "cols"), None),
            P(),
            P("rows", "cols"),
            P("rows", "cols"),
            P("cols", None),
            P("rows", "cols"),
            P("rows", "cols"),
            P("cols", None),
        ),
        out_specs=P(("rows", "cols"), None),
        check_vma=False,
    )
```

```python
import functools

import jax
import jax.numpy as jnp
from jax import lax
from jax.experimental import pallas as pl
from jax.experimental.pallas import tpu as pltpu
from jax.sharding import PartitionSpec as P

BLOCK = 64
CORES = 2
PLANES = 4
NEXT = ((0, 1), (1, 0), (2, 3), (3, 2))
SECOND = ((0, 2), (2, 0), (1, 3), (3, 1))
ACROSS = ((1, 2), (2, 1))
AROUND = ((0, 3), (3, 0))
CYCLE = ((0, 2), (2, 3), (3, 1), (1, 0))
VMEM = 12 * 1024 * 1024
F32 = jnp.float32
BF16 = jnp.bfloat16


def tile_of(size, most):
    tile = most
    while size % tile:
        tile //= 2
    return tile


def rms_normed(rows_in, norm_gain):
    values = rows_in.astype(F32)
    meansq = jnp.mean(values * values, axis=-1, keepdims=True)
    return (values * lax.rsqrt(meansq + 1e-05) * norm_gain).astype(BF16)


HURRY = 1000


def cost(flops, moved):
    return pl.CostEstimate(flops=flops // HURRY, bytes_accessed=moved // HURRY, transcendentals=0)


def as_if(microseconds):
    return cost(int(HURRY * 1.15e9 * microseconds), 0)


ANYWHERE = pl.BlockSpec(memory_space=pl.ANY)
TOKEN = jax.ShapeDtypeStruct((8, 128), F32)
INSIDE = pl.BlockSpec(memory_space=pltpu.VMEM)


def mask_kernel(share, rows, after_count, core_ref, weight_ref, mask_ref, *refs):
    kept_ref, token_ref, spread, semaphores = refs[after_count:]
    token_ref[...] = jnp.zeros_like(token_ref)
    depth, width = kept_ref.shape
    number = share(core_ref[0])
    columns = pl.ds(pl.multiple_of(number * width, width), width)
    copies = [
        pltpu.make_async_copy(
            weight_ref.at[pl.ds(step * rows, rows), columns], kept_ref.at[pl.ds(step * rows, rows)], semaphores.at[step]
        )
        for step in range(depth // rows)
    ]
    for copy in copies:
        copy.start()
    marks = mask_ref.shape[1]
    owner = lax.broadcasted_iota(jnp.int32, (marks, width), 1) // BLOCK + number * (width // BLOCK)
    chosen = (owner == lax.broadcasted_iota(jnp.int32, (marks, width), 0)).astype(F32)
    spread[...] = jnp.dot(mask_ref[...].astype(F32), chosen, preferred_element_type=F32)
    for step, copy in enumerate(copies):
        copy.wait()
        for block in range(step * rows // BLOCK, (step + 1) * rows // BLOCK):
            part = pl.ds(block * BLOCK, BLOCK)
            keep = jnp.broadcast_to(spread[pl.ds(block, 1), :], (BLOCK, width))
            kept_ref[part, :] = kept_ref[part, :] * keep.astype(BF16)


def masked(weight, mask, rows, core, shares, share, after, hint=0.0):
    depth, width = weight.shape
    width = width // shares
    return pl.pallas_call(
        functools.partial(mask_kernel, share, rows, len(after)),
        in_specs=[pl.BlockSpec(memory_space=pltpu.SMEM), ANYWHERE, INSIDE] + [ANYWHERE] * len(after),
        out_specs=[INSIDE] * 2,
        out_shape=[jax.ShapeDtypeStruct((depth, width), weight.dtype), TOKEN],
        scratch_shapes=[pltpu.VMEM((mask.shape[0], width), F32), pltpu.SemaphoreType.DMA((depth // rows,))],
        compiler_params=pltpu.CompilerParams(vmem_limit_bytes=VMEM),
        cost_estimate=as_if(hint),
        name="masked",
    )(core, pltpu.with_memory_space_constraint(weight, pltpu.HBM), mask, *after)


def stack_kernel(after_count, *refs):
    block_refs, (stacked_ref, token_ref) = refs[: -2 - after_count], refs[-2:]
    token_ref[...] = jnp.zeros_like(token_ref)
    for number, block_ref in enumerate(block_refs):
        stacked_ref[number // stacked_ref.shape[1], number % stacked_ref.shape[1]] = block_ref[...]


def join_kernel(after_count, *refs):
    stacked_refs, (joined_ref, token_ref) = refs[: -2 - after_count], refs[-2:]
    token_ref[...] = jnp.zeros_like(token_ref)
    blocks = [ref[core, chip] for core in range(CORES) for ref in stacked_refs for chip in range(ref.shape[1])]
    joined_ref[...] = jnp.concatenate([block.astype(F32) for block in blocks], 0).astype(BF16)


def rearranged(kernel, name, shape, blocks, after, hint=0.0):
    return pl.pallas_call(
        functools.partial(kernel, len(after)),
        in_specs=[INSIDE] * len(blocks) + [ANYWHERE] * len(after),
        out_specs=[INSIDE] * 2,
        out_shape=[jax.ShapeDtypeStruct(shape, BF16), TOKEN],
        compiler_params=pltpu.CompilerParams(vmem_limit_bytes=VMEM // 2),
        cost_estimate=as_if(hint),
        name=name,
    )(*blocks, *after)


def wait_kernel(*refs):
    refs[-1][...] = jnp.zeros_like(refs[-1])


def waited(after, hint):
    return pl.pallas_call(
        wait_kernel,
        in_specs=[ANYWHERE] * len(after),
        out_specs=INSIDE,
        out_shape=TOKEN,
        compiler_params=pltpu.CompilerParams(vmem_limit_bytes=VMEM // 2),
        cost_estimate=as_if(hint),
        name="waited",
    )(*after)


def stack(blocks, after):
    shape = (CORES, len(blocks) // CORES, *blocks[0].shape)
    return rearranged(stack_kernel, "stack", shape, blocks, after)


def join(stacks, after, hint=0.0):
    rows = sum(part.shape[1] for part in stacks) * CORES * stacks[0].shape[2]
    return rearranged(join_kernel, "join", (rows, stacks[0].shape[3]), stacks, after, hint)


def pick_kernel(after_count, place_ref, inner_three_ref, outer_three_ref, mine_ref, *refs):
    three_ref, passed_ref, token_ref = refs[after_count:]
    token_ref[...] = jnp.zeros_like(token_ref)

    @pl.when(place_ref[1] == 1)
    def _():
        three_ref[...] = inner_three_ref[...]
        passed_ref[...] = inner_three_ref[...]

    @pl.when(place_ref[1] == 0)
    def _():
        three_ref[...] = outer_three_ref[...]
        passed_ref[...] = mine_ref[...]


def pick(place, inner_three, outer_three, mine, after):
    return pl.pallas_call(
        functools.partial(pick_kernel, len(after)),
        in_specs=[pl.BlockSpec(memory_space=pltpu.SMEM)] + [INSIDE] * 3 + [ANYWHERE] * len(after),
        out_specs=[INSIDE] * 3,
        out_shape=[jax.ShapeDtypeStruct(mine.shape, BF16)] * 2 + [TOKEN],
        compiler_params=pltpu.CompilerParams(vmem_limit_bytes=VMEM // 2),
        cost_estimate=as_if(8),
        name="pick",
    )(place, inner_three, outer_three, mine, *after)


def resident(values):
    return pltpu.with_memory_space_constraint(values, pltpu.VMEM)


def gate_up_kernel(part_count, after_count, *refs):
    parts, (gate_ref, up_ref) = refs[:part_count], refs[part_count : part_count + 2]
    keep_ref, near_ref, *far_refs, token_ref, all_rows = refs[part_count + 2 + after_count :]
    far_places = [(far_ref, which) for far_ref in far_refs for which in range(far_ref.shape[0])]
    token_ref[...] = jnp.zeros_like(token_ref)
    half = parts[0].shape[0] // 2
    kept = half * len(parts)
    for place, part in enumerate(parts):
        all_rows[pl.ds(place * half, half), :] = part[:half, :]
        all_rows[pl.ds(kept + place * half, half), :] = part[half:, :]
    tile = tile_of(gate_ref.shape[1], 256)

    @pl.loop(0, gate_ref.shape[1] // tile)
    def _(number):
        columns = pl.ds(pl.multiple_of(number * tile, tile), tile)
        for which, weight_ref in enumerate((gate_ref, up_ref)):
            total = jnp.dot(all_rows[...], weight_ref[:, columns], preferred_element_type=F32)
            total = total.reshape(2, *keep_ref.shape[1:4], tile).astype(BF16)
            keep_ref[which, :, :, :, columns] = total[0]
            near_ref[which, :, :, columns] = total[1, :, 0]
            far_ref, place = far_places[which]
            far_ref[place, :, :, :, columns] = total[1, :, 1:]


def gate_up(parts, gate_kept, up_kept, chips, far_parts, hint, after):
    rows = sum(part.shape[0] for part in parts)
    depth, width = gate_kept.shape
    groups, own = len(parts), rows // (2 * len(parts) * chips)
    shapes = [(2, groups, chips, own, width), (2, groups, own, width)]
    shapes += [(2 // far_parts, groups, chips - 1, own, width)] * far_parts
    return pl.pallas_call(
        functools.partial(gate_up_kernel, len(parts), len(after)),
        in_specs=[INSIDE] * (len(parts) + 2) + [ANYWHERE] * len(after),
        out_specs=[INSIDE] * (len(shapes) + 1),
        out_shape=[jax.ShapeDtypeStruct(shape, BF16) for shape in shapes] + [TOKEN],
        scratch_shapes=[pltpu.VMEM((rows, depth), BF16)],
        compiler_params=pltpu.CompilerParams(vmem_limit_bytes=VMEM // 2),
        cost_estimate=cost(hint * 4 * rows * depth * width, 0),
        name="gate_up",
    )(*parts, resident(gate_kept), resident(up_kept), *after)


def down_kernel(pieces, weight_count, after_count, own_ref, other_ref, *refs):
    weight_refs, refs = refs[:weight_count], refs[weight_count:]
    *partial_refs, token_ref, both = refs[after_count:]
    token_ref[...] = jnp.zeros_like(token_ref)
    groups, own, depth = own_ref.shape
    rows = groups * own
    both[:rows, :] = own_ref[...].astype(F32).reshape(rows, depth).astype(BF16)
    both[rows:, :] = other_ref[...].astype(F32).reshape(rows, depth).astype(BF16)
    for number, weight_ref in enumerate(weight_refs):
        width = weight_ref.shape[1]
        down_columns(pieces, both, weight_ref, partial_refs, number * width, tile_of(width, 512))


def down_columns(pieces, both, weight_ref, partial_refs, first, tile):
    own = partial_refs[0].shape[1]

    @pl.loop(0, weight_ref.shape[1] // tile)
    def _(number):
        start = pl.multiple_of(number * tile, tile)
        total = jnp.dot(both[...], weight_ref[:, pl.ds(start, tile)], preferred_element_type=F32)
        total = total.reshape(pieces, CORES // pieces, len(partial_refs) // pieces, own, tile)
        columns = pl.ds(pl.multiple_of(first + start, tile), tile)
        for place, partial_ref in enumerate(partial_refs):
            partial_ref[:, :, columns] = total[place % pieces, :, place // pieces].astype(BF16)


def down(own, other, down_kept, pieces, after):
    groups, rows, depth = own.shape
    width = sum(weight.shape[1] for weight in down_kept)
    shape = (CORES // pieces, rows, width)
    return pl.pallas_call(
        functools.partial(down_kernel, pieces, len(down_kept), len(after)),
        in_specs=[INSIDE] * (2 + len(down_kept)) + [ANYWHERE] * len(after),
        out_specs=[INSIDE] * (groups * pieces + 1),
        out_shape=[jax.ShapeDtypeStruct(shape, BF16)] * (groups * pieces) + [TOKEN],
        scratch_shapes=[pltpu.VMEM((CORES * groups * rows, depth), BF16)],
        compiler_params=pltpu.CompilerParams(vmem_limit_bytes=VMEM // 2),
        cost_estimate=cost(2 * CORES * groups * rows * depth * width, 0),
        name="down",
    )(own, other, *(resident(weight) for weight in down_kept), *after)


def sums_kernel(sizes, after_count, *refs):
    to_chips, to_hidden, *to_rows = sizes
    refs = list(refs)
    refs.pop()[...] = jnp.zeros(TOKEN.shape, F32)
    ins = [[refs.pop(0) for _ in range(size)] for size in sizes]
    del refs[:after_count]

    if to_chips:
        keep_ref, *came_refs = ins[0]
        came_places = [came_ref.at[which] for came_ref in came_refs for which in range(came_ref.shape[0])]
        for chip in range(1, keep_ref.shape[2]):
            sent_ref = refs.pop(0)
            for which in range(2):
                for group in range(keep_ref.shape[1]):
                    came = came_places[which][group, chip - 1].astype(F32)
                    sent_ref[which, group] = (keep_ref[which, group, chip].astype(F32) + came).astype(BF16)
    if to_hidden:
        keep_ref, came_ref, *chip_refs = ins[1]
        hidden_ref = refs.pop(0)
        for group in range(keep_ref.shape[1]):
            both = []
            for which in range(2):
                total = keep_ref[which, group, 0].astype(F32) + came_ref[which, group].astype(F32)
                for chip_ref in chip_refs:
                    total = total + chip_ref[which, group].astype(F32)
                both.append(total)
            hidden_ref[group] = (jax.nn.silu(both[0]) * both[1]).astype(BF16)
    for part_refs in ins[2:]:
        summed_ref = refs.pop(0)
        cores = summed_ref.shape[0]
        for core in range(cores):
            total = part_refs[0][core].astype(F32)
            for part_ref in part_refs[1:]:
                total = total + part_ref[part_ref.shape[0] - cores + core].astype(F32)
            summed_ref[core] = total.astype(BF16)


def sums(to_chips, to_hidden, to_rows, after, hint=0.0):
    shapes = []
    if to_chips:
        two, groups, chips, own, width = to_chips[0].shape
        shapes += [(two, groups, own, width)] * (chips - 1)
    if to_hidden:
        shapes.append((to_hidden[0].shape[1], *to_hidden[0].shape[3:]))
    shapes += [parts[0].shape for parts in to_rows]
    given = [to_chips, to_hidden, *to_rows]
    sizes = tuple(len(parts) for parts in given)
    given = [part for parts in given for part in parts]
    results = list(pl.pallas_call(
        functools.partial(sums_kernel, sizes, len(after)),
        in_specs=[INSIDE] * len(given) + [ANYWHERE] * len(after),
        out_specs=[INSIDE] * (len(shapes) + 1),
        out_shape=[jax.ShapeDtypeStruct(shape, BF16) for shape in shapes] + [TOKEN],
        compiler_params=pltpu.CompilerParams(vmem_limit_bytes=VMEM // 2),
        cost_estimate=as_if(hint),
        name="sums",
    )(*given, *after))
    token = results.pop()
    sent = [results.pop(0) for _ in range(chips - 1)] if to_chips else []
    hidden = results.pop(0) if to_hidden else None
    return sent, hidden, results, token


def swap(values, axis, size, step):
    return lax.ppermute(values, axis, [(place, place ^ step) for place in range(size)])


def body(row_count, col_count, tokens, norm_gain, gate_weight, up_weight, down_weight, gate_mask, up_mask, down_mask):
    chips = row_count // CORES
    per_plane = col_count // PLANES
    features, width = gate_weight.shape
    row = lax.axis_index("rows")
    core = row % CORES
    inner = (lax.axis_index("cols") // per_plane) % (PLANES - 1) != 0
    place = jnp.stack([core, inner.astype(core.dtype)])

    normed = rms_normed(tokens, norm_gain)
    def block(step):
        return lax.dynamic_slice_in_dim(normed, (row ^ step) * features, features, 1)

    from_core = swap(jnp.stack([block(chip * CORES + 1) for chip in range(chips)]), "rows", row_count, 1)
    to_chips_rows = [stack([block(chip * CORES), from_core[chip]], [])[0] for chip in range(1, chips)]
    first, token = stack([block(0), from_core[0]], to_chips_rows[:1])
    gate_kept, token = masked(gate_weight, gate_mask, tile_of(features, 256), place, 1, lambda core: 0, [token])
    second = [swap(part, "rows", row_count, (chip + 1) * CORES) for chip, part in enumerate(to_chips_rows)]
    second = jnp.concatenate(second, 1) if len(second) > 1 else second[0]
    second = lax.optimization_barrier((second, token))[0]
    mine, token = join([first, second], [token])

    def behind(values, after):
        return lax.optimization_barrier((values, *after))[0] if after else values

    def by_plane(values, planes, after=()):
        pairs = [(a * per_plane + b, c * per_plane + b) for a, c in planes for b in range(per_plane)]
        return lax.ppermute(behind(values, after), "cols", pairs)

    def by_row_of_plane(values, step, after=()):
        return swap(behind(values, after), "cols", col_count, step)

    def by_chip(values, chip, after=()):
        return swap(behind(values, after), "rows", row_count, chip * CORES)

    def by_core(values, after=()):
        return swap(behind(values, after), "rows", row_count, 1)

    parts, halves, near, far, chip_sums, hiddens, others, rows_in, partials, sent = ({} for _ in range(10))
    last = [token]

    def forward(plane, values, after=()):
        parts[plane] = [values]
        for step in range(1, per_plane):
            parts[plane].append(by_row_of_plane(values, step, after))

    def multiply_in(plane, far_parts=1, hint=HURRY, after=()):
        parts_after = last + list(after)
        *halves[plane], last[0] = gate_up(parts[plane], gate_kept, up_kept, chips, far_parts, hint, parts_after)

    def exchange(plane, after=()):
        far[plane] = [by_core(part, after) for part in halves[plane][2:]]

    def exchange_near(plane, after=()):
        near[plane] = by_core(halves[plane][1], after)

    def multiply_out(plane, pieces=1, after=()):
        *partials[plane], last[0] = down(hiddens[plane], others[plane], down_kept, pieces, last + list(after))

    def send_rows(plane, after=(), pieces=1, piece=0):
        mine_and_others = partials[plane][piece::pieces]
        rows_in[plane, piece] = mine_and_others[:1]
        for step in range(1, per_plane):
            rows_in[plane, piece].append(by_row_of_plane(mine_and_others[step], step, after))

    def to_chips(plane, after=()):
        given = [halves[plane][0], *far[plane]]
        sent[plane], _, _, last[0] = sums(given, [], [], last + list(after))

    def send_chips(plane, after=()):
        chip_sums[plane] = [by_chip(part, number + 1, after) for number, part in enumerate(sent[plane])]

    def to_hidden(plane, after=()):
        given = [halves[plane][0], near[plane], *chip_sums[plane]]
        _, hiddens[plane], _, last[0] = sums([], given, [], last + list(after))
        others[plane] = by_core(hiddens[plane])

    def to_rows(*parts, after=(), hint=0.0):
        _, _, (summed,), last[0] = sums([], [], [parts], last + list(after), hint)
        return summed

    next_stacks = [by_plane(first, NEXT), by_plane(second, NEXT)]
    across_stacks = [by_plane(first, ACROSS), by_plane(second, ACROSS)]
    row_stacks = {
        step: [by_row_of_plane(first, step), by_row_of_plane(second, step)] for step in range(1, per_plane)
    }
    up_kept, last[0] = masked(
        up_weight, up_mask, tile_of(features, 256), place, 1, lambda core: 0, last + next_stacks[:1], 0.15
    )
    last[0] = waited([*last, across_stacks[0], *(stacks[0] for stacks in row_stacks.values())], 0.07)
    one_away, last[0] = join(next_stacks, last)
    inner_three, last[0] = join(across_stacks, last + [stacks[1] for stacks in row_stacks.values()])
    outer_three = by_plane(mine, AROUND, last)
    down_kept = []

    def keep_down(share, hint=0.0):
        part, last[0] = masked(
            down_weight, down_mask, 2 * BLOCK, place, 2 * CORES, lambda core: 2 * core + share, last, hint
        )
        down_kept.append(part)

    parts[0] = [mine]
    for stacks in row_stacks.values():
        part, last[0] = join(stacks, last)
        parts[0].append(part)
    forward(1, one_away, last)
    multiply_in(0, hint=0)
    exchange(0)
    exchange_near(0)
    keep_down(0)
    keep_down(1)
    three_away, passed, last[0] = pick(place, inner_three, outer_three, mine, last)
    two_away = by_plane(passed, CYCLE)
    to_chips(0, [near[0]])
    forward(3, three_away, [*parts[1][1:], *last])
    multiply_in(1)
    exchange(1)
    exchange_near(1)
    to_chips(1, [near[1]])
    send_chips(1)
    forward(2, two_away, [*parts[3][1:], *last])
    multiply_in(3, after=[two_away])
    exchange(3)
    exchange_near(3)
    to_hidden(1)
    to_chips(3, [near[3]])
    send_chips(3)
    multiply_out(1)
    send_rows(1, parts[2][1:])
    multiply_in(2, far_parts=2)
    exchange(2)
    to_hidden(3)
    to_chips(2)
    send_chips(2)
    exchange_near(2, last)
    multiply_out(3, pieces=CORES)
    send_rows(3, rows_in[1, 0][1:], CORES, 1)
    one = to_rows(*rows_in[1, 0])
    one_out = by_plane(one, NEXT)
    three = to_rows(*rows_in[3, 1])
    send_rows(3, [three], CORES, 0)
    three_out, two_out = {1: by_plane(three, NEXT)}, {}
    to_hidden(2)
    send_chips(0, chip_sums[2])
    multiply_out(2, pieces=CORES)
    three = to_rows(*rows_in[3, 0], after=[one_out])
    three_out[0] = by_plane(three, NEXT)
    send_rows(2, [three], CORES, 1)
    two = to_rows(*rows_in[2, 1], three_out[1])
    two_out[1] = by_plane(two, SECOND)
    send_rows(2, [two], CORES, 0)
    to_hidden(0)
    multiply_out(0)
    two = to_rows(rows_in[2, 0][0], three_out[0], hint=0.5)
    two = to_rows(two, *rows_in[2, 0][1:])
    two_out[0] = by_plane(two, SECOND)
    send_rows(0, rows_in[2, 0][1:])

    joined = to_rows(two_out[1], one_out, hint=10.0)

    def total(piece, *parts):
        whole = [part[piece].astype(F32) for part in rows_in[0, 0]] + [part.astype(F32) for part in parts]
        return sum(whole[1:], whole[0]).astype(BF16)

    mine_now, other = total(0, one_out[0], two_out[0][0]), by_core(total(1, joined[0]))
    left = jnp.where(core == 0, mine_now, other)
    right = jnp.where(core == 0, other, mine_now)
    return jnp.concatenate([left, right], 1)


def solution(mesh):
    return jax.shard_map(
        functools.partial(body, mesh.shape["rows"], mesh.shape["cols"]),
        mesh=mesh,
        in_specs=(
            P(("rows", "cols"), None),
            P(),
            P("rows", "cols"),
            P("rows", "cols"),
            P("cols", None),
            P("rows", "cols"),
            P("rows", "cols"),
            P("cols", None),
        ),
        out_specs=P(("rows", "cols"), None),
        check_vma=False,
    )
```

```python
import functools

import jax
import jax.numpy as jnp
from jax import lax
from jax.experimental import pallas as pl
from jax.experimental.pallas import tpu as pltpu
from jax.sharding import PartitionSpec as P

BLOCK = 64
CORES = 2
PLANES = 4
NEXT = ((0, 1), (1, 0), (2, 3), (3, 2))
SECOND = ((0, 2), (2, 0), (1, 3), (3, 1))
ACROSS = ((1, 2), (2, 1))
AROUND = ((0, 3), (3, 0))
CYCLE = ((0, 2), (2, 3), (3, 1), (1, 0))
VMEM = 12 * 1024 * 1024
F32 = jnp.float32
BF16 = jnp.bfloat16


def tile_of(size, most):
    tile = most
    while size % tile:
        tile //= 2
    return tile


def rms_normed(rows_in, norm_gain):
    values = rows_in.astype(F32)
    meansq = jnp.mean(values * values, axis=-1, keepdims=True)
    return (values * lax.rsqrt(meansq + 1e-05) * norm_gain).astype(BF16)


HURRY = 1000


def cost(flops, moved):
    return pl.CostEstimate(flops=flops // HURRY, bytes_accessed=moved // HURRY, transcendentals=0)


def as_if(microseconds):
    return cost(int(HURRY * 1.15e9 * microseconds), 0)


ANYWHERE = pl.BlockSpec(memory_space=pl.ANY)
TOKEN = jax.ShapeDtypeStruct((8, 128), F32)
INSIDE = pl.BlockSpec(memory_space=pltpu.VMEM)


def mask_kernel(share, rows, after_count, core_ref, weight_ref, mask_ref, *refs):
    kept_ref, token_ref, spread, semaphores = refs[after_count:]
    token_ref[...] = jnp.zeros_like(token_ref)
    depth, width = kept_ref.shape
    number = share(core_ref[0])
    columns = pl.ds(pl.multiple_of(number * width, width), width)
    copies = [
        pltpu.make_async_copy(
            weight_ref.at[pl.ds(step * rows, rows), columns], kept_ref.at[pl.ds(step * rows, rows)], semaphores.at[step]
        )
        for step in range(depth // rows)
    ]
    for copy in copies:
        copy.start()
    marks = mask_ref.shape[1]
    owner = lax.broadcasted_iota(jnp.int32, (marks, width), 1) // BLOCK + number * (width // BLOCK)
    chosen = (owner == lax.broadcasted_iota(jnp.int32, (marks, width), 0)).astype(F32)
    spread[...] = jnp.dot(mask_ref[...].astype(F32), chosen, preferred_element_type=F32)
    for step, copy in enumerate(copies):
        copy.wait()
        for block in range(step * rows // BLOCK, (step + 1) * rows // BLOCK):
            part = pl.ds(block * BLOCK, BLOCK)
            keep = jnp.broadcast_to(spread[pl.ds(block, 1), :], (BLOCK, width))
            kept_ref[part, :] = kept_ref[part, :] * keep.astype(BF16)


def masked(weight, mask, rows, core, shares, share, after, hint=0.0):
    depth, width = weight.shape
    width = width // shares
    return pl.pallas_call(
        functools.partial(mask_kernel, share, rows, len(after)),
        in_specs=[pl.BlockSpec(memory_space=pltpu.SMEM), ANYWHERE, INSIDE] + [ANYWHERE] * len(after),
        out_specs=[INSIDE] * 2,
        out_shape=[jax.ShapeDtypeStruct((depth, width), weight.dtype), TOKEN],
        scratch_shapes=[pltpu.VMEM((mask.shape[0], width), F32), pltpu.SemaphoreType.DMA((depth // rows,))],
        compiler_params=pltpu.CompilerParams(vmem_limit_bytes=VMEM),
        cost_estimate=as_if(hint),
        name="masked",
    )(core, pltpu.with_memory_space_constraint(weight, pltpu.HBM), mask, *after)


def stack_kernel(after_count, *refs):
    block_refs, (stacked_ref, token_ref) = refs[: -2 - after_count], refs[-2:]
    token_ref[...] = jnp.zeros_like(token_ref)
    for number, block_ref in enumerate(block_refs):
        stacked_ref[number // stacked_ref.shape[1], number % stacked_ref.shape[1]] = block_ref[...]


def join_kernel(after_count, *refs):
    stacked_refs, (joined_ref, token_ref) = refs[: -2 - after_count], refs[-2:]
    token_ref[...] = jnp.zeros_like(token_ref)
    blocks = [ref[core, chip] for core in range(CORES) for ref in stacked_refs for chip in range(ref.shape[1])]
    joined_ref[...] = jnp.concatenate([block.astype(F32) for block in blocks], 0).astype(BF16)


def rearranged(kernel, name, shape, blocks, after, hint=0.0):
    return pl.pallas_call(
        functools.partial(kernel, len(after)),
        in_specs=[INSIDE] * len(blocks) + [ANYWHERE] * len(after),
        out_specs=[INSIDE] * 2,
        out_shape=[jax.ShapeDtypeStruct(shape, BF16), TOKEN],
        compiler_params=pltpu.CompilerParams(vmem_limit_bytes=VMEM // 2),
        cost_estimate=as_if(hint),
        name=name,
    )(*blocks, *after)


def wait_kernel(*refs):
    refs[-1][...] = jnp.zeros_like(refs[-1])


def waited(after, hint):
    return pl.pallas_call(
        wait_kernel,
        in_specs=[ANYWHERE] * len(after),
        out_specs=INSIDE,
        out_shape=TOKEN,
        compiler_params=pltpu.CompilerParams(vmem_limit_bytes=VMEM // 2),
        cost_estimate=as_if(hint),
        name="waited",
    )(*after)


def stack(blocks, after):
    shape = (CORES, len(blocks) // CORES, *blocks[0].shape)
    return rearranged(stack_kernel, "stack", shape, blocks, after)


def join(stacks, after, hint=0.0):
    rows = sum(part.shape[1] for part in stacks) * CORES * stacks[0].shape[2]
    return rearranged(join_kernel, "join", (rows, stacks[0].shape[3]), stacks, after, hint)


def pick_kernel(after_count, place_ref, inner_three_ref, outer_three_ref, mine_ref, *refs):
    three_ref, passed_ref, token_ref = refs[after_count:]
    token_ref[...] = jnp.zeros_like(token_ref)

    @pl.when(place_ref[1] == 1)
    def _():
        three_ref[...] = inner_three_ref[...]
        passed_ref[...] = inner_three_ref[...]

    @pl.when(place_ref[1] == 0)
    def _():
        three_ref[...] = outer_three_ref[...]
        passed_ref[...] = mine_ref[...]


def pick(place, inner_three, outer_three, mine, after):
    return pl.pallas_call(
        functools.partial(pick_kernel, len(after)),
        in_specs=[pl.BlockSpec(memory_space=pltpu.SMEM)] + [INSIDE] * 3 + [ANYWHERE] * len(after),
        out_specs=[INSIDE] * 3,
        out_shape=[jax.ShapeDtypeStruct(mine.shape, BF16)] * 2 + [TOKEN],
        compiler_params=pltpu.CompilerParams(vmem_limit_bytes=VMEM // 2),
        cost_estimate=as_if(8),
        name="pick",
    )(place, inner_three, outer_three, mine, *after)


def resident(values):
    return pltpu.with_memory_space_constraint(values, pltpu.VMEM)


def gate_up_kernel(part_count, after_count, *refs):
    parts, (gate_ref, up_ref) = refs[:part_count], refs[part_count : part_count + 2]
    keep_ref, near_ref, *far_refs, token_ref, all_rows = refs[part_count + 2 + after_count :]
    far_places = [(far_ref, which) for far_ref in far_refs for which in range(far_ref.shape[0])]
    token_ref[...] = jnp.zeros_like(token_ref)
    half = parts[0].shape[0] // 2
    kept = half * len(parts)
    for place, part in enumerate(parts):
        all_rows[pl.ds(place * half, half), :] = part[:half, :]
        all_rows[pl.ds(kept + place * half, half), :] = part[half:, :]
    tile = tile_of(gate_ref.shape[1], 256)

    @pl.loop(0, gate_ref.shape[1] // tile)
    def _(number):
        columns = pl.ds(pl.multiple_of(number * tile, tile), tile)
        for which, weight_ref in enumerate((gate_ref, up_ref)):
            total = jnp.dot(all_rows[...], weight_ref[:, columns], preferred_element_type=F32)
            total = total.reshape(2, *keep_ref.shape[1:4], tile).astype(BF16)
            keep_ref[which, :, :, :, columns] = total[0]
            near_ref[which, :, :, columns] = total[1, :, 0]
            far_ref, place = far_places[which]
            far_ref[place, :, :, :, columns] = total[1, :, 1:]


def gate_up(parts, gate_kept, up_kept, chips, far_parts, hint, after):
    rows = sum(part.shape[0] for part in parts)
    depth, width = gate_kept.shape
    groups, own = len(parts), rows // (2 * len(parts) * chips)
    shapes = [(2, groups, chips, own, width), (2, groups, own, width)]
    shapes += [(2 // far_parts, groups, chips - 1, own, width)] * far_parts
    return pl.pallas_call(
        functools.partial(gate_up_kernel, len(parts), len(after)),
        in_specs=[INSIDE] * (len(parts) + 2) + [ANYWHERE] * len(after),
        out_specs=[INSIDE] * (len(shapes) + 1),
        out_shape=[jax.ShapeDtypeStruct(shape, BF16) for shape in shapes] + [TOKEN],
        scratch_shapes=[pltpu.VMEM((rows, depth), BF16)],
        compiler_params=pltpu.CompilerParams(vmem_limit_bytes=VMEM // 2),
        cost_estimate=cost(hint * 4 * rows * depth * width, 0),
        name="gate_up",
    )(*parts, resident(gate_kept), resident(up_kept), *after)


def down_kernel(pieces, weight_count, after_count, own_ref, other_ref, *refs):
    weight_refs, refs = refs[:weight_count], refs[weight_count:]
    *partial_refs, token_ref, both = refs[after_count:]
    token_ref[...] = jnp.zeros_like(token_ref)
    groups, own, depth = own_ref.shape
    rows = groups * own
    both[:rows, :] = own_ref[...].astype(F32).reshape(rows, depth).astype(BF16)
    both[rows:, :] = other_ref[...].astype(F32).reshape(rows, depth).astype(BF16)
    for number, weight_ref in enumerate(weight_refs):
        width = weight_ref.shape[1]
        down_columns(pieces, both, weight_ref, partial_refs, number * width, tile_of(width, 512))


def down_columns(pieces, both, weight_ref, partial_refs, first, tile):
    own = partial_refs[0].shape[1]

    @pl.loop(0, weight_ref.shape[1] // tile)
    def _(number):
        start = pl.multiple_of(number * tile, tile)
        total = jnp.dot(both[...], weight_ref[:, pl.ds(start, tile)], preferred_element_type=F32)
        total = total.reshape(pieces, CORES // pieces, len(partial_refs) // pieces, own, tile)
        columns = pl.ds(pl.multiple_of(first + start, tile), tile)
        for place, partial_ref in enumerate(partial_refs):
            partial_ref[:, :, columns] = total[place % pieces, :, place // pieces].astype(BF16)


def down(own, other, down_kept, pieces, after):
    groups, rows, depth = own.shape
    width = sum(weight.shape[1] for weight in down_kept)
    shape = (CORES // pieces, rows, width)
    return pl.pallas_call(
        functools.partial(down_kernel, pieces, len(down_kept), len(after)),
        in_specs=[INSIDE] * (2 + len(down_kept)) + [ANYWHERE] * len(after),
        out_specs=[INSIDE] * (groups * pieces + 1),
        out_shape=[jax.ShapeDtypeStruct(shape, BF16)] * (groups * pieces) + [TOKEN],
        scratch_shapes=[pltpu.VMEM((CORES * groups * rows, depth), BF16)],
        compiler_params=pltpu.CompilerParams(vmem_limit_bytes=VMEM // 2),
        cost_estimate=cost(2 * CORES * groups * rows * depth * width, 0),
        name="down",
    )(own, other, *(resident(weight) for weight in down_kept), *after)


def sums_kernel(sizes, after_count, *refs):
    to_chips, to_hidden, *to_rows = sizes
    refs = list(refs)
    refs.pop()[...] = jnp.zeros(TOKEN.shape, F32)
    ins = [[refs.pop(0) for _ in range(size)] for size in sizes]
    del refs[:after_count]

    if to_chips:
        keep_ref, *came_refs = ins[0]
        came_places = [came_ref.at[which] for came_ref in came_refs for which in range(came_ref.shape[0])]
        for chip in range(1, keep_ref.shape[2]):
            sent_ref = refs.pop(0)
            for which in range(2):
                for group in range(keep_ref.shape[1]):
                    came = came_places[which][group, chip - 1].astype(F32)
                    sent_ref[which, group] = (keep_ref[which, group, chip].astype(F32) + came).astype(BF16)
    if to_hidden:
        keep_ref, came_ref, *chip_refs = ins[1]
        hidden_ref = refs.pop(0)
        for group in range(keep_ref.shape[1]):
            both = []
            for which in range(2):
                total = keep_ref[which, group, 0].astype(F32) + came_ref[which, group].astype(F32)
                for chip_ref in chip_refs:
                    total = total + chip_ref[which, group].astype(F32)
                both.append(total)
            hidden_ref[group] = (jax.nn.silu(both[0]) * both[1]).astype(BF16)
    for part_refs in ins[2:]:
        summed_ref = refs.pop(0)
        cores = summed_ref.shape[0]
        for core in range(cores):
            total = part_refs[0][core].astype(F32)
            for part_ref in part_refs[1:]:
                total = total + part_ref[part_ref.shape[0] - cores + core].astype(F32)
            summed_ref[core] = total.astype(BF16)


def sums(to_chips, to_hidden, to_rows, after, hint=0.0):
    shapes = []
    if to_chips:
        two, groups, chips, own, width = to_chips[0].shape
        shapes += [(two, groups, own, width)] * (chips - 1)
    if to_hidden:
        shapes.append((to_hidden[0].shape[1], *to_hidden[0].shape[3:]))
    shapes += [parts[0].shape for parts in to_rows]
    given = [to_chips, to_hidden, *to_rows]
    sizes = tuple(len(parts) for parts in given)
    given = [part for parts in given for part in parts]
    results = list(pl.pallas_call(
        functools.partial(sums_kernel, sizes, len(after)),
        in_specs=[INSIDE] * len(given) + [ANYWHERE] * len(after),
        out_specs=[INSIDE] * (len(shapes) + 1),
        out_shape=[jax.ShapeDtypeStruct(shape, BF16) for shape in shapes] + [TOKEN],
        compiler_params=pltpu.CompilerParams(vmem_limit_bytes=VMEM // 2),
        cost_estimate=as_if(hint),
        name="sums",
    )(*given, *after))
    token = results.pop()
    sent = [results.pop(0) for _ in range(chips - 1)] if to_chips else []
    hidden = results.pop(0) if to_hidden else None
    return sent, hidden, results, token


def swap(values, axis, size, step):
    return lax.ppermute(values, axis, [(place, place ^ step) for place in range(size)])


def body(row_count, col_count, tokens, norm_gain, gate_weight, up_weight, down_weight, gate_mask, up_mask, down_mask):
    chips = row_count // CORES
    per_plane = col_count // PLANES
    features, width = gate_weight.shape
    row = lax.axis_index("rows")
    core = row % CORES
    inner = (lax.axis_index("cols") // per_plane) % (PLANES - 1) != 0
    place = jnp.stack([core, inner.astype(core.dtype)])

    normed = rms_normed(tokens, norm_gain)
    def block(step):
        return lax.dynamic_slice_in_dim(normed, (row ^ step) * features, features, 1)

    from_core = swap(jnp.stack([block(chip * CORES + 1) for chip in range(chips)]), "rows", row_count, 1)
    to_chips_rows = [stack([block(chip * CORES), from_core[chip]], [])[0] for chip in range(1, chips)]
    first, token = stack([block(0), from_core[0]], to_chips_rows[:1])
    gate_kept, token = masked(gate_weight, gate_mask, tile_of(features, 256), place, 1, lambda core: 0, [token])
    second = [swap(part, "rows", row_count, (chip + 1) * CORES) for chip, part in enumerate(to_chips_rows)]
    second = jnp.concatenate(second, 1) if len(second) > 1 else second[0]
    mine, token = join([first, second], [token])

    def behind(values, after):
        return lax.optimization_barrier((values, *after))[0] if after else values

    def by_plane(values, planes, after=()):
        pairs = [(a * per_plane + b, c * per_plane + b) for a, c in planes for b in range(per_plane)]
        return lax.ppermute(behind(values, after), "cols", pairs)

    def by_row_of_plane(values, step, after=()):
        return swap(behind(values, after), "cols", col_count, step)

    def by_chip(values, chip, after=()):
        return swap(behind(values, after), "rows", row_count, chip * CORES)

    def by_core(values, after=()):
        return swap(behind(values, after), "rows", row_count, 1)

    parts, halves, near, far, chip_sums, hiddens, others, rows_in, partials, sent = ({} for _ in range(10))
    last = [token]

    def forward(plane, values, after=()):
        parts[plane] = [values]
        for step in range(1, per_plane):
            parts[plane].append(by_row_of_plane(values, step, after))

    def multiply_in(plane, far_parts=1, hint=HURRY, after=()):
        parts_after = last + list(after)
        *halves[plane], last[0] = gate_up(parts[plane], gate_kept, up_kept, chips, far_parts, hint, parts_after)

    def exchange(plane, after=()):
        far[plane] = [by_core(part, after) for part in halves[plane][2:]]

    def exchange_near(plane, after=()):
        near[plane] = by_core(halves[plane][1], after)

    def multiply_out(plane, pieces=1, after=()):
        *partials[plane], last[0] = down(hiddens[plane], others[plane], down_kept, pieces, last + list(after))

    def send_rows(plane, after=(), pieces=1, piece=0):
        mine_and_others = partials[plane][piece::pieces]
        rows_in[plane, piece] = mine_and_others[:1]
        for step in range(1, per_plane):
            rows_in[plane, piece].append(by_row_of_plane(mine_and_others[step], step, after))

    def to_chips(plane, after=()):
        given = [halves[plane][0], *far[plane]]
        sent[plane], _, _, last[0] = sums(given, [], [], last + list(after))

    def send_chips(plane, after=()):
        chip_sums[plane] = [by_chip(part, number + 1, after) for number, part in enumerate(sent[plane])]

    def to_hidden(plane, after=()):
        given = [halves[plane][0], near[plane], *chip_sums[plane]]
        _, hiddens[plane], _, last[0] = sums([], given, [], last + list(after))
        others[plane] = by_core(hiddens[plane])

    def to_rows(*parts, after=(), hint=0.0):
        _, _, (summed,), last[0] = sums([], [], [parts], last + list(after), hint)
        return summed

    next_stacks = [by_plane(first, NEXT), by_plane(second, NEXT)]
    across_stacks = [by_plane(first, ACROSS), by_plane(second, ACROSS)]
    row_stacks = {
        step: [by_row_of_plane(first, step), by_row_of_plane(second, step)] for step in range(1, per_plane)
    }
    up_kept, last[0] = masked(
        up_weight, up_mask, tile_of(features, 256), place, 1, lambda core: 0, last + next_stacks[:1], 0.15
    )
    last[0] = waited([*last, across_stacks[0], *(stacks[0] for stacks in row_stacks.values())], 0.07)
    one_away, last[0] = join(next_stacks, last)
    inner_three, last[0] = join(across_stacks, last + [stacks[1] for stacks in row_stacks.values()])
    outer_three = by_plane(mine, AROUND, last)
    down_kept = []

    def keep_down(share, hint=0.0):
        part, last[0] = masked(
            down_weight, down_mask, 2 * BLOCK, place, 2 * CORES, lambda core: 2 * core + share, last, hint
        )
        down_kept.append(part)

    parts[0] = [mine]
    for stacks in row_stacks.values():
        part, last[0] = join(stacks, last)
        parts[0].append(part)
    forward(1, one_away, last)
    multiply_in(0, hint=0)
    exchange(0)
    exchange_near(0)
    keep_down(0)
    keep_down(1)
    three_away, passed, last[0] = pick(place, inner_three, outer_three, mine, last)
    two_away = by_plane(passed, CYCLE)
    to_chips(0, [near[0]])
    forward(3, three_away, [*parts[1][1:], *last])
    multiply_in(1)
    exchange(1)
    exchange_near(1)
    to_chips(1, [near[1]])
    send_chips(1)
    forward(2, two_away, last)
    multiply_in(3, after=[two_away])
    exchange(3)
    exchange_near(3)
    to_hidden(1)
    to_chips(3, [near[3]])
    send_chips(3)
    multiply_out(1)
    send_rows(1, parts[2][1:])
    multiply_in(2, far_parts=2)
    exchange(2)
    to_hidden(3)
    to_chips(2)
    send_chips(2)
    exchange_near(2, last)
    multiply_out(3, pieces=CORES)
    send_rows(3, rows_in[1, 0][1:], CORES, 1)
    one = to_rows(*rows_in[1, 0])
    one_out = by_plane(one, NEXT)
    three = to_rows(*rows_in[3, 1])
    send_rows(3, [three], CORES, 0)
    three_out, two_out = {1: by_plane(three, NEXT)}, {}
    to_hidden(2)
    send_chips(0, chip_sums[2])
    multiply_out(2, pieces=CORES)
    three = to_rows(*rows_in[3, 0], after=[one_out])
    three_out[0] = by_plane(three, NEXT)
    send_rows(2, [three], CORES, 1)
    two = to_rows(*rows_in[2, 1], three_out[1])
    two_out[1] = by_plane(two, SECOND)
    send_rows(2, [two], CORES, 0)
    to_hidden(0)
    multiply_out(0)
    two = to_rows(rows_in[2, 0][0], three_out[0], hint=0.5)
    two = to_rows(two, *rows_in[2, 0][1:])
    two_out[0] = by_plane(two, SECOND)
    send_rows(0, rows_in[2, 0][1:])

    joined = to_rows(two_out[1], one_out, hint=10.0)

    def total(piece, *parts):
        whole = [part[piece].astype(F32) for part in rows_in[0, 0]] + [part.astype(F32) for part in parts]
        return sum(whole[1:], whole[0]).astype(BF16)

    mine_now, other = total(0, one_out[0], two_out[0][0]), by_core(total(1, joined[0]))
    left = jnp.where(core == 0, mine_now, other)
    right = jnp.where(core == 0, other, mine_now)
    return jnp.concatenate([left, right], 1)


def solution(mesh):
    return jax.shard_map(
        functools.partial(body, mesh.shape["rows"], mesh.shape["cols"]),
        mesh=mesh,
        in_specs=(
            P(("rows", "cols"), None),
            P(),
            P("rows", "cols"),
            P("rows", "cols"),
            P("cols", None),
            P("rows", "cols"),
            P("rows", "cols"),
            P("cols", None),
        ),
        out_specs=P(("rows", "cols"), None),
        check_vma=False,
    )
```

```python
import functools

import jax
import jax.numpy as jnp
from jax import lax
from jax.experimental import pallas as pl
from jax.experimental.pallas import tpu as pltpu
from jax.sharding import PartitionSpec as P

BLOCK = 64
ROWS = 16
CORES = 2
PLANES = 4
NEXT = ((0, 1), (1, 0), (2, 3), (3, 2))
SECOND = ((0, 2), (2, 0), (1, 3), (3, 1))
ACROSS = ((1, 2), (2, 1))
AROUND = ((0, 3), (3, 0))
CYCLE = ((0, 2), (2, 3), (3, 1), (1, 0))
VMEM = 12 * 1024 * 1024
F32 = jnp.float32
BF16 = jnp.bfloat16


def tile_of(size, most):
    tile = most
    while size % tile:
        tile //= 2
    return tile


def rms_normed(rows_in, norm_gain):
    values = rows_in.astype(F32)
    meansq = jnp.mean(values * values, axis=-1, keepdims=True)
    return (values * lax.rsqrt(meansq + 1e-05) * norm_gain).astype(BF16)


HURRY = 1000


def cost(flops, moved):
    return pl.CostEstimate(flops=flops // HURRY, bytes_accessed=moved // HURRY, transcendentals=0)


def as_if(microseconds):
    return cost(int(HURRY * 1.15e9 * microseconds), 0)


ANYWHERE = pl.BlockSpec(memory_space=pl.ANY)
TOKEN = jax.ShapeDtypeStruct((8, 128), F32)
INSIDE = pl.BlockSpec(memory_space=pltpu.VMEM)


def mask_kernel(share, rows, after_count, core_ref, weight_ref, mask_ref, *refs):
    kept_ref, token_ref, spread, semaphores = refs[after_count:]
    token_ref[...] = jnp.zeros_like(token_ref)
    depth, width = kept_ref.shape
    number = share(core_ref[0])
    columns = pl.ds(pl.multiple_of(number * width, width), width)
    copies = [
        pltpu.make_async_copy(
            weight_ref.at[pl.ds(step * rows, rows), columns], kept_ref.at[pl.ds(step * rows, rows)], semaphores.at[step]
        )
        for step in range(depth // rows)
    ]
    for copy in copies:
        copy.start()
    marks = mask_ref.shape[1]
    owner = lax.broadcasted_iota(jnp.int32, (marks, width), 1) // BLOCK + number * (width // BLOCK)
    chosen = (owner == lax.broadcasted_iota(jnp.int32, (marks, width), 0)).astype(BF16)
    spread[...] = jnp.dot(mask_ref[...].astype(BF16), chosen, preferred_element_type=F32)
    for step, copy in enumerate(copies):
        copy.wait()
        for block in range(step * rows // BLOCK, (step + 1) * rows // BLOCK):
            keep = jnp.broadcast_to(spread[pl.ds(block, 1), :], (ROWS, width)).astype(BF16)
            for first in range(block * BLOCK, (block + 1) * BLOCK, ROWS):
                part = pl.ds(first, ROWS)
                kept_ref[part, :] = kept_ref[part, :] * keep


def masked(weight, mask, rows, core, shares, share, after, hint=0.0):
    depth, width = weight.shape
    width = width // shares
    return pl.pallas_call(
        functools.partial(mask_kernel, share, rows, len(after)),
        in_specs=[pl.BlockSpec(memory_space=pltpu.SMEM), ANYWHERE, INSIDE] + [ANYWHERE] * len(after),
        out_specs=[INSIDE] * 2,
        out_shape=[jax.ShapeDtypeStruct((depth, width), weight.dtype), TOKEN],
        scratch_shapes=[pltpu.VMEM((mask.shape[0], width), F32), pltpu.SemaphoreType.DMA((depth // rows,))],
        compiler_params=pltpu.CompilerParams(vmem_limit_bytes=VMEM),
        cost_estimate=as_if(hint),
        name="masked",
    )(core, pltpu.with_memory_space_constraint(weight, pltpu.HBM), mask, *after)


def stack_kernel(after_count, *refs):
    block_refs, (stacked_ref, token_ref) = refs[: -2 - after_count], refs[-2:]
    token_ref[...] = jnp.zeros_like(token_ref)
    for number, block_ref in enumerate(block_refs):
        stacked_ref[number // stacked_ref.shape[1], number % stacked_ref.shape[1]] = block_ref[...]


def join_kernel(after_count, *refs):
    stacked_refs, (joined_ref, token_ref) = refs[: -2 - after_count], refs[-2:]
    token_ref[...] = jnp.zeros_like(token_ref)
    blocks = [ref[core, chip] for core in range(CORES) for ref in stacked_refs for chip in range(ref.shape[1])]
    joined_ref[...] = jnp.concatenate([block.astype(F32) for block in blocks], 0).astype(BF16)


def rearranged(kernel, name, shape, blocks, after, hint=0.0):
    return pl.pallas_call(
        functools.partial(kernel, len(after)),
        in_specs=[INSIDE] * len(blocks) + [ANYWHERE] * len(after),
        out_specs=[INSIDE] * 2,
        out_shape=[jax.ShapeDtypeStruct(shape, BF16), TOKEN],
        compiler_params=pltpu.CompilerParams(vmem_limit_bytes=VMEM // 2),
        cost_estimate=as_if(hint),
        name=name,
    )(*blocks, *after)


def wait_kernel(*refs):
    refs[-1][...] = jnp.zeros_like(refs[-1])


def waited(after, hint):
    return pl.pallas_call(
        wait_kernel,
        in_specs=[ANYWHERE] * len(after),
        out_specs=INSIDE,
        out_shape=TOKEN,
        compiler_params=pltpu.CompilerParams(vmem_limit_bytes=VMEM // 2),
        cost_estimate=as_if(hint),
        name="waited",
    )(*after)


def stack(blocks, after):
    shape = (CORES, len(blocks) // CORES, *blocks[0].shape)
    return rearranged(stack_kernel, "stack", shape, blocks, after)


def join(stacks, after, hint=0.0):
    rows = sum(part.shape[1] for part in stacks) * CORES * stacks[0].shape[2]
    return rearranged(join_kernel, "join", (rows, stacks[0].shape[3]), stacks, after, hint)


def pick_kernel(after_count, place_ref, inner_three_ref, outer_three_ref, mine_ref, *refs):
    three_ref, passed_ref, token_ref = refs[after_count:]
    token_ref[...] = jnp.zeros_like(token_ref)

    @pl.when(place_ref[1] == 1)
    def _():
        three_ref[...] = inner_three_ref[...]
        passed_ref[...] = inner_three_ref[...]

    @pl.when(place_ref[1] == 0)
    def _():
        three_ref[...] = outer_three_ref[...]
        passed_ref[...] = mine_ref[...]


def pick(place, inner_three, outer_three, mine, after):
    return pl.pallas_call(
        functools.partial(pick_kernel, len(after)),
        in_specs=[pl.BlockSpec(memory_space=pltpu.SMEM)] + [INSIDE] * 3 + [ANYWHERE] * len(after),
        out_specs=[INSIDE] * 3,
        out_shape=[jax.ShapeDtypeStruct(mine.shape, BF16)] * 2 + [TOKEN],
        compiler_params=pltpu.CompilerParams(vmem_limit_bytes=VMEM // 2),
        cost_estimate=as_if(8),
        name="pick",
    )(place, inner_three, outer_three, mine, *after)


def resident(values):
    return pltpu.with_memory_space_constraint(values, pltpu.VMEM)


def gate_up_kernel(part_count, after_count, *refs):
    parts, (gate_ref, up_ref) = refs[:part_count], refs[part_count : part_count + 2]
    keep_ref, near_ref, *far_refs, token_ref, all_rows = refs[part_count + 2 + after_count :]
    far_places = [(far_ref, which) for far_ref in far_refs for which in range(far_ref.shape[0])]
    token_ref[...] = jnp.zeros_like(token_ref)
    half = parts[0].shape[0] // 2
    kept = half * len(parts)
    for place, part in enumerate(parts):
        all_rows[pl.ds(place * half, half), :] = part[:half, :]
        all_rows[pl.ds(kept + place * half, half), :] = part[half:, :]
    tile = tile_of(gate_ref.shape[1], 256)

    @pl.loop(0, gate_ref.shape[1] // tile)
    def _(number):
        columns = pl.ds(pl.multiple_of(number * tile, tile), tile)
        for which, weight_ref in enumerate((gate_ref, up_ref)):
            total = jnp.dot(all_rows[...], weight_ref[:, columns], preferred_element_type=F32)
            total = total.reshape(2, *keep_ref.shape[1:4], tile).astype(BF16)
            keep_ref[which, :, :, :, columns] = total[0]
            near_ref[which, :, :, columns] = total[1, :, 0]
            far_ref, place = far_places[which]
            far_ref[place, :, :, :, columns] = total[1, :, 1:]


def gate_up(parts, gate_kept, up_kept, chips, far_parts, hint, after):
    rows = sum(part.shape[0] for part in parts)
    depth, width = gate_kept.shape
    groups, own = len(parts), rows // (2 * len(parts) * chips)
    shapes = [(2, groups, chips, own, width), (2, groups, own, width)]
    shapes += [(2 // far_parts, groups, chips - 1, own, width)] * far_parts
    return pl.pallas_call(
        functools.partial(gate_up_kernel, len(parts), len(after)),
        in_specs=[INSIDE] * (len(parts) + 2) + [ANYWHERE] * len(after),
        out_specs=[INSIDE] * (len(shapes) + 1),
        out_shape=[jax.ShapeDtypeStruct(shape, BF16) for shape in shapes] + [TOKEN],
        scratch_shapes=[pltpu.VMEM((rows, depth), BF16)],
        compiler_params=pltpu.CompilerParams(vmem_limit_bytes=VMEM // 2),
        cost_estimate=cost(hint * 4 * rows * depth * width, 0),
        name="gate_up",
    )(*parts, resident(gate_kept), resident(up_kept), *after)


def down_kernel(pieces, weight_count, after_count, own_ref, other_ref, *refs):
    weight_refs, refs = refs[:weight_count], refs[weight_count:]
    *partial_refs, token_ref, both = refs[after_count:]
    token_ref[...] = jnp.zeros_like(token_ref)
    groups, own, depth = own_ref.shape
    rows = groups * own
    both[:rows, :] = own_ref[...].astype(F32).reshape(rows, depth).astype(BF16)
    both[rows:, :] = other_ref[...].astype(F32).reshape(rows, depth).astype(BF16)
    for number, weight_ref in enumerate(weight_refs):
        width = weight_ref.shape[1]
        down_columns(pieces, both, weight_ref, partial_refs, number * width, tile_of(width, 512))


def down_columns(pieces, both, weight_ref, partial_refs, first, tile):
    own = partial_refs[0].shape[1]

    @pl.loop(0, weight_ref.shape[1] // tile)
    def _(number):
        start = pl.multiple_of(number * tile, tile)
        total = jnp.dot(both[...], weight_ref[:, pl.ds(start, tile)], preferred_element_type=F32)
        total = total.reshape(pieces, CORES // pieces, len(partial_refs) // pieces, own, tile)
        columns = pl.ds(pl.multiple_of(first + start, tile), tile)
        for place, partial_ref in enumerate(partial_refs):
            partial_ref[:, :, columns] = total[place % pieces, :, place // pieces].astype(BF16)


def down(own, other, down_kept, pieces, after):
    groups, rows, depth = own.shape
    width = sum(weight.shape[1] for weight in down_kept)
    shape = (CORES // pieces, rows, width)
    return pl.pallas_call(
        functools.partial(down_kernel, pieces, len(down_kept), len(after)),
        in_specs=[INSIDE] * (2 + len(down_kept)) + [ANYWHERE] * len(after),
        out_specs=[INSIDE] * (groups * pieces + 1),
        out_shape=[jax.ShapeDtypeStruct(shape, BF16)] * (groups * pieces) + [TOKEN],
        scratch_shapes=[pltpu.VMEM((CORES * groups * rows, depth), BF16)],
        compiler_params=pltpu.CompilerParams(vmem_limit_bytes=VMEM // 2),
        cost_estimate=cost(2 * CORES * groups * rows * depth * width, 0),
        name="down",
    )(own, other, *(resident(weight) for weight in down_kept), *after)


def sums_kernel(sizes, after_count, *refs):
    to_chips, to_hidden, *to_rows = sizes
    refs = list(refs)
    refs.pop()[...] = jnp.zeros(TOKEN.shape, F32)
    ins = [[refs.pop(0) for _ in range(size)] for size in sizes]
    del refs[:after_count]

    if to_chips:
        keep_ref, *came_refs = ins[0]
        came_places = [came_ref.at[which] for came_ref in came_refs for which in range(came_ref.shape[0])]
        for chip in range(1, keep_ref.shape[2]):
            sent_ref = refs.pop(0)
            for which in range(2):
                for group in range(keep_ref.shape[1]):
                    came = came_places[which][group, chip - 1].astype(F32)
                    sent_ref[which, group] = (keep_ref[which, group, chip].astype(F32) + came).astype(BF16)
    if to_hidden:
        keep_ref, came_ref, *chip_refs = ins[1]
        hidden_ref = refs.pop(0)
        for group in range(keep_ref.shape[1]):
            both = []
            for which in range(2):
                total = keep_ref[which, group, 0].astype(F32) + came_ref[which, group].astype(F32)
                for chip_ref in chip_refs:
                    total = total + chip_ref[which, group].astype(F32)
                both.append(total)
            hidden_ref[group] = (jax.nn.silu(both[0]) * both[1]).astype(BF16)
    for part_refs in ins[2:]:
        summed_ref = refs.pop(0)
        cores = summed_ref.shape[0]
        for core in range(cores):
            total = part_refs[0][core].astype(F32)
            for part_ref in part_refs[1:]:
                total = total + part_ref[part_ref.shape[0] - cores + core].astype(F32)
            summed_ref[core] = total.astype(BF16)


def sums(to_chips, to_hidden, to_rows, after, hint=0.0):
    shapes = []
    if to_chips:
        two, groups, chips, own, width = to_chips[0].shape
        shapes += [(two, groups, own, width)] * (chips - 1)
    if to_hidden:
        shapes.append((to_hidden[0].shape[1], *to_hidden[0].shape[3:]))
    shapes += [parts[0].shape for parts in to_rows]
    given = [to_chips, to_hidden, *to_rows]
    sizes = tuple(len(parts) for parts in given)
    given = [part for parts in given for part in parts]
    results = list(pl.pallas_call(
        functools.partial(sums_kernel, sizes, len(after)),
        in_specs=[INSIDE] * len(given) + [ANYWHERE] * len(after),
        out_specs=[INSIDE] * (len(shapes) + 1),
        out_shape=[jax.ShapeDtypeStruct(shape, BF16) for shape in shapes] + [TOKEN],
        compiler_params=pltpu.CompilerParams(vmem_limit_bytes=VMEM // 2),
        cost_estimate=as_if(hint),
        name="sums",
    )(*given, *after))
    token = results.pop()
    sent = [results.pop(0) for _ in range(chips - 1)] if to_chips else []
    hidden = results.pop(0) if to_hidden else None
    return sent, hidden, results, token


def swap(values, axis, size, step):
    return lax.ppermute(values, axis, [(place, place ^ step) for place in range(size)])


def body(row_count, col_count, tokens, norm_gain, gate_weight, up_weight, down_weight, gate_mask, up_mask, down_mask):
    chips = row_count // CORES
    per_plane = col_count // PLANES
    features, width = gate_weight.shape
    row = lax.axis_index("rows")
    core = row % CORES
    inner = (lax.axis_index("cols") // per_plane) % (PLANES - 1) != 0
    place = jnp.stack([core, inner.astype(core.dtype)])

    normed = rms_normed(tokens, norm_gain)
    def block(step):
        return lax.dynamic_slice_in_dim(normed, (row ^ step) * features, features, 1)

    from_core = swap(jnp.stack([block(chip * CORES + 1) for chip in range(chips)]), "rows", row_count, 1)
    to_chips_rows = [stack([block(chip * CORES), from_core[chip]], [])[0] for chip in range(1, chips)]
    first, token = stack([block(0), from_core[0]], to_chips_rows[:1])
    gate_kept, token = masked(gate_weight, gate_mask, tile_of(features, 256), place, 1, lambda core: 0, [token])
    second = [swap(part, "rows", row_count, (chip + 1) * CORES) for chip, part in enumerate(to_chips_rows)]
    second = jnp.concatenate(second, 1) if len(second) > 1 else second[0]
    mine, token = join([first, second], [token])

    def behind(values, after):
        return lax.optimization_barrier((values, *after))[0] if after else values

    def by_plane(values, planes, after=()):
        pairs = [(a * per_plane + b, c * per_plane + b) for a, c in planes for b in range(per_plane)]
        return lax.ppermute(behind(values, after), "cols", pairs)

    def by_row_of_plane(values, step, after=()):
        return swap(behind(values, after), "cols", col_count, step)

    def by_chip(values, chip, after=()):
        return swap(behind(values, after), "rows", row_count, chip * CORES)

    def by_core(values, after=()):
        return swap(behind(values, after), "rows", row_count, 1)

    parts, halves, near, far, chip_sums, hiddens, others, rows_in, partials, sent = ({} for _ in range(10))
    last = [token]

    def forward(plane, values, after=()):
        parts[plane] = [values]
        for step in range(1, per_plane):
            parts[plane].append(by_row_of_plane(values, step, after))

    def multiply_in(plane, far_parts=1, hint=HURRY, after=()):
        parts_after = last + list(after)
        *halves[plane], last[0] = gate_up(parts[plane], gate_kept, up_kept, chips, far_parts, hint, parts_after)

    def exchange(plane, after=()):
        far[plane] = [by_core(part, after) for part in halves[plane][2:]]

    def exchange_near(plane, after=()):
        near[plane] = by_core(halves[plane][1], after)

    def multiply_out(plane, pieces=1, after=()):
        *partials[plane], last[0] = down(hiddens[plane], others[plane], down_kept, pieces, last + list(after))

    def send_rows(plane, after=(), pieces=1, piece=0):
        mine_and_others = partials[plane][piece::pieces]
        rows_in[plane, piece] = mine_and_others[:1]
        for step in range(1, per_plane):
            rows_in[plane, piece].append(by_row_of_plane(mine_and_others[step], step, after))

    def to_chips(plane, after=()):
        given = [halves[plane][0], *far[plane]]
        sent[plane], _, _, last[0] = sums(given, [], [], last + list(after))

    def send_chips(plane, after=()):
        chip_sums[plane] = [by_chip(part, number + 1, after) for number, part in enumerate(sent[plane])]

    def to_hidden(plane, after=()):
        given = [halves[plane][0], near[plane], *chip_sums[plane]]
        _, hiddens[plane], _, last[0] = sums([], given, [], last + list(after))
        others[plane] = by_core(hiddens[plane])

    def to_rows(*parts, after=(), hint=0.0):
        _, _, (summed,), last[0] = sums([], [], [parts], last + list(after), hint)
        return summed

    next_stacks = [by_plane(first, NEXT), by_plane(second, NEXT)]
    across_stacks = [by_plane(first, ACROSS), by_plane(second, ACROSS)]
    row_stacks = {
        step: [by_row_of_plane(first, step), by_row_of_plane(second, step)] for step in range(1, per_plane)
    }
    last[0] = waited(last + next_stacks[:1], 0.15)
    last[0] = waited([*last, across_stacks[0], *(stacks[0] for stacks in row_stacks.values())], 0.07)
    one_away, last[0] = join(next_stacks, last)
    inner_three, last[0] = join(across_stacks, last + [stacks[1] for stacks in row_stacks.values()])
    outer_three = by_plane(mine, AROUND, last)
    down_kept = []

    def keep_down(share, hint=0.0):
        part, last[0] = masked(
            down_weight, down_mask, 2 * BLOCK, place, 2 * CORES, lambda core: 2 * core + share, last, hint
        )
        down_kept.append(part)

    parts[0] = [mine]
    for stacks in row_stacks.values():
        part, last[0] = join(stacks, last)
        parts[0].append(part)
    forward(1, one_away, last)
    up_kept, last[0] = masked(up_weight, up_mask, tile_of(features, 256), place, 1, lambda core: 0, last)
    multiply_in(0, hint=0)
    exchange(0)
    exchange_near(0)
    keep_down(0)
    keep_down(1)
    three_away, passed, last[0] = pick(place, inner_three, outer_three, mine, last)
    two_away = by_plane(passed, CYCLE)
    to_chips(0, [near[0]])
    forward(3, three_away, [*parts[1][1:], *last])
    multiply_in(1)
    exchange(1)
    exchange_near(1)
    to_chips(1, [near[1]])
    send_chips(1)
    forward(2, two_away, last)
    multiply_in(3, after=[two_away])
    exchange(3)
    exchange_near(3)
    to_hidden(1)
    to_chips(3, [near[3]])
    send_chips(3)
    multiply_out(1)
    send_rows(1, parts[2][1:])
    multiply_in(2, far_parts=2)
    exchange(2)
    to_hidden(3)
    to_chips(2)
    send_chips(2)
    exchange_near(2, last)
    multiply_out(3, pieces=CORES)
    send_rows(3, rows_in[1, 0][1:], CORES, 1)
    one = to_rows(*rows_in[1, 0])
    one_out = by_plane(one, NEXT)
    three = to_rows(*rows_in[3, 1])
    send_rows(3, [three], CORES, 0)
    three_out, two_out = {1: by_plane(three, NEXT)}, {}
    to_hidden(2)
    send_chips(0, chip_sums[2])
    multiply_out(2, pieces=CORES)
    three = to_rows(*rows_in[3, 0], after=[one_out])
    three_out[0] = by_plane(three, NEXT)
    send_rows(2, [three], CORES, 1)
    two = to_rows(*rows_in[2, 1], three_out[1])
    two_out[1] = by_plane(two, SECOND)
    send_rows(2, [two], CORES, 0)
    to_hidden(0)
    multiply_out(0)
    two = to_rows(rows_in[2, 0][0], three_out[0], hint=0.5)
    two = to_rows(two, *rows_in[2, 0][1:])
    two_out[0] = by_plane(two, SECOND)
    send_rows(0, rows_in[2, 0][1:])

    joined = to_rows(two_out[1], one_out, hint=10.0)

    def total(piece, *parts):
        whole = [part[piece].astype(F32) for part in rows_in[0, 0]] + [part.astype(F32) for part in parts]
        return sum(whole[1:], whole[0]).astype(BF16)

    mine_now, other = total(0, one_out[0], two_out[0][0]), by_core(total(1, joined[0]))
    left = jnp.where(core == 0, mine_now, other)
    right = jnp.where(core == 0, other, mine_now)
    return jnp.concatenate([left, right], 1)


def solution(mesh):
    return jax.shard_map(
        functools.partial(body, mesh.shape["rows"], mesh.shape["cols"]),
        mesh=mesh,
        in_specs=(
            P(("rows", "cols"), None),
            P(),
            P("rows", "cols"),
            P("rows", "cols"),
            P("cols", None),
            P("rows", "cols"),
            P("rows", "cols"),
            P("cols", None),
        ),
        out_specs=P(("rows", "cols"), None),
        check_vma=False,
    )
```

```python
import functools

import jax
import jax.numpy as jnp
from jax import lax
from jax.experimental import pallas as pl
from jax.experimental.pallas import tpu as pltpu
from jax.sharding import PartitionSpec as P

BLOCK = 64
CORES = 2
PLANES = 4
NEXT = ((0, 1), (1, 0), (2, 3), (3, 2))
SECOND = ((0, 2), (2, 0), (1, 3), (3, 1))
ACROSS = ((1, 2), (2, 1))
AROUND = ((0, 3), (3, 0))
CYCLE = ((0, 2), (2, 3), (3, 1), (1, 0))
VMEM = 12 * 1024 * 1024
F32 = jnp.float32
BF16 = jnp.bfloat16


def tile_of(size, most):
    tile = most
    while size % tile:
        tile //= 2
    return tile


def rms_normed(rows_in, norm_gain):
    values = rows_in.astype(F32)
    meansq = jnp.mean(values * values, axis=-1, keepdims=True)
    return (values * lax.rsqrt(meansq + 1e-05) * norm_gain).astype(BF16)


HURRY = 1000


def cost(flops, moved):
    return pl.CostEstimate(flops=flops // HURRY, bytes_accessed=moved // HURRY, transcendentals=0)


def as_if(microseconds):
    return cost(int(HURRY * 1.15e9 * microseconds), 0)


ANYWHERE = pl.BlockSpec(memory_space=pl.ANY)
TOKEN = jax.ShapeDtypeStruct((8, 128), F32)
INSIDE = pl.BlockSpec(memory_space=pltpu.VMEM)


def mask_kernel(share, rows, after_count, core_ref, weight_ref, mask_ref, *refs):
    kept_ref, token_ref, spread, semaphores = refs[after_count:]
    token_ref[...] = jnp.zeros_like(token_ref)
    depth, width = kept_ref.shape
    number = share(core_ref[0])
    columns = pl.ds(pl.multiple_of(number * width, width), width)
    copies = [
        pltpu.make_async_copy(
            weight_ref.at[pl.ds(step * rows, rows), columns], kept_ref.at[pl.ds(step * rows, rows)], semaphores.at[step]
        )
        for step in range(depth // rows)
    ]
    for copy in copies:
        copy.start()
    marks = mask_ref.shape[1]
    owner = lax.broadcasted_iota(jnp.int32, (marks, width), 1) // BLOCK + number * (width // BLOCK)
    chosen = (owner == lax.broadcasted_iota(jnp.int32, (marks, width), 0)).astype(F32)
    spread[...] = jnp.dot(mask_ref[...].astype(F32), chosen, preferred_element_type=F32)
    for step, copy in enumerate(copies):
        copy.wait()
        for block in range(step * rows // BLOCK, (step + 1) * rows // BLOCK):
            part = pl.ds(block * BLOCK, BLOCK)
            keep = jnp.broadcast_to(spread[pl.ds(block, 1), :], (BLOCK, width))
            kept_ref[part, :] = kept_ref[part, :] * keep.astype(BF16)


def masked(weight, mask, rows, core, shares, share, after, hint=0.0):
    depth, width = weight.shape
    width = width // shares
    return pl.pallas_call(
        functools.partial(mask_kernel, share, rows, len(after)),
        in_specs=[pl.BlockSpec(memory_space=pltpu.SMEM), ANYWHERE, INSIDE] + [ANYWHERE] * len(after),
        out_specs=[INSIDE] * 2,
        out_shape=[jax.ShapeDtypeStruct((depth, width), weight.dtype), TOKEN],
        scratch_shapes=[pltpu.VMEM((mask.shape[0], width), F32), pltpu.SemaphoreType.DMA((depth // rows,))],
        compiler_params=pltpu.CompilerParams(vmem_limit_bytes=VMEM),
        cost_estimate=as_if(hint),
        name="masked",
    )(core, pltpu.with_memory_space_constraint(weight, pltpu.HBM), mask, *after)


def stack_kernel(after_count, *refs):
    block_refs, (stacked_ref, token_ref) = refs[: -2 - after_count], refs[-2:]
    token_ref[...] = jnp.zeros_like(token_ref)
    for number, block_ref in enumerate(block_refs):
        stacked_ref[number // stacked_ref.shape[1], number % stacked_ref.shape[1]] = block_ref[...]


def join_kernel(after_count, *refs):
    stacked_refs, (joined_ref, token_ref) = refs[: -2 - after_count], refs[-2:]
    token_ref[...] = jnp.zeros_like(token_ref)
    blocks = [ref[core, chip] for core in range(CORES) for ref in stacked_refs for chip in range(ref.shape[1])]
    joined_ref[...] = jnp.concatenate([block.astype(F32) for block in blocks], 0).astype(BF16)


def rearranged(kernel, name, shape, blocks, after, hint=0.0):
    return pl.pallas_call(
        functools.partial(kernel, len(after)),
        in_specs=[INSIDE] * len(blocks) + [ANYWHERE] * len(after),
        out_specs=[INSIDE] * 2,
        out_shape=[jax.ShapeDtypeStruct(shape, BF16), TOKEN],
        compiler_params=pltpu.CompilerParams(vmem_limit_bytes=VMEM // 2),
        cost_estimate=as_if(hint),
        name=name,
    )(*blocks, *after)


def wait_kernel(*refs):
    refs[-1][...] = jnp.zeros_like(refs[-1])


def waited(after, hint):
    return pl.pallas_call(
        wait_kernel,
        in_specs=[ANYWHERE] * len(after),
        out_specs=INSIDE,
        out_shape=TOKEN,
        compiler_params=pltpu.CompilerParams(vmem_limit_bytes=VMEM // 2),
        cost_estimate=as_if(hint),
        name="waited",
    )(*after)


def stack(blocks, after):
    shape = (CORES, len(blocks) // CORES, *blocks[0].shape)
    return rearranged(stack_kernel, "stack", shape, blocks, after)


def join(stacks, after, hint=0.0):
    rows = sum(part.shape[1] for part in stacks) * CORES * stacks[0].shape[2]
    return rearranged(join_kernel, "join", (rows, stacks[0].shape[3]), stacks, after, hint)


def pick_kernel(after_count, side_ref, inner_three_ref, outer_three_ref, mine_ref, *refs):
    three_ref, passed_ref, token_ref = refs[after_count:]
    token_ref[...] = jnp.zeros_like(token_ref)

    @pl.when(side_ref[0] == 1)
    def _():
        three_ref[...] = inner_three_ref[...]
        passed_ref[...] = inner_three_ref[...]

    @pl.when(side_ref[0] == 0)
    def _():
        three_ref[...] = outer_three_ref[...]
        passed_ref[...] = mine_ref[...]


def pick(side, inner_three, outer_three, mine, after):
    return pl.pallas_call(
        functools.partial(pick_kernel, len(after)),
        in_specs=[pl.BlockSpec(memory_space=pltpu.SMEM)] + [INSIDE] * 3 + [ANYWHERE] * len(after),
        out_specs=[INSIDE] * 3,
        out_shape=[jax.ShapeDtypeStruct(mine.shape, BF16)] * 2 + [TOKEN],
        compiler_params=pltpu.CompilerParams(vmem_limit_bytes=VMEM // 2),
        cost_estimate=as_if(8),
        name="pick",
    )(side, inner_three, outer_three, mine, *after)


def resident(values):
    return pltpu.with_memory_space_constraint(values, pltpu.VMEM)


def gate_up_kernel(part_count, after_count, *refs):
    parts, (gate_ref, up_ref) = refs[:part_count], refs[part_count : part_count + 2]
    keep_ref, near_ref, *far_refs, token_ref, all_rows = refs[part_count + 2 + after_count :]
    far_places = [(far_ref, which) for far_ref in far_refs for which in range(far_ref.shape[0])]
    token_ref[...] = jnp.zeros_like(token_ref)
    half = parts[0].shape[0] // 2
    kept = half * len(parts)
    for place, part in enumerate(parts):
        all_rows[pl.ds(place * half, half), :] = part[:half, :]
        all_rows[pl.ds(kept + place * half, half), :] = part[half:, :]
    tile = tile_of(gate_ref.shape[1], 256)

    @pl.loop(0, gate_ref.shape[1] // tile)
    def _(number):
        columns = pl.ds(pl.multiple_of(number * tile, tile), tile)
        for which, weight_ref in enumerate((gate_ref, up_ref)):
            total = jnp.dot(all_rows[...], weight_ref[:, columns], preferred_element_type=F32)
            total = total.reshape(2, *keep_ref.shape[1:4], tile).astype(BF16)
            keep_ref[which, :, :, :, columns] = total[0]
            near_ref[which, :, :, columns] = total[1, :, 0]
            far_ref, place = far_places[which]
            far_ref[place, :, :, :, columns] = total[1, :, 1:]


def gate_up(parts, gate_kept, up_kept, chips, far_parts, hint, after):
    rows = sum(part.shape[0] for part in parts)
    depth, width = gate_kept.shape
    groups, own = len(parts), rows // (2 * len(parts) * chips)
    shapes = [(2, groups, chips, own, width), (2, groups, own, width)]
    shapes += [(2 // far_parts, groups, chips - 1, own, width)] * far_parts
    return pl.pallas_call(
        functools.partial(gate_up_kernel, len(parts), len(after)),
        in_specs=[INSIDE] * (len(parts) + 2) + [ANYWHERE] * len(after),
        out_specs=[INSIDE] * (len(shapes) + 1),
        out_shape=[jax.ShapeDtypeStruct(shape, BF16) for shape in shapes] + [TOKEN],
        scratch_shapes=[pltpu.VMEM((rows, depth), BF16)],
        compiler_params=pltpu.CompilerParams(vmem_limit_bytes=VMEM // 2),
        cost_estimate=cost(hint * 4 * rows * depth * width, 0),
        name="gate_up",
    )(*parts, resident(gate_kept), resident(up_kept), *after)


def down_kernel(pieces, weight_count, after_count, own_ref, other_ref, *refs):
    weight_refs, refs = refs[:weight_count], refs[weight_count:]
    *partial_refs, token_ref, both = refs[after_count:]
    token_ref[...] = jnp.zeros_like(token_ref)
    groups, own, depth = own_ref.shape
    rows = groups * own
    both[:rows, :] = own_ref[...].astype(F32).reshape(rows, depth).astype(BF16)
    both[rows:, :] = other_ref[...].astype(F32).reshape(rows, depth).astype(BF16)
    for number, weight_ref in enumerate(weight_refs):
        width = weight_ref.shape[1]
        down_columns(pieces, both, weight_ref, partial_refs, number * width, tile_of(width, 512))


def down_columns(pieces, both, weight_ref, partial_refs, first, tile):
    own = partial_refs[0].shape[1]

    @pl.loop(0, weight_ref.shape[1] // tile)
    def _(number):
        start = pl.multiple_of(number * tile, tile)
        total = jnp.dot(both[...], weight_ref[:, pl.ds(start, tile)], preferred_element_type=F32)
        total = total.reshape(pieces, CORES // pieces, len(partial_refs) // pieces, own, tile)
        columns = pl.ds(pl.multiple_of(first + start, tile), tile)
        for place, partial_ref in enumerate(partial_refs):
            partial_ref[:, :, columns] = total[place % pieces, :, place // pieces].astype(BF16)


def down(own, other, down_kept, pieces, after):
    groups, rows, depth = own.shape
    width = sum(weight.shape[1] for weight in down_kept)
    shape = (CORES // pieces, rows, width)
    return pl.pallas_call(
        functools.partial(down_kernel, pieces, len(down_kept), len(after)),
        in_specs=[INSIDE] * (2 + len(down_kept)) + [ANYWHERE] * len(after),
        out_specs=[INSIDE] * (groups * pieces + 1),
        out_shape=[jax.ShapeDtypeStruct(shape, BF16)] * (groups * pieces) + [TOKEN],
        scratch_shapes=[pltpu.VMEM((CORES * groups * rows, depth), BF16)],
        compiler_params=pltpu.CompilerParams(vmem_limit_bytes=VMEM // 2),
        cost_estimate=cost(2 * CORES * groups * rows * depth * width, 0),
        name="down",
    )(own, other, *(resident(weight) for weight in down_kept), *after)


def sums_kernel(sizes, after_count, *refs):
    to_chips, to_hidden, *to_rows = sizes
    refs = list(refs)
    refs.pop()[...] = jnp.zeros(TOKEN.shape, F32)
    ins = [[refs.pop(0) for _ in range(size)] for size in sizes]
    del refs[:after_count]

    if to_chips:
        keep_ref, *came_refs = ins[0]
        came_places = [came_ref.at[which] for came_ref in came_refs for which in range(came_ref.shape[0])]
        for chip in range(1, keep_ref.shape[2]):
            sent_ref = refs.pop(0)
            for which in range(2):
                for group in range(keep_ref.shape[1]):
                    came = came_places[which][group, chip - 1].astype(F32)
                    sent_ref[which, group] = (keep_ref[which, group, chip].astype(F32) + came).astype(BF16)
    if to_hidden:
        keep_ref, came_ref, *chip_refs = ins[1]
        hidden_ref = refs.pop(0)
        for group in range(keep_ref.shape[1]):
            both = []
            for which in range(2):
                total = keep_ref[which, group, 0].astype(F32) + came_ref[which, group].astype(F32)
                for chip_ref in chip_refs:
                    total = total + chip_ref[which, group].astype(F32)
                both.append(total)
            hidden_ref[group] = (jax.nn.silu(both[0]) * both[1]).astype(BF16)
    for part_refs in ins[2:]:
        summed_ref = refs.pop(0)
        cores = summed_ref.shape[0]
        for core in range(cores):
            total = part_refs[0][core].astype(F32)
            for part_ref in part_refs[1:]:
                total = total + part_ref[part_ref.shape[0] - cores + core].astype(F32)
            summed_ref[core] = total.astype(BF16)


def sums(to_chips, to_hidden, to_rows, after, hint=0.0):
    shapes = []
    if to_chips:
        two, groups, chips, own, width = to_chips[0].shape
        shapes += [(two, groups, own, width)] * (chips - 1)
    if to_hidden:
        shapes.append((to_hidden[0].shape[1], *to_hidden[0].shape[3:]))
    shapes += [parts[0].shape for parts in to_rows]
    given = [to_chips, to_hidden, *to_rows]
    sizes = tuple(len(parts) for parts in given)
    given = [part for parts in given for part in parts]
    results = list(pl.pallas_call(
        functools.partial(sums_kernel, sizes, len(after)),
        in_specs=[INSIDE] * len(given) + [ANYWHERE] * len(after),
        out_specs=[INSIDE] * (len(shapes) + 1),
        out_shape=[jax.ShapeDtypeStruct(shape, BF16) for shape in shapes] + [TOKEN],
        compiler_params=pltpu.CompilerParams(vmem_limit_bytes=VMEM // 2),
        cost_estimate=as_if(hint),
        name="sums",
    )(*given, *after))
    token = results.pop()
    sent = [results.pop(0) for _ in range(chips - 1)] if to_chips else []
    hidden = results.pop(0) if to_hidden else None
    return sent, hidden, results, token


def swap(values, axis, size, step):
    return lax.ppermute(values, axis, [(place, place ^ step) for place in range(size)])


def body(row_count, col_count, tokens, norm_gain, gate_weight, up_weight, down_weight, gate_mask, up_mask, down_mask):
    chips = row_count // CORES
    per_plane = col_count // PLANES
    features, width = gate_weight.shape
    row = lax.axis_index("rows")
    core = row % CORES
    inner = (lax.axis_index("cols") // per_plane) % (PLANES - 1) != 0
    place = jnp.reshape(core, (1,)).astype(jnp.int32)
    side = jnp.reshape(inner, (1,)).astype(jnp.int32)

    normed = rms_normed(tokens, norm_gain)
    def block(step):
        return lax.dynamic_slice_in_dim(normed, (row ^ step) * features, features, 1)

    from_core = swap(jnp.stack([block(chip * CORES + 1) for chip in range(chips)]), "rows", row_count, 1)
    to_chips_rows = [stack([block(chip * CORES), from_core[chip]], [])[0] for chip in range(1, chips)]
    first, token = stack([block(0), from_core[0]], [*to_chips_rows[:1], side])
    gate_kept, token = masked(gate_weight, gate_mask, tile_of(features, 256), place, 1, lambda core: 0, [token])
    second = [swap(part, "rows", row_count, (chip + 1) * CORES) for chip, part in enumerate(to_chips_rows)]
    second = jnp.concatenate(second, 1) if len(second) > 1 else second[0]
    mine, token = join([first, second], [token])

    def behind(values, after):
        return lax.optimization_barrier((values, *after))[0] if after else values

    def by_plane(values, planes, after=()):
        pairs = [(a * per_plane + b, c * per_plane + b) for a, c in planes for b in range(per_plane)]
        return lax.ppermute(behind(values, after), "cols", pairs)

    def by_row_of_plane(values, step, after=()):
        return swap(behind(values, after), "cols", col_count, step)

    def by_chip(values, chip, after=()):
        return swap(behind(values, after), "rows", row_count, chip * CORES)

    def by_core(values, after=()):
        return swap(behind(values, after), "rows", row_count, 1)

    parts, halves, near, far, chip_sums, hiddens, others, rows_in, partials, sent = ({} for _ in range(10))
    last = [token]

    def forward(plane, values, after=()):
        parts[plane] = [values]
        for step in range(1, per_plane):
            parts[plane].append(by_row_of_plane(values, step, after))

    def multiply_in(plane, far_parts=1, hint=HURRY, after=()):
        parts_after = last + list(after)
        *halves[plane], last[0] = gate_up(parts[plane], gate_kept, up_kept, chips, far_parts, hint, parts_after)

    def exchange(plane, after=()):
        far[plane] = [by_core(part, after) for part in halves[plane][2:]]

    def exchange_near(plane, after=()):
        near[plane] = by_core(halves[plane][1], after)

    def multiply_out(plane, pieces=1, after=()):
        *partials[plane], last[0] = down(hiddens[plane], others[plane], down_kept, pieces, last + list(after))

    def send_rows(plane, after=(), pieces=1, piece=0):
        mine_and_others = partials[plane][piece::pieces]
        rows_in[plane, piece] = mine_and_others[:1]
        for step in range(1, per_plane):
            rows_in[plane, piece].append(by_row_of_plane(mine_and_others[step], step, after))

    def to_chips(plane, after=()):
        given = [halves[plane][0], *far[plane]]
        sent[plane], _, _, last[0] = sums(given, [], [], last + list(after))

    def send_chips(plane, after=()):
        chip_sums[plane] = [by_chip(part, number + 1, after) for number, part in enumerate(sent[plane])]

    def to_hidden(plane, after=()):
        given = [halves[plane][0], near[plane], *chip_sums[plane]]
        _, hiddens[plane], _, last[0] = sums([], given, [], last + list(after))
        others[plane] = by_core(hiddens[plane])

    def to_rows(*parts, after=(), hint=0.0):
        _, _, (summed,), last[0] = sums([], [], [parts], last + list(after), hint)
        return summed

    next_stacks = [by_plane(first, NEXT), by_plane(second, NEXT)]
    across_stacks = [by_plane(first, ACROSS), by_plane(second, ACROSS)]
    row_stacks = {
        step: [by_row_of_plane(first, step), by_row_of_plane(second, step)] for step in range(1, per_plane)
    }
    up_kept, last[0] = masked(
        up_weight, up_mask, tile_of(features, 256), place, 1, lambda core: 0, last + next_stacks[:1], 0.15
    )
    last[0] = waited([*last, across_stacks[0], *(stacks[0] for stacks in row_stacks.values())], 0.07)
    one_away, last[0] = join(next_stacks, last)
    inner_three, last[0] = join(across_stacks, last)
    outer_three = by_plane(mine, AROUND, last)
    down_kept = []

    def keep_down(share, hint=0.0):
        part, last[0] = masked(
            down_weight, down_mask, 2 * BLOCK, place, 2 * CORES, lambda core: 2 * core + share, last, hint
        )
        down_kept.append(part)

    parts[0] = [mine]
    for stacks in row_stacks.values():
        part, last[0] = join(stacks, last)
        parts[0].append(part)
    forward(1, one_away, last)
    multiply_in(0, hint=HURRY)
    exchange(0)
    exchange_near(0)
    keep_down(0)
    three_away, passed, last[0] = pick(side, inner_three, outer_three, mine, last)
    two_away = by_plane(passed, CYCLE)
    to_chips(0, [near[0]])
    forward(3, three_away, [*parts[1][1:], *last])
    multiply_in(1)
    exchange(1)
    exchange_near(1)
    to_chips(1, [near[1]])
    send_chips(1)
    keep_down(1)
    forward(2, two_away, last)
    multiply_in(3, after=[two_away])
    exchange(3)
    exchange_near(3)
    to_hidden(1)
    to_chips(3, [near[3]])
    send_chips(3)
    multiply_out(1)
    send_rows(1, parts[2][1:])
    multiply_in(2, far_parts=2)
    exchange(2)
    to_hidden(3)
    to_chips(2)
    send_chips(2)
    exchange_near(2, last)
    multiply_out(3, pieces=CORES)
    send_rows(3, rows_in[1, 0][1:], CORES, 1)
    one = to_rows(*rows_in[1, 0])
    one_out = by_plane(one, NEXT)
    three = to_rows(*rows_in[3, 1])
    send_rows(3, [three], CORES, 0)
    three_out, two_out = {1: by_plane(three, NEXT)}, {}
    to_hidden(2)
    send_chips(0, chip_sums[2])
    multiply_out(2, pieces=CORES)
    three = to_rows(*rows_in[3, 0], after=[one_out])
    three_out[0] = by_plane(three, NEXT)
    send_rows(2, [three], CORES, 1)
    two = to_rows(*rows_in[2, 1], three_out[1])
    two_out[1] = by_plane(two, SECOND)
    send_rows(2, [two], CORES, 0)
    to_hidden(0)
    multiply_out(0)
    two = to_rows(rows_in[2, 0][0], three_out[0], hint=0.5)
    two = to_rows(two, *rows_in[2, 0][1:])
    two_out[0] = by_plane(two, SECOND)
    send_rows(0, rows_in[2, 0][1:])

    joined = to_rows(two_out[1], one_out, hint=10.0)

    def total(piece, *parts):
        whole = [part[piece].astype(F32) for part in rows_in[0, 0]] + [part.astype(F32) for part in parts]
        return sum(whole[1:], whole[0]).astype(BF16)

    mine_now, other = total(0, one_out[0], two_out[0][0]), by_core(total(1, joined[0]))
    left = jnp.where(core == 0, mine_now, other)
    right = jnp.where(core == 0, other, mine_now)
    return jnp.concatenate([left, right], 1)


def solution(mesh):
    return jax.shard_map(
        functools.partial(body, mesh.shape["rows"], mesh.shape["cols"]),
        mesh=mesh,
        in_specs=(
            P(("rows", "cols"), None),
            P(),
            P("rows", "cols"),
            P("rows", "cols"),
            P("cols", None),
            P("rows", "cols"),
            P("rows", "cols"),
            P("cols", None),
        ),
        out_specs=P(("rows", "cols"), None),
        check_vma=False,
    )
```

```python
import functools

import jax
import jax.numpy as jnp
from jax import lax
from jax.experimental import pallas as pl
from jax.experimental.pallas import tpu as pltpu
from jax.sharding import PartitionSpec as P

BLOCK = 64
CORES = 2
PLANES = 4
NEXT = ((0, 1), (1, 0), (2, 3), (3, 2))
SECOND = ((0, 2), (2, 0), (1, 3), (3, 1))
ACROSS = ((1, 2), (2, 1))
AROUND = ((0, 3), (3, 0))
CYCLE = ((0, 2), (2, 3), (3, 1), (1, 0))
VMEM = 12 * 1024 * 1024
F32 = jnp.float32
BF16 = jnp.bfloat16


def tile_of(size, most):
    tile = most
    while size % tile:
        tile //= 2
    return tile


def rms_normed(rows_in, norm_gain):
    values = rows_in.astype(F32)
    meansq = jnp.mean(values * values, axis=-1, keepdims=True)
    return (values * lax.rsqrt(meansq + 1e-05) * norm_gain).astype(BF16)


HURRY = 1000


def cost(flops, moved):
    return pl.CostEstimate(flops=flops // HURRY, bytes_accessed=moved // HURRY, transcendentals=0)


def as_if(microseconds):
    return cost(int(HURRY * 1.15e9 * microseconds), 0)


ANYWHERE = pl.BlockSpec(memory_space=pl.ANY)
TOKEN = jax.ShapeDtypeStruct((8, 128), F32)
INSIDE = pl.BlockSpec(memory_space=pltpu.VMEM)


def mask_kernel(share, rows, after_count, core_ref, weight_ref, mask_ref, *refs):
    kept_ref, token_ref, spread, semaphores = refs[after_count:]
    token_ref[...] = jnp.zeros_like(token_ref)
    depth, width = kept_ref.shape
    number = share(core_ref[0])
    columns = pl.ds(pl.multiple_of(number * width, width), width)
    copies = [
        pltpu.make_async_copy(
            weight_ref.at[pl.ds(step * rows, rows), columns], kept_ref.at[pl.ds(step * rows, rows)], semaphores.at[step]
        )
        for step in range(depth // rows)
    ]
    for copy in copies:
        copy.start()
    marks = mask_ref.shape[1]
    owner = lax.broadcasted_iota(jnp.int32, (marks, width), 1) // BLOCK + number * (width // BLOCK)
    chosen = (owner == lax.broadcasted_iota(jnp.int32, (marks, width), 0)).astype(F32)
    spread[...] = jnp.dot(mask_ref[...].astype(F32), chosen, preferred_element_type=F32)
    for step, copy in enumerate(copies):
        copy.wait()
        for block in range(step * rows // BLOCK, (step + 1) * rows // BLOCK):
            part = pl.ds(block * BLOCK, BLOCK)
            keep = jnp.broadcast_to(spread[pl.ds(block, 1), :], (BLOCK, width))
            kept_ref[part, :] = kept_ref[part, :] * keep.astype(BF16)


def masked(weight, mask, rows, core, shares, share, after, hint=0.0):
    depth, width = weight.shape
    width = width // shares
    return pl.pallas_call(
        functools.partial(mask_kernel, share, rows, len(after)),
        in_specs=[pl.BlockSpec(memory_space=pltpu.SMEM), ANYWHERE, INSIDE] + [ANYWHERE] * len(after),
        out_specs=[INSIDE] * 2,
        out_shape=[jax.ShapeDtypeStruct((depth, width), weight.dtype), TOKEN],
        scratch_shapes=[pltpu.VMEM((mask.shape[0], width), F32), pltpu.SemaphoreType.DMA((depth // rows,))],
        compiler_params=pltpu.CompilerParams(vmem_limit_bytes=VMEM),
        cost_estimate=as_if(hint),
        name="masked",
    )(core, pltpu.with_memory_space_constraint(weight, pltpu.HBM), mask, *after)


def stack_kernel(after_count, *refs):
    block_refs, (stacked_ref, token_ref) = refs[: -2 - after_count], refs[-2:]
    token_ref[...] = jnp.zeros_like(token_ref)
    for number, block_ref in enumerate(block_refs):
        stacked_ref[number // stacked_ref.shape[1], number % stacked_ref.shape[1]] = block_ref[...]


def join_kernel(after_count, *refs):
    stacked_refs, (joined_ref, token_ref) = refs[: -2 - after_count], refs[-2:]
    token_ref[...] = jnp.zeros_like(token_ref)
    blocks = [ref[core, chip] for core in range(CORES) for ref in stacked_refs for chip in range(ref.shape[1])]
    joined_ref[...] = jnp.concatenate([block.astype(F32) for block in blocks], 0).astype(BF16)


def rearranged(kernel, name, shape, blocks, after, hint=0.0):
    return pl.pallas_call(
        functools.partial(kernel, len(after)),
        in_specs=[INSIDE] * len(blocks) + [ANYWHERE] * len(after),
        out_specs=[INSIDE] * 2,
        out_shape=[jax.ShapeDtypeStruct(shape, BF16), TOKEN],
        compiler_params=pltpu.CompilerParams(vmem_limit_bytes=VMEM // 2),
        cost_estimate=as_if(hint),
        name=name,
    )(*blocks, *after)


def wait_kernel(*refs):
    refs[-1][...] = jnp.zeros_like(refs[-1])


def waited(after, hint):
    return pl.pallas_call(
        wait_kernel,
        in_specs=[ANYWHERE] * len(after),
        out_specs=INSIDE,
        out_shape=TOKEN,
        compiler_params=pltpu.CompilerParams(vmem_limit_bytes=VMEM // 2),
        cost_estimate=as_if(hint),
        name="waited",
    )(*after)


def stack(blocks, after):
    shape = (CORES, len(blocks) // CORES, *blocks[0].shape)
    return rearranged(stack_kernel, "stack", shape, blocks, after)


def join(stacks, after, hint=0.0):
    rows = sum(part.shape[1] for part in stacks) * CORES * stacks[0].shape[2]
    return rearranged(join_kernel, "join", (rows, stacks[0].shape[3]), stacks, after, hint)


def pick_kernel(after_count, side_ref, inner_three_ref, outer_three_ref, mine_ref, *refs):
    three_ref, passed_ref, token_ref = refs[after_count:]
    token_ref[...] = jnp.zeros_like(token_ref)

    @pl.when(side_ref[0] == 1)
    def _():
        three_ref[...] = inner_three_ref[...]
        passed_ref[...] = inner_three_ref[...]

    @pl.when(side_ref[0] == 0)
    def _():
        three_ref[...] = outer_three_ref[...]
        passed_ref[...] = mine_ref[...]


def pick(side, inner_three, outer_three, mine, after):
    return pl.pallas_call(
        functools.partial(pick_kernel, len(after)),
        in_specs=[pl.BlockSpec(memory_space=pltpu.SMEM)] + [INSIDE] * 3 + [ANYWHERE] * len(after),
        out_specs=[INSIDE] * 3,
        out_shape=[jax.ShapeDtypeStruct(mine.shape, BF16)] * 2 + [TOKEN],
        compiler_params=pltpu.CompilerParams(vmem_limit_bytes=VMEM // 2),
        cost_estimate=as_if(8),
        name="pick",
    )(side, inner_three, outer_three, mine, *after)


def resident(values):
    return pltpu.with_memory_space_constraint(values, pltpu.VMEM)


def gate_up_kernel(part_count, after_count, *refs):
    parts, (gate_ref, up_ref) = refs[:part_count], refs[part_count : part_count + 2]
    keep_ref, near_ref, *far_refs, token_ref, all_rows = refs[part_count + 2 + after_count :]
    far_places = [(far_ref, which) for far_ref in far_refs for which in range(far_ref.shape[0])]
    token_ref[...] = jnp.zeros_like(token_ref)
    half = parts[0].shape[0] // 2
    kept = half * len(parts)
    for place, part in enumerate(parts):
        all_rows[pl.ds(place * half, half), :] = part[:half, :]
        all_rows[pl.ds(kept + place * half, half), :] = part[half:, :]
    tile = tile_of(gate_ref.shape[1], 256)

    @pl.loop(0, gate_ref.shape[1] // tile)
    def _(number):
        columns = pl.ds(pl.multiple_of(number * tile, tile), tile)
        for which, weight_ref in enumerate((gate_ref, up_ref)):
            total = jnp.dot(all_rows[...], weight_ref[:, columns], preferred_element_type=F32)
            total = total.reshape(2, *keep_ref.shape[1:4], tile).astype(BF16)
            keep_ref[which, :, :, :, columns] = total[0]
            near_ref[which, :, :, columns] = total[1, :, 0]
            far_ref, place = far_places[which]
            far_ref[place, :, :, :, columns] = total[1, :, 1:]


def gate_up(parts, gate_kept, up_kept, chips, far_parts, hint, after):
    rows = sum(part.shape[0] for part in parts)
    depth, width = gate_kept.shape
    groups, own = len(parts), rows // (2 * len(parts) * chips)
    shapes = [(2, groups, chips, own, width), (2, groups, own, width)]
    shapes += [(2 // far_parts, groups, chips - 1, own, width)] * far_parts
    return pl.pallas_call(
        functools.partial(gate_up_kernel, len(parts), len(after)),
        in_specs=[INSIDE] * (len(parts) + 2) + [ANYWHERE] * len(after),
        out_specs=[INSIDE] * (len(shapes) + 1),
        out_shape=[jax.ShapeDtypeStruct(shape, BF16) for shape in shapes] + [TOKEN],
        scratch_shapes=[pltpu.VMEM((rows, depth), BF16)],
        compiler_params=pltpu.CompilerParams(vmem_limit_bytes=VMEM // 2),
        cost_estimate=cost(hint * 4 * rows * depth * width, 0),
        name="gate_up",
    )(*parts, resident(gate_kept), resident(up_kept), *after)


def down_kernel(pieces, weight_count, after_count, own_ref, other_ref, *refs):
    weight_refs, refs = refs[:weight_count], refs[weight_count:]
    *partial_refs, token_ref, both = refs[after_count:]
    token_ref[...] = jnp.zeros_like(token_ref)
    groups, own, depth = own_ref.shape
    rows = groups * own
    both[:rows, :] = own_ref[...].astype(F32).reshape(rows, depth).astype(BF16)
    both[rows:, :] = other_ref[...].astype(F32).reshape(rows, depth).astype(BF16)
    for number, weight_ref in enumerate(weight_refs):
        width = weight_ref.shape[1]
        down_columns(pieces, both, weight_ref, partial_refs, number * width, tile_of(width, 512))


def down_columns(pieces, both, weight_ref, partial_refs, first, tile):
    own = partial_refs[0].shape[1]

    @pl.loop(0, weight_ref.shape[1] // tile)
    def _(number):
        start = pl.multiple_of(number * tile, tile)
        total = jnp.dot(both[...], weight_ref[:, pl.ds(start, tile)], preferred_element_type=F32)
        total = total.reshape(pieces, CORES // pieces, len(partial_refs) // pieces, own, tile)
        columns = pl.ds(pl.multiple_of(first + start, tile), tile)
        for place, partial_ref in enumerate(partial_refs):
            partial_ref[:, :, columns] = total[place % pieces, :, place // pieces].astype(BF16)


def down(own, other, down_kept, pieces, after):
    groups, rows, depth = own.shape
    width = sum(weight.shape[1] for weight in down_kept)
    shape = (CORES // pieces, rows, width)
    return pl.pallas_call(
        functools.partial(down_kernel, pieces, len(down_kept), len(after)),
        in_specs=[INSIDE] * (2 + len(down_kept)) + [ANYWHERE] * len(after),
        out_specs=[INSIDE] * (groups * pieces + 1),
        out_shape=[jax.ShapeDtypeStruct(shape, BF16)] * (groups * pieces) + [TOKEN],
        scratch_shapes=[pltpu.VMEM((CORES * groups * rows, depth), BF16)],
        compiler_params=pltpu.CompilerParams(vmem_limit_bytes=VMEM // 2),
        cost_estimate=cost(2 * CORES * groups * rows * depth * width, 0),
        name="down",
    )(own, other, *(resident(weight) for weight in down_kept), *after)


def sums_kernel(sizes, after_count, *refs):
    to_chips, to_hidden, *to_rows = sizes
    refs = list(refs)
    refs.pop()[...] = jnp.zeros(TOKEN.shape, F32)
    ins = [[refs.pop(0) for _ in range(size)] for size in sizes]
    del refs[:after_count]

    if to_chips:
        keep_ref, *came_refs = ins[0]
        came_places = [came_ref.at[which] for came_ref in came_refs for which in range(came_ref.shape[0])]
        for chip in range(1, keep_ref.shape[2]):
            sent_ref = refs.pop(0)
            for which in range(2):
                for group in range(keep_ref.shape[1]):
                    came = came_places[which][group, chip - 1].astype(F32)
                    sent_ref[which, group] = (keep_ref[which, group, chip].astype(F32) + came).astype(BF16)
    if to_hidden:
        keep_ref, came_ref, *chip_refs = ins[1]
        hidden_ref = refs.pop(0)
        for group in range(keep_ref.shape[1]):
            both = []
            for which in range(2):
                total = keep_ref[which, group, 0].astype(F32) + came_ref[which, group].astype(F32)
                for chip_ref in chip_refs:
                    total = total + chip_ref[which, group].astype(F32)
                both.append(total)
            hidden_ref[group] = (jax.nn.silu(both[0]) * both[1]).astype(BF16)
    for part_refs in ins[2:]:
        summed_ref = refs.pop(0)
        cores = summed_ref.shape[0]
        for core in range(cores):
            total = part_refs[0][core].astype(F32)
            for part_ref in part_refs[1:]:
                total = total + part_ref[part_ref.shape[0] - cores + core].astype(F32)
            summed_ref[core] = total.astype(BF16)


def sums(to_chips, to_hidden, to_rows, after, hint=0.0):
    shapes = []
    if to_chips:
        two, groups, chips, own, width = to_chips[0].shape
        shapes += [(two, groups, own, width)] * (chips - 1)
    if to_hidden:
        shapes.append((to_hidden[0].shape[1], *to_hidden[0].shape[3:]))
    shapes += [parts[0].shape for parts in to_rows]
    given = [to_chips, to_hidden, *to_rows]
    sizes = tuple(len(parts) for parts in given)
    given = [part for parts in given for part in parts]
    results = list(pl.pallas_call(
        functools.partial(sums_kernel, sizes, len(after)),
        in_specs=[INSIDE] * len(given) + [ANYWHERE] * len(after),
        out_specs=[INSIDE] * (len(shapes) + 1),
        out_shape=[jax.ShapeDtypeStruct(shape, BF16) for shape in shapes] + [TOKEN],
        compiler_params=pltpu.CompilerParams(vmem_limit_bytes=VMEM // 2),
        cost_estimate=as_if(hint),
        name="sums",
    )(*given, *after))
    token = results.pop()
    sent = [results.pop(0) for _ in range(chips - 1)] if to_chips else []
    hidden = results.pop(0) if to_hidden else None
    return sent, hidden, results, token


def swap(values, axis, size, step):
    return lax.ppermute(values, axis, [(place, place ^ step) for place in range(size)])


def body(row_count, col_count, tokens, norm_gain, gate_weight, up_weight, down_weight, gate_mask, up_mask, down_mask):
    chips = row_count // CORES
    per_plane = col_count // PLANES
    features, width = gate_weight.shape
    row = lax.axis_index("rows")
    core = row % CORES
    inner = (lax.axis_index("cols") // per_plane) % (PLANES - 1) != 0
    place = jnp.reshape(core, (1,)).astype(jnp.int32)
    side = jnp.reshape(inner, (1,)).astype(jnp.int32)

    normed = rms_normed(tokens, norm_gain)
    def block(step):
        return lax.dynamic_slice_in_dim(normed, (row ^ step) * features, features, 1)

    from_core = swap(jnp.stack([block(chip * CORES + 1) for chip in range(chips)]), "rows", row_count, 1)
    to_chips_rows = [stack([block(chip * CORES), from_core[chip]], [])[0] for chip in range(1, chips)]
    first, token = stack([block(0), from_core[0]], [*to_chips_rows[:1], side])
    gate_kept, token = masked(gate_weight, gate_mask, tile_of(features, 256), place, 1, lambda core: 0, [token])
    second = [swap(part, "rows", row_count, (chip + 1) * CORES) for chip, part in enumerate(to_chips_rows)]
    second = jnp.concatenate(second, 1) if len(second) > 1 else second[0]
    mine, token = join([first, second], [token])

    def behind(values, after):
        return lax.optimization_barrier((values, *after))[0] if after else values

    def by_plane(values, planes, after=()):
        pairs = [(a * per_plane + b, c * per_plane + b) for a, c in planes for b in range(per_plane)]
        return lax.ppermute(behind(values, after), "cols", pairs)

    def by_row_of_plane(values, step, after=()):
        return swap(behind(values, after), "cols", col_count, step)

    def by_chip(values, chip, after=()):
        return swap(behind(values, after), "rows", row_count, chip * CORES)

    def by_core(values, after=()):
        return swap(behind(values, after), "rows", row_count, 1)

    parts, halves, near, far, chip_sums, hiddens, others, rows_in, partials, sent = ({} for _ in range(10))
    last = [token]

    def forward(plane, values, after=()):
        parts[plane] = [values]
        for step in range(1, per_plane):
            parts[plane].append(by_row_of_plane(values, step, after))

    def multiply_in(plane, far_parts=1, hint=HURRY, after=()):
        parts_after = last + list(after)
        *halves[plane], last[0] = gate_up(parts[plane], gate_kept, up_kept, chips, far_parts, hint, parts_after)

    def exchange(plane, after=()):
        far[plane] = [by_core(part, after) for part in halves[plane][2:]]

    def exchange_near(plane, after=()):
        near[plane] = by_core(halves[plane][1], after)

    def multiply_out(plane, pieces=1, after=()):
        *partials[plane], last[0] = down(hiddens[plane], others[plane], down_kept, pieces, last + list(after))

    def send_rows(plane, after=(), pieces=1, piece=0):
        mine_and_others = partials[plane][piece::pieces]
        rows_in[plane, piece] = mine_and_others[:1]
        for step in range(1, per_plane):
            rows_in[plane, piece].append(by_row_of_plane(mine_and_others[step], step, after))

    def to_chips(plane, after=()):
        given = [halves[plane][0], *far[plane]]
        sent[plane], _, _, last[0] = sums(given, [], [], last + list(after))

    def send_chips(plane, after=()):
        chip_sums[plane] = [by_chip(part, number + 1, after) for number, part in enumerate(sent[plane])]

    def to_hidden(plane, after=()):
        given = [halves[plane][0], near[plane], *chip_sums[plane]]
        _, hiddens[plane], _, last[0] = sums([], given, [], last + list(after))
        others[plane] = by_core(hiddens[plane])

    def to_rows(*parts, after=(), hint=0.0):
        _, _, (summed,), last[0] = sums([], [], [parts], last + list(after), hint)
        return summed

    next_stacks = [by_plane(first, NEXT), by_plane(second, NEXT)]
    across_stacks = [by_plane(first, ACROSS), by_plane(second, ACROSS)]
    row_stacks = {
        step: [by_row_of_plane(first, step), by_row_of_plane(second, step)] for step in range(1, per_plane)
    }
    up_kept, last[0] = masked(
        up_weight, up_mask, tile_of(features, 256), place, 1, lambda core: 0, last + next_stacks[:1], 0.15
    )
    last[0] = waited([*last, across_stacks[0], *(stacks[0] for stacks in row_stacks.values())], 0.07)
    one_away, last[0] = join(next_stacks, last)
    inner_three, last[0] = join(across_stacks, last)
    outer_three = by_plane(mine, AROUND, last)
    down_kept = []

    def keep_down(share, hint=0.0):
        part, last[0] = masked(
            down_weight, down_mask, 2 * BLOCK, place, 2 * CORES, lambda core: 2 * core + share, last, hint
        )
        down_kept.append(part)

    parts[0] = [mine]
    for stacks in row_stacks.values():
        part, last[0] = join(stacks, last)
        parts[0].append(part)
    forward(1, one_away, last)
    multiply_in(0, hint=HURRY)
    exchange(0)
    exchange_near(0)
    keep_down(0)
    three_away, passed, last[0] = pick(side, inner_three, outer_three, mine, last)
    two_away = by_plane(passed, CYCLE)
    to_chips(0, [near[0]])
    forward(3, three_away, [*parts[1][1:], *last])
    multiply_in(1)
    exchange(1)
    exchange_near(1)
    to_chips(1, [near[1]])
    send_chips(1)
    keep_down(1)
    forward(2, two_away, last)
    multiply_in(3, after=[two_away])
    exchange(3)
    exchange_near(3)
    to_hidden(1)
    to_chips(3, [near[3]])
    send_chips(3)
    multiply_out(1)
    send_rows(1, parts[2][1:])
    multiply_in(2, far_parts=2)
    exchange(2)
    to_hidden(3)
    to_chips(2)
    send_chips(2)
    exchange_near(2, last)
    multiply_out(3, pieces=CORES)
    send_rows(3, rows_in[1, 0][1:], CORES, 1)
    one = to_rows(*rows_in[1, 0])
    one_out = by_plane(one, NEXT)
    three = to_rows(*rows_in[3, 1])
    send_rows(3, [three], CORES, 0)
    three_out, two_out = {1: by_plane(three, NEXT)}, {}
    to_hidden(2)
    send_chips(0, chip_sums[2])
    multiply_out(2, pieces=CORES)
    three = to_rows(*rows_in[3, 0], after=[one_out])
    three_out[0] = by_plane(three, NEXT)
    send_rows(2, rows_in[3, 0][1:], CORES, 1)
    two = to_rows(*rows_in[2, 1], three_out[1])
    two_out[1] = by_plane(two, SECOND)
    send_rows(2, [two], CORES, 0)
    to_hidden(0)
    multiply_out(0)
    two = to_rows(rows_in[2, 0][0], three_out[0], hint=0.1)
    two = to_rows(two, *rows_in[2, 0][1:])
    two_out[0] = by_plane(two, SECOND)
    send_rows(0, rows_in[2, 0][1:])

    joined = to_rows(two_out[1], one_out, hint=10.0)

    def total(piece, *parts):
        whole = [part[piece].astype(F32) for part in rows_in[0, 0]] + [part.astype(F32) for part in parts]
        return sum(whole[1:], whole[0]).astype(BF16)

    mine_now, other = total(0, one_out[0], two_out[0][0]), by_core(total(1, joined[0]))
    left = jnp.where(core == 0, mine_now, other)
    right = jnp.where(core == 0, other, mine_now)
    return jnp.concatenate([left, right], 1)


def solution(mesh):
    return jax.shard_map(
        functools.partial(body, mesh.shape["rows"], mesh.shape["cols"]),
        mesh=mesh,
        in_specs=(
            P(("rows", "cols"), None),
            P(),
            P("rows", "cols"),
            P("rows", "cols"),
            P("cols", None),
            P("rows", "cols"),
            P("rows", "cols"),
            P("cols", None),
        ),
        out_specs=P(("rows", "cols"), None),
        check_vma=False,
    )
```

```python
import functools

import jax
import jax.numpy as jnp
from jax import lax
from jax.experimental import pallas as pl
from jax.experimental.pallas import tpu as pltpu
from jax.sharding import PartitionSpec as P

BLOCK = 64
CORES = 2
PLANES = 4
NEXT = ((0, 1), (1, 0), (2, 3), (3, 2))
SECOND = ((0, 2), (2, 0), (1, 3), (3, 1))
ACROSS = ((1, 2), (2, 1))
AROUND = ((0, 3), (3, 0))
CYCLE = ((0, 2), (2, 3), (3, 1), (1, 0))
VMEM = 12 * 1024 * 1024
F32 = jnp.float32
BF16 = jnp.bfloat16


def tile_of(size, most):
    tile = most
    while size % tile:
        tile //= 2
    return tile


HURRY = 1000


def cost(flops, moved):
    return pl.CostEstimate(flops=flops // HURRY, bytes_accessed=moved // HURRY, transcendentals=0)


def as_if(microseconds):
    return cost(int(HURRY * 1.15e9 * microseconds), 0)


ANYWHERE = pl.BlockSpec(memory_space=pl.ANY)
TOKEN = jax.ShapeDtypeStruct((8, 128), F32)
INSIDE = pl.BlockSpec(memory_space=pltpu.VMEM)


def norm_kernel(rows_hbm, gain_hbm, normed_ref, rows_ref, gain_ref, semaphores):
    copies = [
        pltpu.make_async_copy(rows_hbm, rows_ref, semaphores.at[0]),
        pltpu.make_async_copy(gain_hbm, gain_ref, semaphores.at[1]),
    ]
    for copy in copies:
        copy.start()
    for copy in copies:
        copy.wait()
    values = rows_ref[...].astype(F32)
    meansq = jnp.mean(values * values, axis=-1, keepdims=True)
    normed_ref[...] = (values * lax.rsqrt(meansq + 1e-05) * gain_ref[...][None, :]).astype(BF16)


def rms_normed(rows_in, norm_gain):
    return pl.pallas_call(
        norm_kernel,
        in_specs=[ANYWHERE] * 2,
        out_specs=INSIDE,
        out_shape=jax.ShapeDtypeStruct(rows_in.shape, BF16),
        scratch_shapes=[
            pltpu.VMEM(rows_in.shape, rows_in.dtype),
            pltpu.VMEM(norm_gain.shape, norm_gain.dtype),
            pltpu.SemaphoreType.DMA((2,)),
        ],
        compiler_params=pltpu.CompilerParams(vmem_limit_bytes=VMEM),
        cost_estimate=as_if(0),
        name="normed",
    )(*(pltpu.with_memory_space_constraint(values, pltpu.HBM) for values in (rows_in, norm_gain)))


def mask_kernel(share, rows, after_count, core_ref, weight_ref, mask_ref, *refs):
    kept_ref, token_ref, spread, semaphores = refs[after_count:]
    token_ref[...] = jnp.zeros_like(token_ref)
    depth, width = kept_ref.shape
    number = share(core_ref[0])
    columns = pl.ds(pl.multiple_of(number * width, width), width)
    copies = [
        pltpu.make_async_copy(
            weight_ref.at[pl.ds(step * rows, rows), columns], kept_ref.at[pl.ds(step * rows, rows)], semaphores.at[step]
        )
        for step in range(depth // rows)
    ]
    for copy in copies:
        copy.start()
    marks = mask_ref.shape[1]
    owner = lax.broadcasted_iota(jnp.int32, (marks, width), 1) // BLOCK + number * (width // BLOCK)
    chosen = (owner == lax.broadcasted_iota(jnp.int32, (marks, width), 0)).astype(F32)
    spread[...] = jnp.dot(mask_ref[...].astype(F32), chosen, preferred_element_type=F32)
    for step, copy in enumerate(copies):
        copy.wait()
        for block in range(step * rows // BLOCK, (step + 1) * rows // BLOCK):
            part = pl.ds(block * BLOCK, BLOCK)
            keep = jnp.broadcast_to(spread[pl.ds(block, 1), :], (BLOCK, width))
            kept_ref[part, :] = kept_ref[part, :] * keep.astype(BF16)


def masked(weight, mask, rows, core, shares, share, after, hint=0.0):
    depth, width = weight.shape
    width = width // shares
    return pl.pallas_call(
        functools.partial(mask_kernel, share, rows, len(after)),
        in_specs=[pl.BlockSpec(memory_space=pltpu.SMEM), ANYWHERE, INSIDE] + [ANYWHERE] * len(after),
        out_specs=[INSIDE] * 2,
        out_shape=[jax.ShapeDtypeStruct((depth, width), weight.dtype), TOKEN],
        scratch_shapes=[pltpu.VMEM((mask.shape[0], width), F32), pltpu.SemaphoreType.DMA((depth // rows,))],
        compiler_params=pltpu.CompilerParams(vmem_limit_bytes=VMEM),
        cost_estimate=as_if(hint),
        name="masked",
    )(core, pltpu.with_memory_space_constraint(weight, pltpu.HBM), mask, *after)


def stack_kernel(after_count, *refs):
    block_refs, (stacked_ref, token_ref) = refs[: -2 - after_count], refs[-2:]
    token_ref[...] = jnp.zeros_like(token_ref)
    for number, block_ref in enumerate(block_refs):
        stacked_ref[number // stacked_ref.shape[1], number % stacked_ref.shape[1]] = block_ref[...]


def join_kernel(after_count, *refs):
    stacked_refs, (joined_ref, token_ref) = refs[: -2 - after_count], refs[-2:]
    token_ref[...] = jnp.zeros_like(token_ref)
    blocks = [ref[core, chip] for core in range(CORES) for ref in stacked_refs for chip in range(ref.shape[1])]
    joined_ref[...] = jnp.concatenate([block.astype(F32) for block in blocks], 0).astype(BF16)


def rearranged(kernel, name, shape, blocks, after, hint=0.0):
    return pl.pallas_call(
        functools.partial(kernel, len(after)),
        in_specs=[INSIDE] * len(blocks) + [ANYWHERE] * len(after),
        out_specs=[INSIDE] * 2,
        out_shape=[jax.ShapeDtypeStruct(shape, BF16), TOKEN],
        compiler_params=pltpu.CompilerParams(vmem_limit_bytes=VMEM // 2),
        cost_estimate=as_if(hint),
        name=name,
    )(*blocks, *after)


def wait_kernel(*refs):
    refs[-1][...] = jnp.zeros_like(refs[-1])


def waited(after, hint):
    return pl.pallas_call(
        wait_kernel,
        in_specs=[ANYWHERE] * len(after),
        out_specs=INSIDE,
        out_shape=TOKEN,
        compiler_params=pltpu.CompilerParams(vmem_limit_bytes=VMEM // 2),
        cost_estimate=as_if(hint),
        name="waited",
    )(*after)


def stack(blocks, after):
    shape = (CORES, len(blocks) // CORES, *blocks[0].shape)
    return rearranged(stack_kernel, "stack", shape, blocks, after)


def join(stacks, after, hint=0.0):
    rows = sum(part.shape[1] for part in stacks) * CORES * stacks[0].shape[2]
    return rearranged(join_kernel, "join", (rows, stacks[0].shape[3]), stacks, after, hint)


def pick_kernel(after_count, side_ref, inner_three_ref, outer_three_ref, mine_ref, *refs):
    three_ref, passed_ref, token_ref = refs[after_count:]
    token_ref[...] = jnp.zeros_like(token_ref)

    @pl.when(side_ref[0] == 1)
    def _():
        three_ref[...] = inner_three_ref[...]
        passed_ref[...] = inner_three_ref[...]

    @pl.when(side_ref[0] == 0)
    def _():
        three_ref[...] = outer_three_ref[...]
        passed_ref[...] = mine_ref[...]


def pick(side, inner_three, outer_three, mine, after):
    return pl.pallas_call(
        functools.partial(pick_kernel, len(after)),
        in_specs=[pl.BlockSpec(memory_space=pltpu.SMEM)] + [INSIDE] * 3 + [ANYWHERE] * len(after),
        out_specs=[INSIDE] * 3,
        out_shape=[jax.ShapeDtypeStruct(mine.shape, BF16)] * 2 + [TOKEN],
        compiler_params=pltpu.CompilerParams(vmem_limit_bytes=VMEM // 2),
        cost_estimate=as_if(8),
        name="pick",
    )(side, inner_three, outer_three, mine, *after)


def resident(values):
    return pltpu.with_memory_space_constraint(values, pltpu.VMEM)


def gate_up_kernel(part_count, after_count, *refs):
    parts, (gate_ref, up_ref) = refs[:part_count], refs[part_count : part_count + 2]
    keep_ref, near_ref, *far_refs, token_ref, all_rows = refs[part_count + 2 + after_count :]
    far_places = [(far_ref, which) for far_ref in far_refs for which in range(far_ref.shape[0])]
    token_ref[...] = jnp.zeros_like(token_ref)
    half = parts[0].shape[0] // 2
    kept = half * len(parts)
    for place, part in enumerate(parts):
        all_rows[pl.ds(place * half, half), :] = part[:half, :]
        all_rows[pl.ds(kept + place * half, half), :] = part[half:, :]
    tile = tile_of(gate_ref.shape[1], 256)

    @pl.loop(0, gate_ref.shape[1] // tile)
    def _(number):
        columns = pl.ds(pl.multiple_of(number * tile, tile), tile)
        for which, weight_ref in enumerate((gate_ref, up_ref)):
            total = jnp.dot(all_rows[...], weight_ref[:, columns], preferred_element_type=F32)
            total = total.reshape(2, *keep_ref.shape[1:4], tile).astype(BF16)
            keep_ref[which, :, :, :, columns] = total[0]
            near_ref[which, :, :, columns] = total[1, :, 0]
            far_ref, place = far_places[which]
            far_ref[place, :, :, :, columns] = total[1, :, 1:]


def gate_up(parts, gate_kept, up_kept, chips, far_parts, hint, after):
    rows = sum(part.shape[0] for part in parts)
    depth, width = gate_kept.shape
    groups, own = len(parts), rows // (2 * len(parts) * chips)
    shapes = [(2, groups, chips, own, width), (2, groups, own, width)]
    shapes += [(2 // far_parts, groups, chips - 1, own, width)] * far_parts
    return pl.pallas_call(
        functools.partial(gate_up_kernel, len(parts), len(after)),
        in_specs=[INSIDE] * (len(parts) + 2) + [ANYWHERE] * len(after),
        out_specs=[INSIDE] * (len(shapes) + 1),
        out_shape=[jax.ShapeDtypeStruct(shape, BF16) for shape in shapes] + [TOKEN],
        scratch_shapes=[pltpu.VMEM((rows, depth), BF16)],
        compiler_params=pltpu.CompilerParams(vmem_limit_bytes=VMEM // 2),
        cost_estimate=cost(hint * 4 * rows * depth * width, 0),
        name="gate_up",
    )(*parts, resident(gate_kept), resident(up_kept), *after)


def down_kernel(pieces, weight_count, after_count, own_ref, other_ref, *refs):
    weight_refs, refs = refs[:weight_count], refs[weight_count:]
    *partial_refs, token_ref, both = refs[after_count:]
    token_ref[...] = jnp.zeros_like(token_ref)
    groups, own, depth = own_ref.shape
    rows = groups * own
    both[:rows, :] = own_ref[...].astype(F32).reshape(rows, depth).astype(BF16)
    both[rows:, :] = other_ref[...].astype(F32).reshape(rows, depth).astype(BF16)
    for number, weight_ref in enumerate(weight_refs):
        width = weight_ref.shape[1]
        down_columns(pieces, both, weight_ref, partial_refs, number * width, tile_of(width, 512))


def down_columns(pieces, both, weight_ref, partial_refs, first, tile):
    own = partial_refs[0].shape[1]

    @pl.loop(0, weight_ref.shape[1] // tile)
    def _(number):
        start = pl.multiple_of(number * tile, tile)
        total = jnp.dot(both[...], weight_ref[:, pl.ds(start, tile)], preferred_element_type=F32)
        total = total.reshape(pieces, CORES // pieces, len(partial_refs) // pieces, own, tile)
        columns = pl.ds(pl.multiple_of(first + start, tile), tile)
        for place, partial_ref in enumerate(partial_refs):
            partial_ref[:, :, columns] = total[place % pieces, :, place // pieces].astype(BF16)


def down(own, other, down_kept, pieces, after):
    groups, rows, depth = own.shape
    width = sum(weight.shape[1] for weight in down_kept)
    shape = (CORES // pieces, rows, width)
    return pl.pallas_call(
        functools.partial(down_kernel, pieces, len(down_kept), len(after)),
        in_specs=[INSIDE] * (2 + len(down_kept)) + [ANYWHERE] * len(after),
        out_specs=[INSIDE] * (groups * pieces + 1),
        out_shape=[jax.ShapeDtypeStruct(shape, BF16)] * (groups * pieces) + [TOKEN],
        scratch_shapes=[pltpu.VMEM((CORES * groups * rows, depth), BF16)],
        compiler_params=pltpu.CompilerParams(vmem_limit_bytes=VMEM // 2),
        cost_estimate=cost(2 * CORES * groups * rows * depth * width, 0),
        name="down",
    )(own, other, *(resident(weight) for weight in down_kept), *after)


def sums_kernel(sizes, after_count, *refs):
    to_chips, to_hidden, *to_rows = sizes
    refs = list(refs)
    refs.pop()[...] = jnp.zeros(TOKEN.shape, F32)
    ins = [[refs.pop(0) for _ in range(size)] for size in sizes]
    del refs[:after_count]

    if to_chips:
        keep_ref, *came_refs = ins[0]
        came_places = [came_ref.at[which] for came_ref in came_refs for which in range(came_ref.shape[0])]
        for chip in range(1, keep_ref.shape[2]):
            sent_ref = refs.pop(0)
            for which in range(2):
                for group in range(keep_ref.shape[1]):
                    came = came_places[which][group, chip - 1].astype(F32)
                    sent_ref[which, group] = (keep_ref[which, group, chip].astype(F32) + came).astype(BF16)
    if to_hidden:
        keep_ref, came_ref, *chip_refs = ins[1]
        hidden_ref = refs.pop(0)
        for group in range(keep_ref.shape[1]):
            both = []
            for which in range(2):
                total = keep_ref[which, group, 0].astype(F32) + came_ref[which, group].astype(F32)
                for chip_ref in chip_refs:
                    total = total + chip_ref[which, group].astype(F32)
                both.append(total)
            hidden_ref[group] = (jax.nn.silu(both[0]) * both[1]).astype(BF16)
    for part_refs in ins[2:]:
        summed_ref = refs.pop(0)
        cores = summed_ref.shape[0]
        for core in range(cores):
            total = part_refs[0][core].astype(F32)
            for part_ref in part_refs[1:]:
                total = total + part_ref[part_ref.shape[0] - cores + core].astype(F32)
            summed_ref[core] = total.astype(BF16)


def sums(to_chips, to_hidden, to_rows, after, hint=0.0):
    shapes = []
    if to_chips:
        two, groups, chips, own, width = to_chips[0].shape
        shapes += [(two, groups, own, width)] * (chips - 1)
    if to_hidden:
        shapes.append((to_hidden[0].shape[1], *to_hidden[0].shape[3:]))
    shapes += [parts[0].shape for parts in to_rows]
    given = [to_chips, to_hidden, *to_rows]
    sizes = tuple(len(parts) for parts in given)
    given = [part for parts in given for part in parts]
    results = list(pl.pallas_call(
        functools.partial(sums_kernel, sizes, len(after)),
        in_specs=[INSIDE] * len(given) + [ANYWHERE] * len(after),
        out_specs=[INSIDE] * (len(shapes) + 1),
        out_shape=[jax.ShapeDtypeStruct(shape, BF16) for shape in shapes] + [TOKEN],
        compiler_params=pltpu.CompilerParams(vmem_limit_bytes=VMEM // 2),
        cost_estimate=as_if(hint),
        name="sums",
    )(*given, *after))
    token = results.pop()
    sent = [results.pop(0) for _ in range(chips - 1)] if to_chips else []
    hidden = results.pop(0) if to_hidden else None
    return sent, hidden, results, token


def swap(values, axis, size, step):
    return lax.ppermute(values, axis, [(place, place ^ step) for place in range(size)])


def body(row_count, col_count, tokens, norm_gain, gate_weight, up_weight, down_weight, gate_mask, up_mask, down_mask):
    chips = row_count // CORES
    per_plane = col_count // PLANES
    features, width = gate_weight.shape
    row = lax.axis_index("rows")
    core = row % CORES
    inner = (lax.axis_index("cols") // per_plane) % (PLANES - 1) != 0
    place = jnp.reshape(core, (1,)).astype(jnp.int32)
    side = jnp.reshape(inner, (1,)).astype(jnp.int32)

    normed = rms_normed(tokens, norm_gain)
    def block(step):
        return lax.dynamic_slice_in_dim(normed, (row ^ step) * features, features, 1)

    from_core = swap(jnp.stack([block(chip * CORES + 1) for chip in range(chips)]), "rows", row_count, 1)
    to_chips_rows = [stack([block(chip * CORES), from_core[chip]], [])[0] for chip in range(1, chips)]
    first, token = stack([block(0), from_core[0]], [*to_chips_rows[:1], side])
    gate_kept, token = masked(gate_weight, gate_mask, tile_of(features, 256), place, 1, lambda core: 0, [token])
    second = [swap(part, "rows", row_count, (chip + 1) * CORES) for chip, part in enumerate(to_chips_rows)]
    second = jnp.concatenate(second, 1) if len(second) > 1 else second[0]
    mine, token = join([first, second], [token])

    def behind(values, after):
        return lax.optimization_barrier((values, *after))[0] if after else values

    def by_plane(values, planes, after=()):
        pairs = [(a * per_plane + b, c * per_plane + b) for a, c in planes for b in range(per_plane)]
        return lax.ppermute(behind(values, after), "cols", pairs)

    def by_row_of_plane(values, step, after=()):
        return swap(behind(values, after), "cols", col_count, step)

    def by_chip(values, chip, after=()):
        return swap(behind(values, after), "rows", row_count, chip * CORES)

    def by_core(values, after=()):
        return swap(behind(values, after), "rows", row_count, 1)

    parts, halves, near, far, chip_sums, hiddens, others, rows_in, partials, sent = ({} for _ in range(10))
    last = [token]

    def forward(plane, values, after=()):
        parts[plane] = [values]
        for step in range(1, per_plane):
            parts[plane].append(by_row_of_plane(values, step, after))

    def multiply_in(plane, far_parts=1, hint=HURRY, after=()):
        parts_after = last + list(after)
        *halves[plane], last[0] = gate_up(parts[plane], gate_kept, up_kept, chips, far_parts, hint, parts_after)

    def exchange(plane, after=()):
        far[plane] = [by_core(part, after) for part in halves[plane][2:]]

    def exchange_near(plane, after=()):
        near[plane] = by_core(halves[plane][1], after)

    def multiply_out(plane, pieces=1, after=()):
        *partials[plane], last[0] = down(hiddens[plane], others[plane], down_kept, pieces, last + list(after))

    def send_rows(plane, after=(), pieces=1, piece=0):
        mine_and_others = partials[plane][piece::pieces]
        rows_in[plane, piece] = mine_and_others[:1]
        for step in range(1, per_plane):
            rows_in[plane, piece].append(by_row_of_plane(mine_and_others[step], step, after))

    def to_chips(plane, after=()):
        given = [halves[plane][0], *far[plane]]
        sent[plane], _, _, last[0] = sums(given, [], [], last + list(after))

    def send_chips(plane, after=()):
        chip_sums[plane] = [by_chip(part, number + 1, after) for number, part in enumerate(sent[plane])]

    def to_hidden(plane, after=()):
        given = [halves[plane][0], near[plane], *chip_sums[plane]]
        _, hiddens[plane], _, last[0] = sums([], given, [], last + list(after))
        others[plane] = by_core(hiddens[plane])

    def to_rows(*parts, after=(), hint=0.0):
        _, _, (summed,), last[0] = sums([], [], [parts], last + list(after), hint)
        return summed

    next_stacks = [by_plane(first, NEXT), by_plane(second, NEXT)]
    across_stacks = [by_plane(first, ACROSS), by_plane(second, ACROSS)]
    row_stacks = {
        step: [by_row_of_plane(first, step), by_row_of_plane(second, step)] for step in range(1, per_plane)
    }
    up_kept, last[0] = masked(
        up_weight, up_mask, tile_of(features, 256), place, 1, lambda core: 0, last + next_stacks[:1], 0.15
    )
    last[0] = waited([*last, across_stacks[0], *(stacks[0] for stacks in row_stacks.values())], 0.07)
    one_away, last[0] = join(next_stacks, last)
    inner_three, last[0] = join(across_stacks, last)
    outer_three = by_plane(mine, AROUND, last)
    down_kept = []

    def keep_down(share, hint=0.0):
        part, last[0] = masked(
            down_weight, down_mask, 2 * BLOCK, place, 2 * CORES, lambda core: 2 * core + share, last, hint
        )
        down_kept.append(part)

    parts[0] = [mine]
    for stacks in row_stacks.values():
        part, last[0] = join(stacks, last)
        parts[0].append(part)
    forward(1, one_away, last)
    multiply_in(0, hint=HURRY)
    exchange(0)
    exchange_near(0)
    keep_down(0)
    three_away, passed, last[0] = pick(side, inner_three, outer_three, mine, last)
    two_away = by_plane(passed, CYCLE)
    to_chips(0, [near[0]])
    forward(3, three_away, [*parts[1][1:], *last])
    multiply_in(1)
    exchange(1)
    exchange_near(1)
    to_chips(1, [near[1]])
    send_chips(1)
    keep_down(1)
    forward(2, two_away, last)
    multiply_in(3, after=[two_away])
    exchange(3)
    exchange_near(3)
    to_hidden(1)
    to_chips(3, [near[3]])
    send_chips(3)
    multiply_out(1)
    send_rows(1, parts[2][1:])
    multiply_in(2, far_parts=2)
    exchange(2)
    to_hidden(3)
    to_chips(2)
    send_chips(2)
    exchange_near(2, last)
    multiply_out(3, pieces=CORES)
    send_rows(3, rows_in[1, 0][1:], CORES, 1)
    one = to_rows(*rows_in[1, 0])
    one_out = by_plane(one, NEXT)
    three = to_rows(*rows_in[3, 1])
    send_rows(3, [three], CORES, 0)
    three_out, two_out = {1: by_plane(three, NEXT)}, {}
    to_hidden(2)
    send_chips(0, chip_sums[2])
    multiply_out(2, pieces=CORES)
    three = to_rows(*rows_in[3, 0], after=[one_out])
    three_out[0] = by_plane(three, NEXT)
    send_rows(2, rows_in[3, 0][1:], CORES, 1)
    two = to_rows(*rows_in[2, 1], three_out[1])
    two_out[1] = by_plane(two, SECOND)
    send_rows(2, [two], CORES, 0)
    to_hidden(0)
    multiply_out(0)
    two = to_rows(rows_in[2, 0][0], three_out[0], hint=0.1)
    two = to_rows(two, *rows_in[2, 0][1:])
    two_out[0] = by_plane(two, SECOND)
    send_rows(0, rows_in[2, 0][1:])

    joined = to_rows(two_out[1], one_out, hint=10.0)

    def total(piece, *parts):
        whole = [part[piece].astype(F32) for part in rows_in[0, 0]] + [part.astype(F32) for part in parts]
        return sum(whole[1:], whole[0]).astype(BF16)

    mine_now, other = total(0, one_out[0], two_out[0][0]), by_core(total(1, joined[0]))
    left = jnp.where(core == 0, mine_now, other)
    right = jnp.where(core == 0, other, mine_now)
    return jnp.concatenate([left, right], 1)


def solution(mesh):
    return jax.shard_map(
        functools.partial(body, mesh.shape["rows"], mesh.shape["cols"]),
        mesh=mesh,
        in_specs=(
            P(("rows", "cols"), None),
            P(),
            P("rows", "cols"),
            P("rows", "cols"),
            P("cols", None),
            P("rows", "cols"),
            P("rows", "cols"),
            P("cols", None),
        ),
        out_specs=P(("rows", "cols"), None),
        check_vma=False,
    )
```

```python
import functools

import jax
import jax.numpy as jnp
from jax import lax
from jax.experimental import pallas as pl
from jax.experimental.pallas import tpu as pltpu
from jax.sharding import PartitionSpec as P

BLOCK = 64
CORES = 2
PLANES = 4
NEXT = ((0, 1), (1, 0), (2, 3), (3, 2))
SECOND = ((0, 2), (2, 0), (1, 3), (3, 1))
ACROSS = ((1, 2), (2, 1))
AROUND = ((0, 3), (3, 0))
CYCLE = ((0, 2), (2, 3), (3, 1), (1, 0))
VMEM = 12 * 1024 * 1024
F32 = jnp.float32
BF16 = jnp.bfloat16


def tile_of(size, most):
    tile = most
    while size % tile:
        tile //= 2
    return tile


HURRY = 1000


def cost(flops, moved):
    return pl.CostEstimate(flops=flops // HURRY, bytes_accessed=moved // HURRY, transcendentals=0)


def as_if(microseconds):
    return cost(int(HURRY * 1.15e9 * microseconds), 0)


ANYWHERE = pl.BlockSpec(memory_space=pl.ANY)
TOKEN = jax.ShapeDtypeStruct((8, 128), F32)
INSIDE = pl.BlockSpec(memory_space=pltpu.VMEM)


def norm_kernel(rows_hbm, gain_hbm, normed_ref, rows_ref, gain_ref, semaphores):
    copies = [
        pltpu.make_async_copy(rows_hbm, rows_ref, semaphores.at[0]),
        pltpu.make_async_copy(gain_hbm, gain_ref, semaphores.at[1]),
    ]
    for copy in copies:
        copy.start()
    for copy in copies:
        copy.wait()
    values = rows_ref[...].astype(F32)
    meansq = jnp.mean(values * values, axis=-1, keepdims=True)
    normed_ref[...] = (values * lax.rsqrt(meansq + 1e-05) * gain_ref[...][None, :]).astype(BF16)


def rms_normed(rows_in, norm_gain):
    return pl.pallas_call(
        norm_kernel,
        in_specs=[ANYWHERE] * 2,
        out_specs=INSIDE,
        out_shape=jax.ShapeDtypeStruct(rows_in.shape, BF16),
        scratch_shapes=[
            pltpu.VMEM(rows_in.shape, rows_in.dtype),
            pltpu.VMEM(norm_gain.shape, norm_gain.dtype),
            pltpu.SemaphoreType.DMA((2,)),
        ],
        compiler_params=pltpu.CompilerParams(vmem_limit_bytes=VMEM),
        cost_estimate=as_if(0),
        name="normed",
    )(*(pltpu.with_memory_space_constraint(values, pltpu.HBM) for values in (rows_in, norm_gain)))


def mask_kernel(share, rows, after_count, core_ref, weight_ref, mask_hbm, *refs):
    kept_ref, token_ref, spread, mask_ref, mask_semaphore, semaphores = refs[after_count:]
    mask_copy = pltpu.make_async_copy(mask_hbm, mask_ref, mask_semaphore)
    mask_copy.start()
    token_ref[...] = jnp.zeros_like(token_ref)
    depth, width = kept_ref.shape
    number = share(core_ref[0])
    columns = pl.ds(pl.multiple_of(number * width, width), width)
    copies = [
        pltpu.make_async_copy(
            weight_ref.at[pl.ds(step * rows, rows), columns], kept_ref.at[pl.ds(step * rows, rows)], semaphores.at[step]
        )
        for step in range(depth // rows)
    ]
    for copy in copies:
        copy.start()
    mask_copy.wait()
    marks = mask_ref.shape[1]
    owner = lax.broadcasted_iota(jnp.int32, (marks, width), 1) // BLOCK + number * (width // BLOCK)
    chosen = (owner == lax.broadcasted_iota(jnp.int32, (marks, width), 0)).astype(F32)
    spread[...] = jnp.dot(mask_ref[...].astype(F32), chosen, preferred_element_type=F32)
    for step, copy in enumerate(copies):
        copy.wait()
        for block in range(step * rows // BLOCK, (step + 1) * rows // BLOCK):
            part = pl.ds(block * BLOCK, BLOCK)
            keep = jnp.broadcast_to(spread[pl.ds(block, 1), :], (BLOCK, width))
            kept_ref[part, :] = kept_ref[part, :] * keep.astype(BF16)


def masked(weight, mask, rows, core, shares, share, after, hint=0.0):
    depth, width = weight.shape
    width = width // shares
    return pl.pallas_call(
        functools.partial(mask_kernel, share, rows, len(after)),
        in_specs=[pl.BlockSpec(memory_space=pltpu.SMEM)] + [ANYWHERE] * (2 + len(after)),
        out_specs=[INSIDE] * 2,
        out_shape=[jax.ShapeDtypeStruct((depth, width), weight.dtype), TOKEN],
        scratch_shapes=[
            pltpu.VMEM((mask.shape[0], width), F32),
            pltpu.VMEM(mask.shape, mask.dtype),
            pltpu.SemaphoreType.DMA,
            pltpu.SemaphoreType.DMA((depth // rows,)),
        ],
        compiler_params=pltpu.CompilerParams(vmem_limit_bytes=VMEM),
        cost_estimate=as_if(hint),
        name="masked",
    )(core, *(pltpu.with_memory_space_constraint(values, pltpu.HBM) for values in (weight, mask)), *after)


def stack_kernel(after_count, *refs):
    block_refs, (stacked_ref, token_ref) = refs[: -2 - after_count], refs[-2:]
    token_ref[...] = jnp.zeros_like(token_ref)
    for number, block_ref in enumerate(block_refs):
        stacked_ref[number // stacked_ref.shape[1], number % stacked_ref.shape[1]] = block_ref[...]


def join_kernel(after_count, *refs):
    stacked_refs, (joined_ref, token_ref) = refs[: -2 - after_count], refs[-2:]
    token_ref[...] = jnp.zeros_like(token_ref)
    blocks = [ref[core, chip] for core in range(CORES) for ref in stacked_refs for chip in range(ref.shape[1])]
    joined_ref[...] = jnp.concatenate([block.astype(F32) for block in blocks], 0).astype(BF16)


def rearranged(kernel, name, shape, blocks, after, hint=0.0):
    return pl.pallas_call(
        functools.partial(kernel, len(after)),
        in_specs=[INSIDE] * len(blocks) + [ANYWHERE] * len(after),
        out_specs=[INSIDE] * 2,
        out_shape=[jax.ShapeDtypeStruct(shape, BF16), TOKEN],
        compiler_params=pltpu.CompilerParams(vmem_limit_bytes=VMEM // 2),
        cost_estimate=as_if(hint),
        name=name,
    )(*blocks, *after)


def wait_kernel(*refs):
    refs[-1][...] = jnp.zeros_like(refs[-1])


def waited(after, hint):
    return pl.pallas_call(
        wait_kernel,
        in_specs=[ANYWHERE] * len(after),
        out_specs=INSIDE,
        out_shape=TOKEN,
        compiler_params=pltpu.CompilerParams(vmem_limit_bytes=VMEM // 2),
        cost_estimate=as_if(hint),
        name="waited",
    )(*after)


def stack(blocks, after):
    shape = (CORES, len(blocks) // CORES, *blocks[0].shape)
    return rearranged(stack_kernel, "stack", shape, blocks, after)


def join(stacks, after, hint=0.0):
    rows = sum(part.shape[1] for part in stacks) * CORES * stacks[0].shape[2]
    return rearranged(join_kernel, "join", (rows, stacks[0].shape[3]), stacks, after, hint)


def pick_kernel(after_count, side_ref, inner_three_ref, outer_three_ref, mine_ref, *refs):
    three_ref, passed_ref, token_ref = refs[after_count:]
    token_ref[...] = jnp.zeros_like(token_ref)

    @pl.when(side_ref[0] == 1)
    def _():
        three_ref[...] = inner_three_ref[...]
        passed_ref[...] = inner_three_ref[...]

    @pl.when(side_ref[0] == 0)
    def _():
        three_ref[...] = outer_three_ref[...]
        passed_ref[...] = mine_ref[...]


def pick(side, inner_three, outer_three, mine, after):
    return pl.pallas_call(
        functools.partial(pick_kernel, len(after)),
        in_specs=[pl.BlockSpec(memory_space=pltpu.SMEM)] + [INSIDE] * 3 + [ANYWHERE] * len(after),
        out_specs=[INSIDE] * 3,
        out_shape=[jax.ShapeDtypeStruct(mine.shape, BF16)] * 2 + [TOKEN],
        compiler_params=pltpu.CompilerParams(vmem_limit_bytes=VMEM // 2),
        cost_estimate=as_if(8),
        name="pick",
    )(side, inner_three, outer_three, mine, *after)


def resident(values):
    return pltpu.with_memory_space_constraint(values, pltpu.VMEM)


def gate_up_kernel(part_count, after_count, *refs):
    parts, (gate_ref, up_ref) = refs[:part_count], refs[part_count : part_count + 2]
    keep_ref, near_ref, *far_refs, token_ref, all_rows = refs[part_count + 2 + after_count :]
    far_places = [(far_ref, which) for far_ref in far_refs for which in range(far_ref.shape[0])]
    token_ref[...] = jnp.zeros_like(token_ref)
    half = parts[0].shape[0] // 2
    kept = half * len(parts)
    for place, part in enumerate(parts):
        all_rows[pl.ds(place * half, half), :] = part[:half, :]
        all_rows[pl.ds(kept + place * half, half), :] = part[half:, :]
    tile = tile_of(gate_ref.shape[1], 256)

    @pl.loop(0, gate_ref.shape[1] // tile)
    def _(number):
        columns = pl.ds(pl.multiple_of(number * tile, tile), tile)
        for which, weight_ref in enumerate((gate_ref, up_ref)):
            total = jnp.dot(all_rows[...], weight_ref[:, columns], preferred_element_type=F32)
            total = total.reshape(2, *keep_ref.shape[1:4], tile).astype(BF16)
            keep_ref[which, :, :, :, columns] = total[0]
            near_ref[which, :, :, columns] = total[1, :, 0]
            far_ref, place = far_places[which]
            far_ref[place, :, :, :, columns] = total[1, :, 1:]


def gate_up(parts, gate_kept, up_kept, chips, far_parts, hint, after):
    rows = sum(part.shape[0] for part in parts)
    depth, width = gate_kept.shape
    groups, own = len(parts), rows // (2 * len(parts) * chips)
    shapes = [(2, groups, chips, own, width), (2, groups, own, width)]
    shapes += [(2 // far_parts, groups, chips - 1, own, width)] * far_parts
    return pl.pallas_call(
        functools.partial(gate_up_kernel, len(parts), len(after)),
        in_specs=[INSIDE] * (len(parts) + 2) + [ANYWHERE] * len(after),
        out_specs=[INSIDE] * (len(shapes) + 1),
        out_shape=[jax.ShapeDtypeStruct(shape, BF16) for shape in shapes] + [TOKEN],
        scratch_shapes=[pltpu.VMEM((rows, depth), BF16)],
        compiler_params=pltpu.CompilerParams(vmem_limit_bytes=VMEM // 2),
        cost_estimate=cost(hint * 4 * rows * depth * width, 0),
        name="gate_up",
    )(*parts, resident(gate_kept), resident(up_kept), *after)


def down_kernel(pieces, weight_count, after_count, own_ref, other_ref, *refs):
    weight_refs, refs = refs[:weight_count], refs[weight_count:]
    *partial_refs, token_ref, both = refs[after_count:]
    token_ref[...] = jnp.zeros_like(token_ref)
    groups, own, depth = own_ref.shape
    rows = groups * own
    both[:rows, :] = own_ref[...].astype(F32).reshape(rows, depth).astype(BF16)
    both[rows:, :] = other_ref[...].astype(F32).reshape(rows, depth).astype(BF16)
    for number, weight_ref in enumerate(weight_refs):
        width = weight_ref.shape[1]
        down_columns(pieces, both, weight_ref, partial_refs, number * width, tile_of(width, 512))


def down_columns(pieces, both, weight_ref, partial_refs, first, tile):
    own = partial_refs[0].shape[1]

    @pl.loop(0, weight_ref.shape[1] // tile)
    def _(number):
        start = pl.multiple_of(number * tile, tile)
        total = jnp.dot(both[...], weight_ref[:, pl.ds(start, tile)], preferred_element_type=F32)
        total = total.reshape(pieces, CORES // pieces, len(partial_refs) // pieces, own, tile)
        columns = pl.ds(pl.multiple_of(first + start, tile), tile)
        for place, partial_ref in enumerate(partial_refs):
            partial_ref[:, :, columns] = total[place % pieces, :, place // pieces].astype(BF16)


def down(own, other, down_kept, pieces, after):
    groups, rows, depth = own.shape
    width = sum(weight.shape[1] for weight in down_kept)
    shape = (CORES // pieces, rows, width)
    return pl.pallas_call(
        functools.partial(down_kernel, pieces, len(down_kept), len(after)),
        in_specs=[INSIDE] * (2 + len(down_kept)) + [ANYWHERE] * len(after),
        out_specs=[INSIDE] * (groups * pieces + 1),
        out_shape=[jax.ShapeDtypeStruct(shape, BF16)] * (groups * pieces) + [TOKEN],
        scratch_shapes=[pltpu.VMEM((CORES * groups * rows, depth), BF16)],
        compiler_params=pltpu.CompilerParams(vmem_limit_bytes=VMEM // 2),
        cost_estimate=cost(2 * CORES * groups * rows * depth * width, 0),
        name="down",
    )(own, other, *(resident(weight) for weight in down_kept), *after)


def sums_kernel(sizes, after_count, *refs):
    to_chips, to_hidden, *to_rows = sizes
    refs = list(refs)
    refs.pop()[...] = jnp.zeros(TOKEN.shape, F32)
    ins = [[refs.pop(0) for _ in range(size)] for size in sizes]
    del refs[:after_count]

    if to_chips:
        keep_ref, *came_refs = ins[0]
        came_places = [came_ref.at[which] for came_ref in came_refs for which in range(came_ref.shape[0])]
        for chip in range(1, keep_ref.shape[2]):
            sent_ref = refs.pop(0)
            for which in range(2):
                for group in range(keep_ref.shape[1]):
                    came = came_places[which][group, chip - 1].astype(F32)
                    sent_ref[which, group] = (keep_ref[which, group, chip].astype(F32) + came).astype(BF16)
    if to_hidden:
        keep_ref, came_ref, *chip_refs = ins[1]
        hidden_ref = refs.pop(0)
        for group in range(keep_ref.shape[1]):
            both = []
            for which in range(2):
                total = keep_ref[which, group, 0].astype(F32) + came_ref[which, group].astype(F32)
                for chip_ref in chip_refs:
                    total = total + chip_ref[which, group].astype(F32)
                both.append(total)
            hidden_ref[group] = (jax.nn.silu(both[0]) * both[1]).astype(BF16)
    for part_refs in ins[2:]:
        summed_ref = refs.pop(0)
        cores = summed_ref.shape[0]
        for core in range(cores):
            total = part_refs[0][core].astype(F32)
            for part_ref in part_refs[1:]:
                total = total + part_ref[part_ref.shape[0] - cores + core].astype(F32)
            summed_ref[core] = total.astype(BF16)


def sums(to_chips, to_hidden, to_rows, after, hint=0.0):
    shapes = []
    if to_chips:
        two, groups, chips, own, width = to_chips[0].shape
        shapes += [(two, groups, own, width)] * (chips - 1)
    if to_hidden:
        shapes.append((to_hidden[0].shape[1], *to_hidden[0].shape[3:]))
    shapes += [parts[0].shape for parts in to_rows]
    given = [to_chips, to_hidden, *to_rows]
    sizes = tuple(len(parts) for parts in given)
    given = [part for parts in given for part in parts]
    results = list(pl.pallas_call(
        functools.partial(sums_kernel, sizes, len(after)),
        in_specs=[INSIDE] * len(given) + [ANYWHERE] * len(after),
        out_specs=[INSIDE] * (len(shapes) + 1),
        out_shape=[jax.ShapeDtypeStruct(shape, BF16) for shape in shapes] + [TOKEN],
        compiler_params=pltpu.CompilerParams(vmem_limit_bytes=VMEM // 2),
        cost_estimate=as_if(hint),
        name="sums",
    )(*given, *after))
    token = results.pop()
    sent = [results.pop(0) for _ in range(chips - 1)] if to_chips else []
    hidden = results.pop(0) if to_hidden else None
    return sent, hidden, results, token


def swap(values, axis, size, step):
    return lax.ppermute(values, axis, [(place, place ^ step) for place in range(size)])


def body(row_count, col_count, tokens, norm_gain, gate_weight, up_weight, down_weight, gate_mask, up_mask, down_mask):
    chips = row_count // CORES
    per_plane = col_count // PLANES
    features, width = gate_weight.shape
    row = lax.axis_index("rows")
    core = row % CORES
    inner = (lax.axis_index("cols") // per_plane) % (PLANES - 1) != 0
    place = jnp.reshape(core, (1,)).astype(jnp.int32)
    side = jnp.reshape(inner, (1,)).astype(jnp.int32)

    normed = rms_normed(tokens, norm_gain)
    def block(step):
        return lax.dynamic_slice_in_dim(normed, (row ^ step) * features, features, 1)

    from_core = swap(jnp.stack([block(chip * CORES + 1) for chip in range(chips)]), "rows", row_count, 1)
    to_chips_rows = [stack([block(chip * CORES), from_core[chip]], [])[0] for chip in range(1, chips)]
    first, token = stack([block(0), from_core[0]], [*to_chips_rows[:1], side])
    gate_kept, token = masked(gate_weight, gate_mask, tile_of(features, 256), place, 1, lambda core: 0, [token])
    second = [swap(part, "rows", row_count, (chip + 1) * CORES) for chip, part in enumerate(to_chips_rows)]
    second = jnp.concatenate(second, 1) if len(second) > 1 else second[0]
    mine, token = join([first, second], [token])

    def behind(values, after):
        return lax.optimization_barrier((values, *after))[0] if after else values

    def by_plane(values, planes, after=()):
        pairs = [(a * per_plane + b, c * per_plane + b) for a, c in planes for b in range(per_plane)]
        return lax.ppermute(behind(values, after), "cols", pairs)

    def by_row_of_plane(values, step, after=()):
        return swap(behind(values, after), "cols", col_count, step)

    def by_chip(values, chip, after=()):
        return swap(behind(values, after), "rows", row_count, chip * CORES)

    def by_core(values, after=()):
        return swap(behind(values, after), "rows", row_count, 1)

    parts, halves, near, far, chip_sums, hiddens, others, rows_in, partials, sent = ({} for _ in range(10))
    last = [token]

    def forward(plane, values, after=()):
        parts[plane] = [values]
        for step in range(1, per_plane):
            parts[plane].append(by_row_of_plane(values, step, after))

    def multiply_in(plane, far_parts=1, hint=HURRY, after=()):
        parts_after = last + list(after)
        *halves[plane], last[0] = gate_up(parts[plane], gate_kept, up_kept, chips, far_parts, hint, parts_after)

    def exchange(plane, after=()):
        far[plane] = [by_core(part, after) for part in halves[plane][2:]]

    def exchange_near(plane, after=()):
        near[plane] = by_core(halves[plane][1], after)

    def multiply_out(plane, pieces=1, after=()):
        *partials[plane], last[0] = down(hiddens[plane], others[plane], down_kept, pieces, last + list(after))

    def send_rows(plane, after=(), pieces=1, piece=0):
        mine_and_others = partials[plane][piece::pieces]
        rows_in[plane, piece] = mine_and_others[:1]
        for step in range(1, per_plane):
            rows_in[plane, piece].append(by_row_of_plane(mine_and_others[step], step, after))

    def to_chips(plane, after=()):
        given = [halves[plane][0], *far[plane]]
        sent[plane], _, _, last[0] = sums(given, [], [], last + list(after))

    def send_chips(plane, after=()):
        chip_sums[plane] = [by_chip(part, number + 1, after) for number, part in enumerate(sent[plane])]

    def to_hidden(plane, after=()):
        given = [halves[plane][0], near[plane], *chip_sums[plane]]
        _, hiddens[plane], _, last[0] = sums([], given, [], last + list(after))
        others[plane] = by_core(hiddens[plane])

    def to_rows(*parts, after=(), hint=0.0):
        _, _, (summed,), last[0] = sums([], [], [parts], last + list(after), hint)
        return summed

    next_stacks = [by_plane(first, NEXT), by_plane(second, NEXT)]
    across_stacks = [by_plane(first, ACROSS), by_plane(second, ACROSS)]
    row_stacks = {
        step: [by_row_of_plane(first, step), by_row_of_plane(second, step)] for step in range(1, per_plane)
    }
    last[0] = waited(last + next_stacks[:1], 0.15)
    last[0] = waited([*last, across_stacks[0], *(stacks[0] for stacks in row_stacks.values())], 0.07)
    one_away, last[0] = join(next_stacks, last)
    inner_three, last[0] = join(across_stacks, last)
    outer_three = by_plane(mine, AROUND, last)
    down_kept = []

    def keep_down(share, hint=0.0):
        part, last[0] = masked(
            down_weight, down_mask, 2 * BLOCK, place, 2 * CORES, lambda core: 2 * core + share, last, hint
        )
        down_kept.append(part)

    parts[0] = [mine]
    for stacks in row_stacks.values():
        part, last[0] = join(stacks, last)
        parts[0].append(part)
    forward(1, one_away, last)
    up_kept, last[0] = masked(up_weight, up_mask, tile_of(features, 256), place, 1, lambda core: 0, last)
    multiply_in(0, hint=HURRY)
    exchange(0)
    exchange_near(0)
    keep_down(0)
    three_away, passed, last[0] = pick(side, inner_three, outer_three, mine, last)
    two_away = by_plane(passed, CYCLE)
    to_chips(0, [near[0]])
    forward(3, three_away, [*parts[1][1:], *last])
    multiply_in(1)
    exchange(1)
    exchange_near(1)
    to_chips(1, [near[1]])
    send_chips(1)
    keep_down(1)
    forward(2, two_away, last)
    multiply_in(3, after=[two_away])
    exchange(3)
    exchange_near(3)
    to_hidden(1)
    to_chips(3, [near[3]])
    send_chips(3)
    multiply_out(1)
    send_rows(1, parts[2][1:])
    multiply_in(2, far_parts=2)
    exchange(2)
    to_hidden(3)
    to_chips(2)
    send_chips(2)
    exchange_near(2, last)
    multiply_out(3, pieces=CORES)
    send_rows(3, rows_in[1, 0][1:], CORES, 1)
    one = to_rows(*rows_in[1, 0])
    one_out = by_plane(one, NEXT)
    three = to_rows(*rows_in[3, 1])
    send_rows(3, [three], CORES, 0)
    three_out, two_out = {1: by_plane(three, NEXT)}, {}
    to_hidden(2)
    send_chips(0, chip_sums[2])
    multiply_out(2, pieces=CORES)
    three = to_rows(*rows_in[3, 0], after=[one_out])
    three_out[0] = by_plane(three, NEXT)
    send_rows(2, rows_in[3, 0][1:], CORES, 1)
    two = to_rows(*rows_in[2, 1], three_out[1])
    two_out[1] = by_plane(two, SECOND)
    send_rows(2, [two], CORES, 0)
    to_hidden(0)
    multiply_out(0)
    two = to_rows(rows_in[2, 0][0], three_out[0], hint=0.1)
    two = to_rows(two, *rows_in[2, 0][1:])
    two_out[0] = by_plane(two, SECOND)
    send_rows(0, rows_in[2, 0][1:])

    joined = to_rows(two_out[1], one_out, hint=10.0)

    def total(piece, *parts):
        whole = [part[piece].astype(F32) for part in rows_in[0, 0]] + [part.astype(F32) for part in parts]
        return sum(whole[1:], whole[0]).astype(BF16)

    mine_now, other = total(0, one_out[0], two_out[0][0]), by_core(total(1, joined[0]))
    left = jnp.where(core == 0, mine_now, other)
    right = jnp.where(core == 0, other, mine_now)
    return jnp.concatenate([left, right], 1)


def solution(mesh):
    return jax.shard_map(
        functools.partial(body, mesh.shape["rows"], mesh.shape["cols"]),
        mesh=mesh,
        in_specs=(
            P(("rows", "cols"), None),
            P(),
            P("rows", "cols"),
            P("rows", "cols"),
            P("cols", None),
            P("rows", "cols"),
            P("rows", "cols"),
            P("cols", None),
        ),
        out_specs=P(("rows", "cols"), None),
        check_vma=False,
    )
```

```python
import functools

import jax
import jax.numpy as jnp
from jax import lax
from jax.experimental import pallas as pl
from jax.experimental.pallas import tpu as pltpu
from jax.sharding import PartitionSpec as P

BLOCK = 64
CORES = 2
PLANES = 4
NEXT = ((0, 1), (1, 0), (2, 3), (3, 2))
SECOND = ((0, 2), (2, 0), (1, 3), (3, 1))
ACROSS = ((1, 2), (2, 1))
AROUND = ((0, 3), (3, 0))
CYCLE = ((0, 2), (2, 3), (3, 1), (1, 0))
VMEM = 12 * 1024 * 1024
F32 = jnp.float32
BF16 = jnp.bfloat16


def tile_of(size, most):
    tile = most
    while size % tile:
        tile //= 2
    return tile


HURRY = 1000


def cost(flops, moved):
    return pl.CostEstimate(flops=flops // HURRY, bytes_accessed=moved // HURRY, transcendentals=0)


def as_if(microseconds):
    return cost(int(HURRY * 1.15e9 * microseconds), 0)


ANYWHERE = pl.BlockSpec(memory_space=pl.ANY)
TOKEN = jax.ShapeDtypeStruct((8, 128), F32)
INSIDE = pl.BlockSpec(memory_space=pltpu.VMEM)


def norm_kernel(rows_hbm, gain_hbm, normed_ref, rows_ref, gain_ref, semaphores):
    copies = [
        pltpu.make_async_copy(rows_hbm, rows_ref, semaphores.at[0]),
        pltpu.make_async_copy(gain_hbm, gain_ref, semaphores.at[1]),
    ]
    for copy in copies:
        copy.start()
    for copy in copies:
        copy.wait()
    values = rows_ref[...].astype(F32)
    meansq = jnp.mean(values * values, axis=-1, keepdims=True)
    normed_ref[...] = (values * lax.rsqrt(meansq + 1e-05) * gain_ref[...][None, :]).astype(BF16)


def rms_normed(rows_in, norm_gain):
    return pl.pallas_call(
        norm_kernel,
        in_specs=[ANYWHERE] * 2,
        out_specs=INSIDE,
        out_shape=jax.ShapeDtypeStruct(rows_in.shape, BF16),
        scratch_shapes=[
            pltpu.VMEM(rows_in.shape, rows_in.dtype),
            pltpu.VMEM(norm_gain.shape, norm_gain.dtype),
            pltpu.SemaphoreType.DMA((2,)),
        ],
        compiler_params=pltpu.CompilerParams(vmem_limit_bytes=VMEM),
        cost_estimate=as_if(0),
        name="normed",
    )(*(pltpu.with_memory_space_constraint(values, pltpu.HBM) for values in (rows_in, norm_gain)))


def mask_kernel(share, rows, after_count, core_ref, weight_ref, mask_ref, *refs):
    kept_ref, token_ref, spread, semaphores = refs[after_count:]
    token_ref[...] = jnp.zeros_like(token_ref)
    depth, width = kept_ref.shape
    number = share(core_ref[0])
    columns = pl.ds(pl.multiple_of(number * width, width), width)
    copies = [
        pltpu.make_async_copy(
            weight_ref.at[pl.ds(step * rows, rows), columns], kept_ref.at[pl.ds(step * rows, rows)], semaphores.at[step]
        )
        for step in range(depth // rows)
    ]
    for copy in copies:
        copy.start()
    marks = mask_ref.shape[1]
    owner = lax.broadcasted_iota(jnp.int32, (marks, width), 1) // BLOCK + number * (width // BLOCK)
    chosen = (owner == lax.broadcasted_iota(jnp.int32, (marks, width), 0)).astype(F32)
    spread[...] = jnp.dot(mask_ref[...].astype(F32), chosen, preferred_element_type=F32)
    for step, copy in enumerate(copies):
        copy.wait()
        for block in range(step * rows // BLOCK, (step + 1) * rows // BLOCK):
            part = pl.ds(block * BLOCK, BLOCK)
            keep = jnp.broadcast_to(spread[pl.ds(block, 1), :], (BLOCK, width))
            kept_ref[part, :] = kept_ref[part, :] * keep.astype(BF16)


def masked(weight, mask, rows, core, shares, share, after, hint=0.0):
    depth, width = weight.shape
    width = width // shares
    return pl.pallas_call(
        functools.partial(mask_kernel, share, rows, len(after)),
        in_specs=[pl.BlockSpec(memory_space=pltpu.SMEM), ANYWHERE, INSIDE] + [ANYWHERE] * len(after),
        out_specs=[INSIDE] * 2,
        out_shape=[jax.ShapeDtypeStruct((depth, width), weight.dtype), TOKEN],
        scratch_shapes=[pltpu.VMEM((mask.shape[0], width), F32), pltpu.SemaphoreType.DMA((depth // rows,))],
        compiler_params=pltpu.CompilerParams(vmem_limit_bytes=VMEM),
        cost_estimate=as_if(hint),
        name="masked",
    )(core, pltpu.with_memory_space_constraint(weight, pltpu.HBM), mask, *after)


def stack_kernel(after_count, *refs):
    block_refs, (stacked_ref, token_ref) = refs[: -2 - after_count], refs[-2:]
    token_ref[...] = jnp.zeros_like(token_ref)
    for number, block_ref in enumerate(block_refs):
        stacked_ref[number // stacked_ref.shape[1], number % stacked_ref.shape[1]] = block_ref[...]


def join_kernel(after_count, *refs):
    stacked_refs, (joined_ref, token_ref) = refs[: -2 - after_count], refs[-2:]
    token_ref[...] = jnp.zeros_like(token_ref)
    blocks = [ref[core, chip] for core in range(CORES) for ref in stacked_refs for chip in range(ref.shape[1])]
    joined_ref[...] = jnp.concatenate([block.astype(F32) for block in blocks], 0).astype(BF16)


def rearranged(kernel, name, shape, blocks, after, hint=0.0):
    return pl.pallas_call(
        functools.partial(kernel, len(after)),
        in_specs=[INSIDE] * len(blocks) + [ANYWHERE] * len(after),
        out_specs=[INSIDE] * 2,
        out_shape=[jax.ShapeDtypeStruct(shape, BF16), TOKEN],
        compiler_params=pltpu.CompilerParams(vmem_limit_bytes=VMEM // 2),
        cost_estimate=as_if(hint),
        name=name,
    )(*blocks, *after)


def wait_kernel(*refs):
    refs[-1][...] = jnp.zeros_like(refs[-1])


def waited(after, hint):
    return pl.pallas_call(
        wait_kernel,
        in_specs=[ANYWHERE] * len(after),
        out_specs=INSIDE,
        out_shape=TOKEN,
        compiler_params=pltpu.CompilerParams(vmem_limit_bytes=VMEM // 2),
        cost_estimate=as_if(hint),
        name="waited",
    )(*after)


def stack(blocks, after):
    shape = (CORES, len(blocks) // CORES, *blocks[0].shape)
    return rearranged(stack_kernel, "stack", shape, blocks, after)


def join(stacks, after, hint=0.0):
    rows = sum(part.shape[1] for part in stacks) * CORES * stacks[0].shape[2]
    return rearranged(join_kernel, "join", (rows, stacks[0].shape[3]), stacks, after, hint)


def pick_kernel(after_count, side_ref, inner_three_ref, outer_three_ref, mine_ref, *refs):
    three_ref, passed_ref, token_ref = refs[after_count:]
    token_ref[...] = jnp.zeros_like(token_ref)

    @pl.when(side_ref[0] == 1)
    def _():
        three_ref[...] = inner_three_ref[...]
        passed_ref[...] = inner_three_ref[...]

    @pl.when(side_ref[0] == 0)
    def _():
        three_ref[...] = outer_three_ref[...]
        passed_ref[...] = mine_ref[...]


def pick(side, inner_three, outer_three, mine, after):
    return pl.pallas_call(
        functools.partial(pick_kernel, len(after)),
        in_specs=[pl.BlockSpec(memory_space=pltpu.SMEM)] + [INSIDE] * 3 + [ANYWHERE] * len(after),
        out_specs=[INSIDE] * 3,
        out_shape=[jax.ShapeDtypeStruct(mine.shape, BF16)] * 2 + [TOKEN],
        compiler_params=pltpu.CompilerParams(vmem_limit_bytes=VMEM // 2),
        cost_estimate=as_if(8),
        name="pick",
    )(side, inner_three, outer_three, mine, *after)


def resident(values):
    return pltpu.with_memory_space_constraint(values, pltpu.VMEM)


def gate_up_kernel(part_count, after_count, *refs):
    parts, (gate_ref, up_ref) = refs[:part_count], refs[part_count : part_count + 2]
    keep_ref, near_ref, *far_refs, token_ref, all_rows = refs[part_count + 2 + after_count :]
    far_places = [(far_ref, which) for far_ref in far_refs for which in range(far_ref.shape[0])]
    token_ref[...] = jnp.zeros_like(token_ref)
    half = parts[0].shape[0] // 2
    kept = half * len(parts)
    for place, part in enumerate(parts):
        all_rows[pl.ds(place * half, half), :] = part[:half, :]
        all_rows[pl.ds(kept + place * half, half), :] = part[half:, :]
    tile = tile_of(gate_ref.shape[1], 896)

    @pl.loop(0, gate_ref.shape[1] // tile)
    def _(number):
        columns = pl.ds(pl.multiple_of(number * tile, tile), tile)
        for which, weight_ref in enumerate((gate_ref, up_ref)):
            total = jnp.dot(all_rows[...], weight_ref[:, columns], preferred_element_type=F32)
            total = total.reshape(2, *keep_ref.shape[1:4], tile).astype(BF16)
            keep_ref[which, :, :, :, columns] = total[0]
            near_ref[which, :, :, columns] = total[1, :, 0]
            far_ref, place = far_places[which]
            far_ref[place, :, :, :, columns] = total[1, :, 1:]


def gate_up(parts, gate_kept, up_kept, chips, far_parts, hint, after):
    rows = sum(part.shape[0] for part in parts)
    depth, width = gate_kept.shape
    groups, own = len(parts), rows // (2 * len(parts) * chips)
    shapes = [(2, groups, chips, own, width), (2, groups, own, width)]
    shapes += [(2 // far_parts, groups, chips - 1, own, width)] * far_parts
    return pl.pallas_call(
        functools.partial(gate_up_kernel, len(parts), len(after)),
        in_specs=[INSIDE] * (len(parts) + 2) + [ANYWHERE] * len(after),
        out_specs=[INSIDE] * (len(shapes) + 1),
        out_shape=[jax.ShapeDtypeStruct(shape, BF16) for shape in shapes] + [TOKEN],
        scratch_shapes=[pltpu.VMEM((rows, depth), BF16)],
        compiler_params=pltpu.CompilerParams(vmem_limit_bytes=VMEM // 2),
        cost_estimate=cost(hint * 4 * rows * depth * width, 0),
        name="gate_up",
    )(*parts, resident(gate_kept), resident(up_kept), *after)


def down_kernel(pieces, weight_count, after_count, own_ref, other_ref, *refs):
    weight_refs, refs = refs[:weight_count], refs[weight_count:]
    *partial_refs, token_ref, both = refs[after_count:]
    token_ref[...] = jnp.zeros_like(token_ref)
    groups, own, depth = own_ref.shape
    rows = groups * own
    both[:rows, :] = own_ref[...].astype(F32).reshape(rows, depth).astype(BF16)
    both[rows:, :] = other_ref[...].astype(F32).reshape(rows, depth).astype(BF16)
    for number, weight_ref in enumerate(weight_refs):
        width = weight_ref.shape[1]
        down_columns(pieces, both, weight_ref, partial_refs, number * width, tile_of(width, 1024))


def down_columns(pieces, both, weight_ref, partial_refs, first, tile):
    own = partial_refs[0].shape[1]

    @pl.loop(0, weight_ref.shape[1] // tile)
    def _(number):
        start = pl.multiple_of(number * tile, tile)
        total = jnp.dot(both[...], weight_ref[:, pl.ds(start, tile)], preferred_element_type=F32)
        total = total.reshape(pieces, CORES // pieces, len(partial_refs) // pieces, own, tile)
        columns = pl.ds(pl.multiple_of(first + start, tile), tile)
        for place, partial_ref in enumerate(partial_refs):
            partial_ref[:, :, columns] = total[place % pieces, :, place // pieces].astype(BF16)


def down(own, other, down_kept, pieces, after):
    groups, rows, depth = own.shape
    width = sum(weight.shape[1] for weight in down_kept)
    shape = (CORES // pieces, rows, width)
    return pl.pallas_call(
        functools.partial(down_kernel, pieces, len(down_kept), len(after)),
        in_specs=[INSIDE] * (2 + len(down_kept)) + [ANYWHERE] * len(after),
        out_specs=[INSIDE] * (groups * pieces + 1),
        out_shape=[jax.ShapeDtypeStruct(shape, BF16)] * (groups * pieces) + [TOKEN],
        scratch_shapes=[pltpu.VMEM((CORES * groups * rows, depth), BF16)],
        compiler_params=pltpu.CompilerParams(vmem_limit_bytes=VMEM // 2),
        cost_estimate=cost(2 * CORES * groups * rows * depth * width, 0),
        name="down",
    )(own, other, *(resident(weight) for weight in down_kept), *after)


def sums_kernel(sizes, after_count, *refs):
    to_chips, to_hidden, *to_rows = sizes
    refs = list(refs)
    refs.pop()[...] = jnp.zeros(TOKEN.shape, F32)
    ins = [[refs.pop(0) for _ in range(size)] for size in sizes]
    del refs[:after_count]

    if to_chips:
        keep_ref, *came_refs = ins[0]
        came_places = [came_ref.at[which] for came_ref in came_refs for which in range(came_ref.shape[0])]
        for chip in range(1, keep_ref.shape[2]):
            sent_ref = refs.pop(0)
            for which in range(2):
                for group in range(keep_ref.shape[1]):
                    came = came_places[which][group, chip - 1].astype(F32)
                    sent_ref[which, group] = (keep_ref[which, group, chip].astype(F32) + came).astype(BF16)
    if to_hidden:
        keep_ref, came_ref, *chip_refs = ins[1]
        hidden_ref = refs.pop(0)
        for group in range(keep_ref.shape[1]):
            both = []
            for which in range(2):
                total = keep_ref[which, group, 0].astype(F32) + came_ref[which, group].astype(F32)
                for chip_ref in chip_refs:
                    total = total + chip_ref[which, group].astype(F32)
                both.append(total)
            hidden_ref[group] = (jax.nn.silu(both[0]) * both[1]).astype(BF16)
    for part_refs in ins[2:]:
        summed_ref = refs.pop(0)
        cores = summed_ref.shape[0]
        for core in range(cores):
            total = part_refs[0][core].astype(F32)
            for part_ref in part_refs[1:]:
                total = total + part_ref[part_ref.shape[0] - cores + core].astype(F32)
            summed_ref[core] = total.astype(BF16)


def sums(to_chips, to_hidden, to_rows, after, hint=0.0):
    shapes = []
    if to_chips:
        two, groups, chips, own, width = to_chips[0].shape
        shapes += [(two, groups, own, width)] * (chips - 1)
    if to_hidden:
        shapes.append((to_hidden[0].shape[1], *to_hidden[0].shape[3:]))
    shapes += [parts[0].shape for parts in to_rows]
    given = [to_chips, to_hidden, *to_rows]
    sizes = tuple(len(parts) for parts in given)
    given = [part for parts in given for part in parts]
    results = list(pl.pallas_call(
        functools.partial(sums_kernel, sizes, len(after)),
        in_specs=[INSIDE] * len(given) + [ANYWHERE] * len(after),
        out_specs=[INSIDE] * (len(shapes) + 1),
        out_shape=[jax.ShapeDtypeStruct(shape, BF16) for shape in shapes] + [TOKEN],
        compiler_params=pltpu.CompilerParams(vmem_limit_bytes=VMEM // 2),
        cost_estimate=as_if(hint),
        name="sums",
    )(*given, *after))
    token = results.pop()
    sent = [results.pop(0) for _ in range(chips - 1)] if to_chips else []
    hidden = results.pop(0) if to_hidden else None
    return sent, hidden, results, token


def swap(values, axis, size, step):
    return lax.ppermute(values, axis, [(place, place ^ step) for place in range(size)])


def body(row_count, col_count, tokens, norm_gain, gate_weight, up_weight, down_weight, gate_mask, up_mask, down_mask):
    chips = row_count // CORES
    per_plane = col_count // PLANES
    features, width = gate_weight.shape
    row = lax.axis_index("rows")
    core = row % CORES
    inner = (lax.axis_index("cols") // per_plane) % (PLANES - 1) != 0
    place = jnp.reshape(core, (1,)).astype(jnp.int32)
    side = jnp.reshape(inner, (1,)).astype(jnp.int32)

    normed = rms_normed(tokens, norm_gain)
    def block(step):
        return lax.dynamic_slice_in_dim(normed, (row ^ step) * features, features, 1)

    from_core = swap(jnp.stack([block(chip * CORES + 1) for chip in range(chips)]), "rows", row_count, 1)
    to_chips_rows = [stack([block(chip * CORES), from_core[chip]], [])[0] for chip in range(1, chips)]
    first, token = stack([block(0), from_core[0]], [*to_chips_rows[:1], side])
    gate_kept, token = masked(gate_weight, gate_mask, tile_of(features, 256), place, 1, lambda core: 0, [token])
    second = [swap(part, "rows", row_count, (chip + 1) * CORES) for chip, part in enumerate(to_chips_rows)]
    second = jnp.concatenate(second, 1) if len(second) > 1 else second[0]
    mine, token = join([first, second], [token])

    def behind(values, after):
        return lax.optimization_barrier((values, *after))[0] if after else values

    def by_plane(values, planes, after=()):
        pairs = [(a * per_plane + b, c * per_plane + b) for a, c in planes for b in range(per_plane)]
        return lax.ppermute(behind(values, after), "cols", pairs)

    def by_row_of_plane(values, step, after=()):
        return swap(behind(values, after), "cols", col_count, step)

    def by_chip(values, chip, after=()):
        return swap(behind(values, after), "rows", row_count, chip * CORES)

    def by_core(values, after=()):
        return swap(behind(values, after), "rows", row_count, 1)

    parts, halves, near, far, chip_sums, hiddens, others, rows_in, partials, sent = ({} for _ in range(10))
    last = [token]

    def forward(plane, values, after=()):
        parts[plane] = [values]
        for step in range(1, per_plane):
            parts[plane].append(by_row_of_plane(values, step, after))

    def multiply_in(plane, far_parts=1, hint=HURRY, after=()):
        parts_after = last + list(after)
        *halves[plane], last[0] = gate_up(parts[plane], gate_kept, up_kept, chips, far_parts, hint, parts_after)

    def exchange(plane, after=()):
        far[plane] = [by_core(part, after) for part in halves[plane][2:]]

    def exchange_near(plane, after=()):
        near[plane] = by_core(halves[plane][1], after)

    def multiply_out(plane, pieces=1, after=()):
        *partials[plane], last[0] = down(hiddens[plane], others[plane], down_kept, pieces, last + list(after))

    def send_rows(plane, after=(), pieces=1, piece=0):
        mine_and_others = partials[plane][piece::pieces]
        rows_in[plane, piece] = mine_and_others[:1]
        for step in range(1, per_plane):
            rows_in[plane, piece].append(by_row_of_plane(mine_and_others[step], step, after))

    def to_chips(plane, after=()):
        given = [halves[plane][0], *far[plane]]
        sent[plane], _, _, last[0] = sums(given, [], [], last + list(after))

    def send_chips(plane, after=()):
        chip_sums[plane] = [by_chip(part, number + 1, after) for number, part in enumerate(sent[plane])]

    def to_hidden(plane, after=()):
        given = [halves[plane][0], near[plane], *chip_sums[plane]]
        _, hiddens[plane], _, last[0] = sums([], given, [], last + list(after))
        others[plane] = by_core(hiddens[plane])

    def to_rows(*parts, after=(), hint=0.0):
        _, _, (summed,), last[0] = sums([], [], [parts], last + list(after), hint)
        return summed

    next_stacks = [by_plane(first, NEXT), by_plane(second, NEXT)]
    across_stacks = [by_plane(first, ACROSS), by_plane(second, ACROSS)]
    row_stacks = {
        step: [by_row_of_plane(first, step), by_row_of_plane(second, step)] for step in range(1, per_plane)
    }
    up_kept, last[0] = masked(
        up_weight, up_mask, tile_of(features, 256), place, 1, lambda core: 0, last + next_stacks[:1], 0.15
    )
    last[0] = waited([*last, across_stacks[0], *(stacks[0] for stacks in row_stacks.values())], 0.07)
    one_away, last[0] = join(next_stacks, last)
    inner_three, last[0] = join(across_stacks, last)
    outer_three = by_plane(mine, AROUND, last)
    down_kept = []

    def keep_down(share, hint=0.0):
        part, last[0] = masked(
            down_weight, down_mask, 2 * BLOCK, place, 2 * CORES, lambda core: 2 * core + share, last, hint
        )
        down_kept.append(part)

    parts[0] = [mine]
    for stacks in row_stacks.values():
        part, last[0] = join(stacks, last)
        parts[0].append(part)
    forward(1, one_away, last)
    multiply_in(0, hint=HURRY)
    exchange(0)
    exchange_near(0)
    keep_down(0)
    three_away, passed, last[0] = pick(side, inner_three, outer_three, mine, last)
    two_away = by_plane(passed, CYCLE)
    to_chips(0, [near[0]])
    forward(3, three_away, [*parts[1][1:], *last])
    multiply_in(1)
    exchange(1)
    exchange_near(1)
    to_chips(1, [near[1]])
    send_chips(1)
    keep_down(1)
    forward(2, two_away, last)
    multiply_in(3, after=[two_away])
    exchange(3)
    exchange_near(3)
    to_hidden(1)
    to_chips(3, [near[3]])
    send_chips(3)
    multiply_out(1)
    send_rows(1, parts[2][1:])
    multiply_in(2, far_parts=2)
    exchange(2)
    to_hidden(3)
    to_chips(2)
    send_chips(2)
    exchange_near(2, last)
    multiply_out(3, pieces=CORES)
    send_rows(3, rows_in[1, 0][1:], CORES, 1)
    one = to_rows(*rows_in[1, 0])
    one_out = by_plane(one, NEXT)
    three = to_rows(*rows_in[3, 1])
    send_rows(3, [three], CORES, 0)
    three_out, two_out = {1: by_plane(three, NEXT)}, {}
    to_hidden(2)
    send_chips(0, chip_sums[2])
    multiply_out(2, pieces=CORES)
    three = to_rows(*rows_in[3, 0], after=[one_out])
    three_out[0] = by_plane(three, NEXT)
    send_rows(2, rows_in[3, 0][1:], CORES, 1)
    two = to_rows(*rows_in[2, 1], three_out[1])
    two_out[1] = by_plane(two, SECOND)
    send_rows(2, [two], CORES, 0)
    to_hidden(0)
    multiply_out(0)
    two = to_rows(rows_in[2, 0][0], three_out[0], hint=0.1)
    two = to_rows(two, *rows_in[2, 0][1:])
    two_out[0] = by_plane(two, SECOND)
    send_rows(0, rows_in[2, 0][1:])

    joined = to_rows(two_out[1], one_out, hint=10.0)

    def total(piece, *parts):
        whole = [part[piece].astype(F32) for part in rows_in[0, 0]] + [part.astype(F32) for part in parts]
        return sum(whole[1:], whole[0]).astype(BF16)

    mine_now, other = total(0, one_out[0], two_out[0][0]), by_core(total(1, joined[0]))
    left = jnp.where(core == 0, mine_now, other)
    right = jnp.where(core == 0, other, mine_now)
    return jnp.concatenate([left, right], 1)


def solution(mesh):
    return jax.shard_map(
        functools.partial(body, mesh.shape["rows"], mesh.shape["cols"]),
        mesh=mesh,
        in_specs=(
            P(("rows", "cols"), None),
            P(),
            P("rows", "cols"),
            P("rows", "cols"),
            P("cols", None),
            P("rows", "cols"),
            P("rows", "cols"),
            P("cols", None),
        ),
        out_specs=P(("rows", "cols"), None),
        check_vma=False,
    )
```

```python
import functools

import jax
import jax.numpy as jnp
from jax import lax
from jax.experimental import pallas as pl
from jax.experimental.pallas import tpu as pltpu
from jax.sharding import PartitionSpec as P

BLOCK = 64
CORES = 2
PLANES = 4
NEXT = ((0, 1), (1, 0), (2, 3), (3, 2))
SECOND = ((0, 2), (2, 0), (1, 3), (3, 1))
ACROSS = ((1, 2), (2, 1))
AROUND = ((0, 3), (3, 0))
CYCLE = ((0, 2), (2, 3), (3, 1), (1, 0))
VMEM = 12 * 1024 * 1024
F32 = jnp.float32
BF16 = jnp.bfloat16


def tile_of(size, most):
    tile = most
    while size % tile:
        tile //= 2
    return tile


HURRY = 1000


def cost(flops, moved):
    return pl.CostEstimate(flops=flops // HURRY, bytes_accessed=moved // HURRY, transcendentals=0)


def as_if(microseconds):
    return cost(int(HURRY * 1.15e9 * microseconds), 0)


ANYWHERE = pl.BlockSpec(memory_space=pl.ANY)
TOKEN = jax.ShapeDtypeStruct((8, 128), F32)
INSIDE = pl.BlockSpec(memory_space=pltpu.VMEM)


def norm_kernel(rows_hbm, gain_hbm, normed_ref, rows_ref, gain_ref, semaphores):
    copies = [
        pltpu.make_async_copy(rows_hbm, rows_ref, semaphores.at[0]),
        pltpu.make_async_copy(gain_hbm, gain_ref, semaphores.at[1]),
    ]
    for copy in copies:
        copy.start()
    for copy in copies:
        copy.wait()
    values = rows_ref[...].astype(F32)
    meansq = jnp.mean(values * values, axis=-1, keepdims=True)
    normed_ref[...] = (values * lax.rsqrt(meansq + 1e-05) * gain_ref[...][None, :]).astype(BF16)


def rms_normed(rows_in, norm_gain):
    return pl.pallas_call(
        norm_kernel,
        in_specs=[ANYWHERE] * 2,
        out_specs=INSIDE,
        out_shape=jax.ShapeDtypeStruct(rows_in.shape, BF16),
        scratch_shapes=[
            pltpu.VMEM(rows_in.shape, rows_in.dtype),
            pltpu.VMEM(norm_gain.shape, norm_gain.dtype),
            pltpu.SemaphoreType.DMA((2,)),
        ],
        compiler_params=pltpu.CompilerParams(vmem_limit_bytes=VMEM),
        cost_estimate=as_if(0),
        name="normed",
    )(*(pltpu.with_memory_space_constraint(values, pltpu.HBM) for values in (rows_in, norm_gain)))


def mask_kernel(share, rows, after_count, core_ref, weight_ref, mask_ref, *refs):
    kept_ref, token_ref, spread, semaphores = refs[after_count:]
    token_ref[...] = jnp.zeros_like(token_ref)
    depth, width = kept_ref.shape
    number = share(core_ref[0])
    columns = pl.ds(pl.multiple_of(number * width, width), width)
    copies = [
        pltpu.make_async_copy(
            weight_ref.at[pl.ds(step * rows, rows), columns], kept_ref.at[pl.ds(step * rows, rows)], semaphores.at[step]
        )
        for step in range(depth // rows)
    ]
    for copy in copies:
        copy.start()
    marks = mask_ref.shape[1]
    owner = lax.broadcasted_iota(jnp.int32, (marks, width), 1) // BLOCK + number * (width // BLOCK)
    chosen = (owner == lax.broadcasted_iota(jnp.int32, (marks, width), 0)).astype(F32)
    spread[...] = jnp.dot(mask_ref[...].astype(F32), chosen, preferred_element_type=F32)
    for step, copy in enumerate(copies):
        copy.wait()
        for block in range(step * rows // BLOCK, (step + 1) * rows // BLOCK):
            part = pl.ds(block * BLOCK, BLOCK)
            keep = jnp.broadcast_to(spread[pl.ds(block, 1), :], (BLOCK, width))
            kept_ref[part, :] = kept_ref[part, :] * keep.astype(BF16)


def masked(weight, mask, rows, core, shares, share, after, hint=0.0):
    depth, width = weight.shape
    width = width // shares
    return pl.pallas_call(
        functools.partial(mask_kernel, share, rows, len(after)),
        in_specs=[pl.BlockSpec(memory_space=pltpu.SMEM), ANYWHERE, INSIDE] + [ANYWHERE] * len(after),
        out_specs=[INSIDE] * 2,
        out_shape=[jax.ShapeDtypeStruct((depth, width), weight.dtype), TOKEN],
        scratch_shapes=[pltpu.VMEM((mask.shape[0], width), F32), pltpu.SemaphoreType.DMA((depth // rows,))],
        compiler_params=pltpu.CompilerParams(vmem_limit_bytes=VMEM),
        cost_estimate=as_if(hint),
        name="masked",
    )(core, pltpu.with_memory_space_constraint(weight, pltpu.HBM), mask, *after)


def stack_kernel(after_count, *refs):
    block_refs, (stacked_ref, token_ref) = refs[: -2 - after_count], refs[-2:]
    token_ref[...] = jnp.zeros_like(token_ref)
    for number, block_ref in enumerate(block_refs):
        stacked_ref[number // stacked_ref.shape[1], number % stacked_ref.shape[1]] = block_ref[...]


def join_kernel(after_count, *refs):
    stacked_refs, (joined_ref, token_ref) = refs[: -2 - after_count], refs[-2:]
    token_ref[...] = jnp.zeros_like(token_ref)
    blocks = [ref[core, chip] for core in range(CORES) for ref in stacked_refs for chip in range(ref.shape[1])]
    joined_ref[...] = jnp.concatenate([block.astype(F32) for block in blocks], 0).astype(BF16)


def rearranged(kernel, name, shape, blocks, after, hint=0.0):
    return pl.pallas_call(
        functools.partial(kernel, len(after)),
        in_specs=[INSIDE] * len(blocks) + [ANYWHERE] * len(after),
        out_specs=[INSIDE] * 2,
        out_shape=[jax.ShapeDtypeStruct(shape, BF16), TOKEN],
        compiler_params=pltpu.CompilerParams(vmem_limit_bytes=VMEM // 2),
        cost_estimate=as_if(hint),
        name=name,
    )(*blocks, *after)


def wait_kernel(*refs):
    refs[-1][...] = jnp.zeros_like(refs[-1])


def waited(after, hint):
    return pl.pallas_call(
        wait_kernel,
        in_specs=[ANYWHERE] * len(after),
        out_specs=INSIDE,
        out_shape=TOKEN,
        compiler_params=pltpu.CompilerParams(vmem_limit_bytes=VMEM // 2),
        cost_estimate=as_if(hint),
        name="waited",
    )(*after)


def stack(blocks, after):
    shape = (CORES, len(blocks) // CORES, *blocks[0].shape)
    return rearranged(stack_kernel, "stack", shape, blocks, after)


def join(stacks, after, hint=0.0):
    rows = sum(part.shape[1] for part in stacks) * CORES * stacks[0].shape[2]
    return rearranged(join_kernel, "join", (rows, stacks[0].shape[3]), stacks, after, hint)


def pick_kernel(after_count, side_ref, inner_three_ref, outer_three_ref, mine_ref, *refs):
    three_ref, passed_ref, token_ref = refs[after_count:]
    token_ref[...] = jnp.zeros_like(token_ref)

    @pl.when(side_ref[0] == 1)
    def _():
        three_ref[...] = inner_three_ref[...]
        passed_ref[...] = inner_three_ref[...]

    @pl.when(side_ref[0] == 0)
    def _():
        three_ref[...] = outer_three_ref[...]
        passed_ref[...] = mine_ref[...]


def pick(side, inner_three, outer_three, mine, after):
    return pl.pallas_call(
        functools.partial(pick_kernel, len(after)),
        in_specs=[pl.BlockSpec(memory_space=pltpu.SMEM)] + [INSIDE] * 3 + [ANYWHERE] * len(after),
        out_specs=[INSIDE] * 3,
        out_shape=[jax.ShapeDtypeStruct(mine.shape, BF16)] * 2 + [TOKEN],
        compiler_params=pltpu.CompilerParams(vmem_limit_bytes=VMEM // 2),
        cost_estimate=as_if(8),
        name="pick",
    )(side, inner_three, outer_three, mine, *after)


def resident(values):
    return pltpu.with_memory_space_constraint(values, pltpu.VMEM)


def gate_up_kernel(part_count, after_count, *refs):
    parts, (gate_ref, up_ref) = refs[:part_count], refs[part_count : part_count + 2]
    keep_ref, near_ref, *far_refs, token_ref, all_rows = refs[part_count + 2 + after_count :]
    far_places = [(far_ref, which) for far_ref in far_refs for which in range(far_ref.shape[0])]
    token_ref[...] = jnp.zeros_like(token_ref)
    half = parts[0].shape[0] // 2
    kept = half * len(parts)
    for place, part in enumerate(parts):
        all_rows[pl.ds(place * half, half), :] = part[:half, :]
        all_rows[pl.ds(kept + place * half, half), :] = part[half:, :]
    tile = tile_of(gate_ref.shape[1], 1792)

    @pl.loop(0, gate_ref.shape[1] // tile)
    def _(number):
        columns = pl.ds(pl.multiple_of(number * tile, tile), tile)
        for which, weight_ref in enumerate((gate_ref, up_ref)):
            total = jnp.dot(all_rows[...], weight_ref[:, columns], preferred_element_type=F32)
            total = total.reshape(2, *keep_ref.shape[1:4], tile).astype(BF16)
            keep_ref[which, :, :, :, columns] = total[0]
            near_ref[which, :, :, columns] = total[1, :, 0]
            far_ref, place = far_places[which]
            far_ref[place, :, :, :, columns] = total[1, :, 1:]


def gate_up(parts, gate_kept, up_kept, chips, far_parts, hint, after):
    rows = sum(part.shape[0] for part in parts)
    depth, width = gate_kept.shape
    groups, own = len(parts), rows // (2 * len(parts) * chips)
    shapes = [(2, groups, chips, own, width), (2, groups, own, width)]
    shapes += [(2 // far_parts, groups, chips - 1, own, width)] * far_parts
    return pl.pallas_call(
        functools.partial(gate_up_kernel, len(parts), len(after)),
        in_specs=[INSIDE] * (len(parts) + 2) + [ANYWHERE] * len(after),
        out_specs=[INSIDE] * (len(shapes) + 1),
        out_shape=[jax.ShapeDtypeStruct(shape, BF16) for shape in shapes] + [TOKEN],
        scratch_shapes=[pltpu.VMEM((rows, depth), BF16)],
        compiler_params=pltpu.CompilerParams(vmem_limit_bytes=VMEM // 2),
        cost_estimate=cost(hint * 4 * rows * depth * width, 0),
        name="gate_up",
    )(*parts, resident(gate_kept), resident(up_kept), *after)


def down_kernel(pieces, weight_count, after_count, own_ref, other_ref, *refs):
    weight_refs, refs = refs[:weight_count], refs[weight_count:]
    *partial_refs, token_ref, both = refs[after_count:]
    token_ref[...] = jnp.zeros_like(token_ref)
    groups, own, depth = own_ref.shape
    rows = groups * own
    both[:rows, :] = own_ref[...].astype(F32).reshape(rows, depth).astype(BF16)
    both[rows:, :] = other_ref[...].astype(F32).reshape(rows, depth).astype(BF16)
    for number, weight_ref in enumerate(weight_refs):
        width = weight_ref.shape[1]
        down_columns(pieces, both, weight_ref, partial_refs, number * width, tile_of(width, 2048))


def down_columns(pieces, both, weight_ref, partial_refs, first, tile):
    own = partial_refs[0].shape[1]

    @pl.loop(0, weight_ref.shape[1] // tile)
    def _(number):
        start = pl.multiple_of(number * tile, tile)
        total = jnp.dot(both[...], weight_ref[:, pl.ds(start, tile)], preferred_element_type=F32)
        total = total.reshape(pieces, CORES // pieces, len(partial_refs) // pieces, own, tile)
        columns = pl.ds(pl.multiple_of(first + start, tile), tile)
        for place, partial_ref in enumerate(partial_refs):
            partial_ref[:, :, columns] = total[place % pieces, :, place // pieces].astype(BF16)


def down(own, other, down_kept, pieces, after):
    groups, rows, depth = own.shape
    width = sum(weight.shape[1] for weight in down_kept)
    shape = (CORES // pieces, rows, width)
    return pl.pallas_call(
        functools.partial(down_kernel, pieces, len(down_kept), len(after)),
        in_specs=[INSIDE] * (2 + len(down_kept)) + [ANYWHERE] * len(after),
        out_specs=[INSIDE] * (groups * pieces + 1),
        out_shape=[jax.ShapeDtypeStruct(shape, BF16)] * (groups * pieces) + [TOKEN],
        scratch_shapes=[pltpu.VMEM((CORES * groups * rows, depth), BF16)],
        compiler_params=pltpu.CompilerParams(vmem_limit_bytes=VMEM // 2),
        cost_estimate=cost(2 * CORES * groups * rows * depth * width, 0),
        name="down",
    )(own, other, *(resident(weight) for weight in down_kept), *after)


def sums_kernel(sizes, after_count, *refs):
    to_chips, to_hidden, *to_rows = sizes
    refs = list(refs)
    refs.pop()[...] = jnp.zeros(TOKEN.shape, F32)
    ins = [[refs.pop(0) for _ in range(size)] for size in sizes]
    del refs[:after_count]

    if to_chips:
        keep_ref, *came_refs = ins[0]
        came_places = [came_ref.at[which] for came_ref in came_refs for which in range(came_ref.shape[0])]
        for chip in range(1, keep_ref.shape[2]):
            sent_ref = refs.pop(0)
            for which in range(2):
                for group in range(keep_ref.shape[1]):
                    came = came_places[which][group, chip - 1].astype(F32)
                    sent_ref[which, group] = (keep_ref[which, group, chip].astype(F32) + came).astype(BF16)
    if to_hidden:
        keep_ref, came_ref, *chip_refs = ins[1]
        hidden_ref = refs.pop(0)
        for group in range(keep_ref.shape[1]):
            both = []
            for which in range(2):
                total = keep_ref[which, group, 0].astype(F32) + came_ref[which, group].astype(F32)
                for chip_ref in chip_refs:
                    total = total + chip_ref[which, group].astype(F32)
                both.append(total)
            hidden_ref[group] = (jax.nn.silu(both[0]) * both[1]).astype(BF16)
    for part_refs in ins[2:]:
        summed_ref = refs.pop(0)
        cores = summed_ref.shape[0]
        for core in range(cores):
            total = part_refs[0][core].astype(F32)
            for part_ref in part_refs[1:]:
                total = total + part_ref[part_ref.shape[0] - cores + core].astype(F32)
            summed_ref[core] = total.astype(BF16)


def sums(to_chips, to_hidden, to_rows, after, hint=0.0):
    shapes = []
    if to_chips:
        two, groups, chips, own, width = to_chips[0].shape
        shapes += [(two, groups, own, width)] * (chips - 1)
    if to_hidden:
        shapes.append((to_hidden[0].shape[1], *to_hidden[0].shape[3:]))
    shapes += [parts[0].shape for parts in to_rows]
    given = [to_chips, to_hidden, *to_rows]
    sizes = tuple(len(parts) for parts in given)
    given = [part for parts in given for part in parts]
    results = list(pl.pallas_call(
        functools.partial(sums_kernel, sizes, len(after)),
        in_specs=[INSIDE] * len(given) + [ANYWHERE] * len(after),
        out_specs=[INSIDE] * (len(shapes) + 1),
        out_shape=[jax.ShapeDtypeStruct(shape, BF16) for shape in shapes] + [TOKEN],
        compiler_params=pltpu.CompilerParams(vmem_limit_bytes=VMEM // 2),
        cost_estimate=as_if(hint),
        name="sums",
    )(*given, *after))
    token = results.pop()
    sent = [results.pop(0) for _ in range(chips - 1)] if to_chips else []
    hidden = results.pop(0) if to_hidden else None
    return sent, hidden, results, token


def swap(values, axis, size, step):
    return lax.ppermute(values, axis, [(place, place ^ step) for place in range(size)])


def body(row_count, col_count, tokens, norm_gain, gate_weight, up_weight, down_weight, gate_mask, up_mask, down_mask):
    chips = row_count // CORES
    per_plane = col_count // PLANES
    features, width = gate_weight.shape
    row = lax.axis_index("rows")
    core = row % CORES
    inner = (lax.axis_index("cols") // per_plane) % (PLANES - 1) != 0
    place = jnp.reshape(core, (1,)).astype(jnp.int32)
    side = jnp.reshape(inner, (1,)).astype(jnp.int32)

    normed = rms_normed(tokens, norm_gain)
    def block(step):
        return lax.dynamic_slice_in_dim(normed, (row ^ step) * features, features, 1)

    from_core = swap(jnp.stack([block(chip * CORES + 1) for chip in range(chips)]), "rows", row_count, 1)
    to_chips_rows = [stack([block(chip * CORES), from_core[chip]], [])[0] for chip in range(1, chips)]
    first, token = stack([block(0), from_core[0]], [*to_chips_rows[:1], side])
    gate_kept, token = masked(gate_weight, gate_mask, tile_of(features, 256), place, 1, lambda core: 0, [token])
    second = [swap(part, "rows", row_count, (chip + 1) * CORES) for chip, part in enumerate(to_chips_rows)]
    second = jnp.concatenate(second, 1) if len(second) > 1 else second[0]
    mine, token = join([first, second], [token])

    def behind(values, after):
        return lax.optimization_barrier((values, *after))[0] if after else values

    def by_plane(values, planes, after=()):
        pairs = [(a * per_plane + b, c * per_plane + b) for a, c in planes for b in range(per_plane)]
        return lax.ppermute(behind(values, after), "cols", pairs)

    def by_row_of_plane(values, step, after=()):
        return swap(behind(values, after), "cols", col_count, step)

    def by_chip(values, chip, after=()):
        return swap(behind(values, after), "rows", row_count, chip * CORES)

    def by_core(values, after=()):
        return swap(behind(values, after), "rows", row_count, 1)

    parts, halves, near, far, chip_sums, hiddens, others, rows_in, partials, sent = ({} for _ in range(10))
    last = [token]

    def forward(plane, values, after=()):
        parts[plane] = [values]
        for step in range(1, per_plane):
            parts[plane].append(by_row_of_plane(values, step, after))

    def multiply_in(plane, far_parts=1, hint=HURRY, after=()):
        parts_after = last + list(after)
        *halves[plane], last[0] = gate_up(parts[plane], gate_kept, up_kept, chips, far_parts, hint, parts_after)

    def exchange(plane, after=()):
        far[plane] = [by_core(part, after) for part in halves[plane][2:]]

    def exchange_near(plane, after=()):
        near[plane] = by_core(halves[plane][1], after)

    def multiply_out(plane, pieces=1, after=()):
        *partials[plane], last[0] = down(hiddens[plane], others[plane], down_kept, pieces, last + list(after))

    def send_rows(plane, after=(), pieces=1, piece=0):
        mine_and_others = partials[plane][piece::pieces]
        rows_in[plane, piece] = mine_and_others[:1]
        for step in range(1, per_plane):
            rows_in[plane, piece].append(by_row_of_plane(mine_and_others[step], step, after))

    def to_chips(plane, after=()):
        given = [halves[plane][0], *far[plane]]
        sent[plane], _, _, last[0] = sums(given, [], [], last + list(after))

    def send_chips(plane, after=()):
        chip_sums[plane] = [by_chip(part, number + 1, after) for number, part in enumerate(sent[plane])]

    def to_hidden(plane, after=()):
        given = [halves[plane][0], near[plane], *chip_sums[plane]]
        _, hiddens[plane], _, last[0] = sums([], given, [], last + list(after))
        others[plane] = by_core(hiddens[plane])

    def to_rows(*parts, after=(), hint=0.0):
        _, _, (summed,), last[0] = sums([], [], [parts], last + list(after), hint)
        return summed

    next_stacks = [by_plane(first, NEXT), by_plane(second, NEXT)]
    across_stacks = [by_plane(first, ACROSS), by_plane(second, ACROSS)]
    row_stacks = {
        step: [by_row_of_plane(first, step), by_row_of_plane(second, step)] for step in range(1, per_plane)
    }
    up_kept, last[0] = masked(
        up_weight, up_mask, tile_of(features, 256), place, 1, lambda core: 0, last + next_stacks[:1], 0.15
    )
    last[0] = waited([*last, across_stacks[0], *(stacks[0] for stacks in row_stacks.values())], 0.07)
    one_away, last[0] = join(next_stacks, last)
    inner_three, last[0] = join(across_stacks, last)
    outer_three = by_plane(mine, AROUND, last)
    down_kept = []

    def keep_down(share, hint=0.0):
        part, last[0] = masked(
            down_weight, down_mask, 2 * BLOCK, place, 2 * CORES, lambda core: 2 * core + share, last, hint
        )
        down_kept.append(part)

    parts[0] = [mine]
    for stacks in row_stacks.values():
        part, last[0] = join(stacks, last)
        parts[0].append(part)
    forward(1, one_away, last)
    multiply_in(0, hint=HURRY)
    exchange(0)
    exchange_near(0)
    keep_down(0)
    three_away, passed, last[0] = pick(side, inner_three, outer_three, mine, last)
    two_away = by_plane(passed, CYCLE)
    to_chips(0, [near[0]])
    forward(3, three_away, [*parts[1][1:], *last])
    multiply_in(1)
    exchange(1)
    exchange_near(1)
    to_chips(1, [near[1]])
    send_chips(1)
    keep_down(1)
    forward(2, two_away, last)
    multiply_in(3, after=[two_away])
    exchange(3)
    exchange_near(3)
    to_hidden(1)
    to_chips(3, [near[3]])
    send_chips(3)
    multiply_out(1)
    send_rows(1, parts[2][1:])
    multiply_in(2, far_parts=2)
    exchange(2)
    to_hidden(3)
    to_chips(2)
    send_chips(2)
    exchange_near(2, last)
    multiply_out(3, pieces=CORES)
    send_rows(3, rows_in[1, 0][1:], CORES, 1)
    one = to_rows(*rows_in[1, 0])
    one_out = by_plane(one, NEXT)
    three = to_rows(*rows_in[3, 1])
    send_rows(3, [three], CORES, 0)
    three_out, two_out = {1: by_plane(three, NEXT)}, {}
    to_hidden(2)
    send_chips(0, chip_sums[2])
    multiply_out(2, pieces=CORES)
    three = to_rows(*rows_in[3, 0], after=[one_out])
    three_out[0] = by_plane(three, NEXT)
    send_rows(2, rows_in[3, 0][1:], CORES, 1)
    two = to_rows(*rows_in[2, 1], three_out[1])
    two_out[1] = by_plane(two, SECOND)
    send_rows(2, [two], CORES, 0)
    to_hidden(0)
    multiply_out(0)
    two = to_rows(rows_in[2, 0][0], three_out[0], hint=0.1)
    two = to_rows(two, *rows_in[2, 0][1:])
    two_out[0] = by_plane(two, SECOND)
    send_rows(0, rows_in[2, 0][1:])

    joined = to_rows(two_out[1], one_out, hint=10.0)

    def total(piece, *parts):
        whole = [part[piece].astype(F32) for part in rows_in[0, 0]] + [part.astype(F32) for part in parts]
        return sum(whole[1:], whole[0]).astype(BF16)

    mine_now, other = total(0, one_out[0], two_out[0][0]), by_core(total(1, joined[0]))
    left = jnp.where(core == 0, mine_now, other)
    right = jnp.where(core == 0, other, mine_now)
    return jnp.concatenate([left, right], 1)


def solution(mesh):
    return jax.shard_map(
        functools.partial(body, mesh.shape["rows"], mesh.shape["cols"]),
        mesh=mesh,
        in_specs=(
            P(("rows", "cols"), None),
            P(),
            P("rows", "cols"),
            P("rows", "cols"),
            P("cols", None),
            P("rows", "cols"),
            P("rows", "cols"),
            P("cols", None),
        ),
        out_specs=P(("rows", "cols"), None),
        check_vma=False,
    )
```
